32 devices in a mesh: dp: 8 (over y, x, core), mp: 4 (over z).
Axes of the slice: x: 2, y: 2, z: 4, core: 2. Of those that a mesh axis runs over, the one named last changes fastest.
Arguments:
- tokens: int32 [8, 1024], P('dp'), may hold values from 0 to 31
- lengths: int32 [8], P('dp'), may hold values from 30 to 1024, as said below
- tile_owner: int32 [192], replicated, may hold values from 0 to 191, each once
- step_count: int32 [], replicated, may hold values from 2 to 20
- weight_tiles: float32 [192, 128, 512], P('dp', None, 'mp'), may hold values from -0.1875 to 0.1875
- tiles_first: float32 [192, 128, 512], P('dp', None, 'mp'), may hold values from -9.536743e-06 to 9.536743e-06
- tiles_second: float32 [192, 128, 512], P('dp', None, 'mp'), may hold values from 1.6590697e-12 to 6.6520795e-12
- stats_left: float32 [192, 128, 512], P('dp', None, 'mp'), as said below
- stats_right: float32 [192, 128, 512], P('dp', None, 'mp'), as said below
- basis_left: float32 [192, 128, 512], P('dp', None, 'mp'), as said below
- basis_right: float32 [192, 128, 512], P('dp', None, 'mp'), as said below
- embedding: float32 [32, 1024], replicated, may hold values from -6 to 6
- embedding_first: float32 [32, 1024], replicated, may hold values from -2.670288e-05 to 2.670288e-05
- embedding_second: float32 [32, 1024], replicated, may hold values from 3.7329067e-13 to 1.4971129e-12
- head_table: float32 [1025, 32], replicated, may hold values from -0.1875 to 0.1875
- head_first: float32 [1025, 32], replicated, may hold values from -2.670288e-05 to 2.670288e-05
- head_second: float32 [1025, 32], replicated, may hold values from 1.4931627e-11 to 5.9884514e-11
- vectors: float32 [5, 1024], replicated
- vectors_first: float32 [5, 1024], replicated, may hold values from -2.670288e-05 to 2.670288e-05
- vectors_second: float32 [5, 1024], replicated, may hold values from 1.4931627e-11 to 5.9884514e-11
- fc_bias: float32 [1, 4096], P(None, 'mp'), may hold values from -4 to 4
- fc_bias_first: float32 [1, 4096], P(None, 'mp'), may hold values from -2.670288e-05 to 2.670288e-05
- fc_bias_second: float32 [1, 4096], P(None, 'mp'), may hold values from 1.4931627e-11 to 5.9884514e-11
Outputs:
- loss: float32 [], replicated
- grad_norm: float32 [], replicated
- new_tiles: float32 [192, 128, 512], P('dp', None, 'mp')
- tiles_low: bfloat16 [192, 128, 512], P('dp', None, 'mp')
- new_tiles_first: float32 [192, 128, 512], P('dp', None, 'mp')
- new_tiles_second: float32 [192, 128, 512], P('dp', None, 'mp')
- new_stats_left: float32 [192, 128, 512], P('dp', None, 'mp')
- new_stats_right: float32 [192, 128, 512], P('dp', None, 'mp')
- new_basis_left: float32 [192, 128, 512], P('dp', None, 'mp')
- new_basis_right: float32 [192, 128, 512], P('dp', None, 'mp')
- new_embedding: float32 [32, 1024], replicated
- new_embedding_first: float32 [32, 1024], replicated
- new_embedding_second: float32 [32, 1024], replicated
- new_head: float32 [1025, 32], replicated
- new_head_first: float32 [1025, 32], replicated
- new_head_second: float32 [1025, 32], replicated
- new_vectors: float32 [5, 1024], replicated
- new_vectors_first: float32 [5, 1024], replicated
- new_vectors_second: float32 [5, 1024], replicated
- new_fc_bias: float32 [1, 4096], P(None, 'mp')
- new_fc_bias_first: float32 [1, 4096], P(None, 'mp')
- new_fc_bias_second: float32 [1, 4096], P(None, 'mp')
The draws below stay inside these ranges and needn't reach their ends.
Inputs may be any that keep to these rules, and one draw needn't show every extreme that they name: `lengths`: the 1 proteins of one length bucket stand in consecutive rows; some protein has length 1024. `tile_owner`: A permutation. `stats_left`: each tile is symmetric positive definite. `stats_right`: each tile is symmetric positive definite. `basis_left`: each tile has orthonormal columns. `basis_right`: each tile has orthonormal columns.
All inputs are finite; a program needn't handle non-finite values.
Results may differ from the reference program's by a relative error of at most 0.0063.
The reference program's roundings to bfloat16 on the way count: a program that leaves them out, or rounds other values in their place, can miss the bound.
Values may be sent and summed in bfloat16 or wider, within the bound.
No kernel may reach another device: no remote copies, remote signals or barrier semaphores. Data moves between devices by JAX's collectives and lax.ppermute only.
A program may use at most 192 MiB of HBM per device.

```python
import math
import jax
import jax.numpy as jnp
import numpy as np
from jax import lax

D = 1024
H = 16
HD = 64
FF = 4096
VOCAB = 32
ROT = 32
LAYERS = 1
LEN = 1024
P_DEV = 1
BS = 128
GROUPS = 4
PROTEINS = 8
NBM = 192
MPBS = 512
PARAMS = 12657696


def draw_lengths(key, part):
    floor_len = min(30, LEN // 2)
    group_total = PROTEINS // P_DEV
    tops = jax.random.randint(jax.random.fold_in(key, 1), (group_total,), LEN // 4, LEN + 1)
    tops = jnp.maximum(tops, 2 * floor_len)
    per_top = jnp.repeat(tops, P_DEV)
    lowest = jnp.maximum(per_top // 2, floor_len)
    picks = jax.random.randint(jax.random.fold_in(key, 2), (PROTEINS,), 0, 1 << 20)
    drawn = lowest + picks % (per_top - lowest + 1)
    order = jax.random.permutation(jax.random.fold_in(key, 3), PROTEINS)
    drawn = drawn.at[order[0]].set(LEN)
    drawn = drawn.at[order[1]].set(floor_len)
    return drawn.astype(jnp.int32)


def stats_draw(key):
    group_total = MPBS // BS
    scale_base = 0.0526 * BS * 0.0004 / PARAMS
    level = jax.random.uniform(jax.random.fold_in(key, 1), (NBM, 1, group_total, 1), minval=1.0, maxval=4.0)
    diagonal = jax.random.uniform(jax.random.fold_in(key, 2), (NBM, BS, group_total, 1), minval=0.7, maxval=1.4)
    noise = jax.random.uniform(jax.random.fold_in(key, 3), (NBM, BS, group_total, BS), minval=-1.0, maxval=1.0)
    symmetric = 0.5 * (noise + jnp.transpose(noise, (0, 3, 2, 1))) * (0.6 / BS)
    identity = (jnp.arange(BS)[:, None] == jnp.arange(BS)[None, :]).astype(jnp.float32)[:, None, :]
    matrix = symmetric * (1.0 - identity) + identity * diagonal
    return (level * scale_base * matrix).reshape(NBM, BS, MPBS).astype(jnp.float32)


def basis_draw(key):
    group_total = MPBS // BS
    tile_count = NBM * group_total
    keys_all = jax.random.split(jax.random.fold_in(key, 11), tile_count)
    orders = jax.vmap(lambda one_key: jax.random.permutation(one_key, BS))(keys_all)
    frequency = orders.astype(jnp.float32)
    signs = (2 * jax.random.randint(jax.random.fold_in(key, 12), (tile_count, BS), 0, 2) - 1).astype(jnp.float32)
    row_ids = jnp.arange(BS, dtype=jnp.float32)
    cosines = jnp.cos(math.pi * (row_ids[None, :, None] + 0.5) * frequency[:, None, :] / BS)
    scales = jnp.where(frequency == 0.0, math.sqrt(1.0 / BS), math.sqrt(2.0 / BS))
    basis = signs[:, :, None] * cosines * scales[:, None, :]
    return jnp.transpose(basis.reshape(NBM, group_total, BS, BS), (0, 2, 1, 3)).reshape(NBM, BS, MPBS).astype(jnp.float32)


def draw_stats_left(key, part):
    return stats_draw(jax.random.fold_in(key, 201))


def draw_stats_right(key, part):
    return stats_draw(jax.random.fold_in(key, 202))


def draw_basis_left(key, part):
    return basis_draw(jax.random.fold_in(key, 101))


def draw_basis_right(key, part):
    return basis_draw(jax.random.fold_in(key, 102))


def draw_vectors(key, part):
    row_total = 3 * LAYERS + 2
    base = jax.random.normal(key, (row_total, D), jnp.float32)
    row_ids = jnp.arange(row_total)[:, None]
    is_gain = (row_ids % 3 == 0) & (row_ids < 3 * LAYERS) | (row_ids == 3 * LAYERS)
    return jnp.where(is_gain, 1.0 + 0.2 * base, 0.3 * base).astype(jnp.float32)


def touch_ends(values, own_key, least, largest):
    dims = values.shape
    index_at = [jax.random.randint(jax.random.fold_in(own_key, axis), (), 0, dims[axis]) for axis in range(len(dims))]
    values = values.at[tuple(index_at)].set(least)
    longest = dims.index(max(dims))
    index_at[longest] = (index_at[longest] + 1) % dims[longest]
    return values.at[tuple(index_at)].set(largest)


def level_of(stream_key, extent, cuts, smallest, largest):
    factor_of, own = 1.0, jax.random.fold_in(stream_key, 6)
    for axis_at, blocks in cuts:
        heights = jnp.exp(jax.random.uniform(jax.random.fold_in(own, axis_at), (blocks,), jnp.float32, smallest / len(cuts), largest / len(cuts)))
        factor_of = factor_of * jnp.repeat(heights, extent[axis_at] // blocks).reshape([-1 if axis == axis_at else 1 for axis in range(len(extent))])
    return factor_of


def rank_table(count, lean):
    weights = [(1 << 20) // math.isqrt(rank ** lean) + 1 for rank in range(1, count + 1)]
    deviation = 1 + sum(weights) // (1 << 30)
    return np.cumsum(np.array([max(1, weight // deviation) for weight in weights]))


def skewed_ids(stream_key, dims, count, lean):
    grid = rank_table(count, lean)
    pick = jax.random.randint(jax.random.fold_in(stream_key, 1), dims, 0, int(grid[count - 1]))
    rank = jnp.searchsorted(jnp.asarray(grid, jnp.int32), pick, side="right")
    return jax.random.permutation(jax.random.fold_in(stream_key, 2), count)[rank].astype(jnp.int32)


def scatter_about(key, shape, width, most, pieces=(), held_as=jnp.bfloat16):
    values = jax.random.normal(key, shape, jnp.float32) * width
    if len(pieces) > 0:
        values = level_of(key, shape, pieces, -0.22, 0.18) * values
    return jnp.clip(values, min=-most, max=most).astype(held_as)


def setup_inputs(seed: int = 0) -> dict:
    keys = jax.random.split(jax.random.key(seed), 24)
    tokens = touch_ends(skewed_ids(keys[0], (PROTEINS, LEN), VOCAB, 1), jax.random.fold_in(keys[0], 3), 0, VOCAB - 1).astype(jnp.int32)
    lengths = draw_lengths(jax.random.fold_in(keys[23], 71), 0)
    tile_owner = jax.random.permutation(keys[2], NBM).astype(jnp.int32)
    step_count = jax.random.randint(keys[3], (), 2, 21).astype(jnp.int32)
    weight_tiles = scatter_about(keys[4], (NBM, BS, MPBS), D ** -0.5, 0.1875, ((0, 8), (2, 4)), jnp.float32)
    tiles_first = scatter_about(keys[5], (NBM, BS, MPBS), (0.0022 * PARAMS ** -0.5), 9.5367431640625e-06, ((0, 8), (2, 4)), jnp.float32)
    tiles_second = jnp.clip(jnp.exp(math.log(6.652079494878782e-12) - 1.3886725 * jax.random.uniform(keys[6], (NBM, BS, MPBS), jnp.float32) ** level_of(keys[6], (NBM, BS, MPBS), ((0, 8), (2, 4)), -0.2, 0.2)), 1.6590696915244618e-12, 6.652079494878782e-12)
    stats_left = draw_stats_left(jax.random.fold_in(keys[23], 71), 0)
    stats_right = draw_stats_right(jax.random.fold_in(keys[23], 71), 0)
    basis_left = draw_basis_left(jax.random.fold_in(keys[23], 71), 0)
    basis_right = draw_basis_right(jax.random.fold_in(keys[23], 71), 0)
    embedding = scatter_about(keys[11], (VOCAB, D), 1.0, 6.0, (), jnp.float32)
    embedding_first = scatter_about(keys[12], (VOCAB, D), (0.0067 * PARAMS ** -0.5), 2.6702880859375e-05, (), jnp.float32)
    embedding_second = jnp.clip(jnp.exp(jax.random.uniform(keys[13], (VOCAB, D), jnp.float32, math.log(3.732906724614876e-13), math.log(1.4971128720411842e-12))), 3.732906724614876e-13, 1.4971128720411842e-12)
    head_table = scatter_about(keys[14], (D + 1, VOCAB), D ** -0.5, 0.1875, (), jnp.float32)
    head_first = scatter_about(keys[15], (D + 1, VOCAB), (0.0067 * PARAMS ** -0.5), 2.6702880859375e-05, (), jnp.float32)
    head_second = jnp.clip(jnp.exp(jax.random.uniform(keys[16], (D + 1, VOCAB), jnp.float32, math.log(1.493162711529994e-11), math.log(5.988451401428563e-11))), 1.493162711529994e-11, 5.988451401428563e-11)
    vectors = draw_vectors(jax.random.fold_in(keys[23], 71), 0)
    vectors_first = scatter_about(keys[18], (3 * LAYERS + 2, D), (0.0067 * PARAMS ** -0.5), 2.6702880859375e-05, (), jnp.float32)
    vectors_second = jnp.clip(jnp.exp(jax.random.uniform(keys[19], (3 * LAYERS + 2, D), jnp.float32, math.log(1.493162711529994e-11), math.log(5.988451401428563e-11))), 1.493162711529994e-11, 5.988451401428563e-11)
    fc_bias = scatter_about(keys[20], (LAYERS, FF), 0.3, 4.0, ((1, 4),), jnp.float32)
    fc_bias_first = scatter_about(keys[21], (LAYERS, FF), (0.0067 * PARAMS ** -0.5), 2.6702880859375e-05, ((1, 4),), jnp.float32)
    fc_bias_second = jnp.clip(jnp.exp(math.log(5.988451401428563e-11) - 1.3889364 * jax.random.uniform(keys[22], (LAYERS, FF), jnp.float32) ** level_of(keys[22], (LAYERS, FF), ((1, 4),), -0.2, 0.2)), 1.493162711529994e-11, 5.988451401428563e-11)
    return {"tokens": tokens, "lengths": lengths, "tile_owner": tile_owner, "step_count": step_count, "weight_tiles": weight_tiles, "tiles_first": tiles_first, "tiles_second": tiles_second, "stats_left": stats_left, "stats_right": stats_right, "basis_left": basis_left, "basis_right": basis_right, "embedding": embedding, "embedding_first": embedding_first, "embedding_second": embedding_second, "head_table": head_table, "head_first": head_first, "head_second": head_second, "vectors": vectors, "vectors_first": vectors_first, "vectors_second": vectors_second, "fc_bias": fc_bias, "fc_bias_first": fc_bias_first, "fc_bias_second": fc_bias_second}


@jax.custom_vjp
def low(v):
    return lax.optimization_barrier(v.astype(jnp.bfloat16)).astype(jnp.float32)

@jax.custom_vjp
def low_back(v):
    return v

def low_keep(v):
    return (low(v), None)

def low_pass(kept, grad):
    return (grad,)

def back_keep(v):
    return (v, None)

def back_low(kept, grad):
    return (low(grad),)
low.defvjp(low_keep, low_pass)
low_back.defvjp(back_keep, back_low)
PRECISE = lax.Precision.HIGHEST
NORM_EPS = 1e-05
CLIP_NORM = 0.02
RATE_TILES = 0.02
RATE_SMALL = 0.2
BETA_ONE = 0.9
BETA_TWO = 0.95
ADAM_EPS = 1e-08
WEIGHT_DECAY = 0.01

def layer_norm(values, scale_row, shift_row):
    centred = values - lax.optimization_barrier(jnp.mean(values, axis=-1, keepdims=True))
    spread = lax.optimization_barrier(jnp.mean(centred * centred, axis=-1, keepdims=True))
    return centred * lax.rsqrt(spread + NORM_EPS) * scale_row + shift_row

def rotary(values, positions, direction):
    half_rot = ROT // 2
    frequency = 10000.0 ** (-2.0 * jnp.arange(half_rot, dtype=jnp.float32) / ROT)
    angles = positions.astype(jnp.float32)[:, None] * frequency[None, :]
    cosine = jnp.cos(angles)[:, None, :]
    sine_part = direction * jnp.sin(angles)[:, None, :]
    front_part = values[..., :half_rot]
    back_part = values[..., half_rot:ROT]
    return jnp.concatenate([front_part * cosine - back_part * sine_part, back_part * cosine + front_part * sine_part, values[..., ROT:]], axis=-1)

def tiles_to_matrix(tiles, row_total, col_total):
    leading = tiles.shape[:-3]
    tile_grid = tiles.reshape(leading + (row_total // BS, col_total // BS, BS, BS))
    tile_grid = jnp.swapaxes(tile_grid, -3, -2)
    return tile_grid.reshape(leading + (row_total, col_total))

def matrix_to_tiles(matrix):
    leading = matrix.shape[:-2]
    row_total, col_total = matrix.shape[-2:]
    tile_grid = matrix.reshape(leading + (row_total // BS, BS, col_total // BS, BS))
    tile_grid = jnp.swapaxes(tile_grid, -3, -2)
    return tile_grid.reshape(leading + (row_total // BS * (col_total // BS), BS, BS))

def split_layer(tiles, heads_local, ff_local):
    shapes = ((D, 3 * heads_local * HD), (heads_local * HD, D), (D, ff_local), (ff_local, D))
    result = []
    offset = 0
    for row_total, col_total in shapes:
        amount = row_total // BS * (col_total // BS)
        result.append(tiles_to_matrix(tiles[..., offset:offset + amount, :, :], row_total, col_total))
        offset = offset + amount
    return result

def orthonormal(product):
    gram_matrix = jnp.einsum('...ji,...jk->...ik', product, product, precision=PRECISE)
    lower_factor = lax.linalg.cholesky(gram_matrix)
    return lax.linalg.triangular_solve(lower_factor, product, left_side=False, lower=True, transpose_a=True)

def soap_update(weight, gradient, first_moment, second_moment, stats_one, stats_two, basis_one, basis_two, correct_one, correct_two):
    outer_one = jnp.einsum('...ij,...kj->...ik', gradient, gradient, precision=PRECISE)
    outer_two = jnp.einsum('...ji,...jk->...ik', gradient, gradient, precision=PRECISE)
    stats_one_new = BETA_TWO * stats_one + (1.0 - BETA_TWO) * outer_one
    stats_two_new = BETA_TWO * stats_two + (1.0 - BETA_TWO) * outer_two
    rotated = jnp.einsum('...ji,...jk->...ik', basis_one, gradient, precision=PRECISE)
    rotated = jnp.einsum('...ij,...jk->...ik', rotated, basis_two, precision=PRECISE)
    first_new = BETA_ONE * first_moment + (1.0 - BETA_ONE) * rotated
    second_new = BETA_TWO * second_moment + (1.0 - BETA_TWO) * rotated * rotated
    scaled = first_new / correct_one / (jnp.sqrt(second_new / correct_two) + ADAM_EPS)
    returned = jnp.einsum('...ij,...jk->...ik', basis_one, scaled, precision=PRECISE)
    returned = jnp.einsum('...ij,...kj->...ik', returned, basis_two, precision=PRECISE)
    weight_new = weight - RATE_TILES * (returned + WEIGHT_DECAY * weight)
    mixed_one = jnp.einsum('...ij,...jk->...ik', stats_one_new, basis_one, precision=PRECISE)
    mixed_two = jnp.einsum('...ij,...jk->...ik', stats_two_new, basis_two, precision=PRECISE)
    return (weight_new, first_new, second_new, stats_one_new, stats_two_new, orthonormal(mixed_one), orthonormal(mixed_two))

def adamw_update(weight, gradient, first_moment, second_moment, correct_one, correct_two):
    first_new = BETA_ONE * first_moment + (1.0 - BETA_ONE) * gradient
    second_new = BETA_TWO * second_moment + (1.0 - BETA_TWO) * gradient * gradient
    scaled = first_new / correct_one / (jnp.sqrt(second_new / correct_two) + ADAM_EPS)
    return (weight - RATE_SMALL * (scaled + WEIGHT_DECAY * weight), first_new, second_new)

def protein_loss(weight_set, tokens_row, length, tile_owner):
    weight_tiles, embedding, head_table, vectors, fc_bias = weight_set
    heads_local = H // GROUPS
    ff_local = FF // GROUPS
    rounded = low(weight_tiles).reshape(NBM, BS, GROUPS, BS)
    per_group = jnp.transpose(rounded, (2, 0, 1, 3))
    natural = jnp.take(per_group, tile_owner, axis=1).reshape(GROUPS, LAYERS, -1, BS, BS)
    positions = jnp.arange(LEN, dtype=jnp.int32)
    allowed = (positions[None, :] <= positions[:, None]) & (positions[None, :] < length)
    residual = jnp.take(embedding, tokens_row, axis=0)
    for layer_index in range(LAYERS):
        qkv_w, out_w, up_w, down_w = split_layer(natural[:, layer_index], heads_local, ff_local)
        normed = low(layer_norm(residual, vectors[3 * layer_index], vectors[3 * layer_index + 1]))
        projected = low_back(jnp.einsum('td,mdc->tmc', normed, qkv_w, precision=PRECISE))
        projected = projected.reshape(LEN, GROUPS, 3, heads_local, HD)
        queries = low(rotary(projected[:, :, 0].reshape(LEN, H, HD), positions, 1.0))
        key_rows = low(rotary(projected[:, :, 1].reshape(LEN, H, HD), positions, 1.0))
        values = low(projected[:, :, 2].reshape(LEN, H, HD))
        scores = low_back(jnp.einsum('qhe,khe->hqk', queries, key_rows, precision=PRECISE)) * (1.0 / math.sqrt(HD))
        scores = jnp.where(allowed[None], scores, -1e+30)
        exponent = jnp.exp(scores - lax.optimization_barrier(jnp.max(scores, axis=-1, keepdims=True)))
        weights_soft = exponent / lax.optimization_barrier(jnp.sum(exponent, axis=-1, keepdims=True))
        attended = low(low_back(jnp.einsum('hqk,khe->qhe', low(weights_soft), values, precision=PRECISE)))
        attended = attended.reshape(LEN, GROUPS, heads_local * HD)
        upper_pre = low_back(jnp.einsum('td,mdf->tmf', normed, up_w, precision=PRECISE) + fc_bias[layer_index].reshape(GROUPS, ff_local))
        activated = low(jax.nn.gelu(upper_pre, approximate=True))
        branch = jnp.einsum('tmc,mcd->td', attended, out_w, precision=PRECISE) + jnp.einsum('tmf,mfd->td', activated, down_w, precision=PRECISE)
        residual = residual + low_back(branch + vectors[3 * layer_index + 2])
    final_low = low(layer_norm(residual, vectors[3 * LAYERS], vectors[3 * LAYERS + 1]))
    logits = low_back(jnp.dot(final_low, low(head_table[:-1]), precision=PRECISE) + head_table[-1])
    shifted = logits - lax.optimization_barrier(jnp.max(logits, axis=-1, keepdims=True))
    log_probs = shifted - jnp.log(lax.optimization_barrier(jnp.sum(jnp.exp(shifted), axis=-1, keepdims=True)))
    targets = jnp.roll(tokens_row, -1)
    picked = lax.optimization_barrier(jnp.sum(jnp.where(targets[:, None] == jnp.arange(VOCAB, dtype=jnp.int32)[None, :], log_probs, 0.0), axis=-1))
    slot_weight = jnp.where(positions < length - 1, 1.0 / (length - 1).astype(jnp.float32), 0.0)
    return -jnp.sum(slot_weight * picked)

def as_blocks(array):
    return jnp.transpose(array.reshape(NBM, BS, GROUPS, BS), (0, 2, 1, 3))

def from_blocks(array):
    return jnp.transpose(array, (0, 2, 1, 3)).reshape(NBM, BS, GROUPS * BS)

def reference(tokens, lengths, tile_owner, step_count, weight_tiles, tiles_first, tiles_second, stats_left, stats_right, basis_left, basis_right, embedding, embedding_first, embedding_second, head_table, head_first, head_second, vectors, vectors_first, vectors_second, fc_bias, fc_bias_first, fc_bias_second):
    weight_set = (weight_tiles, embedding, head_table, vectors, fc_bias)

    def one_protein(carried, protein_item):
        tokens_row, length = protein_item
        loss_value, pull_back = jax.vjp(lambda *weights: protein_loss(weights, tokens_row, length, tile_owner), *weight_set)
        gradients = pull_back(jnp.ones_like(loss_value))
        return ((carried[0] + loss_value, jax.tree.map(jnp.add, carried[1], tuple(gradients))), None)
    start = (jnp.zeros((), jnp.float32), jax.tree.map(jnp.zeros_like, weight_set))
    (loss_sum, gradients), unused = lax.scan(one_protein, start, (tokens, lengths))
    protein_count = jnp.sum((lengths >= 2).astype(jnp.float32))
    gradients = jax.tree.map(lambda grad_part: grad_part / protein_count, gradients)
    grad_norm = jnp.sqrt(sum((jnp.sum(grad_part * grad_part) for grad_part in gradients)))
    factor = jnp.minimum(1.0, CLIP_NORM / grad_norm)
    clipped = [factor * grad_part for grad_part in gradients]
    correct_one = 1.0 - jnp.power(BETA_ONE, step_count.astype(jnp.float32))
    correct_two = 1.0 - jnp.power(BETA_TWO, step_count.astype(jnp.float32))
    results = soap_update(as_blocks(weight_tiles), as_blocks(clipped[0]), as_blocks(tiles_first), as_blocks(tiles_second), as_blocks(stats_left), as_blocks(stats_right), as_blocks(basis_left), as_blocks(basis_right), correct_one, correct_two)
    results = [from_blocks(item_part) for item_part in results]
    embed_out = adamw_update(embedding, clipped[1], embedding_first, embedding_second, correct_one, correct_two)
    head_out = adamw_update(head_table, clipped[2], head_first, head_second, correct_one, correct_two)
    vector_out = adamw_update(vectors, clipped[3], vectors_first, vectors_second, correct_one, correct_two)
    bias_out = adamw_update(fc_bias, clipped[4], fc_bias_first, fc_bias_second, correct_one, correct_two)
    return (loss_sum / protein_count, grad_norm, results[0], results[0].astype(jnp.bfloat16), results[1], results[2], results[3], results[4], results[5], results[6], embed_out[0], embed_out[1], embed_out[2], head_out[0], head_out[1], head_out[2], vector_out[0], vector_out[1], vector_out[2], bias_out[0], bias_out[1], bias_out[2])
```

```python
import functools
import math

import jax
import jax.numpy as jnp
from jax import lax
from jax.experimental import pallas as pl
from jax.experimental.pallas import tpu as pltpu
from jax.sharding import PartitionSpec as P

D = 1024
H = 16
HD = 64
ROT = 32
LAYERS = 1
BS = 128


PRECISE = lax.Precision.HIGHEST
NORM_EPS = 1e-05
CLIP_NORM = 0.02
RATE_TILES = 0.02
RATE_SMALL = 0.2
BETA_ONE = 0.9
BETA_TWO = 0.95
ADAM_EPS = 1e-08
WEIGHT_DECAY = 0.01


def layer_norm(values, scale_row, shift_row):
    centred = values - jnp.mean(values, axis=-1, keepdims=True)
    spread = jnp.mean(centred * centred, axis=-1, keepdims=True)
    return centred * lax.rsqrt(spread + NORM_EPS) * scale_row + shift_row


def rotary(values, positions, direction):
    half_rot = ROT // 2
    frequency = 10000.0 ** (-2.0 * jnp.arange(half_rot, dtype=jnp.float32) / ROT)
    angles = positions.astype(jnp.float32)[:, None] * frequency[None, :]
    cosine = jnp.cos(angles)[:, None, :]
    sine_part = direction * jnp.sin(angles)[:, None, :]
    front_part = values[..., :half_rot]
    back_part = values[..., half_rot:ROT]
    return jnp.concatenate(
        [
            front_part * cosine - back_part * sine_part,
            back_part * cosine + front_part * sine_part,
            values[..., ROT:],
        ],
        axis=-1,
    )


def layer_shapes(heads_local, ff_local):
    return ((D, 3 * heads_local * HD), (heads_local * HD, D), (D, ff_local), (ff_local, D))


def tile_places(shapes):
    places = []
    for which, (row_total, col_total) in enumerate(shapes):
        for i in range(row_total // BS):
            for k in range(col_total // BS):
                places.append((which, i * BS, k * BS))
    return places


def assemble_kernel(places, owner, tiles, *matrices):
    for index, (which, row, col) in enumerate(places):
        matrices[which][row : row + BS, col : col + BS] = tiles[owner[index]]


def assemble(tile_owner, tiles, shapes):
    return pl.pallas_call(
        functools.partial(assemble_kernel, tile_places(shapes)),
        in_specs=[
            pl.BlockSpec(memory_space=pltpu.SMEM),
            pl.BlockSpec(memory_space=pltpu.VMEM),
        ],
        out_specs=[pl.BlockSpec(memory_space=pltpu.VMEM)] * len(shapes),
        out_shape=[jax.ShapeDtypeStruct(shape, tiles.dtype) for shape in shapes],
        compiler_params=pltpu.CompilerParams(vmem_limit_bytes=56 * 1024 * 1024),
        name="assemble",
    )(tile_owner, tiles)


def scatter_kernel(places, owner, *refs):
    tiles = refs[-1]
    for index, (which, row, col) in enumerate(places):
        tiles[owner[index]] = refs[which][row : row + BS, col : col + BS]


def scatter_tiles(tile_owner, matrices):
    shapes = [matrix.shape for matrix in matrices]
    places = tile_places(shapes)
    return pl.pallas_call(
        functools.partial(scatter_kernel, places),
        in_specs=[pl.BlockSpec(memory_space=pltpu.SMEM)]
        + [pl.BlockSpec(memory_space=pltpu.VMEM)] * len(matrices),
        out_specs=pl.BlockSpec(memory_space=pltpu.VMEM),
        out_shape=jax.ShapeDtypeStruct((len(places), BS, BS), matrices[0].dtype),
        compiler_params=pltpu.CompilerParams(vmem_limit_bytes=56 * 1024 * 1024),
        name="scatter",
    )(tile_owner, *matrices)


HB = 64
GROUP = 0
UN = 3
NN = (((1,), (0,)), ((), ()))
NT = (((1,), (1,)), ((), ()))
TN = (((0,), (0,)), ((), ()))
f32 = jnp.float32
bf16 = jnp.bfloat16

def split(a):
    hi=a.astype(bf16)
    return hi,(a-hi.astype(f32)).astype(bf16)

def split3(a):
    h=a.astype(bf16); r=a-h.astype(f32); m=r.astype(bf16); return h,m,(r-m.astype(f32)).astype(bf16)

def stack(parts,dims_axis):
    return jnp.concatenate(parts,axis=dims_axis)

def sdot3(a,b,dims):
    (ca,),(cb,)=dims[0]
    ah,al=split(a); bh,bl=split(b)
    return lax.dot_general(stack([ah,ah,al],ca),stack([bh,bl,bh],cb),dims,preferred_element_type=f32)

def sdot6(a,b,dims):
    (ca,),(cb,)=dims[0]
    ah,am,al=split3(a); bh,bm,bl=split3(b)
    return lax.dot_general(stack([ah,ah,am,am,ah,al],ca),stack([bh,bm,bh,bm,bl,bh],cb),dims,preferred_element_type=f32)

D3=sdot3
D6=sdot6

def eliminate(work, count):
    lane=lax.broadcasted_iota(jnp.int32,(HB,BS),1)
    sub=lax.broadcasted_iota(jnp.int32,(HB,BS),0)
    half=jnp.where(lane>=HB,HB,0)
    for g0 in range(HB//8):
        r0=8*g0
        rows=HB-r0
        def body(jj,carry):
            j=r0+jj
            pick=half[:rows]+j
            at_pivot=lane[:rows]==pick
            below=sub[:rows]>jj
            clear=at_pivot&below
            group=GROUP or count
            for t0 in range(0,count,group):
                span=range(t0,t0+group)
                rows_in=[work[t,pl.ds(j,1),:] for t in span]
                kept=[work[t,r0:,:] for t in span]
                wides=[jnp.broadcast_to(row,(8,BS)) for row in rows_in]
                pivots=[jnp.take_along_axis(w,pick[:8],axis=1,mode="promise_in_bounds") for w in wides]
                cs=[jnp.take_along_axis(a,pick,axis=1,mode="promise_in_bounds") for a in kept]
                scaleds=[jnp.where(at_pivot[:8],1.0,w)/p for w,p in zip(wides,pivots)]
                for t,a,c,sc in zip(span,kept,cs,scaleds):
                    work[t,r0:,:]=jnp.where(clear,0.0,a)-jnp.where(below,c,0.0)*sc[:1]
            return carry
        lax.fori_loop(0,8,body,0)

def factor_inverse(packed):
    lane=lax.broadcasted_iota(jnp.int32,(HB,BS),1)
    sub=lax.broadcasted_iota(jnp.int32,(HB,BS),0)
    left=lane<HB
    col=jnp.where(left,lane,lane-HB)
    diag=jnp.where(col==sub,packed,0.0)
    d_left=jnp.sum(jnp.where(left,diag,0.0),axis=1,keepdims=True)
    d_right=jnp.sum(jnp.where(left,0.0,diag),axis=1,keepdims=True)
    scale=lax.rsqrt(jnp.where(left,d_left,d_right))
    unit=jnp.where(col<sub,packed,jnp.where(col==sub,1.0,0.0))
    return unit*scale

def block_diagonal(packed):
    lane=lax.broadcasted_iota(jnp.int32,(HB,BS),1)
    left=lane<HB
    return jnp.concatenate([jnp.where(left,packed,0.0),jnp.where(left,0.0,packed)],axis=0)

def swap(x):
    return pltpu.roll(x,HB,1)

def soap_kernel(count, per, scal, G, W, m, v, L, R, QL, QR, W_o, low_o, m_o, v_o, L_o, R_o, QL_o, QR_o, ML_s, MR_s, work, A21_s, A22_s, W11_s):
    step=pl.program_id(0)
    scale=scal[0]; c1=scal[1]; c2=scal[2]
    left=lax.broadcasted_iota(jnp.int32,(HB,BS),1)<HB
    span=range(per)
    g=[G[s].astype(f32)*scale for s in span]
    gT=[x.T for x in g]
    qT=[QL[s].T for s in span]
    ggl=[D3(x,x,NT) for x in g]
    ggr=[D3(x,x,NT) for x in gT]
    rot=[D3(q,x,NN) for q,x in zip(qT,g)]
    Ln=[BETA_TWO*L[s]+(1-BETA_TWO)*ggl[s] for s in span]
    Rn=[BETA_TWO*R[s]+(1-BETA_TWO)*ggr[s] for s in span]
    rot=[D3(x,QR[s],NN) for s,x in enumerate(rot)]
    for s in span:
        L_o[s]=Ln[s]; R_o[s]=Rn[s]
    ML=[D6(Ln[s],QL[s],NN) for s in span]
    MR=[D6(Rn[s],QR[s],NN) for s in span]
    xs=[]
    for s in span:
        mn=BETA_ONE*m[s]+(1-BETA_ONE)*rot[s]
        vn=BETA_TWO*v[s]+(1-BETA_TWO)*rot[s]*rot[s]
        m_o[s]=mn; v_o[s]=vn
        xs.append((mn/c1)/(jnp.sqrt(vn/c2)+ADAM_EPS))
    back=[D3(QL[s],xs[s],NN) for s in span]
    ML=[x*lax.rsqrt(jnp.sum(x*x,keepdims=True)) for x in ML]
    MR=[x*lax.rsqrt(jnp.sum(x*x,keepdims=True)) for x in MR]
    back=[D3(back[s],QR[s],NT) for s in span]
    AL=[D6(x,x,TN) for x in ML]
    AR=[D6(x,x,TN) for x in MR]
    for s in span:
        w=W[s]
        wn=w-RATE_TILES*(back[s]+WEIGHT_DECAY*w)
        W_o[s]=wn
        low_o[s]=wn.astype(bf16)
        t=step*per+s
        ML_s[t]=ML[s]; MR_s[t]=MR[s]
        work[t]=jnp.where(left,AL[s][:HB],swap(AR[s][:HB]))
        A21_s[t]=jnp.where(left,AL[s][HB:],swap(AR[s][HB:]))
        A22_s[t]=jnp.where(left,swap(AL[s][HB:]),AR[s][HB:])

    @pl.when(step==pl.num_programs(0)-1)
    def _():
        eliminate(work,count)
        def mid(i,carry):
            ts=[i*UN+k for k in range(UN)]
            w11=[factor_inverse(work[t]) for t in ts]
            for t,w in zip(ts,w11): W11_s[t]=w
            l21=[D6(A21_s[t],block_diagonal(w),NT) for t,w in zip(ts,w11)]
            for t,l in zip(ts,l21): A21_s[t]=l
            low=[D6(l,block_diagonal(l),NT) for l in l21]
            for t,l in zip(ts,low): work[t]=A22_s[t]-l
            return carry
        lax.fori_loop(0,count//UN,mid,0)
        eliminate(work,count)
        def last(i,carry):
            ts=[i*UN+k for k in range(UN)]
            w22=[factor_inverse(work[t]) for t in ts]
            w11=[W11_s[t] for t in ts]
            y=[D6(A21_s[t],block_diagonal(w),NN) for t,w in zip(ts,w11)]
            w21=[-D6(w,block_diagonal(x),NN) for w,x in zip(w22,y)]
            cl=[jnp.concatenate([jnp.where(left,a,0.0),jnp.where(left,b,swap(c))],axis=0) for a,b,c in zip(w11,w21,w22)]
            cr=[jnp.concatenate([jnp.where(left,swap(a),0.0),jnp.where(left,swap(b),c)],axis=0) for a,b,c in zip(w11,w21,w22)]
            ol=[D3(ML_s[t],c,NT) for t,c in zip(ts,cl)]
            orr=[D3(MR_s[t],c,NT) for t,c in zip(ts,cr)]
            for t,a,b in zip(ts,ol,orr):
                QL_o[t]=a; QR_o[t]=b
            return carry
        lax.fori_loop(0,count//UN,last,0)

def soap(scal,G,W,m,v,L,R,QL,QR):
    count=W.shape[0]
    per=3 if count%3==0 else 1
    blk=pl.BlockSpec((per,BS,BS),lambda i:(i,0,0))
    full=pl.BlockSpec((count,BS,BS),lambda i:(0,0,0))
    o=lambda dt: jax.ShapeDtypeStruct((count,BS,BS),dt)
    return pl.pallas_call(
        functools.partial(soap_kernel,count,per),
        grid=(count//per,),
        in_specs=[pl.BlockSpec(memory_space=pltpu.SMEM)]+[blk]*8,
        out_specs=[blk]*6+[full]*2,
        out_shape=[o(f32),o(bf16),o(f32),o(f32),o(f32),o(f32),o(f32),o(f32)],
        scratch_shapes=[pltpu.VMEM((count,BS,BS),f32)]*2+[pltpu.VMEM((count,HB,BS),f32)]*4,
        compiler_params=pltpu.CompilerParams(vmem_limit_bytes=56*1024*1024),
        name="soap_tiles",
    )(scal,G,W,m,v,L,R,QL,QR)

def adamw_update(weight, gradient, first_moment, second_moment, correct_one, correct_two):
    first_new = BETA_ONE * first_moment + (1.0 - BETA_ONE) * gradient
    second_new = BETA_TWO * second_moment + (1.0 - BETA_TWO) * gradient * gradient
    scaled = first_new / correct_one / (jnp.sqrt(second_new / correct_two) + ADAM_EPS)
    return (weight - RATE_SMALL * (scaled + WEIGHT_DECAY * weight), first_new, second_new)


def mixed_rows(branch_part):
    return lax.psum(branch_part, "mp")


def normed_combine(normed_grad):
    return lax.psum(normed_grad, "mp")


def block_parts(block_index, queries, key_rows, values, slot_length, block_rows, seq_len):
    row_begin = block_index * block_rows
    seq_start = row_begin // seq_len * seq_len
    query_block = lax.dynamic_slice_in_dim(queries, row_begin, block_rows, 0)
    query_pos = row_begin - seq_start + jnp.arange(block_rows, dtype=jnp.int32)
    key_pos = jnp.arange(seq_len, dtype=jnp.int32)
    allowed = (key_pos[None, :] <= query_pos[:, None]) & (key_pos[None, :] < slot_length[row_begin])
    scores = jnp.einsum(
        "qhe,khe->hqk", query_block, key_rows, preferred_element_type=jnp.float32
    ) * (1.0 / math.sqrt(HD))
    return (
        jnp.where(allowed[None], scores, -1e30),
        query_block,
        key_rows,
        values,
        row_begin,
        seq_start,
    )


def attention_forward(queries, key_rows, values, slot_length, block_rows, seq_len):
    block_count = queries.shape[0] // block_rows

    def one_block(block_index):
        scores, query_block, key_seq, value_seq, row_begin, seq_start = block_parts(
            block_index, queries, key_rows, values, slot_length, block_rows, seq_len
        )
        maximum_row = jnp.max(scores, axis=-1, keepdims=True)
        exponent = jnp.exp(scores - maximum_row)
        row_total = jnp.sum(exponent, axis=-1, keepdims=True)
        weights_soft = (exponent / row_total).astype(jnp.bfloat16)
        output = jnp.einsum(
            "hqk,khe->qhe", weights_soft, value_seq, preferred_element_type=jnp.float32
        )
        return (output, (maximum_row + jnp.log(row_total))[..., 0])

    outputs, log_totals = lax.map(one_block, jnp.arange(block_count, dtype=jnp.int32))
    return (outputs.reshape(queries.shape), log_totals)


def attention_backward(
    queries, key_rows, values, output_grad, log_totals, slot_length, block_rows, seq_len
):
    block_count = queries.shape[0] // block_rows
    scale_value = 1.0 / math.sqrt(HD)

    def one_block(carried, block_index):
        key_grad, value_grad = carried
        scores, query_block, key_seq, value_seq, row_begin, seq_start = block_parts(
            block_index, queries, key_rows, values, slot_length, block_rows, seq_len
        )
        grad_block = lax.dynamic_slice_in_dim(output_grad, row_begin, block_rows, 0)
        weights_soft = jnp.exp(scores - log_totals[block_index][..., None])
        soft_grad = jnp.einsum(
            "qhe,khe->hqk", grad_block, value_seq, preferred_element_type=jnp.float32
        )
        value_part = jnp.einsum(
            "hqk,qhe->khe",
            weights_soft.astype(jnp.bfloat16),
            grad_block,
            preferred_element_type=jnp.float32,
        )
        score_grad = (
            weights_soft * (soft_grad - jnp.sum(weights_soft * soft_grad, axis=-1, keepdims=True))
        ).astype(jnp.bfloat16)
        query_part = (
            jnp.einsum("hqk,khe->qhe", score_grad, key_seq, preferred_element_type=jnp.float32)
            * scale_value
        )
        key_part = (
            jnp.einsum("hqk,qhe->khe", score_grad, query_block, preferred_element_type=jnp.float32)
            * scale_value
        )
        key_grad = key_grad + key_part
        value_grad = value_grad + value_part
        return ((key_grad, value_grad), query_part)

    zero_grad = jnp.zeros(key_rows.shape, jnp.float32)
    (key_grad, value_grad), query_parts = lax.scan(
        one_block, (zero_grad, zero_grad), jnp.arange(block_count, dtype=jnp.int32)
    )
    return (query_parts.reshape(queries.shape), key_grad, value_grad)


def layer_forward(
    residual,
    weights,
    vectors,
    in_bias,
    layer_index,
    positions,
    slot_length,
    block_rows,
    seq_len,
    heads_local,
):
    normed = layer_norm(residual, vectors[3 * layer_index], vectors[3 * layer_index + 1]).astype(
        jnp.bfloat16
    )
    slot_count = normed.shape[0]
    projected = jnp.dot(normed, weights[0], preferred_element_type=jnp.float32).reshape(
        slot_count, 3, heads_local, HD
    )
    queries = rotary(projected[:, 0], positions, 1.0).astype(jnp.bfloat16)
    key_rows = rotary(projected[:, 1], positions, 1.0).astype(jnp.bfloat16)
    values = projected[:, 2].astype(jnp.bfloat16)
    attended, log_totals = attention_forward(
        queries, key_rows, values, slot_length, block_rows, seq_len
    )
    attended_low = attended.reshape(slot_count, heads_local * HD).astype(jnp.bfloat16)
    upper_pre = jnp.dot(normed, weights[2], preferred_element_type=jnp.float32) + in_bias
    activated = jax.nn.gelu(upper_pre, approximate=True).astype(jnp.bfloat16)
    branch_part = jnp.dot(attended_low, weights[1], preferred_element_type=jnp.float32) + jnp.dot(
        activated, weights[3], preferred_element_type=jnp.float32
    )
    branch = mixed_rows(branch_part) + vectors[3 * layer_index + 2]
    kept_values = (residual, normed, queries, key_rows, values, log_totals, attended_low, upper_pre)
    return (residual + branch, kept_values)


def layer_backward(
    residual_grad,
    kept_values,
    weights,
    vectors,
    layer_index,
    positions,
    slot_length,
    block_rows,
    seq_len,
    heads_local,
):
    residual, normed_all, queries, key_rows, values, log_totals, attended_low, upper_pre = (
        kept_values
    )
    slot_count = normed_all.shape[0]
    branch_low = residual_grad.astype(jnp.bfloat16)
    out_bias_grad = jnp.sum(branch_low.astype(jnp.float32), axis=0)
    out_weight_grad = jnp.dot(attended_low.T, branch_low, preferred_element_type=jnp.float32)
    attended_grad = (
        jnp.dot(branch_low, weights[1].T, preferred_element_type=jnp.float32)
        .astype(jnp.bfloat16)
        .reshape(slot_count, heads_local, HD)
    )
    activated = jax.nn.gelu(upper_pre, approximate=True).astype(jnp.bfloat16)
    down_grad = jnp.dot(activated.T, branch_low, preferred_element_type=jnp.float32)
    unused, gelu_pull = jax.vjp(lambda pre_act: jax.nn.gelu(pre_act, approximate=True), upper_pre)
    upper_grad = gelu_pull(jnp.dot(branch_low, weights[3].T, preferred_element_type=jnp.float32))[
        0
    ].astype(jnp.bfloat16)
    up_grad = jnp.dot(normed_all.T, upper_grad, preferred_element_type=jnp.float32)
    in_bias_grad = jnp.sum(upper_grad.astype(jnp.float32), axis=0)
    query_grad, key_grad, value_grad = attention_backward(
        queries, key_rows, values, attended_grad, log_totals, slot_length, block_rows, seq_len
    )
    projected_grad = jnp.stack(
        [rotary(query_grad, positions, -1.0), rotary(key_grad, positions, -1.0), value_grad], axis=1
    )
    projected_grad = projected_grad.reshape(slot_count, 3 * heads_local * HD).astype(jnp.bfloat16)
    qkv_grad = jnp.dot(normed_all.T, projected_grad, preferred_element_type=jnp.float32)
    normed_grad = jnp.dot(
        projected_grad, weights[0].T, preferred_element_type=jnp.float32
    ) + jnp.dot(upper_grad, weights[2].T, preferred_element_type=jnp.float32)
    normed_rows = normed_combine(normed_grad)
    unused_norm, norm_pull = jax.vjp(
        layer_norm, residual, vectors[3 * layer_index], vectors[3 * layer_index + 1]
    )
    input_grad, gain_grad, shift_grad = norm_pull(normed_rows)
    return (
        residual_grad + input_grad,
        (qkv_grad, out_weight_grad, up_grad, down_grad),
        in_bias_grad,
        (gain_grad, shift_grad, out_bias_grad),
    )


def local(
    tokens,
    lengths,
    tile_owner,
    step_count,
    weight_tiles,
    tiles_first,
    tiles_second,
    stats_left,
    stats_right,
    basis_left,
    basis_right,
    embedding,
    embedding_first,
    embedding_second,
    head_table,
    head_first,
    head_second,
    vectors,
    vectors_first,
    vectors_second,
    fc_bias,
    fc_bias_first,
    fc_bias_second,
):
    group_rows, seq_len = tokens.shape
    slot_count = group_rows * seq_len
    mp_count = lax.axis_size("mp")
    dp_count = lax.axis_size("dp")
    heads_local = H // mp_count
    ff_local = fc_bias.shape[1]
    block_rows = min(512, seq_len)
    gathered = lax.all_gather(weight_tiles.astype(jnp.bfloat16), "dp", axis=0, tiled=True)
    shapes = layer_shapes(heads_local, ff_local)
    layer_weights = [assemble(tile_owner, gathered, shapes)]
    flat_tokens = tokens.reshape(slot_count)
    positions = jnp.arange(slot_count, dtype=jnp.int32) % seq_len
    slot_length = jnp.repeat(lengths, seq_len)
    slot_weight = jnp.where(
        positions < slot_length - 1, 1.0 / (slot_length - 1).astype(jnp.float32), 0.0
    )
    row_targets = jnp.roll(flat_tokens, -1)
    vocab_ids = jnp.arange(head_table.shape[1], dtype=jnp.int32)
    token_hot = (flat_tokens[:, None] == vocab_ids[None, :]).astype(jnp.float32)
    target_hot = (row_targets[:, None] == vocab_ids[None, :]).astype(jnp.float32)
    residual = jnp.dot(token_hot, embedding, precision=PRECISE)
    layer_index = 0
    residual, kept_values = layer_forward(
        residual,
        layer_weights[layer_index],
        vectors,
        fc_bias[layer_index],
        layer_index,
        positions,
        slot_length,
        block_rows,
        seq_len,
        heads_local,
    )
    saved = [kept_values]
    final_low = layer_norm(residual, vectors[3 * LAYERS], vectors[3 * LAYERS + 1]).astype(
        jnp.bfloat16
    )
    head_low = head_table[:-1].astype(jnp.bfloat16)
    logits = jnp.dot(final_low, head_low, preferred_element_type=jnp.float32) + head_table[-1]
    shifted = logits - jnp.max(logits, axis=-1, keepdims=True)
    log_probs = shifted - jnp.log(jnp.sum(jnp.exp(shifted), axis=-1, keepdims=True))
    loss_part = -jnp.sum(slot_weight * jnp.sum(target_hot * log_probs, axis=-1))
    logit_grad = ((jnp.exp(log_probs) - target_hot) * slot_weight[:, None]).astype(jnp.bfloat16)
    head_grad = jnp.concatenate(
        [
            jnp.dot(final_low.T, logit_grad, preferred_element_type=jnp.float32),
            jnp.sum(logit_grad.astype(jnp.float32), axis=0)[None],
        ],
        axis=0,
    )
    final_grad = jnp.dot(logit_grad, head_low.T, preferred_element_type=jnp.float32)
    unused_final, final_pull = jax.vjp(
        layer_norm, residual, vectors[3 * LAYERS], vectors[3 * LAYERS + 1]
    )
    residual_grad, final_gain_grad, final_shift_grad = final_pull(final_grad)
    vector_rows = [final_gain_grad] * (3 * LAYERS) + [final_gain_grad, final_shift_grad]
    tile_parts = [None] * LAYERS
    bias_rows = [None] * LAYERS
    for layer_index in reversed(range(LAYERS)):
        residual_grad, weight_grads, in_bias_grad, vector_grads = layer_backward(
            residual_grad,
            saved[layer_index],
            layer_weights[layer_index],
            vectors,
            layer_index,
            positions,
            slot_length,
            block_rows,
            seq_len,
            heads_local,
        )
        tile_parts[layer_index] = scatter_tiles(tile_owner, weight_grads)
        bias_rows[layer_index] = in_bias_grad
        vector_rows[3 * layer_index : 3 * layer_index + 3] = list(vector_grads)
    embed_grad = jnp.dot(token_hot.T, residual_grad, precision=PRECISE)
    vectors_grad = jnp.stack(vector_rows)
    fc_bias_grad = jnp.stack(bias_rows)
    grad_share = lax.psum_scatter(tile_parts[0], "dp", scatter_dimension=0, tiled=True)
    count_part = jnp.sum((lengths >= 2).astype(jnp.float32))
    embed_grad, head_grad, vectors_grad, fc_bias_grad, loss_sum, protein_count = lax.psum(
        (embed_grad, head_grad, vectors_grad, fc_bias_grad, loss_part, count_part), "dp"
    )
    grad_share = grad_share / protein_count
    embed_grad = embed_grad / protein_count
    head_grad = head_grad / protein_count
    vectors_grad = vectors_grad / protein_count
    fc_bias_grad = fc_bias_grad / protein_count
    replicated_sq = (
        jnp.sum(embed_grad * embed_grad)
        + jnp.sum(head_grad * head_grad)
        + jnp.sum(vectors_grad * vectors_grad)
    )
    square_part = (
        jnp.sum(grad_share * grad_share)
        + jnp.sum(fc_bias_grad * fc_bias_grad) / dp_count
        + replicated_sq / (dp_count * mp_count)
    )
    grad_norm = jnp.sqrt(lax.psum(square_part, ("dp", "mp")))
    factor = jnp.minimum(1.0, CLIP_NORM / grad_norm)
    correct_one = 1.0 - jnp.power(BETA_ONE, step_count.astype(jnp.float32))
    correct_two = 1.0 - jnp.power(BETA_TWO, step_count.astype(jnp.float32))
    results = soap(
        jnp.stack([factor, correct_one, correct_two]),
        grad_share,
        weight_tiles,
        tiles_first,
        tiles_second,
        stats_left,
        stats_right,
        basis_left,
        basis_right,
    )
    embed_out = adamw_update(
        embedding, factor * embed_grad, embedding_first, embedding_second, correct_one, correct_two
    )
    head_out = adamw_update(
        head_table, factor * head_grad, head_first, head_second, correct_one, correct_two
    )
    vector_out = adamw_update(
        vectors, factor * vectors_grad, vectors_first, vectors_second, correct_one, correct_two
    )
    bias_out = adamw_update(
        fc_bias, factor * fc_bias_grad, fc_bias_first, fc_bias_second, correct_one, correct_two
    )
    return (
        loss_sum / protein_count,
        grad_norm,
        results[0],
        results[1],
        results[2],
        results[3],
        results[4],
        results[5],
        results[6],
        results[7],
        embed_out[0],
        embed_out[1],
        embed_out[2],
        head_out[0],
        head_out[1],
        head_out[2],
        vector_out[0],
        vector_out[1],
        vector_out[2],
        bias_out[0],
        bias_out[1],
        bias_out[2],
    )


def solution(mesh):
    in_specs = (
        P("dp", None),
        P("dp"),
        P(),
        P(),
        P("dp", None, "mp"),
        P("dp", None, "mp"),
        P("dp", None, "mp"),
        P("dp", None, "mp"),
        P("dp", None, "mp"),
        P("dp", None, "mp"),
        P("dp", None, "mp"),
        P(),
        P(),
        P(),
        P(),
        P(),
        P(),
        P(),
        P(),
        P(),
        P(None, "mp"),
        P(None, "mp"),
        P(None, "mp"),
    )
    out_specs = (
        P(),
        P(),
        P("dp", None, "mp"),
        P("dp", None, "mp"),
        P("dp", None, "mp"),
        P("dp", None, "mp"),
        P("dp", None, "mp"),
        P("dp", None, "mp"),
        P("dp", None, "mp"),
        P("dp", None, "mp"),
        P(),
        P(),
        P(),
        P(),
        P(),
        P(),
        P(),
        P(),
        P(),
        P(None, "mp"),
        P(None, "mp"),
        P(None, "mp"),
    )
    return jax.shard_map(local, mesh=mesh, in_specs=in_specs, out_specs=out_specs, check_vma=False)
```

```python
import functools
import math

import jax
import jax.numpy as jnp
import numpy as np
from jax import lax
from jax.experimental import pallas as pl
from jax.experimental.pallas import tpu as pltpu
from jax.sharding import PartitionSpec as P

D = 1024
H = 16
HD = 64
ROT = 32
BS = 128
HB = 64
ROWS = 256
WIDE = 128
MEGA = 1024 * 1024

NORM_EPS = 1e-05
CLIP_NORM = 0.02
RATE_TILES = 0.02
RATE_SMALL = 0.2
BETA_ONE = 0.9
BETA_TWO = 0.95
ADAM_EPS = 1e-08
WEIGHT_DECAY = 0.01
MASKED = -1e30
GELU_A = math.sqrt(2.0 / math.pi)
GELU_B = 0.044715

NN = (((1,), (0,)), ((), ()))
NT = (((1,), (1,)), ((), ()))
TN = (((0,), (0,)), ((), ()))
f32 = jnp.float32
bf16 = jnp.bfloat16
SMEM = pl.BlockSpec(memory_space=pltpu.SMEM)
VMEM = pl.BlockSpec(memory_space=pltpu.VMEM)
ANY = pl.BlockSpec(memory_space=pl.ANY)


def dot(a, b, dims=NN):
    return lax.dot_general(a, b, dims, preferred_element_type=f32)


def split2(a):
    high = a.astype(bf16)
    return high, (a - high.astype(f32)).astype(bf16)


def split3(a):
    high = a.astype(bf16)
    rest = a - high.astype(f32)
    middle = rest.astype(bf16)
    return high, middle, (rest - middle.astype(f32)).astype(bf16)


def dot3(a, b, dims):
    (axis_a,), (axis_b,) = dims[0]
    ah, al = split2(a)
    bh, bl = split2(b)
    return dot(
        jnp.concatenate([ah, ah, al], axis=axis_a),
        jnp.concatenate([bh, bl, bh], axis=axis_b),
        dims,
    )


def dot6(a, b, dims):
    (axis_a,), (axis_b,) = dims[0]
    ah, am, al = split3(a)
    bh, bm, bl = split3(b)
    return dot(
        jnp.concatenate([ah, ah, am, am, ah, al], axis=axis_a),
        jnp.concatenate([bh, bm, bh, bm, bl, bh], axis=axis_b),
        dims,
    )


def rows_times_low(a, low, dims):
    count = a.shape[0]
    parts = dot(jnp.concatenate(split3(a), axis=0), low, dims)
    return parts[:count] + (parts[count : 2 * count] + parts[2 * count :])


def lanes(shape):
    return lax.broadcasted_iota(jnp.int32, shape, len(shape) - 1)


def sublanes(shape):
    return lax.broadcasted_iota(jnp.int32, shape, len(shape) - 2)


def stats_of(values):
    centred = values - jnp.mean(values, axis=-1, keepdims=True)
    spread = jnp.mean(centred * centred, axis=-1, keepdims=True)
    scale = lax.rsqrt(spread + NORM_EPS)
    return centred * scale, scale


def norm_back(grad, normed, scale, gain):
    inner = grad * gain
    mean_one = jnp.mean(inner, axis=-1, keepdims=True)
    mean_two = jnp.mean(inner * normed, axis=-1, keepdims=True)
    return scale * (inner - mean_one - normed * mean_two)


def swap_with(value, axis, mask):
    count = lax.axis_size(axis)
    return lax.ppermute(value, axis, [(i, i ^ mask) for i in range(count)])


def tree_sum(parts):
    while len(parts) > 1:
        parts = [parts[i] + parts[i + 1] for i in range(0, len(parts), 2)]
    return parts[0]


def gather_xor(value, axis):
    return [value] + [swap_with(value, axis, r) for r in range(1, lax.axis_size(axis))]


def gather_tiles(low):
    count = lax.axis_size("dp")
    bits = [1 << k for k in reversed(range(count.bit_length() - 1))]
    half = low.shape[0] // 2
    result = []
    for which in range(2):
        order = bits if which == 0 or len(bits) < 3 else [bits[1], bits[0]] + bits[2:]
        pieces = {0: low[which * half : (which + 1) * half]}
        for bit in order:
            for mask in list(pieces):
                pieces[mask ^ bit] = swap_with(pieces[mask], "dp", bit)
        result.append([pieces[r] for r in range(count)])
    return result


def sum_dp(value):
    count = lax.axis_size("dp")
    upper = (lax.axis_index("dp") & 1) == 1
    half = value.shape[0] // 2
    first, second = value[:half], value[half:]
    kept = jnp.where(upper, second, first) + swap_with(jnp.where(upper, first, second), "dp", 1)
    total = tree_sum([kept] + [swap_with(kept, "dp", r) for r in range(2, count, 2)])
    other = swap_with(total, "dp", 1)
    return jnp.concatenate([jnp.where(upper, other, total), jnp.where(upper, total, other)], axis=0)


def layer_shapes(heads_local, ff_local):
    return ((D, 3 * heads_local * HD), (heads_local * HD, D), (D, ff_local), (ff_local, D))


def tile_places(shapes):
    places = []
    for which, (row_total, col_total) in enumerate(shapes):
        for i in range(row_total // BS):
            for k in range(col_total // BS):
                places.append((which, i, k))
    return places


def tables_kernel(places, heads, pieces_n, place, *refs):
    pieces = refs[:pieces_n]
    (embed, vec, bias), refs = refs[pieces_n : pieces_n + 3], refs[pieces_n + 3 :]
    mats, (proj_o, upper_o, payload_o, normed_o, act_o, values_o, tiles, sems) = refs[:4], refs[4:]
    size = pieces[0].shape[0]
    copies = [
        pltpu.make_async_copy(piece, tiles.at[pl.ds(k * size, size)], sems.at[k])
        for k, piece in enumerate(pieces)
    ]
    for copy in copies:
        copy.start()
    normed, _ = stats_of(embed[...])
    low = (normed * vec[0:1] + vec[1:2]).astype(bf16)
    normed_o[...] = low
    for copy in copies:
        copy.wait()
    for index, (which, i, k) in enumerate(places):
        mats[which][i * BS : (i + 1) * BS, k * BS : (k + 1) * BS] = tiles[place[index]]
    proj = dot(low, mats[0][...])
    proj_o[...] = proj
    upper = dot(low, mats[2][...]) + bias[...]
    upper_o[...] = upper
    act = (0.5 * upper * (1.0 + jnp.tanh(GELU_A * (upper + GELU_B * (upper * upper * upper))))).astype(
        bf16
    )
    act_o[...] = act
    down = dot(act, mats[3][...])
    vocab = embed.shape[0]
    values = proj[:, 2 * heads * HD :]
    shape = (heads * vocab, heads * HD)
    values = jnp.concatenate([values] * heads, axis=0)
    same = sublanes(shape) // vocab == lanes(shape) // HD
    values = jnp.where(same, values, 0.0).astype(bf16)
    values_o[...] = values
    mixed = dot(values, mats[1][...])
    high, rest = split2(down)
    payload_o[...] = jnp.concatenate([mixed.astype(bf16), high, rest], axis=0)


def tables(place, pieces, embedding, vectors, fc_bias, heads, ff_local):
    shapes = layer_shapes(heads, ff_local)
    vocab = embedding.shape[0]
    o = jax.ShapeDtypeStruct
    total = len(pieces) * pieces[0].shape[0]
    return pl.pallas_call(
        functools.partial(tables_kernel, tile_places(shapes), heads, len(pieces)),
        in_specs=[SMEM] + [ANY] * len(pieces) + [VMEM] * 3,
        out_specs=[VMEM] * 10,
        out_shape=[o(shape, bf16) for shape in shapes]
        + [
            o((vocab, 3 * heads * HD), f32),
            o((vocab, ff_local), f32),
            o(((heads + 2) * vocab, D), bf16),
            o((vocab, D), bf16),
            o((vocab, ff_local), bf16),
            o((heads * vocab, heads * HD), bf16),
        ],
        scratch_shapes=[
            pltpu.VMEM((total, BS, BS), bf16),
            pltpu.SemaphoreType.DMA((len(pieces),)),
        ],
        compiler_params=pltpu.CompilerParams(vmem_limit_bytes=56 * MEGA),
        name="tables",
    )(place, *pieces, embedding, vectors, fc_bias)


def rotary_tables(seq_len):
    half = ROT // 2
    frequency = np.float32(10000.0) ** (
        np.float32(-2.0) * np.arange(half, dtype=np.float32) / np.float32(ROT)
    )
    angles = np.arange(seq_len, dtype=np.float32)[:, None] * frequency[None, :].astype(np.float32)
    cosine = np.cos(angles.astype(np.float64)).astype(np.float32)
    sine = np.sin(angles.astype(np.float64)).astype(np.float32)
    wide_cos = np.ones((seq_len, WIDE), np.float32)
    wide_sin = np.zeros((seq_len, WIDE), np.float32)
    wide_cos[:, :half], wide_cos[:, half:ROT] = cosine, cosine
    wide_sin[:, :half], wide_sin[:, half:ROT] = sine, sine
    return wide_cos, wide_sin, np.ascontiguousarray(cosine.T), np.ascontiguousarray(sine.T)


def turned(x):
    half = ROT // 2
    lane = lanes(x.shape)
    return jnp.where(
        lane < half,
        -pltpu.roll(x, WIDE - half, 1),
        jnp.where(lane < ROT, pltpu.roll(x, half, 1), 0.0),
    )


def head_lanes(table, index):
    begin = index // 2 * WIDE
    chunk = table[:, begin : begin + WIDE]
    if index % 2:
        chunk = pltpu.roll(chunk, HD, 1)
    return jnp.where(lanes(chunk.shape) < HD, chunk, 0.0)


def stack_parts(table):
    high, middle, rest = split3(table)
    return jnp.concatenate([high, middle, rest, jnp.zeros_like(high)], axis=0)


def attention_kernel(
    heads, length, token_col, proj, cosine, sine, query_o, key_o, weight_o, hot, key_hot, queries, wide
):
    seq = token_col.shape[0]
    vocab = proj.shape[0]
    lane = lanes((seq, WIDE))
    hot[...] = jnp.where(lane % vocab == token_col[...], 1.0, 0.0).astype(bf16)
    for h in range(heads):
        key_hot[h] = jnp.where(lane == token_col[...] + h * vocab, 1.0, 0.0).astype(bf16)
    one = lanes((vocab, WIDE)) == HD
    ones = (lanes((vocab, WIDE)) > HD) & (lanes((vocab, WIDE)) < HD + 4)
    for which in range(2):
        for h in range(heads):
            own = head_lanes(proj, which * heads + h)
            other = turned(own)
            if which == 0:
                own = jnp.where(one, 1.0, own * 0.125)
                other = other * 0.125
            else:
                own = jnp.where(one | ones, 1.0, own)
            begin = (which * heads + h) * 2 * WIDE
            wide[:, begin : begin + WIDE] = stack_parts(own)
            wide[:, begin + WIDE : begin + 2 * WIDE] = stack_parts(other)
    for i in range(seq // ROWS):
        span = slice(i * ROWS, (i + 1) * ROWS)
        part = hot[span]
        position = i * ROWS + sublanes((ROWS, WIDE))
        bias = jnp.where(position < length[0], 0.0, MASKED)
        cos, sin = cosine[span], sine[span]
        key_cos = jnp.where(lanes((ROWS, WIDE)) == HD, bias, cos)
        for h in range(heads):
            both = dot(part, wide[:, h * 2 * WIDE : (h + 1) * 2 * WIDE])
            queries[h, span] = (both[:, :WIDE] * cos + both[:, WIDE:] * sin).astype(bf16)
            k = heads + h
            both = dot(part, wide[:, k * 2 * WIDE : (k + 1) * 2 * WIDE])
            key_o[h, span] = (both[:, :WIDE] * key_cos + both[:, WIDE:] * sin).astype(bf16)
    allowed = lanes((ROWS, ROWS)) <= sublanes((ROWS, ROWS))
    small = lanes((ROWS, WIDE))
    for i in range(seq // ROWS):
        span = slice(i * ROWS, (i + 1) * ROWS)
        past = i * ROWS
        weights = jnp.zeros((ROWS, WIDE), f32)
        for h in range(heads):
            query = queries[h, span]
            near = jnp.where(allowed, dot(query, key_o[h, span], NT), MASKED)
            top = jnp.max(near, axis=-1, keepdims=True)
            if past:
                far = dot(query, key_o[h, :past], NT)
                top = jnp.maximum(top, jnp.max(far, axis=-1, keepdims=True))
                far = jnp.exp(far - top)
            near = jnp.exp(near - top)
            total = jnp.sum(near, axis=-1, keepdims=True)
            if past:
                total = total + jnp.sum(far, axis=-1, keepdims=True)
            share = 1.0 / total
            weights = weights + dot((near * share).astype(bf16), key_hot[h, span])
            if past:
                weights = weights + dot((far * share).astype(bf16), key_hot[h, :past])
            minus = -(top + jnp.log(total))
            high = minus.astype(bf16).astype(f32)
            middle = (minus - high).astype(bf16).astype(f32)
            rest = minus - high - middle
            query_o[h, span] = jnp.where(
                small == HD + 1,
                high,
                jnp.where(
                    small == HD + 2, middle, jnp.where(small == HD + 3, rest, query.astype(f32))
                ),
            ).astype(bf16)
        weight_o[span] = weights[:, : heads * vocab]


def attention(length, token_col, proj, cosine, sine, heads):
    seq = token_col.shape[0]
    vocab = proj.shape[0]
    o = jax.ShapeDtypeStruct
    return pl.pallas_call(
        functools.partial(attention_kernel, heads),
        in_specs=[SMEM] + [VMEM] * 4,
        out_specs=[VMEM] * 3,
        out_shape=[
            o((heads, seq, WIDE), bf16),
            o((heads, seq, WIDE), bf16),
            o((seq, heads * vocab), f32),
        ],
        scratch_shapes=[
            pltpu.VMEM((seq, WIDE), bf16),
            pltpu.VMEM((heads, seq, WIDE), bf16),
            pltpu.VMEM((heads, seq, WIDE), bf16),
            pltpu.VMEM((WIDE, heads * 4 * WIDE), bf16),
        ],
        compiler_params=pltpu.CompilerParams(vmem_limit_bytes=56 * MEGA),
        name="attention",
    )(length, token_col, proj, cosine, sine)


def attention_back_kernel(
    heads,
    token_col,
    token_row,
    query,
    key,
    weight,
    weight_grad,
    cosine,
    sine,
    cosine_t,
    sine_t,
    table_o,
    hot,
    mixed,
    query_grad,
    key_grad,
):
    seq = token_col.shape[0]
    vocab = weight.shape[1] // heads
    half = ROT // 2
    lane = lanes((seq, WIDE))
    hot[...] = jnp.where(
        (lane == token_col[...]) | (lane == token_col[...] + vocab) | ((lane >= HD) & (lane < HD + 3)),
        1.0,
        0.0,
    ).astype(bf16)
    both = weight[...] * weight_grad[...]
    grads = weight_grad[...]
    if heads * vocab < WIDE:
        pad = jnp.zeros((seq, WIDE - heads * vocab), f32)
        both = jnp.concatenate([both, pad], axis=1)
        grads = jnp.concatenate([grads, pad], axis=1)
    for h in range(heads):
        inside = (lane >= h * vocab) & (lane < (h + 1) * vocab)
        minus = -jnp.sum(jnp.where(inside, both, 0.0), axis=-1, keepdims=True)
        own = grads if h == 0 else pltpu.roll(grads, WIDE - h * vocab, 1)
        own = jnp.where(lane < vocab, own, 0.0)
        high, rest = split2(own)
        m_high = minus.astype(bf16).astype(f32)
        m_middle = (minus - m_high).astype(bf16).astype(f32)
        m_rest = minus - m_high - m_middle
        value = high.astype(f32) + pltpu.roll(rest.astype(f32), vocab, 1)
        value = jnp.where(lane == HD, m_high, value)
        value = jnp.where(lane == HD + 1, m_middle, value)
        value = jnp.where(lane == HD + 2, m_rest, value)
        mixed[h] = value.astype(bf16)
    allowed = lanes((ROWS, ROWS)) <= sublanes((ROWS, ROWS))
    key_grad[...] = jnp.zeros_like(key_grad)
    for h in range(heads):
        for i in range(seq // ROWS):
            span = slice(i * ROWS, (i + 1) * ROWS)
            past = i * ROWS
            part = query[h, span]
            near = jnp.where(allowed, jnp.exp(dot(part, key[h, span], NT)), 0.0)
            near = (near * dot(mixed[h, span], hot[span], NT)).astype(bf16)
            grad = dot(near, key[h, span])
            key_grad[h, :, span] += dot(part, near, TN)[:HD]
            if past:
                far = jnp.exp(dot(part, key[h, :past], NT))
                far = (far * dot(mixed[h, span], hot[:past], NT)).astype(bf16)
                grad = grad + dot(far, key[h, :past])
                key_grad[h, :, :past] += dot(part, far, TN)[:HD]
            grad = grad * 0.125
            query_grad[h, span] = (grad * cosine[span] - turned(grad) * sine[span]).astype(bf16)
    shape = (vocab, seq)
    token_hot = jnp.where(sublanes(shape) == token_row[...], 1.0, 0.0).astype(bf16)
    small = lanes((vocab, WIDE)) < HD
    cos_t, sin_t = cosine_t[...], sine_t[...]
    for pair in range(heads // 2):
        one = dot(token_hot, query_grad[2 * pair])
        two = pltpu.roll(dot(token_hot, query_grad[2 * pair + 1]), HD, 1)
        table_o[:, pair * WIDE : (pair + 1) * WIDE] = jnp.where(small, one, two)
        turned_keys = []
        for h in (2 * pair, 2 * pair + 1):
            front, back = key_grad[h, :half], key_grad[h, half:ROT]
            turned_keys += [
                front * cos_t + back * sin_t,
                back * cos_t - front * sin_t,
                key_grad[h, ROT:],
            ]
        keys = jnp.concatenate(turned_keys, axis=0).astype(bf16)
        begin = heads * HD + pair * WIDE
        table_o[:, begin : begin + WIDE] = dot(token_hot, keys, NT)


def attention_back(
    token_col, token_row, query, key, weight, weight_grad, cosine, sine, cosine_t, sine_t, heads
):
    seq = token_col.shape[0]
    vocab = weight.shape[1] // heads
    return pl.pallas_call(
        functools.partial(attention_back_kernel, heads),
        in_specs=[VMEM] * 10,
        out_specs=VMEM,
        out_shape=jax.ShapeDtypeStruct((vocab, 2 * heads * HD), f32),
        scratch_shapes=[
            pltpu.VMEM((seq, WIDE), bf16),
            pltpu.VMEM((heads, seq, WIDE), bf16),
            pltpu.VMEM((heads, seq, WIDE), bf16),
            pltpu.VMEM((heads, HD, seq), f32),
        ],
        compiler_params=pltpu.CompilerParams(vmem_limit_bytes=56 * MEGA),
        name="attention_back",
    )(token_col, token_row, query, key, weight, weight_grad, cosine, sine, cosine_t, sine_t)


def loss_kernel(
    parts,
    heads,
    ints,
    floats,
    token_col,
    target_col,
    token_row,
    embed,
    head,
    vec,
    *refs,
):
    weights, refs = refs[:parts], refs[parts:]
    payloads, refs = refs[:parts], refs[parts:]
    sums_o, grad_o, mixing, low_weights, table = refs
    step = pl.program_id(0)
    me, length = ints[0], ints[1]
    vocab = embed.shape[0]
    height = heads * vocab

    @pl.when(step == 0)
    def _():
        for r in range(parts):
            mixing[me ^ r] = payloads[r][...]
        down = jnp.zeros((vocab, D), f32)
        for g in range(parts):
            one = mixing[g, height:].astype(f32)
            down = down + (one[:vocab] + one[vocab:])
        table[...] = stack_parts(embed[...] + (down + vec[2:3]))
        sums_o[...] = jnp.zeros_like(sums_o)

    for r in range(parts):
        low_weights[me ^ r] = weights[r][...]
    token = token_col[...]
    hot = jnp.where(lanes((ROWS, WIDE)) % vocab == token, 1.0, 0.0).astype(bf16)
    x = dot(hot, table[...])
    x = x + dot(
        jnp.concatenate([low_weights[g] for g in range(parts)], axis=1),
        jnp.concatenate([mixing[g, :height] for g in range(parts)], axis=0),
    )
    normed, scale = stats_of(x)
    gain = vec[3:4]
    final = (normed * gain + vec[4:5]).astype(bf16)
    head_low = head[:D].astype(bf16)
    logits = dot(final, head_low) + head[D : D + 1]
    shifted = logits - jnp.max(logits, axis=-1, keepdims=True)
    log_probs = shifted - jnp.log(jnp.sum(jnp.exp(shifted), axis=-1, keepdims=True))
    target = lanes((ROWS, vocab)) == target_col[...]
    position = step * ROWS + sublanes((ROWS, 1))
    slot_weight = jnp.where(position < length - 1, floats[0], 0.0)
    picked = jnp.sum(jnp.where(target, log_probs, 0.0), axis=-1, keepdims=True)
    loss = -jnp.sum(slot_weight * picked, keepdims=True)
    logit_grad = ((jnp.exp(log_probs) - jnp.where(target, 1.0, 0.0)) * slot_weight).astype(bf16)
    final_grad = dot(logit_grad, head_low, NT)
    grad = norm_back(final_grad, normed, scale, gain)
    high, rest = split2(grad)
    token_hot = jnp.where(sublanes((vocab, ROWS)) == token_row[...], 1.0, 0.0).astype(bf16)
    sums_o[0:vocab] += dot(token_hot, high) + dot(token_hot, rest)
    sums_o[vocab : 2 * vocab] += dot(logit_grad, final, TN)
    base = 2 * vocab
    sums_o[base : base + 1] += jnp.sum(final_grad * normed, axis=0, keepdims=True)
    sums_o[base + 1 : base + 2] += jnp.sum(final_grad, axis=0, keepdims=True)
    bias_grad = jnp.sum(logit_grad.astype(f32), axis=0, keepdims=True)
    sums_o[base + 2 : base + 3, :vocab] += bias_grad
    lane = lanes((1, WIDE))
    count = jnp.where((step == 0) & (length >= 2), 1.0, 0.0)
    sums_o[base + 3 : base + 4, :WIDE] += jnp.where(
        lane == 0, loss, jnp.where(lane == 1, count, 0.0)
    )
    sums_o[base + 16 : base + 16 + height] += dot(weights[0][...], high, TN)
    grad_o[...] = dot(high, payloads[0][:height], NT)


def loss_rows(ints, floats, token_col, target_col, token_row, embedding, head, vectors, weights, payloads, heads):
    seq = token_col.shape[0]
    vocab = embedding.shape[0]
    parts = len(weights)
    height = heads * vocab
    col = pl.BlockSpec((ROWS, 1), lambda i: (i, 0))
    o = jax.ShapeDtypeStruct
    full = lambda array: pl.BlockSpec(array.shape, lambda i: (0,) * array.ndim)
    sums_shape = (2 * vocab + 16 + height, D)
    return pl.pallas_call(
        functools.partial(loss_kernel, parts, heads),
        grid=(seq // ROWS,),
        in_specs=[SMEM, SMEM, col, col, pl.BlockSpec((1, ROWS), lambda i: (0, i))]
        + [full(embedding), full(head), full(vectors)]
        + [pl.BlockSpec((ROWS, height), lambda i: (i, 0))] * parts
        + [full(payloads[0])] * parts,
        out_specs=[
            pl.BlockSpec(sums_shape, lambda i: (0, 0)),
            pl.BlockSpec((ROWS, height), lambda i: (i, 0)),
        ],
        out_shape=[o(sums_shape, f32), o((seq, height), f32)],
        scratch_shapes=[
            pltpu.VMEM((parts,) + payloads[0].shape, bf16),
            pltpu.VMEM((parts, ROWS, height), bf16),
            pltpu.VMEM((4 * vocab, D), bf16),
        ],
        compiler_params=pltpu.CompilerParams(vmem_limit_bytes=56 * MEGA),
        name="loss_rows",
    )(ints, floats, token_col, target_col, token_row, embedding, head, vectors, *weights, *payloads)


def padded(block):
    lacking = HB - block.shape[0]
    if lacking:
        block = jnp.concatenate([block, jnp.zeros((lacking, block.shape[1]), block.dtype)], axis=0)
    return block


def factors_kernel(
    heads,
    sums,
    table,
    mat_q,
    mat_o,
    mat_u,
    mat_f,
    upper,
    normed,
    act,
    values,
    left_o,
    right_o,
    hidden_o,
    bias_o,
):
    vocab = normed.shape[0]
    width = mat_u.shape[1]
    rows = sums[0:vocab]
    mixed = sums[2 * vocab + 16 :]
    act_grad = rows_times_low(rows, mat_f[...], NT)
    u = upper[...]
    tanh = jnp.tanh(GELU_A * (u + GELU_B * (u * u * u)))
    slope = 0.5 * (1.0 + tanh) + 0.5 * u * (1.0 - tanh * tanh) * (
        GELU_A * (1.0 + 3.0 * GELU_B * (u * u))
    )
    upper_grad = act_grad * slope
    bias_grad = jnp.sum(upper_grad, axis=0, keepdims=True)
    bias_o[...] = bias_grad
    value_grad = rows_times_low(mixed, mat_o[...], NT)
    shape = value_grad.shape
    value_grad = jnp.where(sublanes(shape) // vocab == lanes(shape) // HD, value_grad, 0.0)
    value_table = value_grad[:vocab]
    for h in range(1, heads):
        value_table = value_table + value_grad[h * vocab : (h + 1) * vocab]
    proj_grad = jnp.concatenate([table[...], value_table], axis=1)
    hidden = rows_times_low(upper_grad, mat_u[...], NT) + rows_times_low(proj_grad, mat_q[...], NT)
    hidden_o[0:vocab] = hidden
    low = normed[...].astype(f32)
    own = act[...].astype(f32)
    val = values[...].astype(f32)
    normed_gram = dot6(low, low, NT)
    square = (
        jnp.sum(normed_gram * dot6(proj_grad, proj_grad, NT), keepdims=True)
        + jnp.sum(normed_gram * dot6(upper_grad, upper_grad, NT), keepdims=True)
        + jnp.sum(dot6(own, own, NT) * dot6(rows, rows, NT), keepdims=True)
        + jnp.sum(dot6(val, val, NT) * dot6(mixed, mixed, NT), keepdims=True)
        + jnp.sum(bias_grad * bias_grad, keepdims=True)
    )
    hidden_o[vocab : vocab + 8] = jnp.broadcast_to(square, (8, D))

    def put_left(index, block):
        block = padded(block)
        left_o[index] = jnp.concatenate([block] * 3, axis=0).astype(bf16)

    def put_right(index, block):
        left_o_parts = split3(padded(block))
        right_o[index] = jnp.concatenate(left_o_parts, axis=0)

    at = 0
    for i in range(D // BS):
        put_left(at, low[:, i * BS : (i + 1) * BS])
        at += 1
    for i in range(width // BS):
        put_left(at, own[:, i * BS : (i + 1) * BS])
        at += 1
    pair = 2 * vocab
    for i in range(heads // 2):
        put_left(at, val[i * pair : (i + 1) * pair, i * BS : (i + 1) * BS])
        at += 1
    at = 0
    for k in range(3 * heads * HD // BS):
        put_right(at, proj_grad[:, k * BS : (k + 1) * BS])
        at += 1
    for i in range(heads // 2):
        for k in range(D // BS):
            put_right(at, mixed[i * pair : (i + 1) * pair, k * BS : (k + 1) * BS])
            at += 1
    for k in range(width // BS):
        put_right(at, upper_grad[:, k * BS : (k + 1) * BS])
        at += 1
    for k in range(D // BS):
        put_right(at, rows[:, k * BS : (k + 1) * BS])
        at += 1


def factor_places(heads, ff_local):
    q_cols = 3 * heads * HD // BS
    o_rows = heads // 2
    across = D // BS
    f_rows = ff_local // BS
    left, right = [], []
    for which, i, k in tile_places(layer_shapes(heads, ff_local)):
        if which == 0:
            left.append(i)
            right.append(k)
        elif which == 1:
            left.append(across + f_rows + i)
            right.append(q_cols + i * across + k)
        elif which == 2:
            left.append(i)
            right.append(q_cols + o_rows * across + k)
        else:
            left.append(across + i)
            right.append(q_cols + o_rows * across + f_rows + k)
    return np.array(left, np.int32), np.array(right, np.int32)


def factors(sums, table, mats, upper, normed, act, values, heads):
    vocab = normed.shape[0]
    ff_local = upper.shape[1]
    n_left = D // BS + ff_local // BS + heads // 2
    n_right = 3 * heads * HD // BS + heads // 2 * (D // BS) + ff_local // BS + D // BS
    o = jax.ShapeDtypeStruct
    return pl.pallas_call(
        functools.partial(factors_kernel, heads),
        in_specs=[VMEM] * 10,
        out_specs=[VMEM] * 4,
        out_shape=[
            o((n_left, 3 * HB, BS), bf16),
            o((n_right, 3 * HB, BS), bf16),
            o((vocab + 8, D), f32),
            o((1, ff_local), f32),
        ],
        compiler_params=pltpu.CompilerParams(vmem_limit_bytes=56 * MEGA),
        name="factors",
    )(sums, table, *mats, upper, normed, act, values)


def small_kernel(parts, corrections, sums, *refs):
    hiddens, refs = refs[:parts], refs[parts:]
    bias_grad, refs = refs[0], refs[1:]
    weights, refs = refs[:12], refs[12:]
    outs, scalars = refs[:12], refs[12]
    vocab = weights[0].shape[0]
    base = 2 * vocab
    total = [ref[...] for ref in hiddens]
    total = tree_sum(total)
    hidden = total[:vocab]
    square = total[vocab : vocab + 1, 0:1]
    rows = sums[0:vocab]
    normed, scale = stats_of(weights[0][...])
    gain = weights[6][0:1]
    embed_grad = rows + norm_back(hidden, normed, scale, gain)
    vector_grad = jnp.concatenate(
        [
            jnp.sum(hidden * normed, axis=0, keepdims=True),
            jnp.sum(hidden, axis=0, keepdims=True),
            jnp.sum(rows, axis=0, keepdims=True),
            sums[base : base + 1],
            sums[base + 1 : base + 2],
        ],
        axis=0,
    )
    head_grad = sums[vocab : 2 * vocab]
    head_bias = sums[base + 2 : base + 3, :vocab]
    add = lambda value: jnp.sum(value * value, keepdims=True)
    square = square + add(embed_grad) + add(vector_grad) + add(head_grad) + add(head_bias)
    count = sums[base + 3 : base + 4, 1:2]
    loss = sums[base + 3 : base + 4, 0:1] / count
    norm = jnp.sqrt(square) / count
    scale_all = jnp.minimum(1.0, CLIP_NORM / norm) / count
    one, two = corrections[0], corrections[1]

    def update(index, pick, grad):
        weight, first, second = (weights[3 * index + k][pick] for k in range(3))
        grad = grad * scale_all
        first = BETA_ONE * first + (1.0 - BETA_ONE) * grad
        second = BETA_TWO * second + (1.0 - BETA_TWO) * grad * grad
        step = first / one / (jnp.sqrt(second / two) + ADAM_EPS)
        outs[3 * index][pick] = weight - RATE_SMALL * (step + WEIGHT_DECAY * weight)
        outs[3 * index + 1][pick] = first
        outs[3 * index + 2][pick] = second

    everything = slice(None)
    update(0, everything, embed_grad)
    update(1, slice(0, D), head_grad.T)
    update(1, slice(D, D + 1), head_bias)
    update(2, everything, vector_grad)
    update(3, everything, bias_grad[...])
    lane = lanes((1, WIDE))
    scalars[...] = jnp.where(
        lane == 0, scale_all, jnp.where(lane == 1, loss, jnp.where(lane == 2, norm, 0.0))
    )


def small(corrections, sums, hiddens, bias_grad, weights):
    o = jax.ShapeDtypeStruct
    return pl.pallas_call(
        functools.partial(small_kernel, len(hiddens)),
        in_specs=[SMEM] + [VMEM] * (1 + len(hiddens) + 1 + 12),
        out_specs=[VMEM] * 13,
        out_shape=[o(weight.shape, f32) for weight in weights] + [o((1, WIDE), f32)],
        compiler_params=pltpu.CompilerParams(vmem_limit_bytes=56 * MEGA),
        name="small",
    )(corrections, sums, *hiddens, bias_grad, *weights)


GROUP = 0
UN = 3


def eliminate(work, count):
    lane=lax.broadcasted_iota(jnp.int32,(HB,BS),1)
    sub=lax.broadcasted_iota(jnp.int32,(HB,BS),0)
    half=jnp.where(lane>=HB,HB,0)
    for g0 in range(HB//8):
        r0=8*g0
        rows=HB-r0
        def body(jj,carry):
            j=r0+jj
            pick=half[:rows]+j
            at_pivot=lane[:rows]==pick
            below=sub[:rows]>jj
            clear=at_pivot&below
            group=GROUP or count
            for t0 in range(0,count,group):
                span=range(t0,t0+group)
                rows_in=[work[t,pl.ds(j,1),:] for t in span]
                kept=[work[t,r0:,:] for t in span]
                wides=[jnp.broadcast_to(row,(8,BS)) for row in rows_in]
                pivots=[jnp.take_along_axis(w,pick[:8],axis=1,mode="promise_in_bounds") for w in wides]
                cs=[jnp.take_along_axis(a,pick,axis=1,mode="promise_in_bounds") for a in kept]
                scaleds=[jnp.where(at_pivot[:8],1.0,w)/p for w,p in zip(wides,pivots)]
                for t,a,c,sc in zip(span,kept,cs,scaleds):
                    work[t,r0:,:]=jnp.where(clear,0.0,a)-jnp.where(below,c,0.0)*sc[:1]
            return carry
        lax.fori_loop(0,8,body,0)

def factor_inverse(packed):
    lane=lax.broadcasted_iota(jnp.int32,(HB,BS),1)
    sub=lax.broadcasted_iota(jnp.int32,(HB,BS),0)
    left=lane<HB
    col=jnp.where(left,lane,lane-HB)
    diag=jnp.where(col==sub,packed,0.0)
    d_left=jnp.sum(jnp.where(left,diag,0.0),axis=1,keepdims=True)
    d_right=jnp.sum(jnp.where(left,0.0,diag),axis=1,keepdims=True)
    scale=lax.rsqrt(jnp.where(left,d_left,d_right))
    unit=jnp.where(col<sub,packed,jnp.where(col==sub,1.0,0.0))
    return unit*scale

def block_diagonal(packed):
    lane=lax.broadcasted_iota(jnp.int32,(HB,BS),1)
    left=lane<HB
    return jnp.concatenate([jnp.where(left,packed,0.0),jnp.where(left,0.0,packed)],axis=0)

def swap(x):
    return pltpu.roll(x,HB,1)

def soap_kernel(count, per, scal, left_at, right_at, lefts, rights, W, m, v, L, R, QL, QR, W_o, low_o, m_o, v_o, L_o, R_o, QL_o, QR_o, ML_s, MR_s, work, A21_s, A22_s, W11_s):
    step=pl.program_id(0)
    scale=scal[0]; c1=scal[1]; c2=scal[2]
    left=lax.broadcasted_iota(jnp.int32,(HB,BS),1)<HB
    span=range(per)
    pairs=[(lefts[left_at[step*per+s]],rights[right_at[step*per+s]]) for s in span]
    g=[dot(a,b,TN)*scale for a,b in pairs]
    gT=[dot(b,a,TN)*scale for a,b in pairs]
    qT=[QL[s].T for s in span]
    ggl=[dot3(x,x,NT) for x in g]
    ggr=[dot3(x,x,NT) for x in gT]
    rot=[dot3(q,x,NN) for q,x in zip(qT,g)]
    Ln=[BETA_TWO*L[s]+(1-BETA_TWO)*ggl[s] for s in span]
    Rn=[BETA_TWO*R[s]+(1-BETA_TWO)*ggr[s] for s in span]
    rot=[dot3(x,QR[s],NN) for s,x in enumerate(rot)]
    for s in span:
        L_o[s]=Ln[s]; R_o[s]=Rn[s]
    ML=[dot6(Ln[s],QL[s],NN) for s in span]
    MR=[dot6(Rn[s],QR[s],NN) for s in span]
    xs=[]
    for s in span:
        mn=BETA_ONE*m[s]+(1-BETA_ONE)*rot[s]
        vn=BETA_TWO*v[s]+(1-BETA_TWO)*rot[s]*rot[s]
        m_o[s]=mn; v_o[s]=vn
        xs.append((mn/c1)/(jnp.sqrt(vn/c2)+ADAM_EPS))
    back=[dot3(QL[s],xs[s],NN) for s in span]
    ML=[x*lax.rsqrt(jnp.sum(x*x,keepdims=True)) for x in ML]
    MR=[x*lax.rsqrt(jnp.sum(x*x,keepdims=True)) for x in MR]
    back=[dot3(back[s],QR[s],NT) for s in span]
    AL=[dot6(x,x,TN) for x in ML]
    AR=[dot6(x,x,TN) for x in MR]
    for s in span:
        w=W[s]
        wn=w-RATE_TILES*(back[s]+WEIGHT_DECAY*w)
        W_o[s]=wn
        low_o[s]=wn.astype(bf16)
        t=step*per+s
        ML_s[t]=ML[s]; MR_s[t]=MR[s]
        work[t]=jnp.where(left,AL[s][:HB],swap(AR[s][:HB]))
        A21_s[t]=jnp.where(left,AL[s][HB:],swap(AR[s][HB:]))
        A22_s[t]=jnp.where(left,swap(AL[s][HB:]),AR[s][HB:])

    @pl.when(step==pl.num_programs(0)-1)
    def _():
        eliminate(work,count)
        def mid(i,carry):
            ts=[i*UN+k for k in range(UN)]
            w11=[factor_inverse(work[t]) for t in ts]
            for t,w in zip(ts,w11): W11_s[t]=w
            l21=[dot6(A21_s[t],block_diagonal(w),NT) for t,w in zip(ts,w11)]
            for t,l in zip(ts,l21): A21_s[t]=l
            low=[dot6(l,block_diagonal(l),NT) for l in l21]
            for t,l in zip(ts,low): work[t]=A22_s[t]-l
            return carry
        lax.fori_loop(0,count//UN,mid,0)
        eliminate(work,count)
        def last(i,carry):
            ts=[i*UN+k for k in range(UN)]
            w22=[factor_inverse(work[t]) for t in ts]
            w11=[W11_s[t] for t in ts]
            y=[dot6(A21_s[t],block_diagonal(w),NN) for t,w in zip(ts,w11)]
            w21=[-dot6(w,block_diagonal(x),NN) for w,x in zip(w22,y)]
            cl=[jnp.concatenate([jnp.where(left,a,0.0),jnp.where(left,b,swap(c))],axis=0) for a,b,c in zip(w11,w21,w22)]
            cr=[jnp.concatenate([jnp.where(left,swap(a),0.0),jnp.where(left,swap(b),c)],axis=0) for a,b,c in zip(w11,w21,w22)]
            ol=[dot3(ML_s[t],c,NT) for t,c in zip(ts,cl)]
            orr=[dot3(MR_s[t],c,NT) for t,c in zip(ts,cr)]
            for t,a,b in zip(ts,ol,orr):
                QL_o[t]=a; QR_o[t]=b
            return carry
        lax.fori_loop(0,count//UN,last,0)

def soap(scal,left_at,right_at,lefts,rights,W,m,v,L,R,QL,QR):
    count=W.shape[0]
    per=3 if count%3==0 else 1
    blk=pl.BlockSpec((per,BS,BS),lambda i:(i,0,0))
    full=pl.BlockSpec((count,BS,BS),lambda i:(0,0,0))
    whole=lambda x:pl.BlockSpec(x.shape,lambda i:(0,0,0))
    o=lambda dt: jax.ShapeDtypeStruct((count,BS,BS),dt)
    return pl.pallas_call(
        functools.partial(soap_kernel,count,per),
        grid=(count//per,),
        in_specs=[SMEM]*3+[whole(lefts),whole(rights)]+[blk]*7,
        out_specs=[blk]*6+[full]*2,
        out_shape=[o(f32),o(bf16),o(f32),o(f32),o(f32),o(f32),o(f32),o(f32)],
        scratch_shapes=[pltpu.VMEM((count,BS,BS),f32)]*2+[pltpu.VMEM((count,HB,BS),f32)]*4,
        compiler_params=pltpu.CompilerParams(vmem_limit_bytes=56*1024*1024),
        name="soap_tiles",
    )(scal,left_at,right_at,lefts,rights,W,m,v,L,R,QL,QR)


def local(
    tokens,
    lengths,
    tile_owner,
    step_count,
    weight_tiles,
    tiles_first,
    tiles_second,
    stats_left,
    stats_right,
    basis_left,
    basis_right,
    embedding,
    embedding_first,
    embedding_second,
    head_table,
    head_first,
    head_second,
    vectors,
    vectors_first,
    vectors_second,
    fc_bias,
    fc_bias_first,
    fc_bias_second,
):
    seq = tokens.shape[1]
    mp_count = lax.axis_size("mp")
    dp_count = lax.axis_size("dp")
    dp_index = lax.axis_index("dp")
    mp_index = lax.axis_index("mp")
    heads = H // mp_count
    ff_local = fc_bias.shape[1]
    count = weight_tiles.shape[0]
    half = count // 2

    halves = gather_tiles(weight_tiles.astype(bf16))
    pieces = halves[0] + halves[1]
    holder = tile_owner // count
    inside = tile_owner - holder * count
    place = (
        jnp.where(inside >= half, dp_count * half - half, 0) + (holder ^ dp_index) * half + inside
    )
    result = tables(place, pieces, embedding, vectors, fc_bias, heads, ff_local)
    mats, (proj, upper, payload, normed, act, values) = result[:4], result[4:]

    token_col = tokens.reshape(seq, 1)
    target_col = jnp.roll(tokens, -1, axis=1).reshape(seq, 1)
    cosine, sine, cosine_t, sine_t = rotary_tables(seq)
    payloads = gather_xor(payload, "mp")
    query, key, weight = attention(lengths, token_col, proj, cosine, sine, heads)
    weights = gather_xor(weight.astype(bf16), "mp")
    length = lengths[0]
    inverse_length = 1.0 / jnp.maximum(length - 1, 1).astype(f32)
    sums, weight_grad = loss_rows(
        jnp.stack([mp_index, length]),
        inverse_length[None],
        token_col,
        target_col,
        tokens,
        embedding,
        head_table,
        vectors,
        weights,
        payloads,
        heads,
    )
    sums = sum_dp(sums)
    table = attention_back(
        token_col, tokens, query, key, weight, weight_grad, cosine, sine, cosine_t, sine_t, heads
    )
    table = sum_dp(table)
    left, right, hidden, bias_grad = factors(
        sums, table, mats, upper, normed, act, values, heads
    )
    hiddens = gather_xor(hidden, "mp")
    corrections = 1.0 - jnp.power(
        jnp.array([BETA_ONE, BETA_TWO], f32), step_count.astype(f32)
    )
    small_weights = (
        embedding,
        embedding_first,
        embedding_second,
        head_table,
        head_first,
        head_second,
        vectors,
        vectors_first,
        vectors_second,
        fc_bias,
        fc_bias_first,
        fc_bias_second,
    )
    *small_out, scalars = small(corrections, sums, hiddens, bias_grad, small_weights)
    slots = dp_index * count + jnp.arange(count, dtype=jnp.int32)
    natural = jnp.sum(
        jnp.where(
            tile_owner[None, :] == slots[:, None],
            jnp.arange(tile_owner.shape[0], dtype=jnp.int32)[None, :],
            0,
        ),
        axis=1,
    )
    left_of, right_of = factor_places(heads, ff_local)
    same = natural[:, None] == jnp.arange(tile_owner.shape[0], dtype=jnp.int32)[None, :]
    left_at = jnp.sum(jnp.where(same, left_of[None, :], 0), axis=1)
    right_at = jnp.sum(jnp.where(same, right_of[None, :], 0), axis=1)
    results = soap(
        jnp.concatenate([scalars[0, :1], corrections]),
        left_at,
        right_at,
        left,
        right,
        weight_tiles,
        tiles_first,
        tiles_second,
        stats_left,
        stats_right,
        basis_left,
        basis_right,
    )
    return (scalars[0, 1], scalars[0, 2], *results, *small_out)


def solution(mesh):
    tiled = P("dp", None, "mp")
    split = P(None, "mp")
    in_specs = (P("dp", None), P("dp"), P(), P(), *[tiled] * 7, *[P()] * 9, *[split] * 3)
    out_specs = (P(), P(), *[tiled] * 8, *[P()] * 9, *[split] * 3)
    return jax.shard_map(local, mesh=mesh, in_specs=in_specs, out_specs=out_specs, check_vma=False)
```

```python
import functools
import math

import jax
import jax.numpy as jnp
import numpy as np
from jax import lax
from jax.experimental import pallas as pl
from jax.experimental.pallas import tpu as pltpu
from jax.sharding import PartitionSpec as P

D = 1024
H = 16
HD = 64
ROT = 32
BS = 128
HB = 64
ROWS = 256
WIDE = 128
MEGA = 1024 * 1024

NORM_EPS = 1e-05
CLIP_NORM = 0.02
RATE_TILES = 0.02
RATE_SMALL = 0.2
BETA_ONE = 0.9
BETA_TWO = 0.95
ADAM_EPS = 1e-08
WEIGHT_DECAY = 0.01
MASKED = -1e30
GELU_A = math.sqrt(2.0 / math.pi)
GELU_B = 0.044715

NN = (((1,), (0,)), ((), ()))
NT = (((1,), (1,)), ((), ()))
TN = (((0,), (0,)), ((), ()))
f32 = jnp.float32
bf16 = jnp.bfloat16
SMEM = pl.BlockSpec(memory_space=pltpu.SMEM)
VMEM = pl.BlockSpec(memory_space=pltpu.VMEM)
ANY = pl.BlockSpec(memory_space=pl.ANY)


def dot(a, b, dims=NN):
    return lax.dot_general(a, b, dims, preferred_element_type=f32)


def split2(a):
    high = a.astype(bf16)
    return high, (a - high.astype(f32)).astype(bf16)


def split3(a):
    high = a.astype(bf16)
    rest = a - high.astype(f32)
    middle = rest.astype(bf16)
    return high, middle, (rest - middle.astype(f32)).astype(bf16)


def dot3(a, b, dims):
    (axis_a,), (axis_b,) = dims[0]
    ah, al = split2(a)
    bh, bl = split2(b)
    return dot(
        jnp.concatenate([ah, ah, al], axis=axis_a),
        jnp.concatenate([bh, bl, bh], axis=axis_b),
        dims,
    )


def dot6(a, b, dims):
    (axis_a,), (axis_b,) = dims[0]
    ah, am, al = split3(a)
    bh, bm, bl = split3(b)
    return dot(
        jnp.concatenate([ah, ah, am, am, ah, al], axis=axis_a),
        jnp.concatenate([bh, bm, bh, bm, bl, bh], axis=axis_b),
        dims,
    )


def rows_times_low(a, low, dims):
    count = a.shape[0]
    parts = dot(jnp.concatenate(split3(a), axis=0), low, dims)
    return parts[:count] + (parts[count : 2 * count] + parts[2 * count :])


def lanes(shape):
    return lax.broadcasted_iota(jnp.int32, shape, len(shape) - 1)


def sublanes(shape):
    return lax.broadcasted_iota(jnp.int32, shape, len(shape) - 2)


def stats_of(values):
    centred = values - jnp.mean(values, axis=-1, keepdims=True)
    spread = jnp.mean(centred * centred, axis=-1, keepdims=True)
    scale = lax.rsqrt(spread + NORM_EPS)
    return centred * scale, scale


def norm_back(grad, normed, scale, gain):
    inner = grad * gain
    mean_one = jnp.mean(inner, axis=-1, keepdims=True)
    mean_two = jnp.mean(inner * normed, axis=-1, keepdims=True)
    return scale * (inner - mean_one - normed * mean_two)


def params(microseconds):
    return dict(
        compiler_params=pltpu.CompilerParams(vmem_limit_bytes=56 * MEGA),
        cost_estimate=pl.CostEstimate(
            flops=int(microseconds * 1.1e9), bytes_accessed=int(microseconds * 1e6), transcendentals=0
        ),
    )


def swap_with(value, axis, mask):
    count = lax.axis_size(axis)
    return lax.ppermute(value, axis, [(i, i ^ mask) for i in range(count)])


def tree_sum(parts):
    while len(parts) > 1:
        parts = [parts[i] + parts[i + 1] for i in range(0, len(parts), 2)]
    return parts[0]


def gather_xor(value, axis):
    return [value] + [swap_with(value, axis, r) for r in range(1, lax.axis_size(axis))]


def gather_shared(value):
    upper = (lax.axis_index("dp") & 1) == 1
    half = value.shape[0] // 2
    mine = jnp.where(upper, value[half:], value[:half])
    parts = [swap_with(mine, "mp", r) for r in range(1, lax.axis_size("mp"))]
    return parts, [swap_with(part, "dp", 1) for part in parts]


def gather_tiles(low):
    count = lax.axis_size("dp")
    bits = [1 << k for k in reversed(range(count.bit_length() - 1))]
    half = low.shape[0] // 2
    result = []
    for which in range(2):
        order = bits if which == 0 or len(bits) < 3 else [bits[1], bits[0]] + bits[2:]
        pieces = {0: low[which * half : (which + 1) * half]}
        for bit in order:
            for mask in list(pieces):
                pieces[mask ^ bit] = swap_with(pieces[mask], "dp", bit)
        result.append([pieces[r] for r in range(count)])
    return result


def sum_dp(value):
    count = lax.axis_size("dp")
    upper = (lax.axis_index("dp") & 1) == 1
    half = value.shape[0] // 2
    first, second = value[:half], value[half:]
    kept = jnp.where(upper, second, first) + swap_with(jnp.where(upper, first, second), "dp", 1)
    total = tree_sum([kept] + [swap_with(kept, "dp", r) for r in range(2, count, 2)])
    other = swap_with(total, "dp", 1)
    return jnp.concatenate([jnp.where(upper, other, total), jnp.where(upper, total, other)], axis=0)


def layer_shapes(heads_local, ff_local):
    return ((D, 3 * heads_local * HD), (heads_local * HD, D), (D, ff_local), (ff_local, D))


def tile_places(shapes):
    places = []
    for which, (row_total, col_total) in enumerate(shapes):
        for i in range(row_total // BS):
            for k in range(col_total // BS):
                places.append((which, i, k))
    return places


def tables_kernel(places, heads, pieces_n, place, *refs):
    pieces = refs[:pieces_n]
    (embed, vec, bias), refs = refs[pieces_n : pieces_n + 3], refs[pieces_n + 3 :]
    mats, (proj_o, upper_o, payload_o, normed_o, act_o, values_o, tiles, sems) = refs[:4], refs[4:]
    size = pieces[0].shape[0]
    copies = [
        pltpu.make_async_copy(piece, tiles.at[pl.ds(k * size, size)], sems.at[k])
        for k, piece in enumerate(pieces)
    ]
    for copy in copies:
        copy.start()
    normed, _ = stats_of(embed[...])
    low = (normed * vec[0:1] + vec[1:2]).astype(bf16)
    normed_o[...] = low
    for copy in copies:
        copy.wait()
    for index, (which, i, k) in enumerate(places):
        mats[which][i * BS : (i + 1) * BS, k * BS : (k + 1) * BS] = tiles[place[index]]
    proj = dot(low, mats[0][...])
    proj_o[...] = proj
    upper = dot(low, mats[2][...]) + bias[...]
    upper_o[...] = upper
    act = (0.5 * upper * (1.0 + jnp.tanh(GELU_A * (upper + GELU_B * (upper * upper * upper))))).astype(
        bf16
    )
    act_o[...] = act
    down = dot(act, mats[3][...])
    vocab = embed.shape[0]
    values = proj[:, 2 * heads * HD :]
    shape = (heads * vocab, heads * HD)
    values = jnp.concatenate([values] * heads, axis=0)
    same = sublanes(shape) // vocab == lanes(shape) // HD
    values = jnp.where(same, values, 0.0).astype(bf16)
    values_o[...] = values
    mixed = dot(values, mats[1][...])
    high, rest = split2(down)
    payload_o[...] = jnp.concatenate([mixed.astype(bf16), high, rest], axis=0)


def tables(place, pieces, embedding, vectors, fc_bias, heads, ff_local):
    shapes = layer_shapes(heads, ff_local)
    vocab = embedding.shape[0]
    o = jax.ShapeDtypeStruct
    total = len(pieces) * pieces[0].shape[0]
    return pl.pallas_call(
        functools.partial(tables_kernel, tile_places(shapes), heads, len(pieces)),
        in_specs=[SMEM] + [ANY] * len(pieces) + [VMEM] * 3,
        out_specs=[VMEM] * 10,
        out_shape=[o(shape, bf16) for shape in shapes]
        + [
            o((vocab, 3 * heads * HD), f32),
            o((vocab, ff_local), f32),
            o(((heads + 2) * vocab, D), bf16),
            o((vocab, D), bf16),
            o((vocab, ff_local), bf16),
            o((heads * vocab, heads * HD), bf16),
        ],
        scratch_shapes=[
            pltpu.VMEM((total, BS, BS), bf16),
            pltpu.SemaphoreType.DMA((len(pieces),)),
        ],
        name="tables",
        **params(8),
    )(place, *pieces, embedding, vectors, fc_bias)


def rotary_tables(seq_len):
    half = ROT // 2
    frequency = np.float32(10000.0) ** (
        np.float32(-2.0) * np.arange(half, dtype=np.float32) / np.float32(ROT)
    )
    angles = np.arange(seq_len, dtype=np.float32)[:, None] * frequency[None, :].astype(np.float32)
    cosine = np.cos(angles.astype(np.float64)).astype(np.float32)
    sine = np.sin(angles.astype(np.float64)).astype(np.float32)
    wide_cos = np.ones((seq_len, WIDE), np.float32)
    wide_sin = np.zeros((seq_len, WIDE), np.float32)
    wide_cos[:, :half], wide_cos[:, half:ROT] = cosine, cosine
    wide_sin[:, :half], wide_sin[:, half:ROT] = sine, sine
    return wide_cos, wide_sin, np.ascontiguousarray(cosine.T), np.ascontiguousarray(sine.T)


def turned(x):
    half = ROT // 2
    lane = lanes(x.shape)
    return jnp.where(
        lane < half,
        -pltpu.roll(x, WIDE - half, 1),
        jnp.where(lane < ROT, pltpu.roll(x, half, 1), 0.0),
    )


def head_lanes(table, index):
    begin = index // 2 * WIDE
    chunk = table[:, begin : begin + WIDE]
    if index % 2:
        chunk = pltpu.roll(chunk, HD, 1)
    return jnp.where(lanes(chunk.shape) < HD, chunk, 0.0)


def stack_parts(table):
    high, middle, rest = split3(table)
    return jnp.concatenate([high, middle, rest, jnp.zeros_like(high)], axis=0)


def attention_kernel(
    heads, length, token_col, proj, cosine, sine, query_o, key_o, weight_o, low_o, hot, key_hot, queries, wide
):
    seq = token_col.shape[0]
    vocab = proj.shape[0]
    lane = lanes((seq, WIDE))
    hot[...] = jnp.where(lane % vocab == token_col[...], 1.0, 0.0).astype(bf16)
    for h in range(heads):
        key_hot[h] = jnp.where(lane == token_col[...] + h * vocab, 1.0, 0.0).astype(bf16)
    one = lanes((vocab, WIDE)) == HD
    ones = (lanes((vocab, WIDE)) > HD) & (lanes((vocab, WIDE)) < HD + 4)
    for which in range(2):
        for h in range(heads):
            own = head_lanes(proj, which * heads + h)
            other = turned(own)
            if which == 0:
                own = jnp.where(one, 1.0, own * 0.125)
                other = other * 0.125
            else:
                own = jnp.where(one | ones, 1.0, own)
            begin = (which * heads + h) * 2 * WIDE
            wide[:, begin : begin + WIDE] = stack_parts(own)
            wide[:, begin + WIDE : begin + 2 * WIDE] = stack_parts(other)
    for i in range(seq // ROWS):
        span = slice(i * ROWS, (i + 1) * ROWS)
        part = hot[span]
        position = i * ROWS + sublanes((ROWS, WIDE))
        bias = jnp.where(position < length[0], 0.0, MASKED)
        cos, sin = cosine[span], sine[span]
        key_cos = jnp.where(lanes((ROWS, WIDE)) == HD, bias, cos)
        for h in range(heads):
            both = dot(part, wide[:, h * 2 * WIDE : (h + 1) * 2 * WIDE])
            queries[h, span] = (both[:, :WIDE] * cos + both[:, WIDE:] * sin).astype(bf16)
            k = heads + h
            both = dot(part, wide[:, k * 2 * WIDE : (k + 1) * 2 * WIDE])
            key_o[h, span] = (both[:, :WIDE] * key_cos + both[:, WIDE:] * sin).astype(bf16)
    allowed = lanes((ROWS, ROWS)) <= sublanes((ROWS, ROWS))
    small = lanes((ROWS, WIDE))
    for i in range(seq // ROWS):
        span = slice(i * ROWS, (i + 1) * ROWS)
        past = i * ROWS
        weights = jnp.zeros((ROWS, WIDE), f32)
        for h in range(heads):
            query = queries[h, span]
            near = jnp.where(allowed, dot(query, key_o[h, span], NT), MASKED)
            top = jnp.max(near, axis=-1, keepdims=True)
            if past:
                far = dot(query, key_o[h, :past], NT)
                top = jnp.maximum(top, jnp.max(far, axis=-1, keepdims=True))
                far = jnp.exp(far - top)
            near = jnp.exp(near - top)
            total = jnp.sum(near, axis=-1, keepdims=True)
            if past:
                total = total + jnp.sum(far, axis=-1, keepdims=True)
            share = 1.0 / total
            weights = weights + dot((near * share).astype(bf16), key_hot[h, span])
            if past:
                weights = weights + dot((far * share).astype(bf16), key_hot[h, :past])
            minus = -(top + jnp.log(total))
            high = minus.astype(bf16).astype(f32)
            middle = (minus - high).astype(bf16).astype(f32)
            rest = minus - high - middle
            query_o[h, span] = jnp.where(
                small == HD + 1,
                high,
                jnp.where(
                    small == HD + 2, middle, jnp.where(small == HD + 3, rest, query.astype(f32))
                ),
            ).astype(bf16)
        weight_o[span] = weights[:, : heads * vocab]
        low_o[span] = weights[:, : heads * vocab].astype(bf16)


def attention(length, token_col, proj, cosine, sine, heads):
    seq = token_col.shape[0]
    vocab = proj.shape[0]
    o = jax.ShapeDtypeStruct
    return pl.pallas_call(
        functools.partial(attention_kernel, heads),
        in_specs=[SMEM] + [VMEM] * 4,
        out_specs=[VMEM] * 4,
        out_shape=[
            o((heads, seq, WIDE), bf16),
            o((heads, seq, WIDE), bf16),
            o((seq, heads * vocab), f32),
            o((seq, heads * vocab), bf16),
        ],
        scratch_shapes=[
            pltpu.VMEM((seq, WIDE), bf16),
            pltpu.VMEM((heads, seq, WIDE), bf16),
            pltpu.VMEM((heads, seq, WIDE), bf16),
            pltpu.VMEM((WIDE, heads * 4 * WIDE), bf16),
        ],
        name="attention",
        **params(11),
    )(length, token_col, proj, cosine, sine)


def attention_back_kernel(
    heads,
    token_col,
    token_row,
    query,
    key,
    weight,
    weight_grad,
    cosine,
    sine,
    cosine_t,
    sine_t,
    table_o,
    hot,
    mixed,
    query_grad,
    key_grad,
):
    seq = token_col.shape[0]
    vocab = weight.shape[1] // heads
    half = ROT // 2
    lane = lanes((seq, WIDE))
    hot[...] = jnp.where(
        (lane == token_col[...]) | (lane == token_col[...] + vocab) | ((lane >= HD) & (lane < HD + 3)),
        1.0,
        0.0,
    ).astype(bf16)
    both = weight[...] * weight_grad[...]
    grads = weight_grad[...]
    if heads * vocab < WIDE:
        pad = jnp.zeros((seq, WIDE - heads * vocab), f32)
        both = jnp.concatenate([both, pad], axis=1)
        grads = jnp.concatenate([grads, pad], axis=1)
    for h in range(heads):
        inside = (lane >= h * vocab) & (lane < (h + 1) * vocab)
        minus = -jnp.sum(jnp.where(inside, both, 0.0), axis=-1, keepdims=True)
        own = grads if h == 0 else pltpu.roll(grads, WIDE - h * vocab, 1)
        own = jnp.where(lane < vocab, own, 0.0)
        high, rest = split2(own)
        m_high = minus.astype(bf16).astype(f32)
        m_middle = (minus - m_high).astype(bf16).astype(f32)
        m_rest = minus - m_high - m_middle
        value = high.astype(f32) + pltpu.roll(rest.astype(f32), vocab, 1)
        value = jnp.where(lane == HD, m_high, value)
        value = jnp.where(lane == HD + 1, m_middle, value)
        value = jnp.where(lane == HD + 2, m_rest, value)
        mixed[h] = value.astype(bf16)
    allowed = lanes((ROWS, ROWS)) <= sublanes((ROWS, ROWS))
    key_grad[...] = jnp.zeros_like(key_grad)
    for h in range(heads):
        for i in range(seq // ROWS):
            span = slice(i * ROWS, (i + 1) * ROWS)
            past = i * ROWS
            part = query[h, span]
            near = jnp.where(allowed, jnp.exp(dot(part, key[h, span], NT)), 0.0)
            near = (near * dot(mixed[h, span], hot[span], NT)).astype(bf16)
            grad = dot(near, key[h, span])
            key_grad[h, :, span] += dot(part, near, TN)[:HD]
            if past:
                far = jnp.exp(dot(part, key[h, :past], NT))
                far = (far * dot(mixed[h, span], hot[:past], NT)).astype(bf16)
                grad = grad + dot(far, key[h, :past])
                key_grad[h, :, :past] += dot(part, far, TN)[:HD]
            grad = grad * 0.125
            query_grad[h, span] = (grad * cosine[span] - turned(grad) * sine[span]).astype(bf16)
    shape = (vocab, seq)
    token_hot = jnp.where(sublanes(shape) == token_row[...], 1.0, 0.0).astype(bf16)
    small = lanes((vocab, WIDE)) < HD
    cos_t, sin_t = cosine_t[...], sine_t[...]
    for pair in range(heads // 2):
        one = dot(token_hot, query_grad[2 * pair])
        two = pltpu.roll(dot(token_hot, query_grad[2 * pair + 1]), HD, 1)
        table_o[:, pair * WIDE : (pair + 1) * WIDE] = jnp.where(small, one, two)
        turned_keys = []
        for h in (2 * pair, 2 * pair + 1):
            front, back = key_grad[h, :half], key_grad[h, half:ROT]
            turned_keys += [
                front * cos_t + back * sin_t,
                back * cos_t - front * sin_t,
                key_grad[h, ROT:],
            ]
        keys = jnp.concatenate(turned_keys, axis=0).astype(bf16)
        begin = heads * HD + pair * WIDE
        table_o[:, begin : begin + WIDE] = dot(token_hot, keys, NT)


def attention_back(
    token_col, token_row, query, key, weight, weight_grad, cosine, sine, cosine_t, sine_t, heads
):
    seq = token_col.shape[0]
    vocab = weight.shape[1] // heads
    return pl.pallas_call(
        functools.partial(attention_back_kernel, heads),
        in_specs=[VMEM] * 10,
        out_specs=VMEM,
        out_shape=jax.ShapeDtypeStruct((vocab, 2 * heads * HD), f32),
        scratch_shapes=[
            pltpu.VMEM((seq, WIDE), bf16),
            pltpu.VMEM((heads, seq, WIDE), bf16),
            pltpu.VMEM((heads, seq, WIDE), bf16),
            pltpu.VMEM((heads, HD, seq), f32),
        ],
        name="attention_back",
        **params(11),
    )(token_col, token_row, query, key, weight, weight_grad, cosine, sine, cosine_t, sine_t)


def loss_kernel(
    parts,
    heads,
    ints,
    floats,
    token_col,
    target_col,
    token_row,
    embed,
    head,
    vec,
    *refs,
):
    weights, refs = refs[:parts], refs[parts:]
    payload, mine, others = refs[0], refs[1:parts], refs[parts : 2 * parts - 1]
    sums_o, grad_o, mixing, low_weights, table = refs[2 * parts - 1 :]
    step = pl.program_id(0)
    me, length, upper = ints[0], ints[1], ints[2]
    vocab = embed.shape[0]
    height = heads * vocab

    @pl.when(step == 0)
    def _():
        mixing[me] = payload[...]
        size = payload.shape[0] // 2
        for r in range(1, parts):
            mixing[me ^ r, pl.ds(pl.multiple_of(upper * size, size), size)] = mine[r - 1][...]
            mixing[me ^ r, pl.ds(pl.multiple_of((1 - upper) * size, size), size)] = others[r - 1][...]
        down = jnp.zeros((vocab, D), f32)
        for g in range(parts):
            one = mixing[g, height:].astype(f32)
            down = down + (one[:vocab] + one[vocab:])
        table[...] = stack_parts(embed[...] + (down + vec[2:3]))
        sums_o[...] = jnp.zeros_like(sums_o)

    for r in range(parts):
        low_weights[me ^ r] = weights[r][...]
    token = token_col[...]
    hot = jnp.where(lanes((ROWS, WIDE)) % vocab == token, 1.0, 0.0).astype(bf16)
    x = dot(hot, table[...])
    x = x + dot(
        jnp.concatenate([low_weights[g] for g in range(parts)], axis=1),
        jnp.concatenate([mixing[g, :height] for g in range(parts)], axis=0),
    )
    normed, scale = stats_of(x)
    gain = vec[3:4]
    final = (normed * gain + vec[4:5]).astype(bf16)
    head_low = head[:, :D].astype(bf16)
    square = (vocab, vocab)
    bias_row = jnp.sum(
        jnp.where(lanes(square) == sublanes(square), head[:, D : D + 1], 0.0), axis=0, keepdims=True
    )
    logits = dot(final, head_low, NT) + bias_row
    shifted = logits - jnp.max(logits, axis=-1, keepdims=True)
    log_probs = shifted - jnp.log(jnp.sum(jnp.exp(shifted), axis=-1, keepdims=True))
    target = lanes((ROWS, vocab)) == target_col[...]
    position = step * ROWS + sublanes((ROWS, 1))
    slot_weight = jnp.where(position < length - 1, floats[0], 0.0)
    picked = jnp.sum(jnp.where(target, log_probs, 0.0), axis=-1, keepdims=True)
    loss = -jnp.sum(slot_weight * picked, keepdims=True)
    logit_grad = ((jnp.exp(log_probs) - jnp.where(target, 1.0, 0.0)) * slot_weight).astype(bf16)
    final_grad = dot(logit_grad, head_low)
    grad = norm_back(final_grad, normed, scale, gain)
    high = grad.astype(bf16)
    token_hot = jnp.where(sublanes((vocab, ROWS)) == token_row[...], 1.0, 0.0).astype(bf16)
    own = weights[0][...].astype(f32)
    if height < WIDE:
        own = jnp.concatenate([own, jnp.zeros((ROWS, WIDE - height), f32)], axis=1)
    both = dot(jnp.concatenate([own.T.astype(bf16), token_hot], axis=0), high)
    sums_o[0:vocab] += both[WIDE:]
    sums_o[vocab : 2 * vocab] += dot(logit_grad, final, TN)
    base = 2 * vocab
    sums_o[base : base + 1] += jnp.sum(final_grad * normed, axis=0, keepdims=True)
    sums_o[base + 1 : base + 2] += jnp.sum(final_grad, axis=0, keepdims=True)
    bias_grad = jnp.sum(logit_grad.astype(f32), axis=0, keepdims=True)
    sums_o[base + 2 : base + 3, :vocab] += bias_grad
    lane = lanes((1, WIDE))
    count = jnp.where((step == 0) & (length >= 2), 1.0, 0.0)
    sums_o[base + 3 : base + 4, :WIDE] += jnp.where(
        lane == 0, loss, jnp.where(lane == 1, count, 0.0)
    )
    sums_o[base + 16 : base + 16 + height] += both[:height]
    grad_o[...] = dot(high, payload[:height], NT)


def loss_rows(
    ints,
    floats,
    token_col,
    target_col,
    token_row,
    embedding,
    head,
    vectors,
    weights,
    payload,
    mine,
    others,
    heads,
):
    seq = token_col.shape[0]
    vocab = embedding.shape[0]
    parts = len(weights)
    height = heads * vocab
    col = pl.BlockSpec((ROWS, 1), lambda i: (i, 0))
    o = jax.ShapeDtypeStruct
    full = lambda array: pl.BlockSpec(array.shape, lambda i: (0,) * array.ndim)
    sums_shape = (2 * vocab + 16 + height, D)
    return pl.pallas_call(
        functools.partial(loss_kernel, parts, heads),
        grid=(seq // ROWS,),
        in_specs=[SMEM, SMEM, col, col, pl.BlockSpec((1, ROWS), lambda i: (0, i))]
        + [full(embedding), full(head), full(vectors)]
        + [pl.BlockSpec((ROWS, height), lambda i: (i, 0))] * parts
        + [full(payload)]
        + [full(mine[0])] * (2 * parts - 2),
        out_specs=[
            pl.BlockSpec(sums_shape, lambda i: (0, 0)),
            pl.BlockSpec((ROWS, height), lambda i: (i, 0)),
        ],
        out_shape=[o(sums_shape, f32), o((seq, height), f32)],
        scratch_shapes=[
            pltpu.VMEM((parts,) + payload.shape, bf16),
            pltpu.VMEM((parts, ROWS, height), bf16),
            pltpu.VMEM((4 * vocab, D), bf16),
        ],
        name="loss_rows",
        **params(12),
    )(
        ints,
        floats,
        token_col,
        target_col,
        token_row,
        embedding,
        head,
        vectors,
        *weights,
        payload,
        *mine,
        *others,
    )


def padded(block):
    lacking = HB - block.shape[0]
    if lacking:
        block = jnp.concatenate([block, jnp.zeros((lacking, block.shape[1]), block.dtype)], axis=0)
    return block


def factors_kernel(
    heads,
    sums,
    table,
    mat_q,
    mat_o,
    mat_u,
    mat_f,
    upper,
    normed,
    act,
    values,
    left_o,
    right_o,
    hidden_o,
    bias_o,
):
    vocab = normed.shape[0]
    width = mat_u.shape[1]
    rows = sums[0:vocab]
    mixed = sums[2 * vocab + 16 :]
    act_grad = rows_times_low(rows, mat_f[...], NT)
    u = upper[...]
    tanh = jnp.tanh(GELU_A * (u + GELU_B * (u * u * u)))
    slope = 0.5 * (1.0 + tanh) + 0.5 * u * (1.0 - tanh * tanh) * (
        GELU_A * (1.0 + 3.0 * GELU_B * (u * u))
    )
    upper_grad = act_grad * slope
    bias_grad = jnp.sum(upper_grad, axis=0, keepdims=True)
    bias_o[...] = bias_grad
    value_grad = rows_times_low(mixed, mat_o[...], NT)
    shape = value_grad.shape
    value_grad = jnp.where(sublanes(shape) // vocab == lanes(shape) // HD, value_grad, 0.0)
    value_table = value_grad[:vocab]
    for h in range(1, heads):
        value_table = value_table + value_grad[h * vocab : (h + 1) * vocab]
    proj_grad = jnp.concatenate([table[...], value_table], axis=1)
    hidden = rows_times_low(upper_grad, mat_u[...], NT) + rows_times_low(proj_grad, mat_q[...], NT)
    hidden_o[0:vocab] = hidden
    low = normed[...].astype(f32)
    own = act[...].astype(f32)
    val = values[...].astype(f32)
    normed_gram = dot6(low, low, NT)
    square = (
        jnp.sum(normed_gram * dot6(proj_grad, proj_grad, NT), keepdims=True)
        + jnp.sum(normed_gram * dot6(upper_grad, upper_grad, NT), keepdims=True)
        + jnp.sum(dot6(own, own, NT) * dot6(rows, rows, NT), keepdims=True)
        + jnp.sum(dot6(val, val, NT) * dot6(mixed, mixed, NT), keepdims=True)
        + jnp.sum(bias_grad * bias_grad, keepdims=True)
    )
    hidden_o[vocab : vocab + 16] = jnp.broadcast_to(square, (16, D))

    def put_left(index, block):
        block = padded(block)
        left_o[index] = jnp.concatenate([block] * 3, axis=0).astype(bf16)

    def put_right(index, block):
        left_o_parts = split3(padded(block))
        right_o[index] = jnp.concatenate(left_o_parts, axis=0)

    at = 0
    for i in range(D // BS):
        put_left(at, low[:, i * BS : (i + 1) * BS])
        at += 1
    for i in range(width // BS):
        put_left(at, own[:, i * BS : (i + 1) * BS])
        at += 1
    pair = 2 * vocab
    for i in range(heads // 2):
        put_left(at, val[i * pair : (i + 1) * pair, i * BS : (i + 1) * BS])
        at += 1
    at = 0
    for k in range(3 * heads * HD // BS):
        put_right(at, proj_grad[:, k * BS : (k + 1) * BS])
        at += 1
    for i in range(heads // 2):
        for k in range(D // BS):
            put_right(at, mixed[i * pair : (i + 1) * pair, k * BS : (k + 1) * BS])
            at += 1
    for k in range(width // BS):
        put_right(at, upper_grad[:, k * BS : (k + 1) * BS])
        at += 1
    for k in range(D // BS):
        put_right(at, rows[:, k * BS : (k + 1) * BS])
        at += 1


def factor_places(heads, ff_local):
    q_cols = 3 * heads * HD // BS
    o_rows = heads // 2
    across = D // BS
    f_rows = ff_local // BS
    left, right = [], []
    for which, i, k in tile_places(layer_shapes(heads, ff_local)):
        if which == 0:
            left.append(i)
            right.append(k)
        elif which == 1:
            left.append(across + f_rows + i)
            right.append(q_cols + i * across + k)
        elif which == 2:
            left.append(i)
            right.append(q_cols + o_rows * across + k)
        else:
            left.append(across + i)
            right.append(q_cols + o_rows * across + f_rows + k)
    return np.array(left, np.int32), np.array(right, np.int32)


def factors(sums, table, mats, upper, normed, act, values, heads):
    vocab = normed.shape[0]
    ff_local = upper.shape[1]
    n_left = D // BS + ff_local // BS + heads // 2
    n_right = 3 * heads * HD // BS + heads // 2 * (D // BS) + ff_local // BS + D // BS
    o = jax.ShapeDtypeStruct
    return pl.pallas_call(
        functools.partial(factors_kernel, heads),
        in_specs=[VMEM] * 10,
        out_specs=[VMEM] * 4,
        out_shape=[
            o((n_left, 3 * HB, BS), bf16),
            o((n_right, 3 * HB, BS), bf16),
            o((vocab + 16, D), f32),
            o((1, ff_local), f32),
        ],
        name="factors",
        **params(7),
    )(sums, table, *mats, upper, normed, act, values)


def small_kernel(parts, corrections, ints, sums, own, *refs):
    mine, others, refs = refs[: parts - 1], refs[parts - 1 : 2 * parts - 2], refs[2 * parts - 2 :]
    bias_grad, refs = refs[0], refs[1:]
    weights, refs = refs[:12], refs[12:]
    outs, scalars, total = refs[:12], refs[12], refs[13]
    vocab = weights[0].shape[0]
    base = 2 * vocab
    size = own.shape[0] // 2
    for place, group in ((ints[0], mine), (1 - ints[0], others)):
        span = pl.ds(pl.multiple_of(place * size, size), size)
        total[span] = tree_sum([own[span]] + [ref[...] for ref in group])
    hidden = total[:vocab]
    square = total[vocab : vocab + 1, 0:1]
    rows = sums[0:vocab]
    normed, scale = stats_of(weights[0][...])
    gain = weights[6][0:1]
    embed_grad = rows + norm_back(hidden, normed, scale, gain)
    vector_grad = jnp.concatenate(
        [
            jnp.sum(hidden * normed, axis=0, keepdims=True),
            jnp.sum(hidden, axis=0, keepdims=True),
            jnp.sum(rows, axis=0, keepdims=True),
            sums[base : base + 1],
            sums[base + 1 : base + 2],
        ],
        axis=0,
    )
    head_grad = sums[vocab : 2 * vocab]
    head_bias = sums[base + 2 : base + 3, :vocab]
    add = lambda value: jnp.sum(value * value, keepdims=True)
    square = square + add(embed_grad) + add(vector_grad) + add(head_grad) + add(head_bias)
    count = sums[base + 3 : base + 4, 1:2]
    loss = sums[base + 3 : base + 4, 0:1] / count
    norm = jnp.sqrt(square) / count
    scale_all = jnp.minimum(1.0, CLIP_NORM / norm) / count
    one, two = corrections[0], corrections[1]

    def update(index, pick, grad):
        weight, first, second = (weights[3 * index + k][pick] for k in range(3))
        grad = grad * scale_all
        first = BETA_ONE * first + (1.0 - BETA_ONE) * grad
        second = BETA_TWO * second + (1.0 - BETA_TWO) * grad * grad
        step = first / one / (jnp.sqrt(second / two) + ADAM_EPS)
        outs[3 * index][pick] = weight - RATE_SMALL * (step + WEIGHT_DECAY * weight)
        outs[3 * index + 1][pick] = first
        outs[3 * index + 2][pick] = second

    everything = slice(None)
    update(0, everything, embed_grad)
    shape = (vocab, vocab)
    head_column = jnp.sum(
        jnp.where(lanes(shape) == sublanes(shape), head_bias, 0.0), axis=1, keepdims=True
    )
    update(1, (everything, slice(0, D)), head_grad)
    update(1, (everything, slice(D, D + 1)), head_column)
    update(2, everything, vector_grad)
    update(3, everything, bias_grad[...])
    lane = lanes((1, WIDE))
    scalars[...] = jnp.where(
        lane == 0, scale_all, jnp.where(lane == 1, loss, jnp.where(lane == 2, norm, 0.0))
    )


def small(corrections, upper, sums, hidden, mine, others, bias_grad, weights):
    o = jax.ShapeDtypeStruct
    return pl.pallas_call(
        functools.partial(small_kernel, 1 + len(mine)),
        in_specs=[SMEM] * 2 + [VMEM] * (2 + 2 * len(mine) + 1 + 12),
        out_specs=[VMEM] * 13,
        out_shape=[o(weight.shape, f32) for weight in weights] + [o((1, WIDE), f32)],
        scratch_shapes=[pltpu.VMEM(hidden.shape, f32)],
        name="small",
        **params(4),
    )(corrections, upper, sums, hidden, *mine, *others, bias_grad, *weights)


GROUP = 0
UN = 3


def eliminate(work, count):
    lane=lax.broadcasted_iota(jnp.int32,(HB,BS),1)
    sub=lax.broadcasted_iota(jnp.int32,(HB,BS),0)
    half=jnp.where(lane>=HB,HB,0)
    for g0 in range(HB//8):
        r0=8*g0
        rows=HB-r0
        def body(jj,carry):
            j=r0+jj
            pick=half[:rows]+j
            at_pivot=lane[:rows]==pick
            below=sub[:rows]>jj
            clear=at_pivot&below
            group=GROUP or count
            for t0 in range(0,count,group):
                span=range(t0,t0+group)
                rows_in=[work[t,pl.ds(j,1),:] for t in span]
                kept=[work[t,r0:,:] for t in span]
                wides=[jnp.broadcast_to(row,(8,BS)) for row in rows_in]
                pivots=[jnp.take_along_axis(w,pick[:8],axis=1,mode="promise_in_bounds") for w in wides]
                cs=[jnp.take_along_axis(a,pick,axis=1,mode="promise_in_bounds") for a in kept]
                scaleds=[jnp.where(at_pivot[:8],1.0,w)/p for w,p in zip(wides,pivots)]
                for t,a,c,sc in zip(span,kept,cs,scaleds):
                    work[t,r0:,:]=jnp.where(clear,0.0,a)-jnp.where(below,c,0.0)*sc[:1]
            return carry
        lax.fori_loop(0,8,body,0)

def factor_inverse(packed):
    lane=lax.broadcasted_iota(jnp.int32,(HB,BS),1)
    sub=lax.broadcasted_iota(jnp.int32,(HB,BS),0)
    left=lane<HB
    col=jnp.where(left,lane,lane-HB)
    diag=jnp.where(col==sub,packed,0.0)
    d_left=jnp.sum(jnp.where(left,diag,0.0),axis=1,keepdims=True)
    d_right=jnp.sum(jnp.where(left,0.0,diag),axis=1,keepdims=True)
    scale=lax.rsqrt(jnp.where(left,d_left,d_right))
    unit=jnp.where(col<sub,packed,jnp.where(col==sub,1.0,0.0))
    return unit*scale

def block_diagonal(packed):
    lane=lax.broadcasted_iota(jnp.int32,(HB,BS),1)
    left=lane<HB
    return jnp.concatenate([jnp.where(left,packed,0.0),jnp.where(left,0.0,packed)],axis=0)

def swap(x):
    return pltpu.roll(x,HB,1)

def soap_kernel(count, per, corrections, scal, left_at, right_at, lefts, rights, W, m, v, L, R, QL, QR, W_o, low_o, m_o, v_o, L_o, R_o, QL_o, QR_o, ML_s, MR_s, work, A21_s, A22_s, W11_s):
    step=pl.program_id(0)
    scale=scal[0:1,0:1]; c1=corrections[0]; c2=corrections[1]
    left=lax.broadcasted_iota(jnp.int32,(HB,BS),1)<HB
    span=range(per)
    pairs=[(lefts[left_at[step*per+s]],rights[right_at[step*per+s]]) for s in span]
    g=[dot(a,b,TN)*scale for a,b in pairs]
    gT=[dot(b,a,TN)*scale for a,b in pairs]
    qT=[QL[s].T for s in span]
    ggl=[dot3(x,x,NT) for x in g]
    ggr=[dot3(x,x,NT) for x in gT]
    rot=[dot3(q,x,NN) for q,x in zip(qT,g)]
    Ln=[BETA_TWO*L[s]+(1-BETA_TWO)*ggl[s] for s in span]
    Rn=[BETA_TWO*R[s]+(1-BETA_TWO)*ggr[s] for s in span]
    rot=[dot3(x,QR[s],NN) for s,x in enumerate(rot)]
    for s in span:
        L_o[s]=Ln[s]; R_o[s]=Rn[s]
    ML=[dot6(Ln[s],QL[s],NN) for s in span]
    MR=[dot6(Rn[s],QR[s],NN) for s in span]
    xs=[]
    for s in span:
        mn=BETA_ONE*m[s]+(1-BETA_ONE)*rot[s]
        vn=BETA_TWO*v[s]+(1-BETA_TWO)*rot[s]*rot[s]
        m_o[s]=mn; v_o[s]=vn
        xs.append((mn/c1)/(jnp.sqrt(vn/c2)+ADAM_EPS))
    back=[dot3(QL[s],xs[s],NN) for s in span]
    ML=[x*lax.rsqrt(jnp.sum(x*x,keepdims=True)) for x in ML]
    MR=[x*lax.rsqrt(jnp.sum(x*x,keepdims=True)) for x in MR]
    back=[dot3(back[s],QR[s],NT) for s in span]
    AL=[dot6(x,x,TN) for x in ML]
    AR=[dot6(x,x,TN) for x in MR]
    for s in span:
        w=W[s]
        wn=w-RATE_TILES*(back[s]+WEIGHT_DECAY*w)
        W_o[s]=wn
        low_o[s]=wn.astype(bf16)
        t=step*per+s
        ML_s[t]=ML[s]; MR_s[t]=MR[s]
        work[t]=jnp.where(left,AL[s][:HB],swap(AR[s][:HB]))
        A21_s[t]=jnp.where(left,AL[s][HB:],swap(AR[s][HB:]))
        A22_s[t]=jnp.where(left,swap(AL[s][HB:]),AR[s][HB:])

    @pl.when(step==pl.num_programs(0)-1)
    def _():
        eliminate(work,count)
        def mid(i,carry):
            ts=[i*UN+k for k in range(UN)]
            w11=[factor_inverse(work[t]) for t in ts]
            for t,w in zip(ts,w11): W11_s[t]=w
            l21=[dot6(A21_s[t],block_diagonal(w),NT) for t,w in zip(ts,w11)]
            for t,l in zip(ts,l21): A21_s[t]=l
            low=[dot6(l,block_diagonal(l),NT) for l in l21]
            for t,l in zip(ts,low): work[t]=A22_s[t]-l
            return carry
        lax.fori_loop(0,count//UN,mid,0)
        eliminate(work,count)
        def last(i,carry):
            ts=[i*UN+k for k in range(UN)]
            w22=[factor_inverse(work[t]) for t in ts]
            w11=[W11_s[t] for t in ts]
            y=[dot6(A21_s[t],block_diagonal(w),NN) for t,w in zip(ts,w11)]
            w21=[-dot6(w,block_diagonal(x),NN) for w,x in zip(w22,y)]
            cl=[jnp.concatenate([jnp.where(left,a,0.0),jnp.where(left,b,swap(c))],axis=0) for a,b,c in zip(w11,w21,w22)]
            cr=[jnp.concatenate([jnp.where(left,swap(a),0.0),jnp.where(left,swap(b),c)],axis=0) for a,b,c in zip(w11,w21,w22)]
            ol=[dot3(ML_s[t],c,NT) for t,c in zip(ts,cl)]
            orr=[dot3(MR_s[t],c,NT) for t,c in zip(ts,cr)]
            for t,a,b in zip(ts,ol,orr):
                QL_o[t]=a; QR_o[t]=b
            return carry
        lax.fori_loop(0,count//UN,last,0)

def soap(corrections,scal,left_at,right_at,lefts,rights,W,m,v,L,R,QL,QR):
    count=W.shape[0]
    per=3 if count%3==0 else 1
    blk=pl.BlockSpec((per,BS,BS),lambda i:(i,0,0))
    full=pl.BlockSpec((count,BS,BS),lambda i:(0,0,0))
    whole=lambda x:pl.BlockSpec(x.shape,lambda i:(0,0,0))
    o=lambda dt: jax.ShapeDtypeStruct((count,BS,BS),dt)
    return pl.pallas_call(
        functools.partial(soap_kernel,count,per),
        grid=(count//per,),
        in_specs=[SMEM,pl.BlockSpec((1,WIDE),lambda i:(0,0)),SMEM,SMEM]+[whole(lefts),whole(rights)]+[blk]*7,
        out_specs=[blk]*6+[full]*2,
        out_shape=[o(f32),o(bf16),o(f32),o(f32),o(f32),o(f32),o(f32),o(f32)],
        scratch_shapes=[pltpu.VMEM((count,BS,BS),f32)]*2+[pltpu.VMEM((count,HB,BS),f32)]*4,
        compiler_params=pltpu.CompilerParams(vmem_limit_bytes=56*1024*1024),
        name="soap_tiles",
    )(corrections,scal,left_at,right_at,lefts,rights,W,m,v,L,R,QL,QR)


def local(
    tokens,
    lengths,
    tile_owner,
    step_count,
    weight_tiles,
    tiles_first,
    tiles_second,
    stats_left,
    stats_right,
    basis_left,
    basis_right,
    embedding,
    embedding_first,
    embedding_second,
    head_table,
    head_first,
    head_second,
    vectors,
    vectors_first,
    vectors_second,
    fc_bias,
    fc_bias_first,
    fc_bias_second,
):
    seq = tokens.shape[1]
    mp_count = lax.axis_size("mp")
    dp_count = lax.axis_size("dp")
    dp_index = lax.axis_index("dp")
    mp_index = lax.axis_index("mp")
    upper_pair = dp_index & 1
    heads = H // mp_count
    ff_local = fc_bias.shape[1]
    count = weight_tiles.shape[0]
    half = count // 2

    halves = gather_tiles(weight_tiles.astype(bf16))
    pieces = halves[0] + halves[1]
    holder = tile_owner // count
    inside = tile_owner - holder * count
    place = (
        jnp.where(inside >= half, dp_count * half - half, 0) + (holder ^ dp_index) * half + inside
    )
    result = tables(place, pieces, embedding, vectors, fc_bias, heads, ff_local)
    mats, (proj, upper, payload, normed, act, values) = result[:4], result[4:]

    token_col = tokens.reshape(seq, 1)
    target_col = jnp.roll(tokens, -1, axis=1).reshape(seq, 1)
    cosine, sine, cosine_t, sine_t = rotary_tables(seq)
    parts, others = gather_shared(payload)
    query, key, weight, weight_low = attention(lengths, token_col, proj, cosine, sine, heads)
    weights = gather_xor(weight_low, "mp")
    length = lengths[0]
    inverse_length = 1.0 / jnp.maximum(length - 1, 1).astype(f32)
    sums, weight_grad = loss_rows(
        jnp.stack([mp_index, length, upper_pair]),
        inverse_length[None],
        token_col,
        target_col,
        tokens,
        embedding,
        head_table.T,
        vectors,
        weights,
        payload,
        parts,
        others,
        heads,
    )
    sums = sum_dp(sums)
    table = attention_back(
        token_col, tokens, query, key, weight, weight_grad, cosine, sine, cosine_t, sine_t, heads
    )
    table = sum_dp(table)
    left, right, hidden, bias_grad = factors(
        sums, table, mats, upper, normed, act, values, heads
    )
    hidden_parts, hidden_others = gather_shared(hidden)
    corrections = 1.0 - jnp.power(
        jnp.array([BETA_ONE, BETA_TWO], f32), step_count.astype(f32)
    )
    small_weights = (
        embedding,
        embedding_first,
        embedding_second,
        head_table.T,
        head_first.T,
        head_second.T,
        vectors,
        vectors_first,
        vectors_second,
        fc_bias,
        fc_bias_first,
        fc_bias_second,
    )
    *small_out, scalars = small(
        corrections,
        upper_pair[None],
        sums,
        hidden,
        hidden_parts,
        hidden_others,
        bias_grad,
        small_weights,
    )
    small_out[3:6] = [value.T for value in small_out[3:6]]
    slots = dp_index * count + jnp.arange(count, dtype=jnp.int32)
    natural = jnp.sum(
        jnp.where(
            tile_owner[None, :] == slots[:, None],
            jnp.arange(tile_owner.shape[0], dtype=jnp.int32)[None, :],
            0,
        ),
        axis=1,
    )
    left_of, right_of = factor_places(heads, ff_local)
    same = natural[:, None] == jnp.arange(tile_owner.shape[0], dtype=jnp.int32)[None, :]
    left_at = jnp.sum(jnp.where(same, left_of[None, :], 0), axis=1)
    right_at = jnp.sum(jnp.where(same, right_of[None, :], 0), axis=1)
    results = soap(
        corrections,
        scalars,
        left_at,
        right_at,
        left,
        right,
        weight_tiles,
        tiles_first,
        tiles_second,
        stats_left,
        stats_right,
        basis_left,
        basis_right,
    )
    return (scalars[0, 1], scalars[0, 2], *results, *small_out)


def solution(mesh):
    tiled = P("dp", None, "mp")
    split = P(None, "mp")
    in_specs = (P("dp", None), P("dp"), P(), P(), *[tiled] * 7, *[P()] * 9, *[split] * 3)
    out_specs = (P(), P(), *[tiled] * 8, *[P()] * 9, *[split] * 3)
    return jax.shard_map(local, mesh=mesh, in_specs=in_specs, out_specs=out_specs, check_vma=False)
```

```python
import functools
import math

import jax
import jax.numpy as jnp
import numpy as np
from jax import lax
from jax.experimental import pallas as pl
from jax.experimental.pallas import tpu as pltpu
from jax.sharding import PartitionSpec as P

D = 1024
H = 16
HD = 64
ROT = 32
BS = 128
HB = 64
ROWS = 256
WIDE = 128
MEGA = 1024 * 1024

NORM_EPS = 1e-05
CLIP_NORM = 0.02
RATE_TILES = 0.02
RATE_SMALL = 0.2
BETA_ONE = 0.9
BETA_TWO = 0.95
ADAM_EPS = 1e-08
WEIGHT_DECAY = 0.01
MASKED = -1e30
GELU_A = math.sqrt(2.0 / math.pi)
GELU_B = 0.044715

NN = (((1,), (0,)), ((), ()))
NT = (((1,), (1,)), ((), ()))
TN = (((0,), (0,)), ((), ()))
f32 = jnp.float32
bf16 = jnp.bfloat16
SMEM = pl.BlockSpec(memory_space=pltpu.SMEM)
VMEM = pl.BlockSpec(memory_space=pltpu.VMEM)
ANY = pl.BlockSpec(memory_space=pl.ANY)


def dot(a, b, dims=NN):
    return lax.dot_general(a, b, dims, preferred_element_type=f32)


def split2(a):
    high = a.astype(bf16)
    return high, (a - high.astype(f32)).astype(bf16)


def split3(a):
    high = a.astype(bf16)
    rest = a - high.astype(f32)
    middle = rest.astype(bf16)
    return high, middle, (rest - middle.astype(f32)).astype(bf16)


def dot3(a, b, dims):
    (axis_a,), (axis_b,) = dims[0]
    ah, al = split2(a)
    bh, bl = split2(b)
    return dot(
        jnp.concatenate([ah, ah, al], axis=axis_a),
        jnp.concatenate([bh, bl, bh], axis=axis_b),
        dims,
    )


def dot6(a, b, dims):
    (axis_a,), (axis_b,) = dims[0]
    ah, am, al = split3(a)
    bh, bm, bl = split3(b)
    return dot(
        jnp.concatenate([ah, ah, am, am, ah, al], axis=axis_a),
        jnp.concatenate([bh, bm, bh, bm, bl, bh], axis=axis_b),
        dims,
    )


def rows_times_low(a, low, dims):
    count = a.shape[0]
    parts = dot(jnp.concatenate(split3(a), axis=0), low, dims)
    return parts[:count] + (parts[count : 2 * count] + parts[2 * count :])


def lanes(shape):
    return lax.broadcasted_iota(jnp.int32, shape, len(shape) - 1)


def sublanes(shape):
    return lax.broadcasted_iota(jnp.int32, shape, len(shape) - 2)


def stats_of(values):
    centred = values - jnp.mean(values, axis=-1, keepdims=True)
    spread = jnp.mean(centred * centred, axis=-1, keepdims=True)
    scale = lax.rsqrt(spread + NORM_EPS)
    return centred * scale, scale


def norm_back(grad, normed, scale, gain):
    inner = grad * gain
    mean_one = jnp.mean(inner, axis=-1, keepdims=True)
    mean_two = jnp.mean(inner * normed, axis=-1, keepdims=True)
    return scale * (inner - mean_one - normed * mean_two)


def params(microseconds):
    return dict(
        compiler_params=pltpu.CompilerParams(vmem_limit_bytes=56 * MEGA),
        cost_estimate=pl.CostEstimate(
            flops=int(microseconds * 1.1e9), bytes_accessed=int(microseconds * 1e6), transcendentals=0
        ),
    )


def swap_with(value, axis, mask):
    count = lax.axis_size(axis)
    return lax.ppermute(value, axis, [(i, i ^ mask) for i in range(count)])


def tree_sum(parts):
    while len(parts) > 1:
        parts = [parts[i] + parts[i + 1] for i in range(0, len(parts), 2)]
    return parts[0]


def gather_xor(value, axis):
    return [value] + [swap_with(value, axis, r) for r in range(1, lax.axis_size(axis))]


def gather_halves(value):
    upper = (lax.axis_index("dp") & 1) == 1
    half = value.shape[0] // 2
    mine = jnp.where(upper, value[half:], value[:half])
    return [swap_with(mine, "mp", r) for r in range(1, lax.axis_size("mp"))]


def swap_pair(parts):
    return [swap_with(part, "dp", 1) for part in parts]


def gather_tiles(low):
    count = lax.axis_size("dp")
    bits = [1 << k for k in reversed(range(count.bit_length() - 1))]
    half = low.shape[0] // 2
    result = []
    for which in range(2):
        order = bits if which == 0 or len(bits) < 3 else [bits[1], bits[0]] + bits[2:]
        pieces = {0: low[which * half : (which + 1) * half]}
        for bit in order:
            for mask in list(pieces):
                pieces[mask ^ bit] = swap_with(pieces[mask], "dp", bit)
        result.append([pieces[r] for r in range(count)])
    return result


def halved(value):
    upper = (lax.axis_index("dp") & 1) == 1
    half = value.shape[0] // 2
    first, second = value[:half], value[half:]
    return jnp.where(upper, second, first) + swap_with(jnp.where(upper, first, second), "dp", 1)


def completed(kept):
    upper = (lax.axis_index("dp") & 1) == 1
    bits = [1 << k for k in range(1, lax.axis_size("dp").bit_length() - 1)]
    half = (kept.shape[0] // 2 + 7) // 8 * 8
    pieces = [kept[:half], kept[half:]]
    for k in range(len(bits)):
        received = [
            swap_with(piece, "dp", order[k])
            for piece, order in zip(pieces, (bits, bits[1:] + bits[:1]))
        ]
        pieces = [piece + other for piece, other in zip(pieces, received)]
    total = jnp.concatenate(pieces, axis=0)
    other = swap_with(total, "dp", 1)
    return jnp.concatenate([jnp.where(upper, other, total), jnp.where(upper, total, other)], axis=0)


def sum_small(value):
    upper = (lax.axis_index("dp") & 1) == 1
    kept = halved(value)
    total = tree_sum(
        [kept] + [swap_with(kept, "dp", r) for r in range(2, lax.axis_size("dp"), 2)]
    )
    other = swap_with(total, "dp", 1)
    return jnp.concatenate([jnp.where(upper, other, total), jnp.where(upper, total, other)], axis=0)


def layer_shapes(heads_local, ff_local):
    return ((D, 3 * heads_local * HD), (heads_local * HD, D), (D, ff_local), (ff_local, D))


def tile_places(shapes):
    places = []
    for which, (row_total, col_total) in enumerate(shapes):
        for i in range(row_total // BS):
            for k in range(col_total // BS):
                places.append((which, i, k))
    return places


def tables_kernel(places, heads, pieces_n, place, *refs):
    pieces = refs[:pieces_n]
    (embed, vec, bias), refs = refs[pieces_n : pieces_n + 3], refs[pieces_n + 3 :]
    mats, (proj_o, upper_o, payload_o, normed_o, act_o, values_o, tiles, sems) = refs[:4], refs[4:]
    size = pieces[0].shape[0]
    copies = [
        pltpu.make_async_copy(piece, tiles.at[pl.ds(k * size, size)], sems.at[k])
        for k, piece in enumerate(pieces)
    ]
    for copy in copies:
        copy.start()
    normed, _ = stats_of(embed[...])
    low = (normed * vec[0:1] + vec[1:2]).astype(bf16)
    normed_o[...] = low
    for copy in copies:
        copy.wait()
    for index, (which, i, k) in enumerate(places):
        mats[which][i * BS : (i + 1) * BS, k * BS : (k + 1) * BS] = tiles[place[index]]
    proj = dot(low, mats[0][...])
    proj_o[...] = proj
    upper = dot(low, mats[2][...]) + bias[...]
    upper_o[...] = upper
    act = (0.5 * upper * (1.0 + jnp.tanh(GELU_A * (upper + GELU_B * (upper * upper * upper))))).astype(
        bf16
    )
    act_o[...] = act
    down = dot(act, mats[3][...])
    vocab = embed.shape[0]
    values = proj[:, 2 * heads * HD :]
    shape = (heads * vocab, heads * HD)
    values = jnp.concatenate([values] * heads, axis=0)
    same = sublanes(shape) // vocab == lanes(shape) // HD
    values = jnp.where(same, values, 0.0).astype(bf16)
    values_o[...] = values
    mixed = dot(values, mats[1][...])
    high, rest = split2(down)
    payload_o[...] = jnp.concatenate([mixed.astype(bf16), high, rest], axis=0)


def tables(place, pieces, embedding, vectors, fc_bias, heads, ff_local):
    shapes = layer_shapes(heads, ff_local)
    vocab = embedding.shape[0]
    o = jax.ShapeDtypeStruct
    total = len(pieces) * pieces[0].shape[0]
    return pl.pallas_call(
        functools.partial(tables_kernel, tile_places(shapes), heads, len(pieces)),
        in_specs=[SMEM] + [ANY] * len(pieces) + [VMEM] * 3,
        out_specs=[VMEM] * 10,
        out_shape=[o(shape, bf16) for shape in shapes]
        + [
            o((vocab, 3 * heads * HD), f32),
            o((vocab, ff_local), f32),
            o(((heads + 2) * vocab, D), bf16),
            o((vocab, D), bf16),
            o((vocab, ff_local), bf16),
            o((heads * vocab, heads * HD), bf16),
        ],
        scratch_shapes=[
            pltpu.VMEM((total, BS, BS), bf16),
            pltpu.SemaphoreType.DMA((len(pieces),)),
        ],
        name="tables",
        **params(8),
    )(place, *pieces, embedding, vectors, fc_bias)


def rotary_tables(seq_len):
    half = ROT // 2
    frequency = np.float32(10000.0) ** (
        np.float32(-2.0) * np.arange(half, dtype=np.float32) / np.float32(ROT)
    )
    angles = np.arange(seq_len, dtype=np.float32)[:, None] * frequency[None, :].astype(np.float32)
    cosine = np.cos(angles.astype(np.float64)).astype(np.float32)
    sine = np.sin(angles.astype(np.float64)).astype(np.float32)
    wide_cos = np.ones((seq_len, WIDE), np.float32)
    wide_sin = np.zeros((seq_len, WIDE), np.float32)
    wide_cos[:, :half], wide_cos[:, half:ROT] = cosine, cosine
    wide_sin[:, :half], wide_sin[:, half:ROT] = sine, sine
    return wide_cos, wide_sin, np.ascontiguousarray(cosine.T), np.ascontiguousarray(sine.T)


def turned(x):
    half = ROT // 2
    lane = lanes(x.shape)
    return jnp.where(
        lane < half,
        -pltpu.roll(x, WIDE - half, 1),
        jnp.where(lane < ROT, pltpu.roll(x, half, 1), 0.0),
    )


def head_lanes(table, index):
    begin = index // 2 * WIDE
    chunk = table[:, begin : begin + WIDE]
    if index % 2:
        chunk = pltpu.roll(chunk, HD, 1)
    return jnp.where(lanes(chunk.shape) < HD, chunk, 0.0)


def stack_parts(table):
    high, middle, rest = split3(table)
    return jnp.concatenate([high, middle, rest, jnp.zeros_like(high)], axis=0)


def attention_kernel(
    heads, length, token_col, proj, cosine, sine, query_o, key_o, weight_o, low_o, hot, key_hot, queries, wide
):
    seq = token_col.shape[0]
    vocab = proj.shape[0]
    lane = lanes((seq, WIDE))
    hot[...] = jnp.where(lane % vocab == token_col[...], 1.0, 0.0).astype(bf16)
    for h in range(heads):
        key_hot[h] = jnp.where(lane == token_col[...] + h * vocab, 1.0, 0.0).astype(bf16)
    one = lanes((vocab, WIDE)) == HD
    ones = (lanes((vocab, WIDE)) > HD) & (lanes((vocab, WIDE)) < HD + 4)
    for which in range(2):
        for h in range(heads):
            own = head_lanes(proj, which * heads + h)
            other = turned(own)
            if which == 0:
                own = jnp.where(one, 1.0, own * 0.125)
                other = other * 0.125
            else:
                own = jnp.where(one | ones, 1.0, own)
            begin = (which * heads + h) * 2 * WIDE
            wide[:, begin : begin + WIDE] = stack_parts(own)
            wide[:, begin + WIDE : begin + 2 * WIDE] = stack_parts(other)
    for i in range(seq // ROWS):
        span = slice(i * ROWS, (i + 1) * ROWS)
        part = hot[span]
        position = i * ROWS + sublanes((ROWS, WIDE))
        bias = jnp.where(position < length[0], 0.0, MASKED)
        cos, sin = cosine[span], sine[span]
        key_cos = jnp.where(lanes((ROWS, WIDE)) == HD, bias, cos)
        for h in range(heads):
            both = dot(part, wide[:, h * 2 * WIDE : (h + 1) * 2 * WIDE])
            queries[h, span] = (both[:, :WIDE] * cos + both[:, WIDE:] * sin).astype(bf16)
            k = heads + h
            both = dot(part, wide[:, k * 2 * WIDE : (k + 1) * 2 * WIDE])
            key_o[h, span] = (both[:, :WIDE] * key_cos + both[:, WIDE:] * sin).astype(bf16)
    allowed = lanes((ROWS, ROWS)) <= sublanes((ROWS, ROWS))
    small = lanes((ROWS, WIDE))
    for i in range(seq // ROWS):
        span = slice(i * ROWS, (i + 1) * ROWS)
        past = i * ROWS
        weights = jnp.zeros((ROWS, WIDE), f32)
        for h in range(heads):
            query = queries[h, span]
            near = jnp.where(allowed, dot(query, key_o[h, span], NT), MASKED)
            top = jnp.max(near, axis=-1, keepdims=True)
            if past:
                far = dot(query, key_o[h, :past], NT)
                top = jnp.maximum(top, jnp.max(far, axis=-1, keepdims=True))
                far = jnp.exp(far - top)
            near = jnp.exp(near - top)
            total = jnp.sum(near, axis=-1, keepdims=True)
            if past:
                total = total + jnp.sum(far, axis=-1, keepdims=True)
            share = 1.0 / total
            weights = weights + dot((near * share).astype(bf16), key_hot[h, span])
            if past:
                weights = weights + dot((far * share).astype(bf16), key_hot[h, :past])
            minus = -(top + jnp.log(total))
            high = minus.astype(bf16).astype(f32)
            middle = (minus - high).astype(bf16).astype(f32)
            rest = minus - high - middle
            query_o[h, span] = jnp.where(
                small == HD + 1,
                high,
                jnp.where(
                    small == HD + 2, middle, jnp.where(small == HD + 3, rest, query.astype(f32))
                ),
            ).astype(bf16)
        weight_o[span] = weights[:, : heads * vocab]
        low_o[span] = weights[:, : heads * vocab].astype(bf16)


def attention(length, token_col, proj, cosine, sine, heads):
    seq = token_col.shape[0]
    vocab = proj.shape[0]
    o = jax.ShapeDtypeStruct
    return pl.pallas_call(
        functools.partial(attention_kernel, heads),
        in_specs=[SMEM] + [VMEM] * 4,
        out_specs=[VMEM] * 4,
        out_shape=[
            o((heads, seq, WIDE), bf16),
            o((heads, seq, WIDE), bf16),
            o((seq, heads * vocab), f32),
            o((seq, heads * vocab), bf16),
        ],
        scratch_shapes=[
            pltpu.VMEM((seq, WIDE), bf16),
            pltpu.VMEM((heads, seq, WIDE), bf16),
            pltpu.VMEM((heads, seq, WIDE), bf16),
            pltpu.VMEM((WIDE, heads * 4 * WIDE), bf16),
        ],
        name="attention",
        **params(11),
    )(length, token_col, proj, cosine, sine)


def attention_back_kernel(
    heads,
    pair,
    token_col,
    token_row,
    query,
    key,
    weight,
    weight_grad,
    cosine,
    sine,
    cosine_t,
    sine_t,
    table_o,
    hot,
    mixed,
    query_grad,
    key_grad,
):
    seq = token_col.shape[0]
    vocab = weight.shape[1] // heads
    half = ROT // 2
    lane = lanes((seq, WIDE))
    hot[...] = jnp.where(
        (lane == token_col[...]) | (lane == token_col[...] + vocab) | ((lane >= HD) & (lane < HD + 3)),
        1.0,
        0.0,
    ).astype(bf16)
    both = weight[...] * weight_grad[...]
    grads = weight_grad[...]
    if heads * vocab < WIDE:
        pad = jnp.zeros((seq, WIDE - heads * vocab), f32)
        both = jnp.concatenate([both, pad], axis=1)
        grads = jnp.concatenate([grads, pad], axis=1)
    for n, h in enumerate((2 * pair, 2 * pair + 1)):
        inside = (lane >= h * vocab) & (lane < (h + 1) * vocab)
        minus = -jnp.sum(jnp.where(inside, both, 0.0), axis=-1, keepdims=True)
        own = grads if h == 0 else pltpu.roll(grads, WIDE - h * vocab, 1)
        own = jnp.where(lane < vocab, own, 0.0)
        high, rest = split2(own)
        m_high = minus.astype(bf16).astype(f32)
        m_middle = (minus - m_high).astype(bf16).astype(f32)
        m_rest = minus - m_high - m_middle
        value = high.astype(f32) + pltpu.roll(rest.astype(f32), vocab, 1)
        value = jnp.where(lane == HD, m_high, value)
        value = jnp.where(lane == HD + 1, m_middle, value)
        value = jnp.where(lane == HD + 2, m_rest, value)
        mixed[n] = value.astype(bf16)
    allowed = lanes((ROWS, ROWS)) <= sublanes((ROWS, ROWS))
    key_grad[...] = jnp.zeros_like(key_grad)
    for n in range(2):
        for i in range(seq // ROWS):
            span = slice(i * ROWS, (i + 1) * ROWS)
            past = i * ROWS
            part = query[n, span]
            near = jnp.where(allowed, jnp.exp(dot(part, key[n, span], NT)), 0.0)
            near = (near * dot(mixed[n, span], hot[span], NT)).astype(bf16)
            grad = dot(near, key[n, span])
            key_grad[n, :, span] += dot(part, near, TN)[:HD]
            if past:
                far = jnp.exp(dot(part, key[n, :past], NT))
                far = (far * dot(mixed[n, span], hot[:past], NT)).astype(bf16)
                grad = grad + dot(far, key[n, :past])
                key_grad[n, :, :past] += dot(part, far, TN)[:HD]
            grad = grad * 0.125
            query_grad[n, span] = (grad * cosine[span] - turned(grad) * sine[span]).astype(bf16)
    shape = (vocab, seq)
    token_hot = jnp.where(sublanes(shape) == token_row[...], 1.0, 0.0).astype(bf16)
    small = lanes((vocab, WIDE)) < HD
    cos_t, sin_t = cosine_t[...], sine_t[...]
    one = dot(token_hot, query_grad[0])
    two = pltpu.roll(dot(token_hot, query_grad[1]), HD, 1)
    table_o[:, :WIDE] = jnp.where(small, one, two)
    turned_keys = []
    for n in range(2):
        front, back = key_grad[n, :half], key_grad[n, half:ROT]
        turned_keys += [front * cos_t + back * sin_t, back * cos_t - front * sin_t, key_grad[n, ROT:]]
    keys = jnp.concatenate(turned_keys, axis=0).astype(bf16)
    table_o[:, WIDE:] = dot(token_hot, keys, NT)


def attention_back(
    pair, token_col, token_row, query, key, weight, weight_grad, cosine, sine, cosine_t, sine_t, heads
):
    seq = token_col.shape[0]
    vocab = weight.shape[1] // heads
    full = lambda array: pl.BlockSpec(array.shape, lambda i: (0,) * array.ndim)
    two = pl.BlockSpec((2, seq, WIDE), lambda i: (pair, 0, 0))
    return pl.pallas_call(
        functools.partial(attention_back_kernel, heads, pair),
        grid=(1,),
        in_specs=[full(token_col), full(token_row), two, two, full(weight), full(weight_grad)]
        + [full(table) for table in (cosine, sine, cosine_t, sine_t)],
        out_specs=pl.BlockSpec((vocab, 2 * WIDE), lambda i: (0, 0)),
        out_shape=jax.ShapeDtypeStruct((vocab, 2 * WIDE), f32),
        scratch_shapes=[
            pltpu.VMEM((seq, WIDE), bf16),
            pltpu.VMEM((2, seq, WIDE), bf16),
            pltpu.VMEM((2, seq, WIDE), bf16),
            pltpu.VMEM((2, HD, seq), f32),
        ],
        name="attention_back",
        **params(6),
    )(token_col, token_row, query, key, weight, weight_grad, cosine, sine, cosine_t, sine_t)


def loss_kernel(
    parts,
    heads,
    ints,
    floats,
    token_col,
    target_col,
    token_row,
    embed,
    head,
    vec,
    *refs,
):
    weights, refs = refs[:parts], refs[parts:]
    payload, mine, others = refs[0], refs[1:parts], refs[parts : 2 * parts - 1]
    sums_o, grad_o, mixing, low_weights, table = refs[2 * parts - 1 :]
    step = pl.program_id(0)
    me, length, upper = ints[0], ints[1], ints[2]
    vocab = embed.shape[0]
    height = heads * vocab

    @pl.when(step == 0)
    def _():
        mixing[me] = payload[...]
        size = payload.shape[0] // 2
        for r in range(1, parts):
            mixing[me ^ r, pl.ds(pl.multiple_of(upper * size, size), size)] = mine[r - 1][...]
            mixing[me ^ r, pl.ds(pl.multiple_of((1 - upper) * size, size), size)] = others[r - 1][...]
        down = jnp.zeros((vocab, D), f32)
        for g in range(parts):
            one = mixing[g, height:].astype(f32)
            down = down + (one[:vocab] + one[vocab:])
        table[...] = stack_parts(embed[...] + (down + vec[2:3]))
        sums_o[...] = jnp.zeros_like(sums_o)

    for r in range(parts):
        low_weights[me ^ r] = weights[r][...]
    token = token_col[...]
    hot = jnp.where(lanes((ROWS, WIDE)) % vocab == token, 1.0, 0.0).astype(bf16)
    x = dot(hot, table[...])
    x = x + dot(
        jnp.concatenate([low_weights[g] for g in range(parts)], axis=1),
        jnp.concatenate([mixing[g, :height] for g in range(parts)], axis=0),
    )
    normed, scale = stats_of(x)
    gain = vec[3:4]
    final = (normed * gain + vec[4:5]).astype(bf16)
    head_low = head[:, :D].astype(bf16)
    square = (vocab, vocab)
    bias_row = jnp.sum(
        jnp.where(lanes(square) == sublanes(square), head[:, D : D + 1], 0.0), axis=0, keepdims=True
    )
    logits = dot(final, head_low, NT) + bias_row
    shifted = logits - jnp.max(logits, axis=-1, keepdims=True)
    log_probs = shifted - jnp.log(jnp.sum(jnp.exp(shifted), axis=-1, keepdims=True))
    target = lanes((ROWS, vocab)) == target_col[...]
    position = step * ROWS + sublanes((ROWS, 1))
    slot_weight = jnp.where(position < length - 1, floats[0], 0.0)
    picked = jnp.sum(jnp.where(target, log_probs, 0.0), axis=-1, keepdims=True)
    loss = -jnp.sum(slot_weight * picked, keepdims=True)
    logit_grad = ((jnp.exp(log_probs) - jnp.where(target, 1.0, 0.0)) * slot_weight).astype(bf16)
    final_grad = dot(logit_grad, head_low)
    grad = norm_back(final_grad, normed, scale, gain)
    high = grad.astype(bf16)
    token_hot = jnp.where(sublanes((vocab, ROWS)) == token_row[...], 1.0, 0.0).astype(bf16)
    own = weights[0][...].astype(f32)
    if height < WIDE:
        own = jnp.concatenate([own, jnp.zeros((ROWS, WIDE - height), f32)], axis=1)
    both = dot(jnp.concatenate([own.T.astype(bf16), token_hot], axis=0), high)
    sums_o[0:vocab] += both[WIDE:]
    sums_o[vocab : 2 * vocab] += dot(logit_grad, final, TN)
    base = 2 * vocab
    sums_o[base : base + 1] += jnp.sum(final_grad * normed, axis=0, keepdims=True)
    sums_o[base + 1 : base + 2] += jnp.sum(final_grad, axis=0, keepdims=True)
    bias_grad = jnp.sum(logit_grad.astype(f32), axis=0, keepdims=True)
    sums_o[base + 2 : base + 3, :vocab] += bias_grad
    lane = lanes((1, WIDE))
    count = jnp.where((step == 0) & (length >= 2), 1.0, 0.0)
    sums_o[base + 3 : base + 4, :WIDE] += jnp.where(
        lane == 0, loss, jnp.where(lane == 1, count, 0.0)
    )
    sums_o[base + 16 : base + 16 + height] += both[:height]
    grad_o[...] = dot(high, payload[:height], NT)


def loss_rows(
    ints,
    floats,
    token_col,
    target_col,
    token_row,
    embedding,
    head,
    vectors,
    weights,
    payload,
    mine,
    others,
    heads,
):
    seq = token_col.shape[0]
    vocab = embedding.shape[0]
    parts = len(weights)
    height = heads * vocab
    col = pl.BlockSpec((ROWS, 1), lambda i: (i, 0))
    o = jax.ShapeDtypeStruct
    full = lambda array: pl.BlockSpec(array.shape, lambda i: (0,) * array.ndim)
    sums_shape = (2 * vocab + 16 + height, D)
    return pl.pallas_call(
        functools.partial(loss_kernel, parts, heads),
        grid=(seq // ROWS,),
        in_specs=[SMEM, SMEM, col, col, pl.BlockSpec((1, ROWS), lambda i: (0, i))]
        + [full(embedding), full(head), full(vectors)]
        + [pl.BlockSpec((ROWS, height), lambda i: (i, 0))] * parts
        + [full(payload)]
        + [full(mine[0])] * (2 * parts - 2),
        out_specs=[
            pl.BlockSpec(sums_shape, lambda i: (0, 0)),
            pl.BlockSpec((ROWS, height), lambda i: (i, 0)),
        ],
        out_shape=[o(sums_shape, f32), o((seq, height), f32)],
        scratch_shapes=[
            pltpu.VMEM((parts,) + payload.shape, bf16),
            pltpu.VMEM((parts, ROWS, height), bf16),
            pltpu.VMEM((4 * vocab, D), bf16),
        ],
        name="loss_rows",
        **params(12),
    )(
        ints,
        floats,
        token_col,
        target_col,
        token_row,
        embedding,
        head,
        vectors,
        *weights,
        payload,
        *mine,
        *others,
    )


def padded(block):
    lacking = HB - block.shape[0]
    if lacking:
        block = jnp.concatenate([block, jnp.zeros((lacking, block.shape[1]), block.dtype)], axis=0)
    return block


def put_left(ref, index, block):
    ref[index] = jnp.concatenate([padded(block)] * 3, axis=0).astype(bf16)


def put_right(ref, index, block):
    ref[index] = jnp.concatenate(split3(padded(block)), axis=0)


def factors_kernel(
    heads,
    sums,
    mat_q,
    mat_o,
    mat_u,
    mat_f,
    upper,
    normed,
    act,
    values,
    left_o,
    right_o,
    hidden_o,
    bias_o,
):
    vocab = normed.shape[0]
    width = mat_u.shape[1]
    rows = sums[0:vocab]
    mixed = sums[2 * vocab + 16 :]
    act_grad = rows_times_low(rows, mat_f[...], NT)
    u = upper[...]
    tanh = jnp.tanh(GELU_A * (u + GELU_B * (u * u * u)))
    slope = 0.5 * (1.0 + tanh) + 0.5 * u * (1.0 - tanh * tanh) * (
        GELU_A * (1.0 + 3.0 * GELU_B * (u * u))
    )
    upper_grad = act_grad * slope
    bias_grad = jnp.sum(upper_grad, axis=0, keepdims=True)
    bias_o[...] = bias_grad
    value_grad = rows_times_low(mixed, mat_o[...], NT)
    shape = value_grad.shape
    value_grad = jnp.where(sublanes(shape) // vocab == lanes(shape) // HD, value_grad, 0.0)
    value_table = value_grad[:vocab]
    for h in range(1, heads):
        value_table = value_table + value_grad[h * vocab : (h + 1) * vocab]
    hidden_o[0:vocab] = rows_times_low(upper_grad, mat_u[...], NT) + rows_times_low(
        value_table, mat_q[:, 2 * heads * HD :], NT
    )
    low = normed[...].astype(f32)
    own = act[...].astype(f32)
    val = values[...].astype(f32)
    square = (
        jnp.sum(
            dot6(low, low, NT)
            * (dot6(value_table, value_table, NT) + dot6(upper_grad, upper_grad, NT)),
            keepdims=True,
        )
        + jnp.sum(dot6(own, own, NT) * dot6(rows, rows, NT), keepdims=True)
        + jnp.sum(dot6(val, val, NT) * dot6(mixed, mixed, NT), keepdims=True)
        + jnp.sum(bias_grad * bias_grad, keepdims=True)
    )
    hidden_o[vocab : vocab + 16] = jnp.broadcast_to(square, (16, D))
    across = D // BS
    f_rows = width // BS
    pair = 2 * vocab
    for i in range(across):
        put_left(left_o, i, low[:, i * BS : (i + 1) * BS])
    for i in range(f_rows):
        put_left(left_o, across + i, own[:, i * BS : (i + 1) * BS])
    for i in range(heads // 2):
        put_left(
            left_o,
            across + f_rows + i,
            val[i * pair : (i + 1) * pair, i * BS : (i + 1) * BS],
        )
    at = 0
    for k in range(heads * HD // BS):
        put_right(right_o, at, value_table[:, k * BS : (k + 1) * BS])
        at += 1
    for i in range(heads // 2):
        for k in range(across):
            put_right(right_o, at, mixed[i * pair : (i + 1) * pair, k * BS : (k + 1) * BS])
            at += 1
    for k in range(f_rows):
        put_right(right_o, at, upper_grad[:, k * BS : (k + 1) * BS])
        at += 1
    for k in range(across):
        put_right(right_o, at, rows[:, k * BS : (k + 1) * BS])
        at += 1


def rest_kernel(pairs, table, hidden, mat_q, normed, right_o, hidden_o):
    vocab = normed.shape[0]
    blocks = [table[p * vocab : (p + 1) * vocab, :WIDE] for p in range(pairs)]
    blocks += [table[p * vocab : (p + 1) * vocab, WIDE:] for p in range(pairs)]
    grad = jnp.concatenate(blocks, axis=1)
    for k, block in enumerate(blocks):
        put_right(right_o, k, block)
    low = normed[...].astype(f32)
    square = jnp.sum(dot6(low, low, NT) * dot6(grad, grad, NT), keepdims=True)
    hidden_o[0:vocab] = hidden[0:vocab] + rows_times_low(grad, mat_q[:, : 2 * pairs * WIDE], NT)
    hidden_o[vocab:] = hidden[vocab:] + square


def factor_places(heads, ff_local):
    q_cols = 3 * heads * HD // BS
    o_rows = heads // 2
    across = D // BS
    f_rows = ff_local // BS
    left, right = [], []
    for which, i, k in tile_places(layer_shapes(heads, ff_local)):
        if which == 0:
            left.append(i)
            right.append(k)
        elif which == 1:
            left.append(across + f_rows + i)
            right.append(q_cols + i * across + k)
        elif which == 2:
            left.append(i)
            right.append(q_cols + o_rows * across + k)
        else:
            left.append(across + i)
            right.append(q_cols + o_rows * across + f_rows + k)
    return np.array(left, np.int32), np.array(right, np.int32)


def factors(sums, mats, upper, normed, act, values, heads):
    vocab = normed.shape[0]
    ff_local = upper.shape[1]
    n_left = D // BS + ff_local // BS + heads // 2
    n_right = heads * HD // BS + heads // 2 * (D // BS) + ff_local // BS + D // BS
    o = jax.ShapeDtypeStruct
    return pl.pallas_call(
        functools.partial(factors_kernel, heads),
        in_specs=[VMEM] * 9,
        out_specs=[VMEM] * 4,
        out_shape=[
            o((n_left, 3 * HB, BS), bf16),
            o((n_right, 3 * HB, BS), bf16),
            o((vocab + 16, D), f32),
            o((1, ff_local), f32),
        ],
        name="factors",
        **params(7),
    )(sums, *mats, upper, normed, act, values)


def factors_rest(table, hidden, mat_q, normed, heads):
    o = jax.ShapeDtypeStruct
    pairs = heads // 2
    return pl.pallas_call(
        functools.partial(rest_kernel, pairs),
        in_specs=[VMEM] * 4,
        out_specs=[VMEM] * 2,
        out_shape=[o((2 * pairs, 3 * HB, BS), bf16), o(hidden.shape, f32)],
        name="factors_rest",
        **params(2),
    )(table, hidden, mat_q, normed)


def small_kernel(parts, corrections, ints, sums, own, *refs):
    mine, others, refs = refs[: parts - 1], refs[parts - 1 : 2 * parts - 2], refs[2 * parts - 2 :]
    bias_grad, refs = refs[0], refs[1:]
    weights, refs = refs[:12], refs[12:]
    outs, scalars, total = refs[:12], refs[12], refs[13]
    vocab = weights[0].shape[0]
    base = 2 * vocab
    size = own.shape[0] // 2
    for place, group in ((ints[0], mine), (1 - ints[0], others)):
        span = pl.ds(pl.multiple_of(place * size, size), size)
        total[span] = tree_sum([own[span]] + [ref[...] for ref in group])
    hidden = total[:vocab]
    square = total[vocab : vocab + 1, 0:1]
    rows = sums[0:vocab]
    normed, scale = stats_of(weights[0][...])
    gain = weights[6][0:1]
    embed_grad = rows + norm_back(hidden, normed, scale, gain)
    vector_grad = jnp.concatenate(
        [
            jnp.sum(hidden * normed, axis=0, keepdims=True),
            jnp.sum(hidden, axis=0, keepdims=True),
            jnp.sum(rows, axis=0, keepdims=True),
            sums[base : base + 1],
            sums[base + 1 : base + 2],
        ],
        axis=0,
    )
    head_grad = sums[vocab : 2 * vocab]
    head_bias = sums[base + 2 : base + 3, :vocab]
    add = lambda value: jnp.sum(value * value, keepdims=True)
    square = square + add(embed_grad) + add(vector_grad) + add(head_grad) + add(head_bias)
    count = sums[base + 3 : base + 4, 1:2]
    loss = sums[base + 3 : base + 4, 0:1] / count
    norm = jnp.sqrt(square) / count
    scale_all = jnp.minimum(1.0, CLIP_NORM / norm) / count
    one, two = corrections[0], corrections[1]

    def update(index, pick, grad):
        weight, first, second = (weights[3 * index + k][pick] for k in range(3))
        grad = grad * scale_all
        first = BETA_ONE * first + (1.0 - BETA_ONE) * grad
        second = BETA_TWO * second + (1.0 - BETA_TWO) * grad * grad
        step = first / one / (jnp.sqrt(second / two) + ADAM_EPS)
        outs[3 * index][pick] = weight - RATE_SMALL * (step + WEIGHT_DECAY * weight)
        outs[3 * index + 1][pick] = first
        outs[3 * index + 2][pick] = second

    everything = slice(None)
    update(0, everything, embed_grad)
    shape = (vocab, vocab)
    head_column = jnp.sum(
        jnp.where(lanes(shape) == sublanes(shape), head_bias, 0.0), axis=1, keepdims=True
    )
    update(1, (everything, slice(0, D)), head_grad)
    update(1, (everything, slice(D, D + 1)), head_column)
    update(2, everything, vector_grad)
    update(3, everything, bias_grad[...])
    lane = lanes((1, WIDE))
    scalars[...] = jnp.where(
        lane == 0, scale_all, jnp.where(lane == 1, loss, jnp.where(lane == 2, norm, 0.0))
    )


def small(corrections, upper, sums, hidden, mine, others, bias_grad, weights):
    o = jax.ShapeDtypeStruct
    return pl.pallas_call(
        functools.partial(small_kernel, 1 + len(mine)),
        in_specs=[SMEM] * 2 + [VMEM] * (2 + 2 * len(mine) + 1 + 12),
        out_specs=[VMEM] * 13,
        out_shape=[o(weight.shape, f32) for weight in weights] + [o((1, WIDE), f32)],
        scratch_shapes=[pltpu.VMEM(hidden.shape, f32)],
        name="small",
        **params(4),
    )(corrections, upper, sums, hidden, *mine, *others, bias_grad, *weights)


QB = 32
UNQ = 6
PER = 6


def take(value, at):
    return jnp.take_along_axis(value, at, axis=1, mode="promise_in_bounds")


def eliminate(packed, count):
    shape = (8, BS)
    lane, sub = lanes(shape), sublanes(shape)
    start = lane // QB * QB
    span = range(count)
    for p in range(QB // 8):
        r0 = 8 * p

        def body(jj, carry):
            pick = start + (r0 + jj)
            mark = lane == pick
            below = sub > jj
            rows = [packed[t, pl.ds(r0 + jj, 1), :] for t in span]
            kept = [[packed[t, 8 * q : 8 * q + 8, :] for q in range(p, QB // 8)] for t in span]
            wide = [jnp.broadcast_to(row, shape) for row in rows]
            pivots = [take(w, pick) for w in wide]
            cs = [[take(a, pick) for a in group] for group in kept]
            scaled = [jnp.where(mark, 1.0, w) / d for w, d in zip(wide, pivots)]
            for t in span:
                for k, q in enumerate(range(p, QB // 8)):
                    a, c = kept[t][k], cs[t][k]
                    if k == 0:
                        a = jnp.where(mark & below, 0.0, a)
                        c = jnp.where(below, c, 0.0)
                    else:
                        a = jnp.where(mark, 0.0, a)
                    packed[t, 8 * q : 8 * q + 8, :] = a - c * scaled[t]
            return carry

        lax.fori_loop(0, 8, body, 0)


def part_inverse(packed):
    shape = (QB, BS)
    lane, sub = lanes(shape), sublanes(shape)
    part, col = lane // QB, lane % QB
    diagonal = jnp.where(col == sub, packed, 0.0)
    pivot = jnp.ones(shape, f32)
    for k in range(BS // QB):
        own = jnp.sum(jnp.where(part == k, diagonal, 0.0), axis=1, keepdims=True)
        pivot = jnp.where(part == k, own, pivot)
    unit = jnp.where(col < sub, packed, jnp.where(col == sub, 1.0, 0.0))
    return unit * lax.rsqrt(pivot)


def inverse_factors(gram, packed, result, count):
    parts = BS // QB
    unroll = next(k for k in (UNQ, 3, 2, 1) if count % k == 0)
    lane32, sub32 = lanes((QB, BS)), sublanes((QB, BS))
    for b in range(parts):
        begin = b * QB
        below = begin + QB
        rows = slice(begin, below)
        here = lane32 // QB == b

        def pack(i, carry):
            for t in [i * unroll + k for k in range(unroll)]:
                value = jnp.zeros((QB, BS), f32)
                for k in range(parts):
                    block = gram[parts * t + k, rows, :]
                    if k != b:
                        block = pltpu.roll(block, (k * QB + BS - begin) % BS, 1)
                    value = jnp.where(lane32 // QB == k, block, value)
                packed[t] = value
            return carry

        lax.fori_loop(0, count // unroll, pack, 0)
        eliminate(packed, count)

        def spread(i, carry):
            groups = [i * unroll + k for k in range(unroll)]
            inverses = [part_inverse(packed[t]) for t in groups]
            firsts = [
                jnp.concatenate([jnp.where(lane32 // QB == k, x, 0.0) for k in range(parts)], axis=0)
                for x in inverses
            ]
            unit = jnp.where(lane32 - begin == sub32, 1.0, 0.0)
            panels = [
                jnp.concatenate(
                    [jnp.where(here, unit, gram[parts * t + k, rows, :]) for k in range(parts)],
                    axis=0,
                )
                for t in groups
            ]
            news = [dot6(x, y, NN) for x, y in zip(firsts, panels)]
            for t, new in zip(groups, news):
                for k in range(parts):
                    value = new[k * QB : (k + 1) * QB]
                    result[parts * t + k, rows, :] = (
                        jnp.where(lane32 < below, value, 0.0) if below < BS else value
                    )
            if below < BS:
                for t, new in zip(groups, news):
                    mats = [new[k * QB : (k + 1) * QB] for k in range(parts)]
                    changes = [dot6(x, x, TN) for x in mats]
                    shape = (BS - below, BS)
                    mark = lanes(shape) // QB == b
                    for k in range(parts):
                        old = gram[parts * t + k, below:, :]
                        gram[parts * t + k, below:, :] = jnp.where(mark, 0.0, old) - changes[k][below:]
            return carry

        lax.fori_loop(0, count // unroll, spread, 0)


def tile_params(count, per):
    blk = pl.BlockSpec((per, BS, BS), lambda i: (i, 0, 0))
    full = pl.BlockSpec((count, BS, BS), lambda i: (0, 0, 0))
    return blk, full, lambda dt: jax.ShapeDtypeStruct((count, BS, BS), dt)


def gradient_kernel(per, rest, left_at, right_at, lefts, rights, more, L, R, QL, QR, *outs):
    step = pl.program_id(0)
    span = range(per)
    pairs = []
    for s in span:
        at = right_at[step * per + s]
        right = jnp.where(
            at < rest, more[jnp.minimum(at, rest - 1)], rights[jnp.maximum(at - rest, 0)]
        )
        pairs.append((lefts[left_at[step * per + s]], right))
    g = [dot(a, b, TN) for a, b in pairs]
    gt = [dot(b, a, TN) for a, b in pairs]
    qt = [QL[s].T for s in span]
    left = [dot3(x, x, NT) for x in g]
    right = [dot3(x, x, NT) for x in gt]
    rot = [dot3(q, x, NN) for q, x in zip(qt, g)]
    mixed_left = [dot3(left[s], QL[s], NN) for s in span]
    mixed_right = [dot3(right[s], QR[s], NN) for s in span]
    rot = [dot3(rot[s], QR[s], NN) for s in span]
    old_left = [dot6(L[s], QL[s], NN) for s in span]
    old_right = [dot6(R[s], QR[s], NN) for s in span]
    for s in span:
        for out, value in zip(
            outs, (left, right, rot, mixed_left, mixed_right, old_left, old_right)
        ):
            out[s] = value[s]


def gradient_products(left_at, right_at, lefts, rights, more, L, R, QL, QR):
    count = QL.shape[0]
    blk, _, o = tile_params(count, PER)
    whole = lambda x: pl.BlockSpec(x.shape, lambda i: (0, 0, 0))
    return pl.pallas_call(
        functools.partial(gradient_kernel, PER, more.shape[0]),
        grid=(count // PER,),
        in_specs=[SMEM] * 2 + [whole(lefts), whole(rights), whole(more)] + [blk] * 4,
        out_specs=[blk] * 7,
        out_shape=[o(f32)] * 7,
        name="gradient_products",
        **params(9),
    )(left_at, right_at, lefts, rights, more, L, R, QL, QR)


def soap_kernel(
    count, per, corrections, scal, GL, GR, GT, BL, BR, AL, AR, W, m, v, L, R, QL, QR,
    W_o, low_o, m_o, v_o, L_o, R_o, QL_o, QR_o, ML_s, MR_s, work, inv_s, packed,
):
    step = pl.program_id(0)
    scale = scal[0:1, 0:1]
    c1, c2 = corrections[0], corrections[1]
    span = range(per)
    share = (1 - BETA_TWO) * (scale * scale)
    xs = []
    for s in span:
        rot = GT[s] * scale
        mn = BETA_ONE * m[s] + (1 - BETA_ONE) * rot
        vn = BETA_TWO * v[s] + (1 - BETA_TWO) * rot * rot
        m_o[s] = mn
        v_o[s] = vn
        xs.append((mn / c1) / (jnp.sqrt(vn / c2) + ADAM_EPS))
    ML = [BETA_TWO * AL[s] + share * BL[s] for s in span]
    MR = [BETA_TWO * AR[s] + share * BR[s] for s in span]
    back = [dot3(QL[s], xs[s], NN) for s in span]
    ML = [x * lax.rsqrt(jnp.sum(x * x, keepdims=True)) for x in ML]
    MR = [x * lax.rsqrt(jnp.sum(x * x, keepdims=True)) for x in MR]
    back = [dot3(back[s], QR[s], NT) for s in span]
    gram_left = [dot6(x, x, TN) for x in ML]
    gram_right = [dot6(x, x, TN) for x in MR]
    for s in span:
        L_o[s] = BETA_TWO * L[s] + share * GL[s]
        R_o[s] = BETA_TWO * R[s] + share * GR[s]
        w = W[s]
        wn = w - RATE_TILES * (back[s] + WEIGHT_DECAY * w)
        W_o[s] = wn
        low_o[s] = wn.astype(bf16)
        t = step * per + s
        ML_s[t] = ML[s]
        MR_s[t] = MR[s]
        work[2 * t] = gram_left[s]
        work[2 * t + 1] = gram_right[s]

    @pl.when(step == pl.num_programs(0) - 1)
    def _():
        inverse_factors(work, packed, inv_s, count // 2)
        unroll = next(k for k in (8, 6, 3, 1) if count % k == 0)

        def last(i, carry):
            ts = [i * unroll + k for k in range(unroll)]
            ol = [dot3(ML_s[t], inv_s[2 * t], NT) for t in ts]
            orr = [dot3(MR_s[t], inv_s[2 * t + 1], NT) for t in ts]
            for t, a, b in zip(ts, ol, orr):
                QL_o[t] = a
                QR_o[t] = b
            return carry

        lax.fori_loop(0, count // unroll, last, 0)


def soap(corrections, scal, products, W, m, v, L, R, QL, QR):
    count = W.shape[0]
    blk, full, o = tile_params(count, PER)
    return pl.pallas_call(
        functools.partial(soap_kernel, count, PER),
        grid=(count // PER,),
        in_specs=[SMEM, pl.BlockSpec((1, WIDE), lambda i: (0, 0))] + [blk] * 14,
        out_specs=[blk] * 6 + [full] * 2,
        out_shape=[o(f32), o(bf16), o(f32), o(f32), o(f32), o(f32), o(f32), o(f32)],
        scratch_shapes=[pltpu.VMEM((count, BS, BS), f32)] * 2
        + [pltpu.VMEM((2 * count, BS, BS), f32)] * 2
        + [pltpu.VMEM((count // 2, QB, BS), f32)],
        name="soap_tiles",
        **params(40),
    )(corrections, scal, *products, W, m, v, L, R, QL, QR)


def local(
    tokens,
    lengths,
    tile_owner,
    step_count,
    weight_tiles,
    tiles_first,
    tiles_second,
    stats_left,
    stats_right,
    basis_left,
    basis_right,
    embedding,
    embedding_first,
    embedding_second,
    head_table,
    head_first,
    head_second,
    vectors,
    vectors_first,
    vectors_second,
    fc_bias,
    fc_bias_first,
    fc_bias_second,
):
    seq = tokens.shape[1]
    mp_count = lax.axis_size("mp")
    dp_count = lax.axis_size("dp")
    dp_index = lax.axis_index("dp")
    mp_index = lax.axis_index("mp")
    upper_pair = dp_index & 1
    heads = H // mp_count
    ff_local = fc_bias.shape[1]
    count = weight_tiles.shape[0]
    half = count // 2

    halves = gather_tiles(weight_tiles.astype(bf16))
    pieces = halves[0] + halves[1]
    holder = tile_owner // count
    inside = tile_owner - holder * count
    place = (
        jnp.where(inside >= half, dp_count * half - half, 0) + (holder ^ dp_index) * half + inside
    )
    result = tables(place, pieces, embedding, vectors, fc_bias, heads, ff_local)
    mats, (proj, upper, payload, normed, act, values) = result[:4], result[4:]

    slots = dp_index * count + jnp.arange(count, dtype=jnp.int32)
    natural = jnp.sum(
        jnp.where(
            tile_owner[None, :] == slots[:, None],
            jnp.arange(tile_owner.shape[0], dtype=jnp.int32)[None, :],
            0,
        ),
        axis=1,
    )
    left_of, right_of = factor_places(heads, ff_local)
    same = natural[:, None] == jnp.arange(tile_owner.shape[0], dtype=jnp.int32)[None, :]
    left_at = jnp.sum(jnp.where(same, left_of[None, :], 0), axis=1)
    right_at = jnp.sum(jnp.where(same, right_of[None, :], 0), axis=1)
    token_col = tokens.reshape(seq, 1)
    target_col = jnp.roll(tokens, -1, axis=1).reshape(seq, 1)
    cosine, sine, cosine_t, sine_t = rotary_tables(seq)
    parts = gather_halves(payload)
    others = swap_pair(parts)
    query, key, weight, weight_low = attention(lengths, token_col, proj, cosine, sine, heads)
    weights = gather_xor(weight_low, "mp")
    length = lengths[0]
    inverse_length = 1.0 / jnp.maximum(length - 1, 1).astype(f32)
    sums, weight_grad = loss_rows(
        jnp.stack([mp_index, length, upper_pair]),
        inverse_length[None],
        token_col,
        target_col,
        tokens,
        embedding,
        head_table.T,
        vectors,
        weights,
        payload,
        parts,
        others,
        heads,
    )
    kept = halved(sums)
    tables_back = []
    for pair in range(heads // 2):
        if pair == 1:
            weight_grad, kept = lax.optimization_barrier((weight_grad, kept))
        tables_back.append(
            attention_back(
                pair,
                token_col,
                tokens,
                query,
                key,
                weight,
                weight_grad,
                cosine,
                sine,
                cosine_t,
                sine_t,
                heads,
            )
        )
    sums = completed(kept)
    table = sum_small(jnp.concatenate(tables_back, axis=0))
    left, right, hidden, bias_grad = factors(sums, mats, upper, normed, act, values, heads)
    more, hidden = factors_rest(table, hidden, mats[0], normed, heads)
    hidden_parts = gather_halves(hidden)
    gradients = gradient_products(
        left_at, right_at, left, right, more, stats_left, stats_right, basis_left, basis_right
    )
    hidden_parts, gradients = lax.optimization_barrier((hidden_parts, gradients))
    hidden_others = swap_pair(hidden_parts)
    corrections = 1.0 - jnp.power(
        jnp.array([BETA_ONE, BETA_TWO], f32), step_count.astype(f32)
    )
    small_weights = (
        embedding,
        embedding_first,
        embedding_second,
        head_table.T,
        head_first.T,
        head_second.T,
        vectors,
        vectors_first,
        vectors_second,
        fc_bias,
        fc_bias_first,
        fc_bias_second,
    )
    *small_out, scalars = small(
        corrections,
        upper_pair[None],
        sums,
        hidden,
        hidden_parts,
        hidden_others,
        bias_grad,
        small_weights,
    )
    small_out[3:6] = [value.T for value in small_out[3:6]]
    results = soap(
        corrections,
        scalars,
        gradients,
        weight_tiles,
        tiles_first,
        tiles_second,
        stats_left,
        stats_right,
        basis_left,
        basis_right,
    )
    return (scalars[0, 1], scalars[0, 2], *results, *small_out)


def solution(mesh):
    tiled = P("dp", None, "mp")
    split = P(None, "mp")
    in_specs = (P("dp", None), P("dp"), P(), P(), *[tiled] * 7, *[P()] * 9, *[split] * 3)
    out_specs = (P(), P(), *[tiled] * 8, *[P()] * 9, *[split] * 3)
    return jax.shard_map(local, mesh=mesh, in_specs=in_specs, out_specs=out_specs, check_vma=False)
```

```python
import functools
import math

import jax
import jax.numpy as jnp
import numpy as np
from jax import lax
from jax.experimental import pallas as pl
from jax.experimental.pallas import tpu as pltpu
from jax.sharding import PartitionSpec as P

D = 1024
H = 16
HD = 64
ROT = 32
BS = 128
HB = 64
ROWS = 256
WIDE = 128
MEGA = 1024 * 1024

NORM_EPS = 1e-05
CLIP_NORM = 0.02
RATE_TILES = 0.02
RATE_SMALL = 0.2
BETA_ONE = 0.9
BETA_TWO = 0.95
ADAM_EPS = 1e-08
WEIGHT_DECAY = 0.01
MASKED = -1e30
GELU_A = math.sqrt(2.0 / math.pi)
GELU_B = 0.044715

NN = (((1,), (0,)), ((), ()))
NT = (((1,), (1,)), ((), ()))
TN = (((0,), (0,)), ((), ()))
f32 = jnp.float32
bf16 = jnp.bfloat16
SMEM = pl.BlockSpec(memory_space=pltpu.SMEM)
VMEM = pl.BlockSpec(memory_space=pltpu.VMEM)
ANY = pl.BlockSpec(memory_space=pl.ANY)


def dot(a, b, dims=NN):
    return lax.dot_general(a, b, dims, preferred_element_type=f32)


def split2(a):
    high = a.astype(bf16)
    return high, (a - high.astype(f32)).astype(bf16)


def split3(a):
    high = a.astype(bf16)
    rest = a - high.astype(f32)
    middle = rest.astype(bf16)
    return high, middle, (rest - middle.astype(f32)).astype(bf16)


def dot3(a, b, dims):
    (axis_a,), (axis_b,) = dims[0]
    ah, al = split2(a)
    bh, bl = split2(b)
    return dot(
        jnp.concatenate([ah, ah, al], axis=axis_a),
        jnp.concatenate([bh, bl, bh], axis=axis_b),
        dims,
    )


def dot6(a, b, dims):
    (axis_a,), (axis_b,) = dims[0]
    ah, am, al = split3(a)
    bh, bm, bl = split3(b)
    return dot(
        jnp.concatenate([ah, ah, am, am, ah, al], axis=axis_a),
        jnp.concatenate([bh, bm, bh, bm, bl, bh], axis=axis_b),
        dims,
    )


def rows_times_low(a, low, dims):
    count = a.shape[0]
    parts = dot(jnp.concatenate(split3(a), axis=0), low, dims)
    return parts[:count] + (parts[count : 2 * count] + parts[2 * count :])


def lanes(shape):
    return lax.broadcasted_iota(jnp.int32, shape, len(shape) - 1)


def sublanes(shape):
    return lax.broadcasted_iota(jnp.int32, shape, len(shape) - 2)


def stats_of(values):
    centred = values - jnp.mean(values, axis=-1, keepdims=True)
    spread = jnp.mean(centred * centred, axis=-1, keepdims=True)
    scale = lax.rsqrt(spread + NORM_EPS)
    return centred * scale, scale


def norm_back(grad, normed, scale, gain):
    inner = grad * gain
    mean_one = jnp.mean(inner, axis=-1, keepdims=True)
    mean_two = jnp.mean(inner * normed, axis=-1, keepdims=True)
    return scale * (inner - mean_one - normed * mean_two)


def params(microseconds, megabytes=20):
    return dict(
        compiler_params=pltpu.CompilerParams(vmem_limit_bytes=megabytes * MEGA),
        cost_estimate=pl.CostEstimate(
            flops=int(microseconds * 1.1e9), bytes_accessed=int(microseconds * 1e6), transcendentals=0
        ),
    )


def swap_with(value, axis, mask):
    count = lax.axis_size(axis)
    return lax.ppermute(value, axis, [(i, i ^ mask) for i in range(count)])


def tree_sum(parts):
    while len(parts) > 1:
        parts = [parts[i] + parts[i + 1] for i in range(0, len(parts), 2)]
    return parts[0]


def gather_xor(value, axis):
    return [value] + [swap_with(value, axis, r) for r in range(1, lax.axis_size(axis))]


def gather_halves(mine):
    return [swap_with(mine, "mp", r) for r in range(1, lax.axis_size("mp"))]


def swap_pair(parts):
    return [swap_with(part, "dp", 1) for part in parts]


def butterfly(kept):
    bits = [1 << k for k in range(1, lax.axis_size("dp").bit_length() - 1)]
    half = (kept.shape[0] // 2 + 7) // 8 * 8
    pieces = [kept[:half], kept[half:]]
    for k in range(len(bits)):
        received = [
            swap_with(piece, "dp", order[k])
            for piece, order in zip(pieces, (bits, bits[1:] + bits[:1]))
        ]
        pieces = [piece + other for piece, other in zip(pieces, received)]
    return jnp.concatenate(pieces, axis=0)


def direct(kept):
    return tree_sum([kept] + [swap_with(kept, "dp", r) for r in range(2, lax.axis_size("dp"), 2)])


def deal(upper, value, keep_o, send_o):
    half = keep_o.shape[0]

    @pl.when(upper == 0)
    def _():
        keep_o[...] = value[:half]
        send_o[...] = value[half : 2 * half]

    @pl.when(upper == 1)
    def _():
        keep_o[...] = value[half : 2 * half]
        send_o[...] = value[:half]


def join(upper, mine, other, whole):
    half = mine.shape[0]

    @pl.when(upper == 0)
    def _():
        whole[:half] = mine[...]
        whole[half:] = other[...]

    @pl.when(upper == 1)
    def _():
        whole[:half] = other[...]
        whole[half:] = mine[...]


def layer_shapes(heads_local, ff_local):
    return ((D, 3 * heads_local * HD), (heads_local * HD, D), (D, ff_local), (ff_local, D))


def tile_places(shapes):
    places = []
    for which, (row_total, col_total) in enumerate(shapes):
        for i in range(row_total // BS):
            for k in range(col_total // BS):
                places.append((which, i, k))
    return places


def first_places(heads, ff_local):
    q_cols = 3 * heads * HD // BS
    rows, blocks = [], []
    for which, i, k in tile_places(layer_shapes(heads, ff_local)):
        used = which in (0, 2)
        rows.append(i if used else 0)
        blocks.append(k if which == 0 else q_cols + k if which == 2 else q_cols + ff_local // BS)
    return np.array(rows, np.int32), np.array(blocks, np.int32)


def first_kernel(owner, ints, row_of, block_of, tiles, embed, vec, natural_o, low_o, normed_o, keep_o, send_o, rows, acc):
    count = tiles.shape[0]
    begin = ints[0] * count

    def find(b, carry):
        slot = owner[b] - begin

        @pl.when((slot >= 0) & (slot < count))
        def _():
            natural_o[slot] = b

        return carry

    lax.fori_loop(0, owner.shape[0], find, 0)
    normed, _ = stats_of(embed[...])
    low = (normed * vec[0:1] + vec[1:2]).astype(bf16)
    normed_o[...] = low
    for i in range(D // BS):
        rows[i] = low[:, i * BS : (i + 1) * BS]
    acc[...] = jnp.zeros_like(acc)
    for s in range(count):
        low_o[s] = tiles[s].astype(bf16)
    products = [dot(rows[row_of[natural_o[s]]], low_o[s]) for s in range(count)]
    for s in range(count):
        acc[block_of[natural_o[s]]] += products[s]
    half = keep_o.shape[0]
    for upper, first, second in ((0, keep_o, send_o), (1, send_o, keep_o)):

        @pl.when((ints[0] & 1) == upper)
        def _():
            first[...] = acc[:half]
            second[...] = acc[half : 2 * half]


def first_tables(owner, ints, tiles, embedding, vectors, heads, ff_local):
    vocab = embedding.shape[0]
    row_of, block_of = first_places(heads, ff_local)
    blocks = int(block_of.max())
    o = jax.ShapeDtypeStruct
    return pl.pallas_call(
        first_kernel,
        in_specs=[SMEM] * 4 + [VMEM] * 3,
        out_specs=[SMEM] + [VMEM] * 4,
        out_shape=[
            o((tiles.shape[0],), jnp.int32),
            o(tiles.shape, bf16),
            o((vocab, D), bf16),
            o(((blocks + 1) // 2, vocab, BS), f32),
            o(((blocks + 1) // 2, vocab, BS), f32),
        ],
        scratch_shapes=[
            pltpu.VMEM((D // BS, vocab, BS), bf16),
            pltpu.VMEM((blocks + 1, vocab, BS), f32),
        ],
        name="first_tables",
        **params(4, 56),
    )(owner, ints, jnp.asarray(row_of), jnp.asarray(block_of), tiles, embedding, vectors)


def second_places(heads, ff_local):
    pairs, across = heads // 2, D // BS
    lefts, blocks = [], []
    for which, i, k in tile_places(layer_shapes(heads, ff_local)):
        lefts.append(i if which == 1 else pairs + i if which == 3 else 0)
        blocks.append(
            i * across + k if which == 1 else (pairs * across + k if which == 3 else pairs * across + across)
        )
    return np.array(lefts, np.int32), np.array(blocks, np.int32)


def segments_of(heads, dp_count):
    return heads // 2 * (D // BS) * HB // dp_count, 32 * (D // BS) // dp_count


def second_kernel(
    heads, dp_count, natural, ints, left_of, block_of, mine, other, bias, low,
    proj_o, upper_o, act_o, values_o, keep_o, send_o, total, lefts, acc,
):
    vocab = proj_o.shape[0]
    me = ints[0]
    count = low.shape[0]
    pairs = heads // 2
    q_cols = 3 * heads * HD // BS
    f_rows = upper_o.shape[1] // BS
    across = D // BS
    join(me & 1, mine, other, total)
    for j in range(q_cols):
        proj_o[:, j * BS : (j + 1) * BS] = total[j]
    upper = jnp.concatenate([total[q_cols + j] for j in range(f_rows)], axis=1)
    upper = upper + bias[...]
    upper_o[...] = upper
    act = 0.5 * upper * (1.0 + jnp.tanh(GELU_A * (upper + GELU_B * (upper * upper * upper))))
    act = act.astype(bf16).astype(f32)
    act_o[...] = act.astype(bf16)
    values = proj_o[:, 2 * heads * HD :]
    shape = (heads * vocab, heads * HD)
    values = jnp.concatenate([values] * heads, axis=0)
    values = jnp.where(sublanes(shape) // vocab == lanes(shape) // HD, values, 0.0)
    values_o[...] = values.astype(bf16)
    for i in range(pairs):
        lefts[i] = values[i * HB : (i + 1) * HB, i * BS : (i + 1) * BS].astype(bf16)
    for i in range(f_rows):
        lefts[pairs + i] = padded(act[:, i * BS : (i + 1) * BS]).astype(bf16)
    acc[...] = jnp.zeros_like(acc)
    products = [dot(lefts[left_of[natural[s]]], low[s]) for s in range(count)]
    for s in range(count):
        rows = pl.ds(pl.multiple_of(block_of[natural[s]] * HB, HB), HB)
        acc[rows] += products[s]
    rows_v, rows_f = segments_of(heads, dp_count)
    base = pairs * across * HB
    for odd, first, second in ((0, keep_o, send_o), (1, send_o, keep_o)):

        @pl.when((me & 1) == odd)
        def _():
            for e in range(dp_count):
                out = second if e & 1 else first
                start = pl.multiple_of(((me ^ e) >> 1) * (rows_v + rows_f), 8)
                out[pl.ds(start, rows_v)] = acc[e * rows_v : (e + 1) * rows_v]
                k, inside = e * rows_f // vocab, e * rows_f % vocab
                at = base + k * HB + inside
                out[pl.ds(pl.multiple_of(start + rows_v, 8), rows_f)] = acc[at : at + rows_f]


def second_tables(natural, ints, mine, other, fc_bias, low, vocab, heads, dp_count):
    ff_local = fc_bias.shape[1]
    left_of, block_of = second_places(heads, ff_local)
    o = jax.ShapeDtypeStruct
    return pl.pallas_call(
        functools.partial(second_kernel, heads, dp_count),
        in_specs=[SMEM] * 4 + [VMEM] * 4,
        out_specs=[VMEM] * 6,
        out_shape=[
            o((vocab, 3 * heads * HD), f32),
            o((vocab, ff_local), f32),
            o((vocab, ff_local), bf16),
            o((heads * vocab, heads * HD), bf16),
            o((dp_count // 2 * sum(segments_of(heads, dp_count)), BS), f32),
            o((dp_count // 2 * sum(segments_of(heads, dp_count)), BS), f32),
        ],
        scratch_shapes=[
            pltpu.VMEM((2 * mine.shape[0],) + mine.shape[1:], f32),
            pltpu.VMEM((heads // 2 + ff_local // BS, HB, BS), bf16),
            pltpu.VMEM(((int(block_of.max()) + 1) * HB, BS), f32),
        ],
        name="second_tables",
        **params(4),
    )(natural, ints, jnp.asarray(left_of), jnp.asarray(block_of), mine, other, fc_bias, low)


def pack_kernel(rows_v, *refs):
    *parts, out = refs
    at = 0
    for part in parts:
        out[at : at + rows_v] = part[:rows_v].astype(bf16)
        at += rows_v
    down = tree_sum([part[rows_v:] for part in parts])
    for piece in split3(down):
        out[at : at + down.shape[0]] = piece
        at += down.shape[0]


def pack_segments(heads, dp_count, parts):
    rows_v, rows_f = segments_of(heads, dp_count)
    return pl.pallas_call(
        functools.partial(pack_kernel, rows_v),
        in_specs=[VMEM] * len(parts),
        out_specs=VMEM,
        out_shape=jax.ShapeDtypeStruct((len(parts) * rows_v + 3 * rows_f, BS), bf16),
        name="pack_segments",
        **params(1),
    )(*parts)


def assemble_kernel(places, owner, tiles, *mats):
    for index, (which, i, k) in enumerate(places):
        mats[which][i * BS : (i + 1) * BS, k * BS : (k + 1) * BS] = tiles[owner[index]]


def assemble(owner, tiles, heads, ff_local):
    shapes = layer_shapes(heads, ff_local)
    return pl.pallas_call(
        functools.partial(assemble_kernel, tile_places(shapes)),
        in_specs=[SMEM, VMEM],
        out_specs=[VMEM] * 4,
        out_shape=[jax.ShapeDtypeStruct(shape, bf16) for shape in shapes],
        name="assemble",
        **params(5),
    )(owner, tiles)


def rotary_tables(seq_len):
    half = ROT // 2
    frequency = np.float32(10000.0) ** (
        np.float32(-2.0) * np.arange(half, dtype=np.float32) / np.float32(ROT)
    )
    angles = np.arange(seq_len, dtype=np.float32)[:, None] * frequency[None, :].astype(np.float32)
    cosine = np.cos(angles.astype(np.float64)).astype(np.float32)
    sine = np.sin(angles.astype(np.float64)).astype(np.float32)
    wide_cos = np.ones((seq_len, WIDE), np.float32)
    wide_sin = np.zeros((seq_len, WIDE), np.float32)
    wide_cos[:, :half], wide_cos[:, half:ROT] = cosine, cosine
    wide_sin[:, :half], wide_sin[:, half:ROT] = sine, sine
    return wide_cos, wide_sin, np.ascontiguousarray(cosine.T), np.ascontiguousarray(sine.T)


def turned(x):
    half = ROT // 2
    lane = lanes(x.shape)
    return jnp.where(
        lane < half,
        -pltpu.roll(x, WIDE - half, 1),
        jnp.where(lane < ROT, pltpu.roll(x, half, 1), 0.0),
    )


def head_lanes(table, index):
    begin = index // 2 * WIDE
    chunk = table[:, begin : begin + WIDE]
    if index % 2:
        chunk = pltpu.roll(chunk, HD, 1)
    return jnp.where(lanes(chunk.shape) < HD, chunk, 0.0)


def stack_parts(table):
    high, middle, rest = split3(table)
    return jnp.concatenate([high, middle, rest, jnp.zeros_like(high)], axis=0)


def attention_kernel(
    heads, pair, length, token_col, proj, cosine, sine, before, query_o, key_o, weight_o, low_o, hot, key_hot, queries, wide
):
    seq = token_col.shape[0]
    vocab = proj.shape[0]
    lane = lanes((seq, WIDE))
    hot[...] = jnp.where(lane % vocab == token_col[...], 1.0, 0.0).astype(bf16)
    for n in range(2):
        first = (2 * pair + n) * vocab
        key_hot[n] = jnp.where(lane == token_col[...] + first, 1.0, 0.0).astype(bf16)
    one = lanes((vocab, WIDE)) == HD
    ones = (lanes((vocab, WIDE)) > HD) & (lanes((vocab, WIDE)) < HD + 4)
    for which in range(2):
        for n in range(2):
            own = head_lanes(proj, which * heads + 2 * pair + n)
            other = turned(own)
            if which == 0:
                own = jnp.where(one, 1.0, own * 0.125)
                other = other * 0.125
            else:
                own = jnp.where(one | ones, 1.0, own)
            begin = (which * 2 + n) * 2 * WIDE
            wide[:, begin : begin + WIDE] = stack_parts(own)
            wide[:, begin + WIDE : begin + 2 * WIDE] = stack_parts(other)
    for i in range(seq // ROWS):
        span = slice(i * ROWS, (i + 1) * ROWS)
        part = hot[span]
        position = i * ROWS + sublanes((ROWS, WIDE))
        bias = jnp.where(position < length[0], 0.0, MASKED)
        cos, sin = cosine[span], sine[span]
        key_cos = jnp.where(lanes((ROWS, WIDE)) == HD, bias, cos)
        for h in range(2):
            both = dot(part, wide[:, h * 2 * WIDE : (h + 1) * 2 * WIDE])
            queries[h, span] = (both[:, :WIDE] * cos + both[:, WIDE:] * sin).astype(bf16)
            k = 2 + h
            both = dot(part, wide[:, k * 2 * WIDE : (k + 1) * 2 * WIDE])
            key_o[h, span] = (both[:, :WIDE] * key_cos + both[:, WIDE:] * sin).astype(bf16)
    allowed = lanes((ROWS, ROWS)) <= sublanes((ROWS, ROWS))
    small = lanes((ROWS, WIDE))
    halves = []
    for i in range(seq // ROWS):
        span = slice(i * ROWS, (i + 1) * ROWS)
        past = i * ROWS
        weights = before[span] if pair else jnp.zeros((ROWS, WIDE), f32)
        query = [queries[h, span] for h in range(2)]
        near = [dot(query[h], key_o[h, span], NT) for h in range(2)]
        if past:
            far = [dot(query[h], key_o[h, :past], NT) for h in range(2)]
        near = [jnp.where(allowed, x, MASKED) for x in near]
        top = [jnp.max(x, axis=-1, keepdims=True) for x in near]
        if past:
            top = [jnp.maximum(m, jnp.max(x, axis=-1, keepdims=True)) for m, x in zip(top, far)]
            far = [jnp.exp(x - m) for m, x in zip(top, far)]
        near = [jnp.exp(x - m) for m, x in zip(top, near)]
        total = [jnp.sum(x, axis=-1, keepdims=True) for x in near]
        if past:
            total = [a + jnp.sum(x, axis=-1, keepdims=True) for a, x in zip(total, far)]
        share = [1.0 / a for a in total]
        near = [(x * a).astype(bf16) for x, a in zip(near, share)]
        if past:
            far = [(x * a).astype(bf16) for x, a in zip(far, share)]
        for h in range(2):
            weights = weights + dot(near[h], key_hot[h, span])
            if past:
                weights = weights + dot(far[h], key_hot[h, :past])
        for h in range(2):
            minus = -(top[h] + jnp.log(total[h]))
            high = minus.astype(bf16).astype(f32)
            middle = (minus - high).astype(bf16).astype(f32)
            rest = minus - high - middle
            value = jnp.where(small == HD + 3, rest, query[h].astype(f32))
            value = jnp.where(small == HD + 2, middle, value)
            query_o[h, span] = jnp.where(small == HD + 1, high, value).astype(bf16)
        weight_o[span] = weights
        own = weights if pair % 2 == 0 else pltpu.roll(weights, HD, 1)
        own = jnp.where(small < HD, own, 0.0)
        if i < seq // ROWS // 2:
            halves.append(own)
        else:
            k = i - seq // ROWS // 2
            low_o[k * ROWS : (k + 1) * ROWS] = (halves[k] + pltpu.roll(own, HD, 1)).astype(bf16)


def attention(pair, length, token_col, proj, cosine, sine, before, heads):
    seq = token_col.shape[0]
    vocab = proj.shape[0]
    o = jax.ShapeDtypeStruct
    return pl.pallas_call(
        functools.partial(attention_kernel, heads, pair),
        in_specs=[SMEM] + [VMEM] * 5,
        out_specs=[VMEM] * 4,
        out_shape=[
            o((2, seq, WIDE), bf16),
            o((2, seq, WIDE), bf16),
            o((seq, WIDE), f32),
            o((seq // 2, WIDE), bf16),
        ],
        scratch_shapes=[
            pltpu.VMEM((seq, WIDE), bf16),
            pltpu.VMEM((2, seq, WIDE), bf16),
            pltpu.VMEM((2, seq, WIDE), bf16),
            pltpu.VMEM((WIDE, 8 * WIDE), bf16),
        ],
        name="attention",
        **params(6),
    )(length, token_col, proj, cosine, sine, before)


def attention_back_kernel(
    heads,
    pair,
    token_col,
    token_row,
    query,
    key,
    weight,
    weight_grad,
    cosine,
    sine,
    cosine_t,
    sine_t,
    table_o,
    hot,
    mixed,
    query_grad,
    key_grad,
):
    seq = token_col.shape[0]
    vocab = table_o.shape[0]
    half = ROT // 2
    lane = lanes((seq, WIDE))
    hot[...] = jnp.where(
        (lane == token_col[...]) | (lane == token_col[...] + vocab) | ((lane >= HD) & (lane < HD + 3)),
        1.0,
        0.0,
    ).astype(bf16)
    grads = weight_grad[...]
    if heads * vocab < WIDE:
        grads = jnp.concatenate([grads, jnp.zeros((seq, WIDE - heads * vocab), f32)], axis=1)
    both = weight[...] * grads
    for n, h in enumerate((2 * pair, 2 * pair + 1)):
        inside = (lane >= h * vocab) & (lane < (h + 1) * vocab)
        minus = -jnp.sum(jnp.where(inside, both, 0.0), axis=-1, keepdims=True)
        own = grads if h == 0 else pltpu.roll(grads, WIDE - h * vocab, 1)
        own = jnp.where(lane < vocab, own, 0.0)
        high, rest = split2(own)
        m_high = minus.astype(bf16).astype(f32)
        m_middle = (minus - m_high).astype(bf16).astype(f32)
        m_rest = minus - m_high - m_middle
        value = high.astype(f32) + pltpu.roll(rest.astype(f32), vocab, 1)
        value = jnp.where(lane == HD, m_high, value)
        value = jnp.where(lane == HD + 1, m_middle, value)
        value = jnp.where(lane == HD + 2, m_rest, value)
        mixed[n] = value.astype(bf16)
    allowed = lanes((ROWS, ROWS)) <= sublanes((ROWS, ROWS))
    key_grad[...] = jnp.zeros_like(key_grad)
    both = range(2)
    for i in range(seq // ROWS):
        span = slice(i * ROWS, (i + 1) * ROWS)
        past = i * ROWS
        part = [query[n, span] for n in both]
        near = [dot(part[n], key[n, span], NT) for n in both]
        slope = [dot(mixed[n, span], hot[span], NT) for n in both]
        if past:
            far = [dot(part[n], key[n, :past], NT) for n in both]
            far_slope = [dot(mixed[n, span], hot[:past], NT) for n in both]
        near = [jnp.where(allowed, jnp.exp(x), 0.0) for x in near]
        near = [(x * y).astype(bf16) for x, y in zip(near, slope)]
        if past:
            far = [(jnp.exp(x) * y).astype(bf16) for x, y in zip(far, far_slope)]
        grad = [dot(near[n], key[n, span]) for n in both]
        if past:
            grad = [grad[n] + dot(far[n], key[n, :past]) for n in both]
        for n in both:
            key_grad[n, :, span] += dot(part[n], near[n], TN)[:HD]
            if past:
                key_grad[n, :, :past] += dot(part[n], far[n], TN)[:HD]
        for n in both:
            x = grad[n] * 0.125
            query_grad[n, span] = (x * cosine[span] - turned(x) * sine[span]).astype(bf16)
    shape = (vocab, seq)
    token_hot = jnp.where(sublanes(shape) == token_row[...], 1.0, 0.0).astype(bf16)
    small = lanes((vocab, WIDE)) < HD
    cos_t, sin_t = cosine_t[...], sine_t[...]
    one = dot(token_hot, query_grad[0])
    two = pltpu.roll(dot(token_hot, query_grad[1]), HD, 1)
    table_o[:, :WIDE] = jnp.where(small, one, two)
    turned_keys = []
    for n in range(2):
        front, back = key_grad[n, :half], key_grad[n, half:ROT]
        turned_keys += [front * cos_t + back * sin_t, back * cos_t - front * sin_t, key_grad[n, ROT:]]
    keys = jnp.concatenate(turned_keys, axis=0).astype(bf16)
    table_o[:, WIDE:] = dot(token_hot, keys, NT)


def attention_back(
    pair, token_col, token_row, query, key, weight, weight_grad, cosine, sine, cosine_t, sine_t, heads
):
    seq = token_col.shape[0]
    vocab = weight_grad.shape[1] // heads
    full = lambda array: pl.BlockSpec(array.shape, lambda i: (0,) * array.ndim)
    two = full(query)
    return pl.pallas_call(
        functools.partial(attention_back_kernel, heads, pair),
        grid=(1,),
        in_specs=[full(token_col), full(token_row), two, two, full(weight), full(weight_grad)]
        + [full(table) for table in (cosine, sine, cosine_t, sine_t)],
        out_specs=pl.BlockSpec((vocab, 2 * WIDE), lambda i: (0, 0)),
        out_shape=jax.ShapeDtypeStruct((vocab, 2 * WIDE), f32),
        scratch_shapes=[
            pltpu.VMEM((seq, WIDE), bf16),
            pltpu.VMEM((2, seq, WIDE), bf16),
            pltpu.VMEM((2, seq, WIDE), bf16),
            pltpu.VMEM((2, HD, seq), f32),
        ],
        name="attention_back",
        **params(6),
    )(token_col, token_row, query, key, weight, weight_grad, cosine, sine, cosine_t, sine_t)


def loss_kernel(
    parts,
    members,
    heads,
    ints,
    floats,
    token_col,
    target_col,
    token_row,
    embed,
    head,
    vec,
    *refs,
):
    pairs = heads // 2
    weights, refs = refs[: pairs * parts], refs[pairs * parts :]
    pieces, refs = refs[:members], refs[members:]
    keep_o, send_o, grad_o, sums_o, mixing, low_weights, table, down = refs
    step = pl.program_id(0)
    me, length, member = ints[0], ints[1], ints[2]
    vocab = embed.shape[0]
    height = heads * vocab

    @pl.when(step == 0)
    def _():
        rows_v, rows_f = segments_of(heads, members)
        small_v = min(rows_v, HB)
        for r in range(members):
            owner = member ^ r
            piece = pieces[r]
            for place in range(parts):
                for u in range(rows_v // small_v):
                    row = owner * rows_v + u * small_v
                    block, inside = row // HB, row % HB
                    i, k = block // (D // BS), block % (D // BS)
                    at = place * rows_v + u * small_v
                    mixing[
                        me ^ place,
                        pl.ds(pl.multiple_of(i * HB + inside, 32), small_v),
                        pl.ds(pl.multiple_of(k * BS, BS), BS),
                    ] = piece[at : at + small_v]
            at = parts * rows_v
            one, two, three = (
                piece[at + n * rows_f : at + (n + 1) * rows_f].astype(f32) for n in range(3)
            )
            row = owner * rows_f
            down[
                pl.ds(pl.multiple_of(row % vocab, 8), rows_f),
                pl.ds(pl.multiple_of(row // vocab * BS, BS), BS),
            ] = one + (two + three)
        table[...] = stack_parts(embed[...] + (down[...] + vec[2:3]))
        sums_o[...] = jnp.zeros_like(sums_o)

    second = step >= pl.num_programs(0) // 2
    small = lanes((ROWS, WIDE)) < HD

    def weights_of(r):
        value = weights[r][...].astype(f32)
        turned_value = pltpu.roll(value, HD, 1)
        value = jnp.where(second, turned_value, value)
        if pairs == 1:
            return jnp.where(small, value, 0.0)
        other = weights[parts + r][...].astype(f32)
        other = jnp.where(second, other, pltpu.roll(other, HD, 1))
        return jnp.where(small, value, other)

    own = weights_of(0)
    low_weights[me] = own.astype(bf16)[:, :height]
    for r in range(1, parts):
        low_weights[me ^ r] = weights_of(r).astype(bf16)[:, :height]
    token = token_col[...]
    hot = jnp.where(lanes((ROWS, WIDE)) % vocab == token, 1.0, 0.0).astype(bf16)
    x = dot(hot, table[...])
    x = x + dot(
        jnp.concatenate([low_weights[g] for g in range(parts)], axis=1),
        jnp.concatenate([mixing[g] for g in range(parts)], axis=0),
    )
    normed, scale = stats_of(x)
    gain = vec[3:4]
    final = (normed * gain + vec[4:5]).astype(bf16)
    head_low = head[:, :D].astype(bf16)
    square = (vocab, vocab)
    bias_row = jnp.sum(
        jnp.where(lanes(square) == sublanes(square), head[:, D : D + 1], 0.0), axis=0, keepdims=True
    )
    logits = dot(final, head_low, NT) + bias_row
    shifted = logits - jnp.max(logits, axis=-1, keepdims=True)
    log_probs = shifted - jnp.log(jnp.sum(jnp.exp(shifted), axis=-1, keepdims=True))
    target = lanes((ROWS, vocab)) == target_col[...]
    position = step * ROWS + sublanes((ROWS, 1))
    slot_weight = jnp.where(position < length - 1, floats[0], 0.0)
    picked = jnp.sum(jnp.where(target, log_probs, 0.0), axis=-1, keepdims=True)
    loss = -jnp.sum(slot_weight * picked, keepdims=True)
    logit_grad = ((jnp.exp(log_probs) - jnp.where(target, 1.0, 0.0)) * slot_weight).astype(bf16)
    final_grad = dot(logit_grad, head_low)
    grad = norm_back(final_grad, normed, scale, gain)
    high = grad.astype(bf16)
    token_hot = jnp.where(sublanes((vocab, ROWS)) == token_row[...], 1.0, 0.0).astype(bf16)
    both = dot(jnp.concatenate([own.T.astype(bf16), token_hot], axis=0), high)
    sums_o[0:vocab] += both[WIDE:]
    sums_o[vocab : 2 * vocab] += dot(logit_grad, final, TN)
    base = 2 * vocab
    sums_o[base : base + 1] += jnp.sum(final_grad * normed, axis=0, keepdims=True)
    sums_o[base + 1 : base + 2] += jnp.sum(final_grad, axis=0, keepdims=True)
    bias_grad = jnp.sum(logit_grad.astype(f32), axis=0, keepdims=True)
    sums_o[base + 2 : base + 3, :vocab] += bias_grad
    lane = lanes((1, WIDE))
    count = jnp.where((step == 0) & (length >= 2), 1.0, 0.0)
    sums_o[base + 3 : base + 4, :WIDE] += jnp.where(
        lane == 0, loss, jnp.where(lane == 1, count, 0.0)
    )
    sums_o[base + 16 : base + 16 + height] += both[:height]
    grad_o[...] = dot(high, mixing[me], NT)

    @pl.when(step == pl.num_programs(0) - 1)
    def _():
        deal(member & 1, sums_o, keep_o, send_o)


def loss_rows(
    ints,
    floats,
    token_col,
    target_col,
    token_row,
    embedding,
    head,
    vectors,
    weights,
    pieces,
    heads,
):
    seq = token_col.shape[0]
    vocab = embedding.shape[0]
    parts = len(weights) // (heads // 2)
    height = heads * vocab
    blocks = seq // ROWS // 2
    col = pl.BlockSpec((ROWS, 1), lambda i: (i, 0))
    o = jax.ShapeDtypeStruct
    full = lambda array: pl.BlockSpec(array.shape, lambda i: (0,) * array.ndim)
    sums_shape = (2 * vocab + 16 + height, D)
    return pl.pallas_call(
        functools.partial(loss_kernel, parts, len(pieces), heads),
        grid=(seq // ROWS,),
        in_specs=[SMEM, SMEM, col, col, pl.BlockSpec((1, ROWS), lambda i: (0, i))]
        + [full(embedding), full(head), full(vectors)]
        + [pl.BlockSpec((ROWS, WIDE), lambda i: (i % blocks, 0))] * len(weights)
        + [full(pieces[0])] * len(pieces),
        out_specs=[
            pl.BlockSpec((sums_shape[0] // 2, D), lambda i: (0, 0)),
            pl.BlockSpec((sums_shape[0] // 2, D), lambda i: (0, 0)),
            pl.BlockSpec((ROWS, height), lambda i: (i, 0)),
        ],
        out_shape=[o((sums_shape[0] // 2, D), f32)] * 2 + [o((seq, height), f32)],
        scratch_shapes=[
            pltpu.VMEM(sums_shape, f32),
            pltpu.VMEM((parts, height, D), bf16),
            pltpu.VMEM((parts, ROWS, height), bf16),
            pltpu.VMEM((4 * vocab, D), bf16),
            pltpu.VMEM((vocab, D), f32),
        ],
        name="loss_rows",
        **params(12),
    )(
        ints,
        floats,
        token_col,
        target_col,
        token_row,
        embedding,
        head,
        vectors,
        *weights,
        *pieces,
    )


def padded(block):
    lacking = HB - block.shape[0]
    if lacking:
        block = jnp.concatenate([block, jnp.zeros((lacking, block.shape[1]), block.dtype)], axis=0)
    return block


def put_left(ref, index, block):
    ref[index] = jnp.concatenate([padded(block)] * 3, axis=0).astype(bf16)


def put_right(ref, index, block):
    ref[index] = jnp.concatenate(split3(padded(block)), axis=0)


def factors_kernel(
    heads,
    ints,
    mine,
    other,
    mat_q,
    mat_o,
    mat_u,
    mat_f,
    upper,
    normed,
    act,
    values,
    left_o,
    right_o,
    hidden_o,
    bias_o,
    small_o,
    sums,
):
    vocab = normed.shape[0]
    width = mat_u.shape[1]
    join(ints[0] & 1, mine, other, sums)
    small_o[...] = sums[: small_o.shape[0]]
    rows = sums[0:vocab]
    mixed = sums[2 * vocab + 16 :]
    act_grad = rows_times_low(rows, mat_f[...], NT)
    u = upper[...]
    tanh = jnp.tanh(GELU_A * (u + GELU_B * (u * u * u)))
    slope = 0.5 * (1.0 + tanh) + 0.5 * u * (1.0 - tanh * tanh) * (
        GELU_A * (1.0 + 3.0 * GELU_B * (u * u))
    )
    upper_grad = act_grad * slope
    bias_grad = jnp.sum(upper_grad, axis=0, keepdims=True)
    bias_o[...] = bias_grad
    value_grad = rows_times_low(mixed, mat_o[...], NT)
    shape = value_grad.shape
    value_grad = jnp.where(sublanes(shape) // vocab == lanes(shape) // HD, value_grad, 0.0)
    value_table = value_grad[:vocab]
    for h in range(1, heads):
        value_table = value_table + value_grad[h * vocab : (h + 1) * vocab]
    hidden_o[0:vocab] = rows_times_low(upper_grad, mat_u[...], NT) + rows_times_low(
        value_table, mat_q[:, 2 * heads * HD :], NT
    )
    low = normed[...].astype(f32)
    own = act[...].astype(f32)
    val = values[...].astype(f32)
    square = (
        jnp.sum(
            dot6(low, low, NT)
            * (dot6(value_table, value_table, NT) + dot6(upper_grad, upper_grad, NT)),
            keepdims=True,
        )
        + jnp.sum(dot6(own, own, NT) * dot6(rows, rows, NT), keepdims=True)
        + jnp.sum(dot6(val, val, NT) * dot6(mixed, mixed, NT), keepdims=True)
        + jnp.sum(bias_grad * bias_grad, keepdims=True)
    )
    hidden_o[vocab : vocab + 16] = jnp.broadcast_to(square, (16, D))
    across = D // BS
    f_rows = width // BS
    pair = 2 * vocab
    for i in range(across):
        put_left(left_o, i, low[:, i * BS : (i + 1) * BS])
    for i in range(f_rows):
        put_left(left_o, across + i, own[:, i * BS : (i + 1) * BS])
    for i in range(heads // 2):
        put_left(
            left_o,
            across + f_rows + i,
            val[i * pair : (i + 1) * pair, i * BS : (i + 1) * BS],
        )
    at = 0
    for k in range(heads * HD // BS):
        put_right(right_o, at, value_table[:, k * BS : (k + 1) * BS])
        at += 1
    for i in range(heads // 2):
        for k in range(across):
            put_right(right_o, at, mixed[i * pair : (i + 1) * pair, k * BS : (k + 1) * BS])
            at += 1
    for k in range(f_rows):
        put_right(right_o, at, upper_grad[:, k * BS : (k + 1) * BS])
        at += 1
    for k in range(across):
        put_right(right_o, at, rows[:, k * BS : (k + 1) * BS])
        at += 1


def rest_kernel(pairs, ints, mine, other, hidden, mat_q, normed, right_o, hidden_o, half_o, table):
    vocab = normed.shape[0]
    join(ints[0] & 1, mine, other, table)
    blocks = [table[p * vocab : (p + 1) * vocab, :WIDE] for p in range(pairs)]
    blocks += [table[p * vocab : (p + 1) * vocab, WIDE:] for p in range(pairs)]
    grad = jnp.concatenate(blocks, axis=1)
    for k, block in enumerate(blocks):
        put_right(right_o, k, block)
    low = normed[...].astype(f32)
    square = jnp.sum(dot6(low, low, NT) * dot6(grad, grad, NT), keepdims=True)
    hidden_o[0:vocab] = hidden[0:vocab] + rows_times_low(grad, mat_q[:, : 2 * pairs * WIDE], NT)
    hidden_o[vocab:] = hidden[vocab:] + square
    size = half_o.shape[0]
    half_o[...] = hidden_o[pl.ds(pl.multiple_of((ints[0] & 1) * size, size), size)]


def factor_places(heads, ff_local):
    q_cols = 3 * heads * HD // BS
    o_rows = heads // 2
    across = D // BS
    f_rows = ff_local // BS
    left, right = [], []
    for which, i, k in tile_places(layer_shapes(heads, ff_local)):
        if which == 0:
            left.append(i)
            right.append(k)
        elif which == 1:
            left.append(across + f_rows + i)
            right.append(q_cols + i * across + k)
        elif which == 2:
            left.append(i)
            right.append(q_cols + o_rows * across + k)
        else:
            left.append(across + i)
            right.append(q_cols + o_rows * across + f_rows + k)
    return np.array(left, np.int32), np.array(right, np.int32)


def factors(ints, mine, other, mats, upper, normed, act, values, heads):
    vocab = normed.shape[0]
    ff_local = upper.shape[1]
    n_left = D // BS + ff_local // BS + heads // 2
    n_right = heads * HD // BS + heads // 2 * (D // BS) + ff_local // BS + D // BS
    o = jax.ShapeDtypeStruct
    return pl.pallas_call(
        functools.partial(factors_kernel, heads),
        in_specs=[SMEM] + [VMEM] * 10,
        out_specs=[VMEM] * 5,
        out_shape=[
            o((n_left, 3 * HB, BS), bf16),
            o((n_right, 3 * HB, BS), bf16),
            o((vocab + 16, D), f32),
            o((1, ff_local), f32),
            o((2 * vocab + 16, D), f32),
        ],
        scratch_shapes=[pltpu.VMEM((2 * mine.shape[0], D), f32)],
        name="factors",
        **params(7),
    )(ints, mine, other, *mats, upper, normed, act, values)


def factors_rest(ints, mine, other, hidden, mat_q, normed, heads):
    o = jax.ShapeDtypeStruct
    pairs = heads // 2
    return pl.pallas_call(
        functools.partial(rest_kernel, pairs),
        in_specs=[SMEM] + [VMEM] * 5,
        out_specs=[VMEM] * 3,
        out_shape=[
            o((2 * pairs, 3 * HB, BS), bf16),
            o(hidden.shape, f32),
            o((hidden.shape[0] // 2, D), f32),
        ],
        scratch_shapes=[pltpu.VMEM((2 * mine.shape[0], 2 * WIDE), f32)],
        name="factors_rest",
        **params(2),
    )(ints, mine, other, hidden, mat_q, normed)


def small_kernel(parts, corrections, ints, sums, own, *refs):
    mine, others, refs = refs[: parts - 1], refs[parts - 1 : 2 * parts - 2], refs[2 * parts - 2 :]
    bias_grad, refs = refs[0], refs[1:]
    weights, refs = refs[:12], refs[12:]
    outs, scalars, total = refs[:12], refs[12], refs[13]
    vocab = weights[0].shape[0]
    base = 2 * vocab
    size = own.shape[0] // 2
    for place, group in ((ints[0], mine), (1 - ints[0], others)):
        span = pl.ds(pl.multiple_of(place * size, size), size)
        total[span] = tree_sum([own[span]] + [ref[...] for ref in group])
    hidden = total[:vocab]
    square = total[vocab : vocab + 1, 0:1]
    rows = sums[0:vocab]
    normed, scale = stats_of(weights[0][...])
    gain = weights[6][0:1]
    embed_grad = rows + norm_back(hidden, normed, scale, gain)
    vector_grad = jnp.concatenate(
        [
            jnp.sum(hidden * normed, axis=0, keepdims=True),
            jnp.sum(hidden, axis=0, keepdims=True),
            jnp.sum(rows, axis=0, keepdims=True),
            sums[base : base + 1],
            sums[base + 1 : base + 2],
        ],
        axis=0,
    )
    head_grad = sums[vocab : 2 * vocab]
    head_bias = sums[base + 2 : base + 3, :vocab]
    add = lambda value: jnp.sum(value * value, keepdims=True)
    square = square + add(embed_grad) + add(vector_grad) + add(head_grad) + add(head_bias)
    count = sums[base + 3 : base + 4, 1:2]
    loss = sums[base + 3 : base + 4, 0:1] / count
    norm = jnp.sqrt(square) / count
    scale_all = jnp.minimum(1.0, CLIP_NORM / norm) / count
    one, two = corrections[0], corrections[1]

    def update(index, pick, grad):
        weight, first, second = (weights[3 * index + k][pick] for k in range(3))
        grad = grad * scale_all
        first = BETA_ONE * first + (1.0 - BETA_ONE) * grad
        second = BETA_TWO * second + (1.0 - BETA_TWO) * grad * grad
        step = first / one / (jnp.sqrt(second / two) + ADAM_EPS)
        outs[3 * index][pick] = weight - RATE_SMALL * (step + WEIGHT_DECAY * weight)
        outs[3 * index + 1][pick] = first
        outs[3 * index + 2][pick] = second

    everything = slice(None)
    update(0, everything, embed_grad)
    shape = (vocab, vocab)
    head_column = jnp.sum(
        jnp.where(lanes(shape) == sublanes(shape), head_bias, 0.0), axis=1, keepdims=True
    )
    update(1, (everything, slice(0, D)), head_grad)
    update(1, (everything, slice(D, D + 1)), head_column)
    update(2, everything, vector_grad)
    update(3, everything, bias_grad[...])
    lane = lanes((1, WIDE))
    scalars[...] = jnp.where(
        lane == 0, scale_all, jnp.where(lane == 1, loss, jnp.where(lane == 2, norm, 0.0))
    )


def small(corrections, upper, sums, hidden, mine, others, bias_grad, weights):
    o = jax.ShapeDtypeStruct
    return pl.pallas_call(
        functools.partial(small_kernel, 1 + len(mine)),
        in_specs=[SMEM] * 2 + [VMEM] * (2 + 2 * len(mine) + 1 + 12),
        out_specs=[VMEM] * 13,
        out_shape=[o(weight.shape, f32) for weight in weights] + [o((1, WIDE), f32)],
        scratch_shapes=[pltpu.VMEM(hidden.shape, f32)],
        name="small",
        **params(4),
    )(corrections, upper, sums, hidden, *mine, *others, bias_grad, *weights)


QB = 32
UNQ = 6
PER = 6


def take(value, at):
    return jnp.take_along_axis(value, at, axis=1, mode="promise_in_bounds")


def eliminate(packed, count):
    shape = (8, BS)
    lane, sub = lanes(shape), sublanes(shape)
    start = lane // QB * QB
    span = range(count)
    for p in range(QB // 8):
        r0 = 8 * p

        def body(step, carry):
            jj = 2 * step
            j = r0 + jj
            pick, pick_two = start + j, start + (j + 1)
            mark, mark_two = lane == pick, lane == pick_two
            below, below_two = sub > jj, sub > jj + 1
            wide = [jnp.broadcast_to(packed[t, pl.ds(j, 1), :], shape) for t in span]
            next_wide = [jnp.broadcast_to(packed[t, pl.ds(j + 1, 1), :], shape) for t in span]
            kept = [[packed[t, 8 * q : 8 * q + 8, :] for q in range(p, QB // 8)] for t in span]
            pivot = [take(w, pick) for w in wide]
            right = [take(w, pick_two) for w in wide]
            lower = [take(w, pick) for w in next_wide]
            corner = [take(w, pick_two) for w in next_wide]
            ones = [[take(a, pick) for a in group] for group in kept]
            twos = [[take(a, pick_two) for a in group] for group in kept]
            inverse = [1.0 / d for d in pivot]
            ratio = [b * i for b, i in zip(right, inverse)]
            inverse_two = [1.0 / (e - b * r) for e, b, r in zip(corner, lower, ratio)]
            scaled = [jnp.where(mark, 1.0, w) * i for w, i in zip(wide, inverse)]
            scaled_two = [
                jnp.where(mark_two, 1.0, jnp.where(mark, 0.0, w) - b * x) * i
                for w, b, x, i in zip(next_wide, lower, scaled, inverse_two)
            ]
            for t in span:
                for k, q in enumerate(range(p, QB // 8)):
                    a, c, d = kept[t][k], ones[t][k], twos[t][k]
                    d = d - c * ratio[t]
                    first = jnp.where(mark, 0.0, a) - c * scaled[t]
                    if k == 0:
                        first = jnp.where(below, first, a)
                    second = jnp.where(mark_two, 0.0, first) - d * scaled_two[t]
                    if k == 0:
                        second = jnp.where(below_two, second, first)
                    packed[t, 8 * q : 8 * q + 8, :] = second
            return carry

        lax.fori_loop(0, 4, body, 0)


def part_inverse(packed):
    shape = (QB, BS)
    lane, sub = lanes(shape), sublanes(shape)
    part, col = lane // QB, lane % QB
    diagonal = jnp.where(col == sub, packed, 0.0)
    pivot = jnp.ones(shape, f32)
    for k in range(BS // QB):
        own = jnp.sum(jnp.where(part == k, diagonal, 0.0), axis=1, keepdims=True)
        pivot = jnp.where(part == k, own, pivot)
    unit = jnp.where(col < sub, packed, jnp.where(col == sub, 1.0, 0.0))
    return unit * lax.rsqrt(pivot)


def inverse_factors(gram, packed, result, count):
    parts = BS // QB
    unroll = next(k for k in (UNQ, 3, 2, 1) if count % k == 0)
    lane32, sub32 = lanes((QB, BS)), sublanes((QB, BS))
    for b in range(parts):
        begin = b * QB
        below = begin + QB
        rows = slice(begin, below)
        here = lane32 // QB == b

        def pack(i, carry):
            for t in [i * unroll + k for k in range(unroll)]:
                value = jnp.zeros((QB, BS), f32)
                for k in range(parts):
                    block = gram[parts * t + k, rows, :]
                    if k != b:
                        block = pltpu.roll(block, (k * QB + BS - begin) % BS, 1)
                    value = jnp.where(lane32 // QB == k, block, value)
                packed[t] = value
            return carry

        lax.fori_loop(0, count // unroll, pack, 0)
        eliminate(packed, count)

        def spread(i, carry):
            groups = [i * unroll + k for k in range(unroll)]
            inverses = [part_inverse(packed[t]) for t in groups]
            firsts = [
                jnp.concatenate([jnp.where(lane32 // QB == k, x, 0.0) for k in range(parts)], axis=0)
                for x in inverses
            ]
            unit = jnp.where(lane32 - begin == sub32, 1.0, 0.0)
            panels = [
                jnp.concatenate(
                    [jnp.where(here, unit, gram[parts * t + k, rows, :]) for k in range(parts)],
                    axis=0,
                )
                for t in groups
            ]
            news = [dot6(x, y, NN) for x, y in zip(firsts, panels)]
            for t, new in zip(groups, news):
                for k in range(parts):
                    value = new[k * QB : (k + 1) * QB]
                    result[parts * t + k, rows, :] = (
                        jnp.where(lane32 < below, value, 0.0) if below < BS else value
                    )
            if below < BS:
                for t, new in zip(groups, news):
                    mats = [new[k * QB : (k + 1) * QB] for k in range(parts)]
                    changes = [dot6(x, x, TN) for x in mats]
                    shape = (BS - below, BS)
                    mark = lanes(shape) // QB == b
                    for k in range(parts):
                        old = gram[parts * t + k, below:, :]
                        gram[parts * t + k, below:, :] = jnp.where(mark, 0.0, old) - changes[k][below:]
            return carry

        lax.fori_loop(0, count // unroll, spread, 0)


def tile_params(count, per):
    blk = pl.BlockSpec((per, BS, BS), lambda i: (i, 0, 0))
    full = pl.BlockSpec((count, BS, BS), lambda i: (0, 0, 0))
    return blk, full, lambda dt: jax.ShapeDtypeStruct((count, BS, BS), dt)


def gradient_kernel(per, rest, natural, left_at, right_at, lefts, rights, more, L, R, QL, QR, *outs):
    step = pl.program_id(0)
    span = range(per)
    pairs = []
    for s in span:
        tile = natural[step * per + s]
        at = right_at[tile]
        right = jnp.where(
            at < rest, more[jnp.minimum(at, rest - 1)], rights[jnp.maximum(at - rest, 0)]
        )
        pairs.append((lefts[left_at[tile]], right))
    g = [dot(a, b, TN) for a, b in pairs]
    gt = [dot(b, a, TN) for a, b in pairs]
    qt = [QL[s].T for s in span]
    left = [dot3(x, x, NT) for x in g]
    right = [dot3(x, x, NT) for x in gt]
    rot = [dot3(q, x, NN) for q, x in zip(qt, g)]
    mixed_left = [dot3(left[s], QL[s], NN) for s in span]
    mixed_right = [dot3(right[s], QR[s], NN) for s in span]
    rot = [dot3(rot[s], QR[s], NN) for s in span]
    old_left = [dot6(L[s], QL[s], NN) for s in span]
    old_right = [dot6(R[s], QR[s], NN) for s in span]
    for s in span:
        for out, value in zip(
            outs, (left, right, rot, mixed_left, mixed_right, old_left, old_right)
        ):
            out[s] = value[s]


def gradient_products(natural, left_at, right_at, lefts, rights, more, L, R, QL, QR):
    count = QL.shape[0]
    blk, _, o = tile_params(count, PER)
    whole = lambda x: pl.BlockSpec(x.shape, lambda i: (0, 0, 0))
    return pl.pallas_call(
        functools.partial(gradient_kernel, PER, more.shape[0]),
        grid=(count // PER,),
        in_specs=[SMEM] * 3 + [whole(lefts), whole(rights), whole(more)] + [blk] * 4,
        out_specs=[blk] * 7,
        out_shape=[o(f32)] * 7,
        name="gradient_products",
        **params(9),
    )(natural, left_at, right_at, lefts, rights, more, L, R, QL, QR)


def soap_kernel(
    count, per, corrections, scal, GL, GR, GT, BL, BR, AL, AR, W, m, v, L, R, QL, QR,
    W_o, low_o, m_o, v_o, L_o, R_o, QL_o, QR_o, ML_s, MR_s, work, inv_s, packed,
):
    step = pl.program_id(0)
    scale = scal[0:1, 0:1]
    c1, c2 = corrections[0], corrections[1]
    span = range(per)
    share = (1 - BETA_TWO) * (scale * scale)
    xs = []
    for s in span:
        rot = GT[s] * scale
        mn = BETA_ONE * m[s] + (1 - BETA_ONE) * rot
        vn = BETA_TWO * v[s] + (1 - BETA_TWO) * rot * rot
        m_o[s] = mn
        v_o[s] = vn
        xs.append((mn / c1) / (jnp.sqrt(vn / c2) + ADAM_EPS))
    ML = [BETA_TWO * AL[s] + share * BL[s] for s in span]
    MR = [BETA_TWO * AR[s] + share * BR[s] for s in span]
    back = [dot3(QL[s], xs[s], NN) for s in span]
    ML = [x * lax.rsqrt(jnp.sum(x * x, keepdims=True)) for x in ML]
    MR = [x * lax.rsqrt(jnp.sum(x * x, keepdims=True)) for x in MR]
    back = [dot3(back[s], QR[s], NT) for s in span]
    gram_left = [dot6(x, x, TN) for x in ML]
    gram_right = [dot6(x, x, TN) for x in MR]
    for s in span:
        L_o[s] = BETA_TWO * L[s] + share * GL[s]
        R_o[s] = BETA_TWO * R[s] + share * GR[s]
        w = W[s]
        wn = w - RATE_TILES * (back[s] + WEIGHT_DECAY * w)
        W_o[s] = wn
        low_o[s] = wn.astype(bf16)
        t = step * per + s
        ML_s[t] = ML[s]
        MR_s[t] = MR[s]
        work[2 * t] = gram_left[s]
        work[2 * t + 1] = gram_right[s]

    @pl.when(step == pl.num_programs(0) - 1)
    def _():
        inverse_factors(work, packed, inv_s, count // 2)
        unroll = next(k for k in (8, 6, 3, 1) if count % k == 0)

        def last(i, carry):
            ts = [i * unroll + k for k in range(unroll)]
            ol = [dot3(ML_s[t], inv_s[2 * t], NT) for t in ts]
            orr = [dot3(MR_s[t], inv_s[2 * t + 1], NT) for t in ts]
            for t, a, b in zip(ts, ol, orr):
                QL_o[t] = a
                QR_o[t] = b
            return carry

        lax.fori_loop(0, count // unroll, last, 0)


def soap(corrections, scal, products, W, m, v, L, R, QL, QR):
    count = W.shape[0]
    blk, full, o = tile_params(count, PER)
    return pl.pallas_call(
        functools.partial(soap_kernel, count, PER),
        grid=(count // PER,),
        in_specs=[SMEM, pl.BlockSpec((1, WIDE), lambda i: (0, 0))] + [blk] * 14,
        out_specs=[blk] * 6 + [full] * 2,
        out_shape=[o(f32), o(bf16), o(f32), o(f32), o(f32), o(f32), o(f32), o(f32)],
        scratch_shapes=[pltpu.VMEM((count, BS, BS), f32)] * 2
        + [pltpu.VMEM((2 * count, BS, BS), f32)] * 2
        + [pltpu.VMEM((count // 2, QB, BS), f32)],
        name="soap_tiles",
        **params(40, 48),
    )(corrections, scal, *products, W, m, v, L, R, QL, QR)


def local(
    tokens,
    lengths,
    tile_owner,
    step_count,
    weight_tiles,
    tiles_first,
    tiles_second,
    stats_left,
    stats_right,
    basis_left,
    basis_right,
    embedding,
    embedding_first,
    embedding_second,
    head_table,
    head_first,
    head_second,
    vectors,
    vectors_first,
    vectors_second,
    fc_bias,
    fc_bias_first,
    fc_bias_second,
):
    seq = tokens.shape[1]
    mp_count = lax.axis_size("mp")
    dp_count = lax.axis_size("dp")
    dp_index = lax.axis_index("dp")
    mp_index = lax.axis_index("mp")
    upper_pair = dp_index & 1
    heads = H // mp_count
    ff_local = fc_bias.shape[1]
    count = weight_tiles.shape[0]
    vocab = embedding.shape[0]
    own_index = dp_index[None]

    natural, low_tiles, normed, keep, send = first_tables(
        tile_owner, own_index, weight_tiles, embedding, vectors, heads, ff_local
    )
    token_col = tokens.reshape(seq, 1)
    target_col = jnp.roll(tokens, -1, axis=1).reshape(seq, 1)
    keep = keep + swap_with(send, "dp", 1)
    mine = direct(keep)
    low_tiles, mine = lax.optimization_barrier((low_tiles, mine))
    gathered = lax.all_gather(low_tiles, "dp", axis=0, tiled=True)
    proj, upper, act, values, keep, send = second_tables(
        natural, own_index, mine, swap_with(mine, "dp", 1), fc_bias, low_tiles, vocab, heads, dp_count
    )
    cosine, sine, cosine_t, sine_t = rotary_tables(seq)
    segment = sum(segments_of(heads, dp_count))
    places = range(1, dp_count // 2)
    received = [swap_with(send, "dp", 1)]
    queries, keys = [], []
    weight = jnp.zeros((8, WIDE), f32)
    for pair in range(heads // 2):
        query, key, weight, weight_low = attention(
            pair, lengths, token_col, proj, cosine, sine, weight, heads
        )
        queries.append(query)
        keys.append(key)
        if pair == 0:
            received, weight, weight_low = lax.optimization_barrier((received, weight, weight_low))
            keep = keep + received[0]
            received = [
                swap_with(keep[q * segment : (q + 1) * segment], "dp", 2 * q) for q in places
            ]
            keep, weight = lax.optimization_barrier((keep, weight))
            weights = gather_xor(weight_low, "mp")
    if heads > 2:
        more = gather_xor(weight_low, "mp")
        received, weights, more[0] = lax.optimization_barrier((received, weights, more[0]))
    mine = tree_sum([keep[:segment]] + list(received))
    packed = pack_segments(heads, dp_count, gather_xor(mine, "mp"))
    even = [packed] + [swap_with(packed, "dp", 2 * q) for q in places]
    if heads > 2:
        even, more = lax.optimization_barrier((even, more))
        weights = weights + more
    odd = [swap_with(piece, "dp", 1) for piece in even]
    pieces = [piece for two in zip(even, odd) for piece in two]
    length = lengths[0]
    inverse_length = 1.0 / jnp.maximum(length - 1, 1).astype(f32)
    keep, send, weight_grad = loss_rows(
        jnp.stack([mp_index, length, dp_index]),
        inverse_length[None],
        token_col,
        target_col,
        tokens,
        embedding,
        head_table.T,
        vectors,
        weights,
        pieces,
        heads,
    )
    keep = keep + swap_with(send, "dp", 1)
    tables_back = []
    for pair in range(heads // 2):
        if pair == 1:
            weight_grad, keep = lax.optimization_barrier((weight_grad, keep))
        tables_back.append(
            attention_back(
                pair,
                token_col,
                tokens,
                queries[pair],
                keys[pair],
                weight,
                weight_grad,
                cosine,
                sine,
                cosine_t,
                sine_t,
                heads,
            )
        )
    mine = butterfly(keep)
    table = jnp.concatenate(tables_back, axis=0)
    half = table.shape[0] // 2
    first, second = table[:half], table[half:]
    is_upper = upper_pair == 1
    table = jnp.where(is_upper, second, first) + swap_with(
        jnp.where(is_upper, first, second), "dp", 1
    )
    gathered, table = lax.optimization_barrier((gathered, table))
    mats = assemble(tile_owner, gathered, heads, ff_local)
    table = direct(table)
    mine, mats = lax.optimization_barrier((mine, mats))
    left, right, hidden, bias_grad, sums = factors(
        own_index, mine, swap_with(mine, "dp", 1), mats, upper, normed, act, values, heads
    )
    more, hidden, hidden_half = factors_rest(
        own_index, table, swap_with(table, "dp", 1), hidden, mats[0], normed, heads
    )
    hidden_parts = gather_halves(hidden_half)
    left_at, right_at = (jnp.asarray(places) for places in factor_places(heads, ff_local))
    gradients = gradient_products(
        natural, left_at, right_at, left, right, more, stats_left, stats_right, basis_left, basis_right
    )
    hidden_parts, gradients = lax.optimization_barrier((hidden_parts, gradients))
    hidden_others = swap_pair(hidden_parts)
    corrections = 1.0 - jnp.power(
        jnp.array([BETA_ONE, BETA_TWO], f32), step_count.astype(f32)
    )
    small_weights = (
        embedding,
        embedding_first,
        embedding_second,
        head_table.T,
        head_first.T,
        head_second.T,
        vectors,
        vectors_first,
        vectors_second,
        fc_bias,
        fc_bias_first,
        fc_bias_second,
    )
    *small_out, scalars = small(
        corrections,
        upper_pair[None],
        sums,
        hidden,
        hidden_parts,
        hidden_others,
        bias_grad,
        small_weights,
    )
    small_out[3:6] = [value.T for value in small_out[3:6]]
    results = soap(
        corrections,
        scalars,
        gradients,
        weight_tiles,
        tiles_first,
        tiles_second,
        stats_left,
        stats_right,
        basis_left,
        basis_right,
    )
    return (scalars[0, 1], scalars[0, 2], *results, *small_out)


def solution(mesh):
    tiled = P("dp", None, "mp")
    split = P(None, "mp")
    in_specs = (P("dp", None), P("dp"), P(), P(), *[tiled] * 7, *[P()] * 9, *[split] * 3)
    out_specs = (P(), P(), *[tiled] * 8, *[P()] * 9, *[split] * 3)
    return jax.shard_map(local, mesh=mesh, in_specs=in_specs, out_specs=out_specs, check_vma=False)
```

```python
import functools
import math

import jax
import jax.numpy as jnp
import numpy as np
from jax import lax
from jax.experimental import pallas as pl
from jax.experimental.pallas import tpu as pltpu
from jax.sharding import PartitionSpec as P

D = 1024
H = 16
HD = 64
ROT = 32
BS = 128
HB = 64
ROWS = 256
WIDE = 128
MEGA = 1024 * 1024

NORM_EPS = 1e-05
CLIP_NORM = 0.02
RATE_TILES = 0.02
RATE_SMALL = 0.2
BETA_ONE = 0.9
BETA_TWO = 0.95
ADAM_EPS = 1e-08
WEIGHT_DECAY = 0.01
MASKED = -1e30
GELU_A = math.sqrt(2.0 / math.pi)
GELU_B = 0.044715

NN = (((1,), (0,)), ((), ()))
NT = (((1,), (1,)), ((), ()))
TN = (((0,), (0,)), ((), ()))
f32 = jnp.float32
bf16 = jnp.bfloat16
SMEM = pl.BlockSpec(memory_space=pltpu.SMEM)
VMEM = pl.BlockSpec(memory_space=pltpu.VMEM)
ANY = pl.BlockSpec(memory_space=pl.ANY)


def dot(a, b, dims=NN):
    return lax.dot_general(a, b, dims, preferred_element_type=f32)


def split2(a):
    high = a.astype(bf16)
    return high, (a - high.astype(f32)).astype(bf16)


def split3(a):
    high = a.astype(bf16)
    rest = a - high.astype(f32)
    middle = rest.astype(bf16)
    return high, middle, (rest - middle.astype(f32)).astype(bf16)


def dot3(a, b, dims):
    (axis_a,), (axis_b,) = dims[0]
    ah, al = split2(a)
    bh, bl = split2(b)
    return dot(
        jnp.concatenate([ah, ah, al], axis=axis_a),
        jnp.concatenate([bh, bl, bh], axis=axis_b),
        dims,
    )


def dot6(a, b, dims):
    (axis_a,), (axis_b,) = dims[0]
    ah, am, al = split3(a)
    bh, bm, bl = split3(b)
    return dot(
        jnp.concatenate([ah, ah, am, am, ah, al], axis=axis_a),
        jnp.concatenate([bh, bm, bh, bm, bl, bh], axis=axis_b),
        dims,
    )


def rows_times_low(a, low, dims):
    count = a.shape[0]
    parts = dot(jnp.concatenate(split3(a), axis=0), low, dims)
    return parts[:count] + (parts[count : 2 * count] + parts[2 * count :])


def lanes(shape):
    return lax.broadcasted_iota(jnp.int32, shape, len(shape) - 1)


def sublanes(shape):
    return lax.broadcasted_iota(jnp.int32, shape, len(shape) - 2)


def stats_of(values):
    centred = values - jnp.mean(values, axis=-1, keepdims=True)
    spread = jnp.mean(centred * centred, axis=-1, keepdims=True)
    scale = lax.rsqrt(spread + NORM_EPS)
    return centred * scale, scale


def norm_back(grad, normed, scale, gain):
    inner = grad * gain
    mean_one = jnp.mean(inner, axis=-1, keepdims=True)
    mean_two = jnp.mean(inner * normed, axis=-1, keepdims=True)
    return scale * (inner - mean_one - normed * mean_two)


def params(microseconds, megabytes=20):
    return dict(
        compiler_params=pltpu.CompilerParams(vmem_limit_bytes=megabytes * MEGA),
        cost_estimate=pl.CostEstimate(
            flops=int(microseconds * 1.1e9), bytes_accessed=int(microseconds * 1e6), transcendentals=0
        ),
    )


def swap_with(value, axis, mask):
    count = lax.axis_size(axis)
    return lax.ppermute(value, axis, [(i, i ^ mask) for i in range(count)])


def tree_sum(parts):
    while len(parts) > 1:
        parts = [parts[i] + parts[i + 1] for i in range(0, len(parts), 2)]
    return parts[0]


def gather_xor(value, axis):
    return [value] + [swap_with(value, axis, r) for r in range(1, lax.axis_size(axis))]


def gather_halves(mine):
    return [swap_with(mine, "mp", r) for r in range(1, lax.axis_size("mp"))]


def swap_pair(parts):
    return [swap_with(part, "dp", 1) for part in parts]


def butterfly(kept):
    bits = [1 << k for k in range(1, lax.axis_size("dp").bit_length() - 1)]
    half = (kept.shape[0] // 2 + 7) // 8 * 8
    pieces = [kept[:half], kept[half:]]
    for k in range(len(bits)):
        received = [
            swap_with(piece, "dp", order[k])
            for piece, order in zip(pieces, (bits, bits[1:] + bits[:1]))
        ]
        pieces = [piece + other for piece, other in zip(pieces, received)]
    return jnp.concatenate(pieces, axis=0)


def direct(kept):
    return tree_sum([kept] + [swap_with(kept, "dp", r) for r in range(2, lax.axis_size("dp"), 2)])


def deal(upper, value, keep_o, send_o):
    half = keep_o.shape[0]

    @pl.when(upper == 0)
    def _():
        keep_o[...] = value[:half]
        send_o[...] = value[half : 2 * half]

    @pl.when(upper == 1)
    def _():
        keep_o[...] = value[half : 2 * half]
        send_o[...] = value[:half]


def join(upper, mine, other, whole):
    half = mine.shape[0]

    @pl.when(upper == 0)
    def _():
        whole[:half] = mine[...]
        whole[half:] = other[...]

    @pl.when(upper == 1)
    def _():
        whole[:half] = other[...]
        whole[half:] = mine[...]


def layer_shapes(heads_local, ff_local):
    return ((D, 3 * heads_local * HD), (heads_local * HD, D), (D, ff_local), (ff_local, D))


def tile_places(shapes):
    places = []
    for which, (row_total, col_total) in enumerate(shapes):
        for i in range(row_total // BS):
            for k in range(col_total // BS):
                places.append((which, i, k))
    return places


def first_places(heads, ff_local):
    q_cols = 3 * heads * HD // BS
    rows, blocks = [], []
    for which, i, k in tile_places(layer_shapes(heads, ff_local)):
        used = which in (0, 2)
        rows.append(i if used else 0)
        blocks.append(k if which == 0 else q_cols + k if which == 2 else q_cols + ff_local // BS)
    return np.array(rows, np.int32), np.array(blocks, np.int32)


def first_kernel(owner, ints, row_of, block_of, tiles, embed, vec, natural_o, low_o, normed_o, keep_o, send_o, rows, acc):
    count = tiles.shape[0]
    begin = ints[0] * count

    def find(b, carry):
        slot = owner[b] - begin

        @pl.when((slot >= 0) & (slot < count))
        def _():
            natural_o[slot] = b

        return carry

    lax.fori_loop(0, owner.shape[0], find, 0)
    normed, _ = stats_of(embed[...])
    low = (normed * vec[0:1] + vec[1:2]).astype(bf16)
    normed_o[...] = low
    for i in range(D // BS):
        rows[i] = low[:, i * BS : (i + 1) * BS]
    acc[...] = jnp.zeros_like(acc)
    for s in range(count):
        low_o[s] = tiles[s].astype(bf16)
    products = [dot(rows[row_of[natural_o[s]]], low_o[s]) for s in range(count)]
    for s in range(count):
        acc[block_of[natural_o[s]]] += products[s]
    half = keep_o.shape[0]
    for upper, first, second in ((0, keep_o, send_o), (1, send_o, keep_o)):

        @pl.when((ints[0] & 1) == upper)
        def _():
            first[...] = acc[:half]
            second[...] = acc[half : 2 * half]


def first_tables(owner, ints, tiles, embedding, vectors, heads, ff_local):
    vocab = embedding.shape[0]
    row_of, block_of = first_places(heads, ff_local)
    blocks = int(block_of.max())
    o = jax.ShapeDtypeStruct
    return pl.pallas_call(
        first_kernel,
        in_specs=[SMEM] * 4 + [VMEM] * 3,
        out_specs=[SMEM] + [VMEM] * 4,
        out_shape=[
            o((tiles.shape[0],), jnp.int32),
            o(tiles.shape, bf16),
            o((vocab, D), bf16),
            o(((blocks + 1) // 2, vocab, BS), f32),
            o(((blocks + 1) // 2, vocab, BS), f32),
        ],
        scratch_shapes=[
            pltpu.VMEM((D // BS, vocab, BS), bf16),
            pltpu.VMEM((blocks + 1, vocab, BS), f32),
        ],
        name="first_tables",
        **params(4, 56),
    )(owner, ints, jnp.asarray(row_of), jnp.asarray(block_of), tiles, embedding, vectors)


def second_places(heads, ff_local):
    pairs, across = heads // 2, D // BS
    lefts, blocks = [], []
    for which, i, k in tile_places(layer_shapes(heads, ff_local)):
        lefts.append(i if which == 1 else pairs + i if which == 3 else 0)
        blocks.append(
            i * across + k if which == 1 else (pairs * across + k if which == 3 else pairs * across + across)
        )
    return np.array(lefts, np.int32), np.array(blocks, np.int32)


def segments_of(heads, dp_count):
    return heads // 2 * (D // BS) * HB // dp_count, 32 * (D // BS) // dp_count


def second_kernel(
    heads, dp_count, natural, ints, left_of, block_of, mine, other, bias, low,
    proj_o, upper_o, act_o, values_o, keep_o, send_o, total, lefts, acc,
):
    vocab = proj_o.shape[0]
    me = ints[0]
    count = low.shape[0]
    pairs = heads // 2
    q_cols = 3 * heads * HD // BS
    f_rows = upper_o.shape[1] // BS
    across = D // BS
    join(me & 1, mine, other, total)
    for j in range(q_cols):
        proj_o[:, j * BS : (j + 1) * BS] = total[j]
    upper = jnp.concatenate([total[q_cols + j] for j in range(f_rows)], axis=1)
    upper = upper + bias[...]
    upper_o[...] = upper
    act = 0.5 * upper * (1.0 + jnp.tanh(GELU_A * (upper + GELU_B * (upper * upper * upper))))
    act = act.astype(bf16).astype(f32)
    act_o[...] = act.astype(bf16)
    values = proj_o[:, 2 * heads * HD :]
    shape = (heads * vocab, heads * HD)
    values = jnp.concatenate([values] * heads, axis=0)
    values = jnp.where(sublanes(shape) // vocab == lanes(shape) // HD, values, 0.0)
    values_o[...] = values.astype(bf16)
    for i in range(pairs):
        lefts[i] = values[i * HB : (i + 1) * HB, i * BS : (i + 1) * BS].astype(bf16)
    for i in range(f_rows):
        lefts[pairs + i] = padded(act[:, i * BS : (i + 1) * BS]).astype(bf16)
    acc[...] = jnp.zeros_like(acc)
    products = [dot(lefts[left_of[natural[s]]], low[s]) for s in range(count)]
    for s in range(count):
        rows = pl.ds(pl.multiple_of(block_of[natural[s]] * HB, HB), HB)
        acc[rows] += products[s]
    rows_v, rows_f = segments_of(heads, dp_count)
    base = pairs * across * HB
    for odd, first, second in ((0, keep_o, send_o), (1, send_o, keep_o)):

        @pl.when((me & 1) == odd)
        def _():
            for e in range(dp_count):
                out = second if e & 1 else first
                start = pl.multiple_of(((me ^ e) >> 1) * (rows_v + rows_f), 8)
                out[pl.ds(start, rows_v)] = acc[e * rows_v : (e + 1) * rows_v]
                k, inside = e * rows_f // vocab, e * rows_f % vocab
                at = base + k * HB + inside
                out[pl.ds(pl.multiple_of(start + rows_v, 8), rows_f)] = acc[at : at + rows_f]


def second_tables(natural, ints, mine, other, fc_bias, low, vocab, heads, dp_count):
    ff_local = fc_bias.shape[1]
    left_of, block_of = second_places(heads, ff_local)
    o = jax.ShapeDtypeStruct
    return pl.pallas_call(
        functools.partial(second_kernel, heads, dp_count),
        in_specs=[SMEM] * 4 + [VMEM] * 4,
        out_specs=[VMEM] * 6,
        out_shape=[
            o((vocab, 3 * heads * HD), f32),
            o((vocab, ff_local), f32),
            o((vocab, ff_local), bf16),
            o((heads * vocab, heads * HD), bf16),
            o((dp_count // 2 * sum(segments_of(heads, dp_count)), BS), f32),
            o((dp_count // 2 * sum(segments_of(heads, dp_count)), BS), f32),
        ],
        scratch_shapes=[
            pltpu.VMEM((2 * mine.shape[0],) + mine.shape[1:], f32),
            pltpu.VMEM((heads // 2 + ff_local // BS, HB, BS), bf16),
            pltpu.VMEM(((int(block_of.max()) + 1) * HB, BS), f32),
        ],
        name="second_tables",
        **params(4),
    )(natural, ints, jnp.asarray(left_of), jnp.asarray(block_of), mine, other, fc_bias, low)


def pack_kernel(rows_v, *refs):
    *parts, out = refs
    at = 0
    for part in parts:
        out[at : at + rows_v] = part[:rows_v].astype(bf16)
        at += rows_v
    down = tree_sum([part[rows_v:] for part in parts])
    for piece in split3(down):
        out[at : at + down.shape[0]] = piece
        at += down.shape[0]


def pack_segments(heads, dp_count, parts):
    rows_v, rows_f = segments_of(heads, dp_count)
    return pl.pallas_call(
        functools.partial(pack_kernel, rows_v),
        in_specs=[VMEM] * len(parts),
        out_specs=VMEM,
        out_shape=jax.ShapeDtypeStruct((len(parts) * rows_v + 3 * rows_f, BS), bf16),
        name="pack_segments",
        **params(1),
    )(*parts)


def rotary_tables(seq_len):
    half = ROT // 2
    frequency = np.float32(10000.0) ** (
        np.float32(-2.0) * np.arange(half, dtype=np.float32) / np.float32(ROT)
    )
    angles = np.arange(seq_len, dtype=np.float32)[:, None] * frequency[None, :].astype(np.float32)
    cosine = np.cos(angles.astype(np.float64)).astype(np.float32)
    sine = np.sin(angles.astype(np.float64)).astype(np.float32)
    wide_cos = np.ones((seq_len, WIDE), np.float32)
    wide_sin = np.zeros((seq_len, WIDE), np.float32)
    wide_cos[:, :half], wide_cos[:, half:ROT] = cosine, cosine
    wide_sin[:, :half], wide_sin[:, half:ROT] = sine, sine
    return wide_cos, wide_sin, np.ascontiguousarray(cosine.T), np.ascontiguousarray(sine.T)


def turned(x):
    half = ROT // 2
    lane = lanes(x.shape)
    return jnp.where(
        lane < half,
        -pltpu.roll(x, WIDE - half, 1),
        jnp.where(lane < ROT, pltpu.roll(x, half, 1), 0.0),
    )


def head_lanes(table, index):
    begin = index // 2 * WIDE
    chunk = table[:, begin : begin + WIDE]
    if index % 2:
        chunk = pltpu.roll(chunk, HD, 1)
    return jnp.where(lanes(chunk.shape) < HD, chunk, 0.0)


def stack_parts(table):
    high, middle, rest = split3(table)
    return jnp.concatenate([high, middle, rest, jnp.zeros_like(high)], axis=0)


def attention_kernel(
    heads, pair, length, token_col, proj, cosine, sine, before, query_o, key_o, weight_o, low_o, hot, key_hot, queries, wide
):
    seq = token_col.shape[0]
    vocab = proj.shape[0]
    lane = lanes((seq, WIDE))
    hot[...] = jnp.where(lane % vocab == token_col[...], 1.0, 0.0).astype(bf16)
    for n in range(2):
        first = (2 * pair + n) * vocab
        key_hot[n] = jnp.where(lane == token_col[...] + first, 1.0, 0.0).astype(bf16)
    one = lanes((vocab, WIDE)) == HD
    ones = (lanes((vocab, WIDE)) > HD) & (lanes((vocab, WIDE)) < HD + 4)
    for which in range(2):
        for n in range(2):
            own = head_lanes(proj, which * heads + 2 * pair + n)
            other = turned(own)
            if which == 0:
                own = jnp.where(one, 1.0, own * 0.125)
                other = other * 0.125
            else:
                own = jnp.where(one | ones, 1.0, own)
            begin = (which * 2 + n) * 2 * WIDE
            wide[:, begin : begin + WIDE] = stack_parts(own)
            wide[:, begin + WIDE : begin + 2 * WIDE] = stack_parts(other)
    for i in range(seq // ROWS):
        span = slice(i * ROWS, (i + 1) * ROWS)
        part = hot[span]
        position = i * ROWS + sublanes((ROWS, WIDE))
        bias = jnp.where(position < length[0], 0.0, MASKED)
        cos, sin = cosine[span], sine[span]
        key_cos = jnp.where(lanes((ROWS, WIDE)) == HD, bias, cos)
        for h in range(2):
            both = dot(part, wide[:, h * 2 * WIDE : (h + 1) * 2 * WIDE])
            queries[h, span] = (both[:, :WIDE] * cos + both[:, WIDE:] * sin).astype(bf16)
            k = 2 + h
            both = dot(part, wide[:, k * 2 * WIDE : (k + 1) * 2 * WIDE])
            key_o[h, span] = (both[:, :WIDE] * key_cos + both[:, WIDE:] * sin).astype(bf16)
    allowed = lanes((ROWS, ROWS)) <= sublanes((ROWS, ROWS))
    small = lanes((ROWS, WIDE))
    halves = []
    for i in range(seq // ROWS):
        span = slice(i * ROWS, (i + 1) * ROWS)
        past = i * ROWS
        weights = before[span] if pair else jnp.zeros((ROWS, WIDE), f32)
        query = [queries[h, span] for h in range(2)]
        near = [dot(query[h], key_o[h, span], NT) for h in range(2)]
        if past:
            far = [dot(query[h], key_o[h, :past], NT) for h in range(2)]
        near = [jnp.where(allowed, x, MASKED) for x in near]
        top = [jnp.max(x, axis=-1, keepdims=True) for x in near]
        if past:
            top = [jnp.maximum(m, jnp.max(x, axis=-1, keepdims=True)) for m, x in zip(top, far)]
            far = [jnp.exp(x - m) for m, x in zip(top, far)]
        near = [jnp.exp(x - m) for m, x in zip(top, near)]
        total = [jnp.sum(x, axis=-1, keepdims=True) for x in near]
        if past:
            total = [a + jnp.sum(x, axis=-1, keepdims=True) for a, x in zip(total, far)]
        share = [1.0 / a for a in total]
        near = [(x * a).astype(bf16) for x, a in zip(near, share)]
        if past:
            far = [(x * a).astype(bf16) for x, a in zip(far, share)]
        for h in range(2):
            weights = weights + dot(near[h], key_hot[h, span])
            if past:
                weights = weights + dot(far[h], key_hot[h, :past])
        for h in range(2):
            minus = -(top[h] + jnp.log(total[h]))
            high = minus.astype(bf16).astype(f32)
            middle = (minus - high).astype(bf16).astype(f32)
            rest = minus - high - middle
            value = jnp.where(small == HD + 3, rest, query[h].astype(f32))
            value = jnp.where(small == HD + 2, middle, value)
            query_o[h, span] = jnp.where(small == HD + 1, high, value).astype(bf16)
        weight_o[span] = weights
        own = weights if pair % 2 == 0 else pltpu.roll(weights, HD, 1)
        own = jnp.where(small < HD, own, 0.0)
        if i < seq // ROWS // 2:
            halves.append(own)
        else:
            k = i - seq // ROWS // 2
            low_o[k * ROWS : (k + 1) * ROWS] = (halves[k] + pltpu.roll(own, HD, 1)).astype(bf16)


def attention(pair, length, token_col, proj, cosine, sine, before, heads):
    seq = token_col.shape[0]
    vocab = proj.shape[0]
    o = jax.ShapeDtypeStruct
    return pl.pallas_call(
        functools.partial(attention_kernel, heads, pair),
        in_specs=[SMEM] + [VMEM] * 5,
        out_specs=[VMEM] * 4,
        out_shape=[
            o((2, seq, WIDE), bf16),
            o((2, seq, WIDE), bf16),
            o((seq, WIDE), f32),
            o((seq // 2, WIDE), bf16),
        ],
        scratch_shapes=[
            pltpu.VMEM((seq, WIDE), bf16),
            pltpu.VMEM((2, seq, WIDE), bf16),
            pltpu.VMEM((2, seq, WIDE), bf16),
            pltpu.VMEM((WIDE, 8 * WIDE), bf16),
        ],
        name="attention",
        **params(6),
    )(length, token_col, proj, cosine, sine, before)


def attention_back_kernel(
    heads,
    pair,
    token_col,
    token_row,
    query,
    key,
    weight,
    weight_grad,
    cosine,
    sine,
    cosine_t,
    sine_t,
    table_o,
    hot,
    mixed,
    query_grad,
    key_grad,
):
    seq = token_col.shape[0]
    vocab = table_o.shape[0]
    half = ROT // 2
    lane = lanes((seq, WIDE))
    hot[...] = jnp.where(
        (lane == token_col[...]) | (lane == token_col[...] + vocab) | ((lane >= HD) & (lane < HD + 3)),
        1.0,
        0.0,
    ).astype(bf16)
    grads = weight_grad[...]
    if heads * vocab < WIDE:
        grads = jnp.concatenate([grads, jnp.zeros((seq, WIDE - heads * vocab), f32)], axis=1)
    both = weight[...] * grads
    for n, h in enumerate((2 * pair, 2 * pair + 1)):
        inside = (lane >= h * vocab) & (lane < (h + 1) * vocab)
        minus = -jnp.sum(jnp.where(inside, both, 0.0), axis=-1, keepdims=True)
        own = grads if h == 0 else pltpu.roll(grads, WIDE - h * vocab, 1)
        own = jnp.where(lane < vocab, own, 0.0)
        high, rest = split2(own)
        m_high = minus.astype(bf16).astype(f32)
        m_middle = (minus - m_high).astype(bf16).astype(f32)
        m_rest = minus - m_high - m_middle
        value = high.astype(f32) + pltpu.roll(rest.astype(f32), vocab, 1)
        value = jnp.where(lane == HD, m_high, value)
        value = jnp.where(lane == HD + 1, m_middle, value)
        value = jnp.where(lane == HD + 2, m_rest, value)
        mixed[n] = value.astype(bf16)
    allowed = lanes((ROWS, ROWS)) <= sublanes((ROWS, ROWS))
    key_grad[...] = jnp.zeros_like(key_grad)
    both = range(2)
    for i in range(seq // ROWS):
        span = slice(i * ROWS, (i + 1) * ROWS)
        past = i * ROWS
        part = [query[n, span] for n in both]
        near = [dot(part[n], key[n, span], NT) for n in both]
        slope = [dot(mixed[n, span], hot[span], NT) for n in both]
        if past:
            far = [dot(part[n], key[n, :past], NT) for n in both]
            far_slope = [dot(mixed[n, span], hot[:past], NT) for n in both]
        near = [jnp.where(allowed, jnp.exp(x), 0.0) for x in near]
        near = [(x * y).astype(bf16) for x, y in zip(near, slope)]
        if past:
            far = [(jnp.exp(x) * y).astype(bf16) for x, y in zip(far, far_slope)]
        grad = [dot(near[n], key[n, span]) for n in both]
        if past:
            grad = [grad[n] + dot(far[n], key[n, :past]) for n in both]
        for n in both:
            key_grad[n, :, span] += dot(part[n], near[n], TN)[:HD]
            if past:
                key_grad[n, :, :past] += dot(part[n], far[n], TN)[:HD]
        for n in both:
            x = grad[n] * 0.125
            query_grad[n, span] = (x * cosine[span] - turned(x) * sine[span]).astype(bf16)
    shape = (vocab, seq)
    token_hot = jnp.where(sublanes(shape) == token_row[...], 1.0, 0.0).astype(bf16)
    small = lanes((vocab, WIDE)) < HD
    cos_t, sin_t = cosine_t[...], sine_t[...]
    one = dot(token_hot, query_grad[0])
    two = pltpu.roll(dot(token_hot, query_grad[1]), HD, 1)
    table_o[:, :WIDE] = jnp.where(small, one, two)
    turned_keys = []
    for n in range(2):
        front, back = key_grad[n, :half], key_grad[n, half:ROT]
        turned_keys += [front * cos_t + back * sin_t, back * cos_t - front * sin_t, key_grad[n, ROT:]]
    keys = jnp.concatenate(turned_keys, axis=0).astype(bf16)
    table_o[:, WIDE:] = dot(token_hot, keys, NT)


def attention_back(
    pair, token_col, token_row, query, key, weight, weight_grad, cosine, sine, cosine_t, sine_t, heads
):
    seq = token_col.shape[0]
    vocab = weight_grad.shape[1] // heads
    full = lambda array: pl.BlockSpec(array.shape, lambda i: (0,) * array.ndim)
    two = full(query)
    return pl.pallas_call(
        functools.partial(attention_back_kernel, heads, pair),
        grid=(1,),
        in_specs=[full(token_col), full(token_row), two, two, full(weight), full(weight_grad)]
        + [full(table) for table in (cosine, sine, cosine_t, sine_t)],
        out_specs=pl.BlockSpec((vocab, 2 * WIDE), lambda i: (0, 0)),
        out_shape=jax.ShapeDtypeStruct((vocab, 2 * WIDE), f32),
        scratch_shapes=[
            pltpu.VMEM((seq, WIDE), bf16),
            pltpu.VMEM((2, seq, WIDE), bf16),
            pltpu.VMEM((2, seq, WIDE), bf16),
            pltpu.VMEM((2, HD, seq), f32),
        ],
        name="attention_back",
        **params(6),
    )(token_col, token_row, query, key, weight, weight_grad, cosine, sine, cosine_t, sine_t)


def loss_kernel(
    parts,
    members,
    heads,
    ints,
    floats,
    token_col,
    target_col,
    token_row,
    embed,
    head,
    vec,
    *refs,
):
    pairs = heads // 2
    weights, refs = refs[: pairs * parts], refs[pairs * parts :]
    pieces, refs = refs[:members], refs[members:]
    keep_o, send_o, grad_o, sums_o, mixing, low_weights, table, down = refs
    step = pl.program_id(0)
    me, length, member = ints[0], ints[1], ints[2]
    vocab = embed.shape[0]
    height = heads * vocab

    @pl.when(step == 0)
    def _():
        rows_v, rows_f = segments_of(heads, members)
        small_v = min(rows_v, HB)
        for r in range(members):
            owner = member ^ r
            piece = pieces[r]
            for place in range(parts):
                for u in range(rows_v // small_v):
                    row = owner * rows_v + u * small_v
                    block, inside = row // HB, row % HB
                    i, k = block // (D // BS), block % (D // BS)
                    at = place * rows_v + u * small_v
                    mixing[
                        me ^ place,
                        pl.ds(pl.multiple_of(i * HB + inside, 32), small_v),
                        pl.ds(pl.multiple_of(k * BS, BS), BS),
                    ] = piece[at : at + small_v]
            at = parts * rows_v
            one, two, three = (
                piece[at + n * rows_f : at + (n + 1) * rows_f].astype(f32) for n in range(3)
            )
            row = owner * rows_f
            down[
                pl.ds(pl.multiple_of(row % vocab, 8), rows_f),
                pl.ds(pl.multiple_of(row // vocab * BS, BS), BS),
            ] = one + (two + three)
        table[...] = stack_parts(embed[...] + (down[...] + vec[2:3]))
        sums_o[...] = jnp.zeros_like(sums_o)

    second = step >= pl.num_programs(0) // 2
    small = lanes((ROWS, WIDE)) < HD

    def weights_of(r):
        value = weights[r][...].astype(f32)
        turned_value = pltpu.roll(value, HD, 1)
        value = jnp.where(second, turned_value, value)
        if pairs == 1:
            return jnp.where(small, value, 0.0)
        other = weights[parts + r][...].astype(f32)
        other = jnp.where(second, other, pltpu.roll(other, HD, 1))
        return jnp.where(small, value, other)

    own = weights_of(0)
    low_weights[me] = own.astype(bf16)[:, :height]
    for r in range(1, parts):
        low_weights[me ^ r] = weights_of(r).astype(bf16)[:, :height]
    token = token_col[...]
    hot = jnp.where(lanes((ROWS, WIDE)) % vocab == token, 1.0, 0.0).astype(bf16)
    x = dot(hot, table[...])
    x = x + dot(
        jnp.concatenate([low_weights[g] for g in range(parts)], axis=1),
        jnp.concatenate([mixing[g] for g in range(parts)], axis=0),
    )
    normed, scale = stats_of(x)
    gain = vec[3:4]
    final = (normed * gain + vec[4:5]).astype(bf16)
    head_low = head[:, :D].astype(bf16)
    square = (vocab, vocab)
    bias_row = jnp.sum(
        jnp.where(lanes(square) == sublanes(square), head[:, D : D + 1], 0.0), axis=0, keepdims=True
    )
    logits = dot(final, head_low, NT) + bias_row
    shifted = logits - jnp.max(logits, axis=-1, keepdims=True)
    log_probs = shifted - jnp.log(jnp.sum(jnp.exp(shifted), axis=-1, keepdims=True))
    target = lanes((ROWS, vocab)) == target_col[...]
    position = step * ROWS + sublanes((ROWS, 1))
    slot_weight = jnp.where(position < length - 1, floats[0], 0.0)
    picked = jnp.sum(jnp.where(target, log_probs, 0.0), axis=-1, keepdims=True)
    loss = -jnp.sum(slot_weight * picked, keepdims=True)
    logit_grad = ((jnp.exp(log_probs) - jnp.where(target, 1.0, 0.0)) * slot_weight).astype(bf16)
    final_grad = dot(logit_grad, head_low)
    grad = norm_back(final_grad, normed, scale, gain)
    high = grad.astype(bf16)
    token_hot = jnp.where(sublanes((vocab, ROWS)) == token_row[...], 1.0, 0.0).astype(bf16)
    both = dot(jnp.concatenate([own.T.astype(bf16), token_hot], axis=0), high)
    sums_o[0:vocab] += both[WIDE:]
    sums_o[vocab : 2 * vocab] += dot(logit_grad, final, TN)
    base = 2 * vocab
    sums_o[base : base + 1] += jnp.sum(final_grad * normed, axis=0, keepdims=True)
    sums_o[base + 1 : base + 2] += jnp.sum(final_grad, axis=0, keepdims=True)
    bias_grad = jnp.sum(logit_grad.astype(f32), axis=0, keepdims=True)
    sums_o[base + 2 : base + 3, :vocab] += bias_grad
    lane = lanes((1, WIDE))
    count = jnp.where((step == 0) & (length >= 2), 1.0, 0.0)
    sums_o[base + 3 : base + 4, :WIDE] += jnp.where(
        lane == 0, loss, jnp.where(lane == 1, count, 0.0)
    )
    sums_o[base + 16 : base + 16 + height] += both[:height]
    grad_o[...] = dot(high, mixing[me], NT)

    @pl.when(step == pl.num_programs(0) - 1)
    def _():
        deal(member & 1, sums_o, keep_o, send_o)


def loss_rows(
    ints,
    floats,
    token_col,
    target_col,
    token_row,
    embedding,
    head,
    vectors,
    weights,
    pieces,
    heads,
):
    seq = token_col.shape[0]
    vocab = embedding.shape[0]
    parts = len(weights) // (heads // 2)
    height = heads * vocab
    blocks = seq // ROWS // 2
    col = pl.BlockSpec((ROWS, 1), lambda i: (i, 0))
    o = jax.ShapeDtypeStruct
    full = lambda array: pl.BlockSpec(array.shape, lambda i: (0,) * array.ndim)
    sums_shape = (2 * vocab + 16 + height, D)
    return pl.pallas_call(
        functools.partial(loss_kernel, parts, len(pieces), heads),
        grid=(seq // ROWS,),
        in_specs=[SMEM, SMEM, col, col, pl.BlockSpec((1, ROWS), lambda i: (0, i))]
        + [full(embedding), full(head), full(vectors)]
        + [pl.BlockSpec((ROWS, WIDE), lambda i: (i % blocks, 0))] * len(weights)
        + [full(pieces[0])] * len(pieces),
        out_specs=[
            pl.BlockSpec((sums_shape[0] // 2, D), lambda i: (0, 0)),
            pl.BlockSpec((sums_shape[0] // 2, D), lambda i: (0, 0)),
            pl.BlockSpec((ROWS, height), lambda i: (i, 0)),
        ],
        out_shape=[o((sums_shape[0] // 2, D), f32)] * 2 + [o((seq, height), f32)],
        scratch_shapes=[
            pltpu.VMEM(sums_shape, f32),
            pltpu.VMEM((parts, height, D), bf16),
            pltpu.VMEM((parts, ROWS, height), bf16),
            pltpu.VMEM((4 * vocab, D), bf16),
            pltpu.VMEM((vocab, D), f32),
        ],
        name="loss_rows",
        **params(12),
    )(
        ints,
        floats,
        token_col,
        target_col,
        token_row,
        embedding,
        head,
        vectors,
        *weights,
        *pieces,
    )


def padded(block):
    lacking = HB - block.shape[0]
    if lacking:
        block = jnp.concatenate([block, jnp.zeros((lacking, block.shape[1]), block.dtype)], axis=0)
    return block


def put_left(ref, index, block):
    ref[index] = jnp.concatenate([padded(block)] * 3, axis=0).astype(bf16)


def put_right(ref, index, block):
    ref[index] = jnp.concatenate(split3(padded(block)), axis=0)


def factors_kernel(
    heads,
    ints,
    owner,
    mine,
    other,
    tiles,
    upper,
    normed,
    act,
    values,
    left_o,
    right_o,
    hidden_o,
    bias_o,
    small_o,
    part_o,
    sums,
    *mats,
):
    vocab = normed.shape[0]
    width = upper.shape[1]
    for index, (which, i, k) in enumerate(tile_places(layer_shapes(heads, width))):
        mats[which][i * BS : (i + 1) * BS, k * BS : (k + 1) * BS] = tiles[owner[index]]
    mat_q, mat_o, mat_u, mat_f = mats
    part_o[...] = mat_q[:, : 2 * heads * HD]
    join(ints[0] & 1, mine, other, sums)
    small_o[...] = sums[: small_o.shape[0]]
    rows = sums[0:vocab]
    mixed = sums[2 * vocab + 16 :]
    act_grad = rows_times_low(rows, mat_f[...], NT)
    u = upper[...]
    tanh = jnp.tanh(GELU_A * (u + GELU_B * (u * u * u)))
    slope = 0.5 * (1.0 + tanh) + 0.5 * u * (1.0 - tanh * tanh) * (
        GELU_A * (1.0 + 3.0 * GELU_B * (u * u))
    )
    upper_grad = act_grad * slope
    bias_grad = jnp.sum(upper_grad, axis=0, keepdims=True)
    bias_o[...] = bias_grad
    value_grad = rows_times_low(mixed, mat_o[...], NT)
    shape = value_grad.shape
    value_grad = jnp.where(sublanes(shape) // vocab == lanes(shape) // HD, value_grad, 0.0)
    value_table = value_grad[:vocab]
    for h in range(1, heads):
        value_table = value_table + value_grad[h * vocab : (h + 1) * vocab]
    hidden_o[0:vocab] = rows_times_low(upper_grad, mat_u[...], NT) + rows_times_low(
        value_table, mat_q[:, 2 * heads * HD :], NT
    )
    low = normed[...].astype(f32)
    own = act[...].astype(f32)
    val = values[...].astype(f32)
    square = (
        jnp.sum(
            dot6(low, low, NT)
            * (dot6(value_table, value_table, NT) + dot6(upper_grad, upper_grad, NT)),
            keepdims=True,
        )
        + jnp.sum(dot6(own, own, NT) * dot6(rows, rows, NT), keepdims=True)
        + jnp.sum(dot6(val, val, NT) * dot6(mixed, mixed, NT), keepdims=True)
        + jnp.sum(bias_grad * bias_grad, keepdims=True)
    )
    hidden_o[vocab : vocab + 16] = jnp.broadcast_to(square, (16, D))
    across = D // BS
    f_rows = width // BS
    pair = 2 * vocab
    for i in range(across):
        put_left(left_o, i, low[:, i * BS : (i + 1) * BS])
    for i in range(f_rows):
        put_left(left_o, across + i, own[:, i * BS : (i + 1) * BS])
    for i in range(heads // 2):
        put_left(
            left_o,
            across + f_rows + i,
            val[i * pair : (i + 1) * pair, i * BS : (i + 1) * BS],
        )
    at = 0
    for k in range(heads * HD // BS):
        put_right(right_o, at, value_table[:, k * BS : (k + 1) * BS])
        at += 1
    for i in range(heads // 2):
        for k in range(across):
            put_right(right_o, at, mixed[i * pair : (i + 1) * pair, k * BS : (k + 1) * BS])
            at += 1
    for k in range(f_rows):
        put_right(right_o, at, upper_grad[:, k * BS : (k + 1) * BS])
        at += 1
    for k in range(across):
        put_right(right_o, at, rows[:, k * BS : (k + 1) * BS])
        at += 1


def rest_kernel(pairs, ints, mine, other, hidden, mat_q, normed, right_o, hidden_o, half_o, table):
    vocab = normed.shape[0]
    join(ints[0] & 1, mine, other, table)
    blocks = [table[p * vocab : (p + 1) * vocab, :WIDE] for p in range(pairs)]
    blocks += [table[p * vocab : (p + 1) * vocab, WIDE:] for p in range(pairs)]
    grad = jnp.concatenate(blocks, axis=1)
    for k, block in enumerate(blocks):
        put_right(right_o, k, block)
    low = normed[...].astype(f32)
    square = jnp.sum(dot6(low, low, NT) * dot6(grad, grad, NT), keepdims=True)
    hidden_o[0:vocab] = hidden[0:vocab] + rows_times_low(grad, mat_q[...], NT)
    hidden_o[vocab:] = hidden[vocab:] + square
    size = half_o.shape[0]
    half_o[...] = hidden_o[pl.ds(pl.multiple_of((ints[0] & 1) * size, size), size)]


def factor_places(heads, ff_local):
    q_cols = 3 * heads * HD // BS
    o_rows = heads // 2
    across = D // BS
    f_rows = ff_local // BS
    left, right = [], []
    for which, i, k in tile_places(layer_shapes(heads, ff_local)):
        if which == 0:
            left.append(i)
            right.append(k)
        elif which == 1:
            left.append(across + f_rows + i)
            right.append(q_cols + i * across + k)
        elif which == 2:
            left.append(i)
            right.append(q_cols + o_rows * across + k)
        else:
            left.append(across + i)
            right.append(q_cols + o_rows * across + f_rows + k)
    return np.array(left, np.int32), np.array(right, np.int32)


def factors(ints, owner, mine, other, tiles, upper, normed, act, values, heads):
    vocab = normed.shape[0]
    ff_local = upper.shape[1]
    n_left = D // BS + ff_local // BS + heads // 2
    n_right = heads * HD // BS + heads // 2 * (D // BS) + ff_local // BS + D // BS
    o = jax.ShapeDtypeStruct
    return pl.pallas_call(
        functools.partial(factors_kernel, heads),
        in_specs=[SMEM] * 2 + [VMEM] * 7,
        out_specs=[VMEM] * 6,
        out_shape=[
            o((n_left, 3 * HB, BS), bf16),
            o((n_right, 3 * HB, BS), bf16),
            o((vocab + 16, D), f32),
            o((1, ff_local), f32),
            o((2 * vocab + 16, D), f32),
            o((D, 2 * heads * HD), bf16),
        ],
        scratch_shapes=[pltpu.VMEM((2 * mine.shape[0], D), f32)]
        + [pltpu.VMEM(shape, bf16) for shape in layer_shapes(heads, ff_local)],
        name="factors",
        **params(7),
    )(ints, owner, mine, other, tiles, upper, normed, act, values)


def factors_rest(ints, mine, other, hidden, mat_q, normed, heads):
    o = jax.ShapeDtypeStruct
    pairs = heads // 2
    return pl.pallas_call(
        functools.partial(rest_kernel, pairs),
        in_specs=[SMEM] + [VMEM] * 5,
        out_specs=[VMEM] * 3,
        out_shape=[
            o((2 * pairs, 3 * HB, BS), bf16),
            o(hidden.shape, f32),
            o((hidden.shape[0] // 2, D), f32),
        ],
        scratch_shapes=[pltpu.VMEM((2 * mine.shape[0], 2 * WIDE), f32)],
        name="factors_rest",
        **params(2),
    )(ints, mine, other, hidden, mat_q, normed)


def small_kernel(parts, corrections, ints, sums, own, *refs):
    mine, others, refs = refs[: parts - 1], refs[parts - 1 : 2 * parts - 2], refs[2 * parts - 2 :]
    bias_grad, refs = refs[0], refs[1:]
    weights, refs = refs[:12], refs[12:]
    outs, scalars, total = refs[:12], refs[12], refs[13]
    vocab = weights[0].shape[0]
    base = 2 * vocab
    size = own.shape[0] // 2
    for place, group in ((ints[0], mine), (1 - ints[0], others)):
        span = pl.ds(pl.multiple_of(place * size, size), size)
        total[span] = tree_sum([own[span]] + [ref[...] for ref in group])
    hidden = total[:vocab]
    square = total[vocab : vocab + 1, 0:1]
    rows = sums[0:vocab]
    normed, scale = stats_of(weights[0][...])
    gain = weights[6][0:1]
    embed_grad = rows + norm_back(hidden, normed, scale, gain)
    vector_grad = jnp.concatenate(
        [
            jnp.sum(hidden * normed, axis=0, keepdims=True),
            jnp.sum(hidden, axis=0, keepdims=True),
            jnp.sum(rows, axis=0, keepdims=True),
            sums[base : base + 1],
            sums[base + 1 : base + 2],
        ],
        axis=0,
    )
    head_grad = sums[vocab : 2 * vocab]
    head_bias = sums[base + 2 : base + 3, :vocab]
    add = lambda value: jnp.sum(value * value, keepdims=True)
    square = square + add(embed_grad) + add(vector_grad) + add(head_grad) + add(head_bias)
    count = sums[base + 3 : base + 4, 1:2]
    loss = sums[base + 3 : base + 4, 0:1] / count
    norm = jnp.sqrt(square) / count
    scale_all = jnp.minimum(1.0, CLIP_NORM / norm) / count
    one, two = corrections[0], corrections[1]

    def update(index, pick, grad):
        weight, first, second = (weights[3 * index + k][pick] for k in range(3))
        grad = grad * scale_all
        first = BETA_ONE * first + (1.0 - BETA_ONE) * grad
        second = BETA_TWO * second + (1.0 - BETA_TWO) * grad * grad
        step = first / one / (jnp.sqrt(second / two) + ADAM_EPS)
        outs[3 * index][pick] = weight - RATE_SMALL * (step + WEIGHT_DECAY * weight)
        outs[3 * index + 1][pick] = first
        outs[3 * index + 2][pick] = second

    everything = slice(None)
    update(0, everything, embed_grad)
    shape = (vocab, vocab)
    head_column = jnp.sum(
        jnp.where(lanes(shape) == sublanes(shape), head_bias, 0.0), axis=1, keepdims=True
    )
    update(1, (everything, slice(0, D)), head_grad)
    update(1, (everything, slice(D, D + 1)), head_column)
    update(2, everything, vector_grad)
    update(3, everything, bias_grad[...])
    lane = lanes((1, WIDE))
    scalars[...] = jnp.where(
        lane == 0, scale_all, jnp.where(lane == 1, loss, jnp.where(lane == 2, norm, 0.0))
    )


def small(corrections, upper, sums, hidden, mine, others, bias_grad, weights):
    o = jax.ShapeDtypeStruct
    return pl.pallas_call(
        functools.partial(small_kernel, 1 + len(mine)),
        in_specs=[SMEM] * 2 + [VMEM] * (2 + 2 * len(mine) + 1 + 12),
        out_specs=[VMEM] * 13,
        out_shape=[o(weight.shape, f32) for weight in weights] + [o((1, WIDE), f32)],
        scratch_shapes=[pltpu.VMEM(hidden.shape, f32)],
        name="small",
        **params(4),
    )(corrections, upper, sums, hidden, *mine, *others, bias_grad, *weights)


QB = 32
UNQ = 6
PER = 6


def take(value, at):
    return jnp.take_along_axis(value, at, axis=1, mode="promise_in_bounds")


def eliminate(packed, count):
    shape = (8, BS)
    lane, sub = lanes(shape), sublanes(shape)
    start = lane // QB * QB
    span = range(count)
    for p in range(QB // 8):
        r0 = 8 * p

        def body(step, carry):
            jj = 2 * step
            j = r0 + jj
            pick, pick_two = start + j, start + (j + 1)
            mark, mark_two = lane == pick, lane == pick_two
            below, below_two = sub > jj, sub > jj + 1
            wide = [jnp.broadcast_to(packed[t, pl.ds(j, 1), :], shape) for t in span]
            next_wide = [jnp.broadcast_to(packed[t, pl.ds(j + 1, 1), :], shape) for t in span]
            kept = [[packed[t, 8 * q : 8 * q + 8, :] for q in range(p, QB // 8)] for t in span]
            pivot = [take(w, pick) for w in wide]
            right = [take(w, pick_two) for w in wide]
            lower = [take(w, pick) for w in next_wide]
            corner = [take(w, pick_two) for w in next_wide]
            ones = [[take(a, pick) for a in group] for group in kept]
            twos = [[take(a, pick_two) for a in group] for group in kept]
            inverse = [1.0 / d for d in pivot]
            ratio = [b * i for b, i in zip(right, inverse)]
            inverse_two = [1.0 / (e - b * r) for e, b, r in zip(corner, lower, ratio)]
            scaled = [jnp.where(mark, 1.0, w) * i for w, i in zip(wide, inverse)]
            scaled_two = [
                jnp.where(mark_two, 1.0, jnp.where(mark, 0.0, w) - b * x) * i
                for w, b, x, i in zip(next_wide, lower, scaled, inverse_two)
            ]
            for t in span:
                for k, q in enumerate(range(p, QB // 8)):
                    a, c, d = kept[t][k], ones[t][k], twos[t][k]
                    d = d - c * ratio[t]
                    first = jnp.where(mark, 0.0, a) - c * scaled[t]
                    if k == 0:
                        first = jnp.where(below, first, a)
                    second = jnp.where(mark_two, 0.0, first) - d * scaled_two[t]
                    if k == 0:
                        second = jnp.where(below_two, second, first)
                    packed[t, 8 * q : 8 * q + 8, :] = second
            return carry

        lax.fori_loop(0, 4, body, 0)


def part_inverse(packed):
    shape = (QB, BS)
    lane, sub = lanes(shape), sublanes(shape)
    part, col = lane // QB, lane % QB
    diagonal = jnp.where(col == sub, packed, 0.0)
    pivot = jnp.ones(shape, f32)
    for k in range(BS // QB):
        own = jnp.sum(jnp.where(part == k, diagonal, 0.0), axis=1, keepdims=True)
        pivot = jnp.where(part == k, own, pivot)
    unit = jnp.where(col < sub, packed, jnp.where(col == sub, 1.0, 0.0))
    return unit * lax.rsqrt(pivot)


def inverse_factors(gram, packed, result, count):
    parts = BS // QB
    unroll = next(k for k in (UNQ, 3, 2, 1) if count % k == 0)
    lane32, sub32 = lanes((QB, BS)), sublanes((QB, BS))
    for b in range(parts):
        begin = b * QB
        below = begin + QB
        rows = slice(begin, below)
        here = lane32 // QB == b

        def pack(i, carry):
            for t in [i * unroll + k for k in range(unroll)]:
                value = jnp.zeros((QB, BS), f32)
                for k in range(parts):
                    block = gram[parts * t + k, rows, :]
                    if k != b:
                        block = pltpu.roll(block, (k * QB + BS - begin) % BS, 1)
                    value = jnp.where(lane32 // QB == k, block, value)
                packed[t] = value
            return carry

        lax.fori_loop(0, count // unroll, pack, 0)
        eliminate(packed, count)

        def spread(i, carry):
            groups = [i * unroll + k for k in range(unroll)]
            inverses = [part_inverse(packed[t]) for t in groups]
            firsts = [
                jnp.concatenate([jnp.where(lane32 // QB == k, x, 0.0) for k in range(parts)], axis=0)
                for x in inverses
            ]
            unit = jnp.where(lane32 - begin == sub32, 1.0, 0.0)
            panels = [
                jnp.concatenate(
                    [jnp.where(here, unit, gram[parts * t + k, rows, :]) for k in range(parts)],
                    axis=0,
                )
                for t in groups
            ]
            news = [dot6(x, y, NN) for x, y in zip(firsts, panels)]
            for t, new in zip(groups, news):
                for k in range(parts):
                    value = new[k * QB : (k + 1) * QB]
                    result[parts * t + k, rows, :] = (
                        jnp.where(lane32 < below, value, 0.0) if below < BS else value
                    )
            if below < BS:
                for t, new in zip(groups, news):
                    mats = [new[k * QB : (k + 1) * QB] for k in range(parts)]
                    changes = [dot6(x, x, TN) for x in mats]
                    shape = (BS - below, BS)
                    mark = lanes(shape) // QB == b
                    for k in range(parts):
                        old = gram[parts * t + k, below:, :]
                        gram[parts * t + k, below:, :] = jnp.where(mark, 0.0, old) - changes[k][below:]
            return carry

        lax.fori_loop(0, count // unroll, spread, 0)


def tile_params(count, per):
    blk = pl.BlockSpec((per, BS, BS), lambda i: (i, 0, 0))
    full = pl.BlockSpec((count, BS, BS), lambda i: (0, 0, 0))
    return blk, full, lambda dt: jax.ShapeDtypeStruct((count, BS, BS), dt)


def gradient_kernel(per, rest, natural, left_at, right_at, lefts, rights, more, L, R, QL, QR, *outs):
    step = pl.program_id(0)
    span = range(per)
    pairs = []
    for s in span:
        tile = natural[step * per + s]
        at = right_at[tile]
        right = jnp.where(
            at < rest, more[jnp.minimum(at, rest - 1)], rights[jnp.maximum(at - rest, 0)]
        )
        pairs.append((lefts[left_at[tile]], right))
    g = [dot(a, b, TN) for a, b in pairs]
    gt = [dot(b, a, TN) for a, b in pairs]
    qt = [QL[s].T for s in span]
    left = [dot3(x, x, NT) for x in g]
    right = [dot3(x, x, NT) for x in gt]
    rot = [dot3(q, x, NN) for q, x in zip(qt, g)]
    mixed_left = [dot3(left[s], QL[s], NN) for s in span]
    mixed_right = [dot3(right[s], QR[s], NN) for s in span]
    rot = [dot3(rot[s], QR[s], NN) for s in span]
    old_left = [dot6(L[s], QL[s], NN) for s in span]
    old_right = [dot6(R[s], QR[s], NN) for s in span]
    for s in span:
        for out, value in zip(
            outs, (left, right, rot, mixed_left, mixed_right, old_left, old_right)
        ):
            out[s] = value[s]


def gradient_products(natural, left_at, right_at, lefts, rights, more, L, R, QL, QR):
    count = QL.shape[0]
    blk, _, o = tile_params(count, PER)
    whole = lambda x: pl.BlockSpec(x.shape, lambda i: (0, 0, 0))
    return pl.pallas_call(
        functools.partial(gradient_kernel, PER, more.shape[0]),
        grid=(count // PER,),
        in_specs=[SMEM] * 3 + [whole(lefts), whole(rights), whole(more)] + [blk] * 4,
        out_specs=[blk] * 7,
        out_shape=[o(f32)] * 7,
        name="gradient_products",
        **params(9),
    )(natural, left_at, right_at, lefts, rights, more, L, R, QL, QR)


def soap_kernel(
    count, per, corrections, scal, GL, GR, GT, BL, BR, AL, AR, W, m, v, L, R, QL, QR,
    W_o, low_o, m_o, v_o, L_o, R_o, QL_o, QR_o, ML_s, MR_s, work, inv_s, packed,
):
    step = pl.program_id(0)
    scale = scal[0:1, 0:1]
    c1, c2 = corrections[0], corrections[1]
    span = range(per)
    share = (1 - BETA_TWO) * (scale * scale)
    xs = []
    for s in span:
        rot = GT[s] * scale
        mn = BETA_ONE * m[s] + (1 - BETA_ONE) * rot
        vn = BETA_TWO * v[s] + (1 - BETA_TWO) * rot * rot
        m_o[s] = mn
        v_o[s] = vn
        xs.append((mn / c1) / (jnp.sqrt(vn / c2) + ADAM_EPS))
    ML = [BETA_TWO * AL[s] + share * BL[s] for s in span]
    MR = [BETA_TWO * AR[s] + share * BR[s] for s in span]
    back = [dot3(QL[s], xs[s], NN) for s in span]
    ML = [x * lax.rsqrt(jnp.sum(x * x, keepdims=True)) for x in ML]
    MR = [x * lax.rsqrt(jnp.sum(x * x, keepdims=True)) for x in MR]
    back = [dot3(back[s], QR[s], NT) for s in span]
    gram_left = [dot6(x, x, TN) for x in ML]
    gram_right = [dot6(x, x, TN) for x in MR]
    for s in span:
        L_o[s] = BETA_TWO * L[s] + share * GL[s]
        R_o[s] = BETA_TWO * R[s] + share * GR[s]
        w = W[s]
        wn = w - RATE_TILES * (back[s] + WEIGHT_DECAY * w)
        W_o[s] = wn
        low_o[s] = wn.astype(bf16)
        t = step * per + s
        ML_s[t] = ML[s]
        MR_s[t] = MR[s]
        work[2 * t] = gram_left[s]
        work[2 * t + 1] = gram_right[s]

    @pl.when(step == pl.num_programs(0) - 1)
    def _():
        inverse_factors(work, packed, inv_s, count // 2)
        unroll = next(k for k in (8, 6, 3, 1) if count % k == 0)

        def last(i, carry):
            ts = [i * unroll + k for k in range(unroll)]
            ol = [dot3(ML_s[t], inv_s[2 * t], NT) for t in ts]
            orr = [dot3(MR_s[t], inv_s[2 * t + 1], NT) for t in ts]
            for t, a, b in zip(ts, ol, orr):
                QL_o[t] = a
                QR_o[t] = b
            return carry

        lax.fori_loop(0, count // unroll, last, 0)


def soap(corrections, scal, products, W, m, v, L, R, QL, QR):
    count = W.shape[0]
    blk, full, o = tile_params(count, PER)
    return pl.pallas_call(
        functools.partial(soap_kernel, count, PER),
        grid=(count // PER,),
        in_specs=[SMEM, pl.BlockSpec((1, WIDE), lambda i: (0, 0))] + [blk] * 14,
        out_specs=[blk] * 6 + [full] * 2,
        out_shape=[o(f32), o(bf16), o(f32), o(f32), o(f32), o(f32), o(f32), o(f32)],
        scratch_shapes=[pltpu.VMEM((count, BS, BS), f32)] * 2
        + [pltpu.VMEM((2 * count, BS, BS), f32)] * 2
        + [pltpu.VMEM((count // 2, QB, BS), f32)],
        name="soap_tiles",
        **params(40, 36),
    )(corrections, scal, *products, W, m, v, L, R, QL, QR)


def local(
    tokens,
    lengths,
    tile_owner,
    step_count,
    weight_tiles,
    tiles_first,
    tiles_second,
    stats_left,
    stats_right,
    basis_left,
    basis_right,
    embedding,
    embedding_first,
    embedding_second,
    head_table,
    head_first,
    head_second,
    vectors,
    vectors_first,
    vectors_second,
    fc_bias,
    fc_bias_first,
    fc_bias_second,
):
    seq = tokens.shape[1]
    mp_count = lax.axis_size("mp")
    dp_count = lax.axis_size("dp")
    dp_index = lax.axis_index("dp")
    mp_index = lax.axis_index("mp")
    upper_pair = dp_index & 1
    heads = H // mp_count
    ff_local = fc_bias.shape[1]
    count = weight_tiles.shape[0]
    vocab = embedding.shape[0]
    own_index = dp_index[None]

    natural, low_tiles, normed, keep, send = first_tables(
        tile_owner, own_index, weight_tiles, embedding, vectors, heads, ff_local
    )
    token_col = tokens.reshape(seq, 1)
    target_col = jnp.roll(tokens, -1, axis=1).reshape(seq, 1)
    keep = keep + swap_with(send, "dp", 1)
    mine = direct(keep)
    low_tiles, mine = lax.optimization_barrier((low_tiles, mine))
    gathered = lax.all_gather(low_tiles, "dp", axis=0, tiled=True)
    proj, upper, act, values, keep, send = second_tables(
        natural, own_index, mine, swap_with(mine, "dp", 1), fc_bias, low_tiles, vocab, heads, dp_count
    )
    cosine, sine, cosine_t, sine_t = rotary_tables(seq)
    segment = sum(segments_of(heads, dp_count))
    places = range(1, dp_count // 2)
    received = [swap_with(send, "dp", 1)]
    queries, keys = [], []
    weight = jnp.zeros((8, WIDE), f32)
    for pair in range(heads // 2):
        query, key, weight, weight_low = attention(
            pair, lengths, token_col, proj, cosine, sine, weight, heads
        )
        queries.append(query)
        keys.append(key)
        if pair == 0:
            received, weight, weight_low = lax.optimization_barrier((received, weight, weight_low))
            keep = keep + received[0]
            received = [
                swap_with(keep[q * segment : (q + 1) * segment], "dp", 2 * q) for q in places
            ]
            keep, weight = lax.optimization_barrier((keep, weight))
            weights = gather_xor(weight_low, "mp")
    if heads > 2:
        more = gather_xor(weight_low, "mp")
        received, weights, more[0] = lax.optimization_barrier((received, weights, more[0]))
    mine = tree_sum([keep[:segment]] + list(received))
    packed = pack_segments(heads, dp_count, gather_xor(mine, "mp"))
    even = [packed] + [swap_with(packed, "dp", 2 * q) for q in places]
    if heads > 2:
        weights = weights + more
    odd = [swap_with(piece, "dp", 1) for piece in even]
    pieces = [piece for two in zip(even, odd) for piece in two]
    length = lengths[0]
    inverse_length = 1.0 / jnp.maximum(length - 1, 1).astype(f32)
    keep, send, weight_grad = loss_rows(
        jnp.stack([mp_index, length, dp_index]),
        inverse_length[None],
        token_col,
        target_col,
        tokens,
        embedding,
        head_table.T,
        vectors,
        weights,
        pieces,
        heads,
    )
    keep = keep + swap_with(send, "dp", 1)
    tables_back = []
    for pair in range(heads // 2):
        if pair == 1:
            weight_grad, keep = lax.optimization_barrier((weight_grad, keep))
        tables_back.append(
            attention_back(
                pair,
                token_col,
                tokens,
                queries[pair],
                keys[pair],
                weight,
                weight_grad,
                cosine,
                sine,
                cosine_t,
                sine_t,
                heads,
            )
        )
    mine = butterfly(keep)
    table = jnp.concatenate(tables_back, axis=0)
    half = table.shape[0] // 2
    first, second = table[:half], table[half:]
    is_upper = upper_pair == 1
    table = jnp.where(is_upper, second, first) + swap_with(
        jnp.where(is_upper, first, second), "dp", 1
    )
    table = direct(table)
    left, right, hidden, bias_grad, sums, mat_part = factors(
        own_index, tile_owner, mine, swap_with(mine, "dp", 1), gathered, upper, normed, act, values, heads
    )
    more, hidden, hidden_half = factors_rest(
        own_index, table, swap_with(table, "dp", 1), hidden, mat_part, normed, heads
    )
    hidden_parts = gather_halves(hidden_half)
    left_at, right_at = (jnp.asarray(places) for places in factor_places(heads, ff_local))
    gradients = gradient_products(
        natural, left_at, right_at, left, right, more, stats_left, stats_right, basis_left, basis_right
    )
    hidden_parts, gradients = lax.optimization_barrier((hidden_parts, gradients))
    hidden_others = swap_pair(hidden_parts)
    corrections = 1.0 - jnp.power(
        jnp.array([BETA_ONE, BETA_TWO], f32), step_count.astype(f32)
    )
    small_weights = (
        embedding,
        embedding_first,
        embedding_second,
        head_table.T,
        head_first.T,
        head_second.T,
        vectors,
        vectors_first,
        vectors_second,
        fc_bias,
        fc_bias_first,
        fc_bias_second,
    )
    *small_out, scalars = small(
        corrections,
        upper_pair[None],
        sums,
        hidden,
        hidden_parts,
        hidden_others,
        bias_grad,
        small_weights,
    )
    small_out[3:6] = [value.T for value in small_out[3:6]]
    results = soap(
        corrections,
        scalars,
        gradients,
        weight_tiles,
        tiles_first,
        tiles_second,
        stats_left,
        stats_right,
        basis_left,
        basis_right,
    )
    return (scalars[0, 1], scalars[0, 2], *results, *small_out)


def solution(mesh):
    tiled = P("dp", None, "mp")
    split = P(None, "mp")
    in_specs = (P("dp", None), P("dp"), P(), P(), *[tiled] * 7, *[P()] * 9, *[split] * 3)
    out_specs = (P(), P(), *[tiled] * 8, *[P()] * 9, *[split] * 3)
    return jax.shard_map(local, mesh=mesh, in_specs=in_specs, out_specs=out_specs, check_vma=False)
```

```python
import functools
import math

import jax
import jax.numpy as jnp
import numpy as np
from jax import lax
from jax.experimental import pallas as pl
from jax.experimental.pallas import tpu as pltpu
from jax.sharding import PartitionSpec as P

D = 1024
H = 16
HD = 64
ROT = 32
BS = 128
HB = 64
ROWS = 256
WIDE = 128
MEGA = 1024 * 1024

NORM_EPS = 1e-05
CLIP_NORM = 0.02
RATE_TILES = 0.02
RATE_SMALL = 0.2
BETA_ONE = 0.9
BETA_TWO = 0.95
ADAM_EPS = 1e-08
WEIGHT_DECAY = 0.01
MASKED = -1e30
GELU_A = math.sqrt(2.0 / math.pi)
GELU_B = 0.044715

NN = (((1,), (0,)), ((), ()))
NT = (((1,), (1,)), ((), ()))
TN = (((0,), (0,)), ((), ()))
f32 = jnp.float32
bf16 = jnp.bfloat16
SMEM = pl.BlockSpec(memory_space=pltpu.SMEM)
VMEM = pl.BlockSpec(memory_space=pltpu.VMEM)
ANY = pl.BlockSpec(memory_space=pl.ANY)


def dot(a, b, dims=NN):
    return lax.dot_general(a, b, dims, preferred_element_type=f32)


def split2(a):
    high = a.astype(bf16)
    return high, (a - high.astype(f32)).astype(bf16)


def split3(a):
    high = a.astype(bf16)
    rest = a - high.astype(f32)
    middle = rest.astype(bf16)
    return high, middle, (rest - middle.astype(f32)).astype(bf16)


def dot3(a, b, dims):
    (axis_a,), (axis_b,) = dims[0]
    ah, al = split2(a)
    bh, bl = split2(b)
    return dot(
        jnp.concatenate([ah, ah, al], axis=axis_a),
        jnp.concatenate([bh, bl, bh], axis=axis_b),
        dims,
    )


def dot6(a, b, dims):
    (axis_a,), (axis_b,) = dims[0]
    ah, am, al = split3(a)
    bh, bm, bl = split3(b)
    return dot(
        jnp.concatenate([ah, ah, am, am, ah, al], axis=axis_a),
        jnp.concatenate([bh, bm, bh, bm, bl, bh], axis=axis_b),
        dims,
    )


def rows_times_low(a, low, dims):
    count = a.shape[0]
    parts = dot(jnp.concatenate(split3(a), axis=0), low, dims)
    return parts[:count] + (parts[count : 2 * count] + parts[2 * count :])


def lanes(shape):
    return lax.broadcasted_iota(jnp.int32, shape, len(shape) - 1)


def sublanes(shape):
    return lax.broadcasted_iota(jnp.int32, shape, len(shape) - 2)


def stats_of(values):
    centred = values - jnp.mean(values, axis=-1, keepdims=True)
    spread = jnp.mean(centred * centred, axis=-1, keepdims=True)
    scale = lax.rsqrt(spread + NORM_EPS)
    return centred * scale, scale


def norm_back(grad, normed, scale, gain):
    inner = grad * gain
    mean_one = jnp.mean(inner, axis=-1, keepdims=True)
    mean_two = jnp.mean(inner * normed, axis=-1, keepdims=True)
    return scale * (inner - mean_one - normed * mean_two)


def params(microseconds, megabytes=20):
    return dict(
        compiler_params=pltpu.CompilerParams(vmem_limit_bytes=megabytes * MEGA),
        cost_estimate=pl.CostEstimate(
            flops=int(microseconds * 1.1e9), bytes_accessed=int(microseconds * 1e6), transcendentals=0
        ),
    )


def swap_with(value, axis, mask):
    count = lax.axis_size(axis)
    return lax.ppermute(value, axis, [(i, i ^ mask) for i in range(count)])


def tree_sum(parts):
    while len(parts) > 1:
        parts = [parts[i] + parts[i + 1] for i in range(0, len(parts), 2)]
    return parts[0]


def gather_xor(value, axis):
    return [value] + [swap_with(value, axis, r) for r in range(1, lax.axis_size(axis))]


def gather_halves(mine):
    return [swap_with(mine, "mp", r) for r in range(1, lax.axis_size("mp"))]


def swap_pair(parts):
    return [swap_with(part, "dp", 1) for part in parts]


def butterfly(kept):
    bits = [1 << k for k in range(1, lax.axis_size("dp").bit_length() - 1)]
    half = (kept.shape[0] // 2 + 7) // 8 * 8
    pieces = [kept[:half], kept[half:]]
    for k in range(len(bits)):
        received = [
            swap_with(piece, "dp", order[k])
            for piece, order in zip(pieces, (bits, bits[1:] + bits[:1]))
        ]
        pieces = [piece + other for piece, other in zip(pieces, received)]
    return jnp.concatenate(pieces, axis=0)


def direct(kept):
    return tree_sum([kept] + [swap_with(kept, "dp", r) for r in range(2, lax.axis_size("dp"), 2)])


def deal(upper, value, keep_o, send_o):
    half = keep_o.shape[0]

    @pl.when(upper == 0)
    def _():
        keep_o[...] = value[:half]
        send_o[...] = value[half : 2 * half]

    @pl.when(upper == 1)
    def _():
        keep_o[...] = value[half : 2 * half]
        send_o[...] = value[:half]


def join(upper, mine, other, whole):
    half = mine.shape[0]

    @pl.when(upper == 0)
    def _():
        whole[:half] = mine[...]
        whole[half:] = other[...]

    @pl.when(upper == 1)
    def _():
        whole[:half] = other[...]
        whole[half:] = mine[...]


def layer_shapes(heads_local, ff_local):
    return ((D, 3 * heads_local * HD), (heads_local * HD, D), (D, ff_local), (ff_local, D))


def tile_places(shapes):
    places = []
    for which, (row_total, col_total) in enumerate(shapes):
        for i in range(row_total // BS):
            for k in range(col_total // BS):
                places.append((which, i, k))
    return places


def first_places(heads, ff_local):
    q_cols = 3 * heads * HD // BS
    rows, blocks = [], []
    for which, i, k in tile_places(layer_shapes(heads, ff_local)):
        used = which in (0, 2)
        rows.append(i if used else 0)
        blocks.append(k if which == 0 else q_cols + k if which == 2 else q_cols + ff_local // BS)
    return np.array(rows, np.int32), np.array(blocks, np.int32)


def first_kernel(owner, ints, row_of, block_of, tiles, embed, vec, natural_o, low_o, normed_o, keep_o, send_o, rows, acc):
    count = tiles.shape[0]
    begin = ints[0] * count

    def find(b, carry):
        slot = owner[b] - begin

        @pl.when((slot >= 0) & (slot < count))
        def _():
            natural_o[slot] = b

        return carry

    lax.fori_loop(0, owner.shape[0], find, 0)
    normed, _ = stats_of(embed[...])
    low = (normed * vec[0:1] + vec[1:2]).astype(bf16)
    normed_o[...] = low
    for i in range(D // BS):
        rows[i] = low[:, i * BS : (i + 1) * BS]
    acc[...] = jnp.zeros_like(acc)
    for s in range(count):
        low_o[s] = tiles[s].astype(bf16)
    products = [dot(rows[row_of[natural_o[s]]], low_o[s]) for s in range(count)]
    for s in range(count):
        acc[block_of[natural_o[s]]] += products[s]
    half = keep_o.shape[0]
    for upper, first, second in ((0, keep_o, send_o), (1, send_o, keep_o)):

        @pl.when((ints[0] & 1) == upper)
        def _():
            first[...] = acc[:half]
            second[...] = acc[half : 2 * half]


def first_tables(owner, ints, tiles, embedding, vectors, heads, ff_local):
    vocab = embedding.shape[0]
    row_of, block_of = first_places(heads, ff_local)
    blocks = int(block_of.max())
    o = jax.ShapeDtypeStruct
    return pl.pallas_call(
        first_kernel,
        in_specs=[SMEM] * 4 + [VMEM] * 3,
        out_specs=[SMEM] + [VMEM] * 4,
        out_shape=[
            o((tiles.shape[0],), jnp.int32),
            o(tiles.shape, bf16),
            o((vocab, D), bf16),
            o(((blocks + 1) // 2, vocab, BS), f32),
            o(((blocks + 1) // 2, vocab, BS), f32),
        ],
        scratch_shapes=[
            pltpu.VMEM((D // BS, vocab, BS), bf16),
            pltpu.VMEM((blocks + 1, vocab, BS), f32),
        ],
        name="first_tables",
        **params(4, 56),
    )(owner, ints, jnp.asarray(row_of), jnp.asarray(block_of), tiles, embedding, vectors)


def second_places(heads, ff_local):
    pairs, across = heads // 2, D // BS
    lefts, blocks = [], []
    for which, i, k in tile_places(layer_shapes(heads, ff_local)):
        lefts.append(i if which == 1 else pairs + i if which == 3 else 0)
        blocks.append(
            i * across + k if which == 1 else (pairs * across + k if which == 3 else pairs * across + across)
        )
    return np.array(lefts, np.int32), np.array(blocks, np.int32)


def segments_of(heads, dp_count):
    return heads // 2 * (D // BS) * HB // dp_count, 32 * (D // BS) // dp_count


def second_kernel(
    heads, dp_count, natural, ints, left_of, block_of, mine, other, bias, low,
    proj_o, upper_o, act_o, values_o, keep_o, send_o, total, lefts, acc,
):
    vocab = proj_o.shape[0]
    me = ints[0]
    count = low.shape[0]
    pairs = heads // 2
    q_cols = 3 * heads * HD // BS
    f_rows = upper_o.shape[1] // BS
    across = D // BS
    join(me & 1, mine, other, total)
    for j in range(q_cols):
        proj_o[:, j * BS : (j + 1) * BS] = total[j]
    upper = jnp.concatenate([total[q_cols + j] for j in range(f_rows)], axis=1)
    upper = upper + bias[...]
    upper_o[...] = upper
    act = 0.5 * upper * (1.0 + jnp.tanh(GELU_A * (upper + GELU_B * (upper * upper * upper))))
    act = act.astype(bf16).astype(f32)
    act_o[...] = act.astype(bf16)
    values = proj_o[:, 2 * heads * HD :]
    shape = (heads * vocab, heads * HD)
    values = jnp.concatenate([values] * heads, axis=0)
    values = jnp.where(sublanes(shape) // vocab == lanes(shape) // HD, values, 0.0)
    values_o[...] = values.astype(bf16)
    for i in range(pairs):
        lefts[i] = values[i * HB : (i + 1) * HB, i * BS : (i + 1) * BS].astype(bf16)
    for i in range(f_rows):
        lefts[pairs + i] = padded(act[:, i * BS : (i + 1) * BS]).astype(bf16)
    acc[...] = jnp.zeros_like(acc)
    products = [dot(lefts[left_of[natural[s]]], low[s]) for s in range(count)]
    for s in range(count):
        rows = pl.ds(pl.multiple_of(block_of[natural[s]] * HB, HB), HB)
        acc[rows] += products[s]
    rows_v, rows_f = segments_of(heads, dp_count)
    base = pairs * across * HB
    for odd, first, second in ((0, keep_o, send_o), (1, send_o, keep_o)):

        @pl.when((me & 1) == odd)
        def _():
            for e in range(dp_count):
                out = second if e & 1 else first
                start = pl.multiple_of(((me ^ e) >> 1) * (rows_v + rows_f), 8)
                out[pl.ds(start, rows_v)] = acc[e * rows_v : (e + 1) * rows_v]
                k, inside = e * rows_f // vocab, e * rows_f % vocab
                at = base + k * HB + inside
                out[pl.ds(pl.multiple_of(start + rows_v, 8), rows_f)] = acc[at : at + rows_f]


def second_tables(natural, ints, mine, other, fc_bias, low, vocab, heads, dp_count):
    ff_local = fc_bias.shape[1]
    left_of, block_of = second_places(heads, ff_local)
    o = jax.ShapeDtypeStruct
    return pl.pallas_call(
        functools.partial(second_kernel, heads, dp_count),
        in_specs=[SMEM] * 4 + [VMEM] * 4,
        out_specs=[VMEM] * 6,
        out_shape=[
            o((vocab, 3 * heads * HD), f32),
            o((vocab, ff_local), f32),
            o((vocab, ff_local), bf16),
            o((heads * vocab, heads * HD), bf16),
            o((dp_count // 2 * sum(segments_of(heads, dp_count)), BS), f32),
            o((dp_count // 2 * sum(segments_of(heads, dp_count)), BS), f32),
        ],
        scratch_shapes=[
            pltpu.VMEM((2 * mine.shape[0],) + mine.shape[1:], f32),
            pltpu.VMEM((heads // 2 + ff_local // BS, HB, BS), bf16),
            pltpu.VMEM(((int(block_of.max()) + 1) * HB, BS), f32),
        ],
        name="second_tables",
        **params(4),
    )(natural, ints, jnp.asarray(left_of), jnp.asarray(block_of), mine, other, fc_bias, low)


def pack_kernel(rows_v, *refs):
    *parts, out = refs
    at = 0
    for part in parts:
        out[at : at + rows_v] = part[:rows_v].astype(bf16)
        at += rows_v
    down = tree_sum([part[rows_v:] for part in parts])
    for piece in split3(down):
        out[at : at + down.shape[0]] = piece
        at += down.shape[0]


def pack_segments(heads, dp_count, parts):
    rows_v, rows_f = segments_of(heads, dp_count)
    return pl.pallas_call(
        functools.partial(pack_kernel, rows_v),
        in_specs=[VMEM] * len(parts),
        out_specs=VMEM,
        out_shape=jax.ShapeDtypeStruct((len(parts) * rows_v + 3 * rows_f, BS), bf16),
        name="pack_segments",
        **params(1),
    )(*parts)


def rotary_tables(seq_len):
    half = ROT // 2
    frequency = np.float32(10000.0) ** (
        np.float32(-2.0) * np.arange(half, dtype=np.float32) / np.float32(ROT)
    )
    angles = np.arange(seq_len, dtype=np.float32)[:, None] * frequency[None, :].astype(np.float32)
    cosine = np.cos(angles.astype(np.float64)).astype(np.float32)
    sine = np.sin(angles.astype(np.float64)).astype(np.float32)
    wide_cos = np.ones((seq_len, WIDE), np.float32)
    wide_sin = np.zeros((seq_len, WIDE), np.float32)
    wide_cos[:, :half], wide_cos[:, half:ROT] = cosine, cosine
    wide_sin[:, :half], wide_sin[:, half:ROT] = sine, sine
    return wide_cos, wide_sin, np.ascontiguousarray(cosine.T), np.ascontiguousarray(sine.T)


def turned(x):
    half = ROT // 2
    lane = lanes(x.shape)
    return jnp.where(
        lane < half,
        -pltpu.roll(x, WIDE - half, 1),
        jnp.where(lane < ROT, pltpu.roll(x, half, 1), 0.0),
    )


def head_lanes(table, index):
    begin = index // 2 * WIDE
    chunk = table[:, begin : begin + WIDE]
    if index % 2:
        chunk = pltpu.roll(chunk, HD, 1)
    return jnp.where(lanes(chunk.shape) < HD, chunk, 0.0)


def stack_parts(table):
    high, middle, rest = split3(table)
    return jnp.concatenate([high, middle, rest, jnp.zeros_like(high)], axis=0)


def attention_kernel(
    heads, pair, length, token_col, proj, cosine, sine, before, query_o, key_o, weight_o, low_o, hot, key_hot, queries, wide
):
    seq = token_col.shape[0]
    vocab = proj.shape[0]
    lane = lanes((seq, WIDE))
    hot[...] = jnp.where(lane % vocab == token_col[...], 1.0, 0.0).astype(bf16)
    for n in range(2):
        first = (2 * pair + n) * vocab
        key_hot[n] = jnp.where(lane == token_col[...] + first, 1.0, 0.0).astype(bf16)
    one = lanes((vocab, WIDE)) == HD
    ones = (lanes((vocab, WIDE)) > HD) & (lanes((vocab, WIDE)) < HD + 4)
    for which in range(2):
        for n in range(2):
            own = head_lanes(proj, which * heads + 2 * pair + n)
            other = turned(own)
            if which == 0:
                own = jnp.where(one, 1.0, own * 0.125)
                other = other * 0.125
            else:
                own = jnp.where(one | ones, 1.0, own)
            begin = (which * 2 + n) * 2 * WIDE
            wide[:, begin : begin + WIDE] = stack_parts(own)
            wide[:, begin + WIDE : begin + 2 * WIDE] = stack_parts(other)
    for i in range(seq // ROWS):
        span = slice(i * ROWS, (i + 1) * ROWS)
        part = hot[span]
        position = i * ROWS + sublanes((ROWS, WIDE))
        bias = jnp.where(position < length[0], 0.0, MASKED)
        cos, sin = cosine[span], sine[span]
        key_cos = jnp.where(lanes((ROWS, WIDE)) == HD, bias, cos)
        for h in range(2):
            both = dot(part, wide[:, h * 2 * WIDE : (h + 1) * 2 * WIDE])
            queries[h, span] = (both[:, :WIDE] * cos + both[:, WIDE:] * sin).astype(bf16)
            k = 2 + h
            both = dot(part, wide[:, k * 2 * WIDE : (k + 1) * 2 * WIDE])
            key_o[h, span] = (both[:, :WIDE] * key_cos + both[:, WIDE:] * sin).astype(bf16)
    allowed = lanes((ROWS, ROWS)) <= sublanes((ROWS, ROWS))
    small = lanes((ROWS, WIDE))
    halves = []
    for i in range(seq // ROWS):
        span = slice(i * ROWS, (i + 1) * ROWS)
        past = i * ROWS
        weights = before[span] if pair else jnp.zeros((ROWS, WIDE), f32)
        query = [queries[h, span] for h in range(2)]
        near = [dot(query[h], key_o[h, span], NT) for h in range(2)]
        if past:
            far = [dot(query[h], key_o[h, :past], NT) for h in range(2)]
        near = [jnp.where(allowed, x, MASKED) for x in near]
        top = [jnp.max(x, axis=-1, keepdims=True) for x in near]
        if past:
            top = [jnp.maximum(m, jnp.max(x, axis=-1, keepdims=True)) for m, x in zip(top, far)]
            far = [jnp.exp(x - m) for m, x in zip(top, far)]
        near = [jnp.exp(x - m) for m, x in zip(top, near)]
        total = [jnp.sum(x, axis=-1, keepdims=True) for x in near]
        if past:
            total = [a + jnp.sum(x, axis=-1, keepdims=True) for a, x in zip(total, far)]
        share = [1.0 / a for a in total]
        near = [(x * a).astype(bf16) for x, a in zip(near, share)]
        if past:
            far = [(x * a).astype(bf16) for x, a in zip(far, share)]
        for h in range(2):
            weights = weights + dot(near[h], key_hot[h, span])
            if past:
                weights = weights + dot(far[h], key_hot[h, :past])
        for h in range(2):
            minus = -(top[h] + jnp.log(total[h]))
            high = minus.astype(bf16).astype(f32)
            middle = (minus - high).astype(bf16).astype(f32)
            rest = minus - high - middle
            value = jnp.where(small == HD + 3, rest, query[h].astype(f32))
            value = jnp.where(small == HD + 2, middle, value)
            query_o[h, span] = jnp.where(small == HD + 1, high, value).astype(bf16)
        weight_o[span] = weights
        own = weights if pair % 2 == 0 else pltpu.roll(weights, HD, 1)
        own = jnp.where(small < HD, own, 0.0)
        if i < seq // ROWS // 2:
            halves.append(own)
        else:
            k = i - seq // ROWS // 2
            low_o[k * ROWS : (k + 1) * ROWS] = (halves[k] + pltpu.roll(own, HD, 1)).astype(bf16)


def attention(pair, length, token_col, proj, cosine, sine, before, heads):
    seq = token_col.shape[0]
    vocab = proj.shape[0]
    o = jax.ShapeDtypeStruct
    return pl.pallas_call(
        functools.partial(attention_kernel, heads, pair),
        in_specs=[SMEM] + [VMEM] * 5,
        out_specs=[VMEM] * 4,
        out_shape=[
            o((2, seq, WIDE), bf16),
            o((2, seq, WIDE), bf16),
            o((seq, WIDE), f32),
            o((seq // 2, WIDE), bf16),
        ],
        scratch_shapes=[
            pltpu.VMEM((seq, WIDE), bf16),
            pltpu.VMEM((2, seq, WIDE), bf16),
            pltpu.VMEM((2, seq, WIDE), bf16),
            pltpu.VMEM((WIDE, 8 * WIDE), bf16),
        ],
        name="attention",
        **params(6),
    )(length, token_col, proj, cosine, sine, before)


def attention_back_kernel(
    heads,
    pair,
    token_col,
    token_row,
    query,
    key,
    weight,
    weight_grad,
    cosine,
    sine,
    cosine_t,
    sine_t,
    table_o,
    hot,
    mixed,
    query_grad,
    key_grad,
):
    seq = token_col.shape[0]
    vocab = table_o.shape[0]
    half = ROT // 2
    lane = lanes((seq, WIDE))
    hot[...] = jnp.where(
        (lane == token_col[...]) | (lane == token_col[...] + vocab) | ((lane >= HD) & (lane < HD + 3)),
        1.0,
        0.0,
    ).astype(bf16)
    grads = weight_grad[...]
    if heads * vocab < WIDE:
        grads = jnp.concatenate([grads, jnp.zeros((seq, WIDE - heads * vocab), f32)], axis=1)
    both = weight[...] * grads
    for n, h in enumerate((2 * pair, 2 * pair + 1)):
        inside = (lane >= h * vocab) & (lane < (h + 1) * vocab)
        minus = -jnp.sum(jnp.where(inside, both, 0.0), axis=-1, keepdims=True)
        own = grads if h == 0 else pltpu.roll(grads, WIDE - h * vocab, 1)
        own = jnp.where(lane < vocab, own, 0.0)
        high, rest = split2(own)
        m_high = minus.astype(bf16).astype(f32)
        m_middle = (minus - m_high).astype(bf16).astype(f32)
        m_rest = minus - m_high - m_middle
        value = high.astype(f32) + pltpu.roll(rest.astype(f32), vocab, 1)
        value = jnp.where(lane == HD, m_high, value)
        value = jnp.where(lane == HD + 1, m_middle, value)
        value = jnp.where(lane == HD + 2, m_rest, value)
        mixed[n] = value.astype(bf16)
    allowed = lanes((ROWS, ROWS)) <= sublanes((ROWS, ROWS))
    key_grad[...] = jnp.zeros_like(key_grad)
    both = range(2)
    for i in range(seq // ROWS):
        span = slice(i * ROWS, (i + 1) * ROWS)
        past = i * ROWS
        part = [query[n, span] for n in both]
        near = [dot(part[n], key[n, span], NT) for n in both]
        slope = [dot(mixed[n, span], hot[span], NT) for n in both]
        if past:
            far = [dot(part[n], key[n, :past], NT) for n in both]
            far_slope = [dot(mixed[n, span], hot[:past], NT) for n in both]
        near = [jnp.where(allowed, jnp.exp(x), 0.0) for x in near]
        near = [(x * y).astype(bf16) for x, y in zip(near, slope)]
        if past:
            far = [(jnp.exp(x) * y).astype(bf16) for x, y in zip(far, far_slope)]
        grad = [dot(near[n], key[n, span]) for n in both]
        if past:
            grad = [grad[n] + dot(far[n], key[n, :past]) for n in both]
        for n in both:
            key_grad[n, :, span] += dot(part[n], near[n], TN)[:HD]
            if past:
                key_grad[n, :, :past] += dot(part[n], far[n], TN)[:HD]
        for n in both:
            x = grad[n] * 0.125
            query_grad[n, span] = (x * cosine[span] - turned(x) * sine[span]).astype(bf16)
    shape = (vocab, seq)
    token_hot = jnp.where(sublanes(shape) == token_row[...], 1.0, 0.0).astype(bf16)
    small = lanes((vocab, WIDE)) < HD
    cos_t, sin_t = cosine_t[...], sine_t[...]
    one = dot(token_hot, query_grad[0])
    two = pltpu.roll(dot(token_hot, query_grad[1]), HD, 1)
    table_o[:, :WIDE] = jnp.where(small, one, two)
    turned_keys = []
    for n in range(2):
        front, back = key_grad[n, :half], key_grad[n, half:ROT]
        turned_keys += [front * cos_t + back * sin_t, back * cos_t - front * sin_t, key_grad[n, ROT:]]
    keys = jnp.concatenate(turned_keys, axis=0).astype(bf16)
    table_o[:, WIDE:] = dot(token_hot, keys, NT)


def attention_back(
    pair, token_col, token_row, query, key, weight, weight_grad, cosine, sine, cosine_t, sine_t, heads
):
    seq = token_col.shape[0]
    vocab = weight_grad.shape[1] // heads
    full = lambda array: pl.BlockSpec(array.shape, lambda i: (0,) * array.ndim)
    two = full(query)
    return pl.pallas_call(
        functools.partial(attention_back_kernel, heads, pair),
        grid=(1,),
        in_specs=[full(token_col), full(token_row), two, two, full(weight), full(weight_grad)]
        + [full(table) for table in (cosine, sine, cosine_t, sine_t)],
        out_specs=pl.BlockSpec((vocab, 2 * WIDE), lambda i: (0, 0)),
        out_shape=jax.ShapeDtypeStruct((vocab, 2 * WIDE), f32),
        scratch_shapes=[
            pltpu.VMEM((seq, WIDE), bf16),
            pltpu.VMEM((2, seq, WIDE), bf16),
            pltpu.VMEM((2, seq, WIDE), bf16),
            pltpu.VMEM((2, HD, seq), f32),
        ],
        name="attention_back",
        **params(6),
    )(token_col, token_row, query, key, weight, weight_grad, cosine, sine, cosine_t, sine_t)


def loss_kernel(
    parts,
    members,
    heads,
    ints,
    floats,
    token_col,
    target_col,
    token_row,
    embed,
    head,
    vec,
    *refs,
):
    pairs = heads // 2
    weights, refs = refs[: pairs * parts], refs[pairs * parts :]
    pieces, refs = refs[:members], refs[members:]
    keep_o, send_o, grad_o, sums_o, mixing, low_weights, table, down = refs
    step = pl.program_id(0)
    me, length, member = ints[0], ints[1], ints[2]
    vocab = embed.shape[0]
    height = heads * vocab

    @pl.when(step == 0)
    def _():
        rows_v, rows_f = segments_of(heads, members)
        small_v = min(rows_v, HB)
        for r in range(members):
            owner = member ^ r
            piece = pieces[r]
            for place in range(parts):
                for u in range(rows_v // small_v):
                    row = owner * rows_v + u * small_v
                    block, inside = row // HB, row % HB
                    i, k = block // (D // BS), block % (D // BS)
                    at = place * rows_v + u * small_v
                    mixing[
                        me ^ place,
                        pl.ds(pl.multiple_of(i * HB + inside, 32), small_v),
                        pl.ds(pl.multiple_of(k * BS, BS), BS),
                    ] = piece[at : at + small_v]
            at = parts * rows_v
            one, two, three = (
                piece[at + n * rows_f : at + (n + 1) * rows_f].astype(f32) for n in range(3)
            )
            row = owner * rows_f
            down[
                pl.ds(pl.multiple_of(row % vocab, 8), rows_f),
                pl.ds(pl.multiple_of(row // vocab * BS, BS), BS),
            ] = one + (two + three)
        table[...] = stack_parts(embed[...] + (down[...] + vec[2:3]))
        sums_o[...] = jnp.zeros_like(sums_o)

    second = step >= pl.num_programs(0) // 2
    small = lanes((ROWS, WIDE)) < HD

    def weights_of(r):
        value = weights[r][...].astype(f32)
        turned_value = pltpu.roll(value, HD, 1)
        value = jnp.where(second, turned_value, value)
        if pairs == 1:
            return jnp.where(small, value, 0.0)
        other = weights[parts + r][...].astype(f32)
        other = jnp.where(second, other, pltpu.roll(other, HD, 1))
        return jnp.where(small, value, other)

    own = weights_of(0)
    low_weights[me] = own.astype(bf16)[:, :height]
    for r in range(1, parts):
        low_weights[me ^ r] = weights_of(r).astype(bf16)[:, :height]
    token = token_col[...]
    hot = jnp.where(lanes((ROWS, WIDE)) % vocab == token, 1.0, 0.0).astype(bf16)
    x = dot(hot, table[...])
    x = x + dot(
        jnp.concatenate([low_weights[g] for g in range(parts)], axis=1),
        jnp.concatenate([mixing[g] for g in range(parts)], axis=0),
    )
    normed, scale = stats_of(x)
    gain = vec[3:4]
    final = (normed * gain + vec[4:5]).astype(bf16)
    head_low = head[:, :D].astype(bf16)
    square = (vocab, vocab)
    bias_row = jnp.sum(
        jnp.where(lanes(square) == sublanes(square), head[:, D : D + 1], 0.0), axis=0, keepdims=True
    )
    logits = dot(final, head_low, NT) + bias_row
    shifted = logits - jnp.max(logits, axis=-1, keepdims=True)
    log_probs = shifted - jnp.log(jnp.sum(jnp.exp(shifted), axis=-1, keepdims=True))
    target = lanes((ROWS, vocab)) == target_col[...]
    position = step * ROWS + sublanes((ROWS, 1))
    slot_weight = jnp.where(position < length - 1, floats[0], 0.0)
    picked = jnp.sum(jnp.where(target, log_probs, 0.0), axis=-1, keepdims=True)
    loss = -jnp.sum(slot_weight * picked, keepdims=True)
    logit_grad = ((jnp.exp(log_probs) - jnp.where(target, 1.0, 0.0)) * slot_weight).astype(bf16)
    final_grad = dot(logit_grad, head_low)
    grad = norm_back(final_grad, normed, scale, gain)
    high = grad.astype(bf16)
    token_hot = jnp.where(sublanes((vocab, ROWS)) == token_row[...], 1.0, 0.0).astype(bf16)
    both = dot(jnp.concatenate([own.T.astype(bf16), token_hot], axis=0), high)
    sums_o[0:vocab] += both[WIDE:]
    sums_o[vocab : 2 * vocab] += dot(logit_grad, final, TN)
    base = 2 * vocab
    sums_o[base : base + 1] += jnp.sum(final_grad * normed, axis=0, keepdims=True)
    sums_o[base + 1 : base + 2] += jnp.sum(final_grad, axis=0, keepdims=True)
    bias_grad = jnp.sum(logit_grad.astype(f32), axis=0, keepdims=True)
    sums_o[base + 2 : base + 3, :vocab] += bias_grad
    lane = lanes((1, WIDE))
    count = jnp.where((step == 0) & (length >= 2), 1.0, 0.0)
    sums_o[base + 3 : base + 4, :WIDE] += jnp.where(
        lane == 0, loss, jnp.where(lane == 1, count, 0.0)
    )
    sums_o[base + 16 : base + 16 + height] += both[:height]
    grad_o[...] = dot(high, mixing[me], NT)

    @pl.when(step == pl.num_programs(0) - 1)
    def _():
        deal(member & 1, sums_o, keep_o, send_o)


def loss_rows(
    ints,
    floats,
    token_col,
    target_col,
    token_row,
    embedding,
    head,
    vectors,
    weights,
    pieces,
    heads,
):
    seq = token_col.shape[0]
    vocab = embedding.shape[0]
    parts = len(weights) // (heads // 2)
    height = heads * vocab
    blocks = seq // ROWS // 2
    col = pl.BlockSpec((ROWS, 1), lambda i: (i, 0))
    o = jax.ShapeDtypeStruct
    full = lambda array: pl.BlockSpec(array.shape, lambda i: (0,) * array.ndim)
    sums_shape = (2 * vocab + 16 + height, D)
    return pl.pallas_call(
        functools.partial(loss_kernel, parts, len(pieces), heads),
        grid=(seq // ROWS,),
        in_specs=[SMEM, SMEM, col, col, pl.BlockSpec((1, ROWS), lambda i: (0, i))]
        + [full(embedding), full(head), full(vectors)]
        + [pl.BlockSpec((ROWS, WIDE), lambda i: (i % blocks, 0))] * len(weights)
        + [full(pieces[0])] * len(pieces),
        out_specs=[
            pl.BlockSpec((sums_shape[0] // 2, D), lambda i: (0, 0)),
            pl.BlockSpec((sums_shape[0] // 2, D), lambda i: (0, 0)),
            pl.BlockSpec((ROWS, height), lambda i: (i, 0)),
        ],
        out_shape=[o((sums_shape[0] // 2, D), f32)] * 2 + [o((seq, height), f32)],
        scratch_shapes=[
            pltpu.VMEM(sums_shape, f32),
            pltpu.VMEM((parts, height, D), bf16),
            pltpu.VMEM((parts, ROWS, height), bf16),
            pltpu.VMEM((4 * vocab, D), bf16),
            pltpu.VMEM((vocab, D), f32),
        ],
        name="loss_rows",
        **params(12),
    )(
        ints,
        floats,
        token_col,
        target_col,
        token_row,
        embedding,
        head,
        vectors,
        *weights,
        *pieces,
    )


def padded(block):
    lacking = HB - block.shape[0]
    if lacking:
        block = jnp.concatenate([block, jnp.zeros((lacking, block.shape[1]), block.dtype)], axis=0)
    return block


def put_left(ref, index, block):
    ref[index] = jnp.concatenate([padded(block)] * 3, axis=0).astype(bf16)


def put_right(ref, index, block):
    ref[index] = jnp.concatenate(split3(padded(block)), axis=0)


def factors_kernel(
    heads,
    ints,
    owner,
    mine,
    other,
    gathered,
    upper,
    normed,
    act,
    values,
    left_o,
    right_o,
    hidden_o,
    bias_o,
    small_o,
    part_o,
    sums,
    tiles,
    sem,
    *mats,
):
    vocab = normed.shape[0]
    width = upper.shape[1]
    copy = pltpu.make_async_copy(gathered, tiles, sem)
    copy.start()
    join(ints[0] & 1, mine, other, sums)
    small_o[...] = sums[: small_o.shape[0]]
    rows = sums[0:vocab]
    mixed = sums[2 * vocab + 16 :]
    low = normed[...].astype(f32)
    own = act[...].astype(f32)
    val = values[...].astype(f32)
    normed_gram = dot6(low, low, NT)
    square = jnp.sum(dot6(own, own, NT) * dot6(rows, rows, NT), keepdims=True) + jnp.sum(
        dot6(val, val, NT) * dot6(mixed, mixed, NT), keepdims=True
    )
    across = D // BS
    f_rows = width // BS
    pair = 2 * vocab
    for i in range(across):
        put_left(left_o, i, low[:, i * BS : (i + 1) * BS])
    for i in range(f_rows):
        put_left(left_o, across + i, own[:, i * BS : (i + 1) * BS])
    for i in range(heads // 2):
        put_left(
            left_o,
            across + f_rows + i,
            val[i * pair : (i + 1) * pair, i * BS : (i + 1) * BS],
        )
    at = heads * HD // BS
    for i in range(heads // 2):
        for k in range(across):
            put_right(right_o, at, mixed[i * pair : (i + 1) * pair, k * BS : (k + 1) * BS])
            at += 1
    for k in range(across):
        put_right(right_o, at + f_rows + k, rows[:, k * BS : (k + 1) * BS])
    copy.wait()
    for index, (which, i, k) in enumerate(tile_places(layer_shapes(heads, width))):
        mats[which][i * BS : (i + 1) * BS, k * BS : (k + 1) * BS] = tiles[owner[index]]
    mat_q, mat_o, mat_u, mat_f = mats
    part_o[...] = mat_q[:, : 2 * heads * HD]
    act_grad = rows_times_low(rows, mat_f[...], NT)
    u = upper[...]
    tanh = jnp.tanh(GELU_A * (u + GELU_B * (u * u * u)))
    slope = 0.5 * (1.0 + tanh) + 0.5 * u * (1.0 - tanh * tanh) * (
        GELU_A * (1.0 + 3.0 * GELU_B * (u * u))
    )
    upper_grad = act_grad * slope
    bias_grad = jnp.sum(upper_grad, axis=0, keepdims=True)
    bias_o[...] = bias_grad
    value_grad = rows_times_low(mixed, mat_o[...], NT)
    shape = value_grad.shape
    value_grad = jnp.where(sublanes(shape) // vocab == lanes(shape) // HD, value_grad, 0.0)
    value_table = value_grad[:vocab]
    for h in range(1, heads):
        value_table = value_table + value_grad[h * vocab : (h + 1) * vocab]
    hidden_o[0:vocab] = rows_times_low(upper_grad, mat_u[...], NT) + rows_times_low(
        value_table, mat_q[:, 2 * heads * HD :], NT
    )
    square = (
        square
        + jnp.sum(
            normed_gram
            * (dot6(value_table, value_table, NT) + dot6(upper_grad, upper_grad, NT)),
            keepdims=True,
        )
        + jnp.sum(bias_grad * bias_grad, keepdims=True)
    )
    hidden_o[vocab : vocab + 16] = jnp.broadcast_to(square, (16, D))
    for k in range(heads * HD // BS):
        put_right(right_o, k, value_table[:, k * BS : (k + 1) * BS])
    for k in range(f_rows):
        put_right(right_o, at + k, upper_grad[:, k * BS : (k + 1) * BS])


def rest_kernel(pairs, ints, mine, other, hidden, mat_q, normed, right_o, hidden_o, half_o, table):
    vocab = normed.shape[0]
    join(ints[0] & 1, mine, other, table)
    blocks = [table[p * vocab : (p + 1) * vocab, :WIDE] for p in range(pairs)]
    blocks += [table[p * vocab : (p + 1) * vocab, WIDE:] for p in range(pairs)]
    grad = jnp.concatenate(blocks, axis=1)
    for k, block in enumerate(blocks):
        put_right(right_o, k, block)
    low = normed[...].astype(f32)
    square = jnp.sum(dot6(low, low, NT) * dot6(grad, grad, NT), keepdims=True)
    hidden_o[0:vocab] = hidden[0:vocab] + rows_times_low(grad, mat_q[...], NT)
    hidden_o[vocab:] = hidden[vocab:] + square
    size = half_o.shape[0]
    half_o[...] = hidden_o[pl.ds(pl.multiple_of((ints[0] & 1) * size, size), size)]


def factor_places(heads, ff_local):
    q_cols = 3 * heads * HD // BS
    o_rows = heads // 2
    across = D // BS
    f_rows = ff_local // BS
    left, right = [], []
    for which, i, k in tile_places(layer_shapes(heads, ff_local)):
        if which == 0:
            left.append(i)
            right.append(k)
        elif which == 1:
            left.append(across + f_rows + i)
            right.append(q_cols + i * across + k)
        elif which == 2:
            left.append(i)
            right.append(q_cols + o_rows * across + k)
        else:
            left.append(across + i)
            right.append(q_cols + o_rows * across + f_rows + k)
    return np.array(left, np.int32), np.array(right, np.int32)


def factors(ints, owner, mine, other, tiles, upper, normed, act, values, heads):
    vocab = normed.shape[0]
    ff_local = upper.shape[1]
    n_left = D // BS + ff_local // BS + heads // 2
    n_right = heads * HD // BS + heads // 2 * (D // BS) + ff_local // BS + D // BS
    o = jax.ShapeDtypeStruct
    return pl.pallas_call(
        functools.partial(factors_kernel, heads),
        in_specs=[SMEM] * 2 + [VMEM] * 2 + [ANY] + [VMEM] * 4,
        out_specs=[VMEM] * 6,
        out_shape=[
            o((n_left, 3 * HB, BS), bf16),
            o((n_right, 3 * HB, BS), bf16),
            o((vocab + 16, D), f32),
            o((1, ff_local), f32),
            o((2 * vocab + 16, D), f32),
            o((D, 2 * heads * HD), bf16),
        ],
        scratch_shapes=[
            pltpu.VMEM((2 * mine.shape[0], D), f32),
            pltpu.VMEM(tiles.shape, bf16),
            pltpu.SemaphoreType.DMA,
        ]
        + [pltpu.VMEM(shape, bf16) for shape in layer_shapes(heads, ff_local)],
        name="factors",
        **params(7, 24),
    )(ints, owner, mine, other, tiles, upper, normed, act, values)


def factors_rest(ints, mine, other, hidden, mat_q, normed, heads):
    o = jax.ShapeDtypeStruct
    pairs = heads // 2
    return pl.pallas_call(
        functools.partial(rest_kernel, pairs),
        in_specs=[SMEM] + [VMEM] * 5,
        out_specs=[VMEM] * 3,
        out_shape=[
            o((2 * pairs, 3 * HB, BS), bf16),
            o(hidden.shape, f32),
            o((hidden.shape[0] // 2, D), f32),
        ],
        scratch_shapes=[pltpu.VMEM((2 * mine.shape[0], 2 * WIDE), f32)],
        name="factors_rest",
        **params(2),
    )(ints, mine, other, hidden, mat_q, normed)


def small_kernel(parts, corrections, ints, sums, own, *refs):
    mine, others, refs = refs[: parts - 1], refs[parts - 1 : 2 * parts - 2], refs[2 * parts - 2 :]
    bias_grad, refs = refs[0], refs[1:]
    weights, refs = refs[:12], refs[12:]
    outs, scalars, total = refs[:12], refs[12], refs[13]
    vocab = weights[0].shape[0]
    base = 2 * vocab
    size = own.shape[0] // 2
    for place, group in ((ints[0], mine), (1 - ints[0], others)):
        span = pl.ds(pl.multiple_of(place * size, size), size)
        total[span] = tree_sum([own[span]] + [ref[...] for ref in group])
    hidden = total[:vocab]
    square = total[vocab : vocab + 1, 0:1]
    rows = sums[0:vocab]
    normed, scale = stats_of(weights[0][...])
    gain = weights[6][0:1]
    embed_grad = rows + norm_back(hidden, normed, scale, gain)
    vector_grad = jnp.concatenate(
        [
            jnp.sum(hidden * normed, axis=0, keepdims=True),
            jnp.sum(hidden, axis=0, keepdims=True),
            jnp.sum(rows, axis=0, keepdims=True),
            sums[base : base + 1],
            sums[base + 1 : base + 2],
        ],
        axis=0,
    )
    head_grad = sums[vocab : 2 * vocab]
    head_bias = sums[base + 2 : base + 3, :vocab]
    add = lambda value: jnp.sum(value * value, keepdims=True)
    square = square + add(embed_grad) + add(vector_grad) + add(head_grad) + add(head_bias)
    count = sums[base + 3 : base + 4, 1:2]
    loss = sums[base + 3 : base + 4, 0:1] / count
    norm = jnp.sqrt(square) / count
    scale_all = jnp.minimum(1.0, CLIP_NORM / norm) / count
    one, two = corrections[0], corrections[1]

    def update(index, pick, grad):
        weight, first, second = (weights[3 * index + k][pick] for k in range(3))
        grad = grad * scale_all
        first = BETA_ONE * first + (1.0 - BETA_ONE) * grad
        second = BETA_TWO * second + (1.0 - BETA_TWO) * grad * grad
        step = first / one / (jnp.sqrt(second / two) + ADAM_EPS)
        outs[3 * index][pick] = weight - RATE_SMALL * (step + WEIGHT_DECAY * weight)
        outs[3 * index + 1][pick] = first
        outs[3 * index + 2][pick] = second

    everything = slice(None)
    update(0, everything, embed_grad)
    shape = (vocab, vocab)
    head_column = jnp.sum(
        jnp.where(lanes(shape) == sublanes(shape), head_bias, 0.0), axis=1, keepdims=True
    )
    update(1, (everything, slice(0, D)), head_grad)
    update(1, (everything, slice(D, D + 1)), head_column)
    update(2, everything, vector_grad)
    update(3, everything, bias_grad[...])
    lane = lanes((1, WIDE))
    scalars[...] = jnp.where(
        lane == 0, scale_all, jnp.where(lane == 1, loss, jnp.where(lane == 2, norm, 0.0))
    )


def small(corrections, upper, sums, hidden, mine, others, bias_grad, weights):
    o = jax.ShapeDtypeStruct
    return pl.pallas_call(
        functools.partial(small_kernel, 1 + len(mine)),
        in_specs=[SMEM] * 2 + [VMEM] * (2 + 2 * len(mine) + 1 + 12),
        out_specs=[VMEM] * 13,
        out_shape=[o(weight.shape, f32) for weight in weights] + [o((1, WIDE), f32)],
        scratch_shapes=[pltpu.VMEM(hidden.shape, f32)],
        name="small",
        **params(4),
    )(corrections, upper, sums, hidden, *mine, *others, bias_grad, *weights)


QB = 32
UNQ = 12
PER = 6


def take(value, at):
    return jnp.take_along_axis(value, at, axis=1, mode="promise_in_bounds")


def eliminate(packed, count):
    shape = (8, BS)
    lane, sub = lanes(shape), sublanes(shape)
    start = lane // QB * QB
    span = range(count)
    for p in range(QB // 8):
        r0 = 8 * p

        def body(step, carry):
            jj = 2 * step
            j = r0 + jj
            pick, pick_two = start + j, start + (j + 1)
            mark, mark_two = lane == pick, lane == pick_two
            below, below_two = sub > jj, sub > jj + 1
            wide = [jnp.broadcast_to(packed[t, pl.ds(j, 1), :], shape) for t in span]
            next_wide = [jnp.broadcast_to(packed[t, pl.ds(j + 1, 1), :], shape) for t in span]
            kept = [[packed[t, 8 * q : 8 * q + 8, :] for q in range(p, QB // 8)] for t in span]
            pivot = [take(w, pick) for w in wide]
            right = [take(w, pick_two) for w in wide]
            lower = [take(w, pick) for w in next_wide]
            corner = [take(w, pick_two) for w in next_wide]
            ones = [[take(a, pick) for a in group] for group in kept]
            twos = [[take(a, pick_two) for a in group] for group in kept]
            inverse = [1.0 / d for d in pivot]
            ratio = [b * i for b, i in zip(right, inverse)]
            inverse_two = [1.0 / (e - b * r) for e, b, r in zip(corner, lower, ratio)]
            scaled = [jnp.where(mark, 1.0, w) * i for w, i in zip(wide, inverse)]
            scaled_two = [
                jnp.where(mark_two, 1.0, jnp.where(mark, 0.0, w) - b * x) * i
                for w, b, x, i in zip(next_wide, lower, scaled, inverse_two)
            ]
            for t in span:
                for k, q in enumerate(range(p, QB // 8)):
                    a, c, d = kept[t][k], ones[t][k], twos[t][k]
                    d = d - c * ratio[t]
                    first = jnp.where(mark, 0.0, a) - c * scaled[t]
                    if k == 0:
                        first = jnp.where(below, first, a)
                    second = jnp.where(mark_two, 0.0, first) - d * scaled_two[t]
                    if k == 0:
                        second = jnp.where(below_two, second, first)
                    packed[t, 8 * q : 8 * q + 8, :] = second
            return carry

        lax.fori_loop(0, 4, body, 0)


def part_inverse(packed):
    shape = (QB, BS)
    lane, sub = lanes(shape), sublanes(shape)
    part, col = lane // QB, lane % QB
    diagonal = jnp.where(col == sub, packed, 0.0)
    pivot = jnp.ones(shape, f32)
    for k in range(BS // QB):
        own = jnp.sum(jnp.where(part == k, diagonal, 0.0), axis=1, keepdims=True)
        pivot = jnp.where(part == k, own, pivot)
    unit = jnp.where(col < sub, packed, jnp.where(col == sub, 1.0, 0.0))
    return unit * lax.rsqrt(pivot)


def inverse_factors(gram, packed, result, count):
    parts = BS // QB
    unroll = next(k for k in (UNQ, 3, 2, 1) if count % k == 0)
    lane32, sub32 = lanes((QB, BS)), sublanes((QB, BS))
    for b in range(parts):
        begin = b * QB
        below = begin + QB
        rows = slice(begin, below)
        here = lane32 // QB == b

        def pack(i, carry):
            for t in [i * unroll + k for k in range(unroll)]:
                value = jnp.zeros((QB, BS), f32)
                for k in range(parts):
                    block = gram[parts * t + k, rows, :]
                    if k != b:
                        block = pltpu.roll(block, (k * QB + BS - begin) % BS, 1)
                    value = jnp.where(lane32 // QB == k, block, value)
                packed[t] = value
            return carry

        lax.fori_loop(0, count // unroll, pack, 0)
        eliminate(packed, count)

        def spread(i, carry):
            groups = [i * unroll + k for k in range(unroll)]
            inverses = [part_inverse(packed[t]) for t in groups]
            firsts = [
                jnp.concatenate([jnp.where(lane32 // QB == k, x, 0.0) for k in range(parts)], axis=0)
                for x in inverses
            ]
            unit = jnp.where(lane32 - begin == sub32, 1.0, 0.0)
            panels = [
                jnp.concatenate(
                    [jnp.where(here, unit, gram[parts * t + k, rows, :]) for k in range(parts)],
                    axis=0,
                )
                for t in groups
            ]
            news = [dot6(x, y, NN) for x, y in zip(firsts, panels)]
            for t, new in zip(groups, news):
                for k in range(parts):
                    value = new[k * QB : (k + 1) * QB]
                    result[parts * t + k, rows, :] = (
                        jnp.where(lane32 < below, value, 0.0) if below < BS else value
                    )
            if below < BS:
                for t, new in zip(groups, news):
                    mats = [new[k * QB : (k + 1) * QB] for k in range(parts)]
                    changes = [dot6(x, x, TN) for x in mats]
                    shape = (BS - below, BS)
                    mark = lanes(shape) // QB == b
                    for k in range(parts):
                        old = gram[parts * t + k, below:, :]
                        gram[parts * t + k, below:, :] = jnp.where(mark, 0.0, old) - changes[k][below:]
            return carry

        lax.fori_loop(0, count // unroll, spread, 0)


def tile_params(count, per):
    blk = pl.BlockSpec((per, BS, BS), lambda i: (i, 0, 0))
    full = pl.BlockSpec((count, BS, BS), lambda i: (0, 0, 0))
    return blk, full, lambda dt: jax.ShapeDtypeStruct((count, BS, BS), dt)


def gradient_kernel(per, rest, natural, left_at, right_at, lefts, rights, more, L, R, QL, QR, *outs):
    step = pl.program_id(0)
    span = range(per)
    pairs = []
    for s in span:
        tile = natural[step * per + s]
        at = right_at[tile]
        right = jnp.where(
            at < rest, more[jnp.minimum(at, rest - 1)], rights[jnp.maximum(at - rest, 0)]
        )
        pairs.append((lefts[left_at[tile]], right))
    g = [dot(a, b, TN) for a, b in pairs]
    gt = [dot(b, a, TN) for a, b in pairs]
    qt = [QL[s].T for s in span]
    left = [dot3(x, x, NT) for x in g]
    right = [dot3(x, x, NT) for x in gt]
    rot = [dot3(q, x, NN) for q, x in zip(qt, g)]
    mixed_left = [dot3(left[s], QL[s], NN) for s in span]
    mixed_right = [dot3(right[s], QR[s], NN) for s in span]
    rot = [dot3(rot[s], QR[s], NN) for s in span]
    old_left = [dot6(L[s], QL[s], NN) for s in span]
    old_right = [dot6(R[s], QR[s], NN) for s in span]
    for s in span:
        for out, value in zip(
            outs, (left, right, rot, mixed_left, mixed_right, old_left, old_right)
        ):
            out[s] = value[s]


def gradient_products(natural, left_at, right_at, lefts, rights, more, L, R, QL, QR):
    count = QL.shape[0]
    blk, _, o = tile_params(count, PER)
    whole = lambda x: pl.BlockSpec(x.shape, lambda i: (0, 0, 0))
    return pl.pallas_call(
        functools.partial(gradient_kernel, PER, more.shape[0]),
        grid=(count // PER,),
        in_specs=[SMEM] * 3 + [whole(lefts), whole(rights), whole(more)] + [blk] * 4,
        out_specs=[blk] * 7,
        out_shape=[o(f32)] * 7,
        name="gradient_products",
        **params(9),
    )(natural, left_at, right_at, lefts, rights, more, L, R, QL, QR)


def soap_kernel(
    count, per, corrections, scal, GL, GR, GT, BL, BR, AL, AR, W, m, v, L, R, QL, QR,
    W_o, low_o, m_o, v_o, L_o, R_o, QL_o, QR_o, ML_s, MR_s, work, inv_s, packed,
):
    step = pl.program_id(0)
    scale = scal[0:1, 0:1]
    c1, c2 = corrections[0], corrections[1]
    span = range(per)
    share = (1 - BETA_TWO) * (scale * scale)
    xs = []
    for s in span:
        rot = GT[s] * scale
        mn = BETA_ONE * m[s] + (1 - BETA_ONE) * rot
        vn = BETA_TWO * v[s] + (1 - BETA_TWO) * rot * rot
        m_o[s] = mn
        v_o[s] = vn
        xs.append((mn / c1) / (jnp.sqrt(vn / c2) + ADAM_EPS))
    ML = [BETA_TWO * AL[s] + share * BL[s] for s in span]
    MR = [BETA_TWO * AR[s] + share * BR[s] for s in span]
    back = [dot3(QL[s], xs[s], NN) for s in span]
    ML = [x * lax.rsqrt(jnp.sum(x * x, keepdims=True)) for x in ML]
    MR = [x * lax.rsqrt(jnp.sum(x * x, keepdims=True)) for x in MR]
    back = [dot3(back[s], QR[s], NT) for s in span]
    gram_left = [dot6(x, x, TN) for x in ML]
    gram_right = [dot6(x, x, TN) for x in MR]
    for s in span:
        L_o[s] = BETA_TWO * L[s] + share * GL[s]
        R_o[s] = BETA_TWO * R[s] + share * GR[s]
        w = W[s]
        wn = w - RATE_TILES * (back[s] + WEIGHT_DECAY * w)
        W_o[s] = wn
        low_o[s] = wn.astype(bf16)
        t = step * per + s
        ML_s[t] = ML[s]
        MR_s[t] = MR[s]
        work[2 * t] = gram_left[s]
        work[2 * t + 1] = gram_right[s]

    @pl.when(step == pl.num_programs(0) - 1)
    def _():
        inverse_factors(work, packed, inv_s, count // 2)
        unroll = next(k for k in (8, 6, 3, 1) if count % k == 0)

        def last(i, carry):
            ts = [i * unroll + k for k in range(unroll)]
            ol = [dot3(ML_s[t], inv_s[2 * t], NT) for t in ts]
            orr = [dot3(MR_s[t], inv_s[2 * t + 1], NT) for t in ts]
            for t, a, b in zip(ts, ol, orr):
                QL_o[t] = a
                QR_o[t] = b
            return carry

        lax.fori_loop(0, count // unroll, last, 0)


def soap(corrections, scal, products, W, m, v, L, R, QL, QR):
    count = W.shape[0]
    blk, full, o = tile_params(count, PER)
    return pl.pallas_call(
        functools.partial(soap_kernel, count, PER),
        grid=(count // PER,),
        in_specs=[SMEM, pl.BlockSpec((1, WIDE), lambda i: (0, 0))] + [blk] * 14,
        out_specs=[blk] * 6 + [full] * 2,
        out_shape=[o(f32), o(bf16), o(f32), o(f32), o(f32), o(f32), o(f32), o(f32)],
        scratch_shapes=[pltpu.VMEM((count, BS, BS), f32)] * 2
        + [pltpu.VMEM((2 * count, BS, BS), f32)] * 2
        + [pltpu.VMEM((count // 2, QB, BS), f32)],
        name="soap_tiles",
        **params(40, 36),
    )(corrections, scal, *products, W, m, v, L, R, QL, QR)


def local(
    tokens,
    lengths,
    tile_owner,
    step_count,
    weight_tiles,
    tiles_first,
    tiles_second,
    stats_left,
    stats_right,
    basis_left,
    basis_right,
    embedding,
    embedding_first,
    embedding_second,
    head_table,
    head_first,
    head_second,
    vectors,
    vectors_first,
    vectors_second,
    fc_bias,
    fc_bias_first,
    fc_bias_second,
):
    seq = tokens.shape[1]
    mp_count = lax.axis_size("mp")
    dp_count = lax.axis_size("dp")
    dp_index = lax.axis_index("dp")
    mp_index = lax.axis_index("mp")
    upper_pair = dp_index & 1
    heads = H // mp_count
    ff_local = fc_bias.shape[1]
    count = weight_tiles.shape[0]
    vocab = embedding.shape[0]
    own_index = dp_index[None]

    natural, low_tiles, normed, keep, send = first_tables(
        tile_owner, own_index, weight_tiles, embedding, vectors, heads, ff_local
    )
    token_col = tokens.reshape(seq, 1)
    target_col = jnp.roll(tokens, -1, axis=1).reshape(seq, 1)
    keep = keep + swap_with(send, "dp", 1)
    mine = direct(keep)
    low_tiles, mine = lax.optimization_barrier((low_tiles, mine))
    gathered = lax.all_gather(low_tiles, "dp", axis=0, tiled=True)
    proj, upper, act, values, keep, send = second_tables(
        natural, own_index, mine, swap_with(mine, "dp", 1), fc_bias, low_tiles, vocab, heads, dp_count
    )
    cosine, sine, cosine_t, sine_t = rotary_tables(seq)
    segment = sum(segments_of(heads, dp_count))
    places = range(1, dp_count // 2)
    received = [swap_with(send, "dp", 1)]
    queries, keys = [], []
    weight = jnp.zeros((8, WIDE), f32)
    for pair in range(heads // 2):
        query, key, weight, weight_low = attention(
            pair, lengths, token_col, proj, cosine, sine, weight, heads
        )
        queries.append(query)
        keys.append(key)
        if pair == 0:
            received, weight, weight_low = lax.optimization_barrier((received, weight, weight_low))
            keep = keep + received[0]
            received = [
                swap_with(keep[q * segment : (q + 1) * segment], "dp", 2 * q) for q in places
            ]
            keep, weight = lax.optimization_barrier((keep, weight))
            weights = gather_xor(weight_low, "mp")
    if heads > 2:
        more = gather_xor(weight_low, "mp")
        received, weights, more[0] = lax.optimization_barrier((received, weights, more[0]))
    mine = tree_sum([keep[:segment]] + list(received))
    packed = pack_segments(heads, dp_count, gather_xor(mine, "mp"))
    even = [packed] + [swap_with(packed, "dp", 2 * q) for q in places]
    if heads > 2:
        weights = weights + more
    odd = [swap_with(piece, "dp", 1) for piece in even]
    pieces = [piece for two in zip(even, odd) for piece in two]
    length = lengths[0]
    inverse_length = 1.0 / jnp.maximum(length - 1, 1).astype(f32)
    keep, send, weight_grad = loss_rows(
        jnp.stack([mp_index, length, dp_index]),
        inverse_length[None],
        token_col,
        target_col,
        tokens,
        embedding,
        head_table.T,
        vectors,
        weights,
        pieces,
        heads,
    )
    keep = keep + swap_with(send, "dp", 1)
    tables_back = []
    for pair in range(heads // 2):
        if pair == 1:
            weight_grad, keep = lax.optimization_barrier((weight_grad, keep))
        tables_back.append(
            attention_back(
                pair,
                token_col,
                tokens,
                queries[pair],
                keys[pair],
                weight,
                weight_grad,
                cosine,
                sine,
                cosine_t,
                sine_t,
                heads,
            )
        )
    mine = butterfly(keep)
    table = jnp.concatenate(tables_back, axis=0)
    half = table.shape[0] // 2
    first, second = table[:half], table[half:]
    is_upper = upper_pair == 1
    table = jnp.where(is_upper, second, first) + swap_with(
        jnp.where(is_upper, first, second), "dp", 1
    )
    table = direct(table)
    left, right, hidden, bias_grad, sums, mat_part = factors(
        own_index, tile_owner, mine, swap_with(mine, "dp", 1), gathered, upper, normed, act, values, heads
    )
    more, hidden, hidden_half = factors_rest(
        own_index, table, swap_with(table, "dp", 1), hidden, mat_part, normed, heads
    )
    hidden_parts = gather_halves(hidden_half)
    left_at, right_at = (jnp.asarray(places) for places in factor_places(heads, ff_local))
    gradients = gradient_products(
        natural, left_at, right_at, left, right, more, stats_left, stats_right, basis_left, basis_right
    )
    hidden_parts, gradients = lax.optimization_barrier((hidden_parts, gradients))
    hidden_others = swap_pair(hidden_parts)
    corrections = 1.0 - jnp.power(
        jnp.array([BETA_ONE, BETA_TWO], f32), step_count.astype(f32)
    )
    small_weights = (
        embedding,
        embedding_first,
        embedding_second,
        head_table.T,
        head_first.T,
        head_second.T,
        vectors,
        vectors_first,
        vectors_second,
        fc_bias,
        fc_bias_first,
        fc_bias_second,
    )
    *small_out, scalars = small(
        corrections,
        upper_pair[None],
        sums,
        hidden,
        hidden_parts,
        hidden_others,
        bias_grad,
        small_weights,
    )
    small_out[3:6] = [value.T for value in small_out[3:6]]
    results = soap(
        corrections,
        scalars,
        gradients,
        weight_tiles,
        tiles_first,
        tiles_second,
        stats_left,
        stats_right,
        basis_left,
        basis_right,
    )
    return (scalars[0, 1], scalars[0, 2], *results, *small_out)


def solution(mesh):
    tiled = P("dp", None, "mp")
    split = P(None, "mp")
    in_specs = (P("dp", None), P("dp"), P(), P(), *[tiled] * 7, *[P()] * 9, *[split] * 3)
    out_specs = (P(), P(), *[tiled] * 8, *[P()] * 9, *[split] * 3)
    return jax.shard_map(local, mesh=mesh, in_specs=in_specs, out_specs=out_specs, check_vma=False)
```

```python
import functools
import math

import jax
import jax.numpy as jnp
import numpy as np
from jax import lax
from jax.experimental import pallas as pl
from jax.experimental.pallas import tpu as pltpu
from jax.sharding import PartitionSpec as P

D = 1024
H = 16
HD = 64
ROT = 32
BS = 128
HB = 64
ROWS = 256
WIDE = 128
MEGA = 1024 * 1024

NORM_EPS = 1e-05
CLIP_NORM = 0.02
RATE_TILES = 0.02
RATE_SMALL = 0.2
BETA_ONE = 0.9
BETA_TWO = 0.95
ADAM_EPS = 1e-08
WEIGHT_DECAY = 0.01
MASKED = -1e30
GELU_A = math.sqrt(2.0 / math.pi)
GELU_B = 0.044715

NN = (((1,), (0,)), ((), ()))
NT = (((1,), (1,)), ((), ()))
TN = (((0,), (0,)), ((), ()))
f32 = jnp.float32
bf16 = jnp.bfloat16
SMEM = pl.BlockSpec(memory_space=pltpu.SMEM)
VMEM = pl.BlockSpec(memory_space=pltpu.VMEM)
ANY = pl.BlockSpec(memory_space=pl.ANY)


def dot(a, b, dims=NN):
    return lax.dot_general(a, b, dims, preferred_element_type=f32)


def split2(a):
    high = a.astype(bf16)
    return high, (a - high.astype(f32)).astype(bf16)


def split3(a):
    high = a.astype(bf16)
    rest = a - high.astype(f32)
    middle = rest.astype(bf16)
    return high, middle, (rest - middle.astype(f32)).astype(bf16)


def dot3(a, b, dims):
    (axis_a,), (axis_b,) = dims[0]
    ah, al = split2(a)
    bh, bl = split2(b)
    return dot(
        jnp.concatenate([ah, ah, al], axis=axis_a),
        jnp.concatenate([bh, bl, bh], axis=axis_b),
        dims,
    )


def dot6(a, b, dims):
    (axis_a,), (axis_b,) = dims[0]
    ah, am, al = split3(a)
    bh, bm, bl = split3(b)
    return dot(
        jnp.concatenate([ah, ah, am, am, ah, al], axis=axis_a),
        jnp.concatenate([bh, bm, bh, bm, bl, bh], axis=axis_b),
        dims,
    )


def rows_times_low(a, low, dims):
    count = a.shape[0]
    parts = dot(jnp.concatenate(split3(a), axis=0), low, dims)
    return parts[:count] + (parts[count : 2 * count] + parts[2 * count :])


def lanes(shape):
    return lax.broadcasted_iota(jnp.int32, shape, len(shape) - 1)


def sublanes(shape):
    return lax.broadcasted_iota(jnp.int32, shape, len(shape) - 2)


def stats_of(values):
    centred = values - jnp.mean(values, axis=-1, keepdims=True)
    spread = jnp.mean(centred * centred, axis=-1, keepdims=True)
    scale = lax.rsqrt(spread + NORM_EPS)
    return centred * scale, scale


def norm_back(grad, normed, scale, gain):
    inner = grad * gain
    mean_one = jnp.mean(inner, axis=-1, keepdims=True)
    mean_two = jnp.mean(inner * normed, axis=-1, keepdims=True)
    return scale * (inner - mean_one - normed * mean_two)


def params(microseconds, megabytes=20):
    return dict(
        compiler_params=pltpu.CompilerParams(vmem_limit_bytes=megabytes * MEGA),
        cost_estimate=pl.CostEstimate(
            flops=int(microseconds * 1.1e9), bytes_accessed=int(microseconds * 1e6), transcendentals=0
        ),
    )


def swap_with(value, axis, mask):
    count = lax.axis_size(axis)
    return lax.ppermute(value, axis, [(i, i ^ mask) for i in range(count)])


def tree_sum(parts):
    while len(parts) > 1:
        parts = [parts[i] + parts[i + 1] for i in range(0, len(parts), 2)]
    return parts[0]


def gather_xor(value, axis):
    return [value] + [swap_with(value, axis, r) for r in range(1, lax.axis_size(axis))]


def gather_halves(mine):
    return [swap_with(mine, "mp", r) for r in range(1, lax.axis_size("mp"))]


def swap_pair(parts):
    return [swap_with(part, "dp", 1) for part in parts]


def butterfly(kept):
    bits = [1 << k for k in range(1, lax.axis_size("dp").bit_length() - 1)]
    half = (kept.shape[0] // 2 + 7) // 8 * 8
    pieces = [kept[:half], kept[half:]]
    for k in range(len(bits)):
        received = [
            swap_with(piece, "dp", order[k])
            for piece, order in zip(pieces, (bits, bits[1:] + bits[:1]))
        ]
        pieces = [piece + other for piece, other in zip(pieces, received)]
    return jnp.concatenate(pieces, axis=0)


def direct(kept):
    return tree_sum([kept] + [swap_with(kept, "dp", r) for r in range(2, lax.axis_size("dp"), 2)])


def deal(upper, value, keep_o, send_o):
    half = keep_o.shape[0]

    @pl.when(upper == 0)
    def _():
        keep_o[...] = value[:half]
        send_o[...] = value[half : 2 * half]

    @pl.when(upper == 1)
    def _():
        keep_o[...] = value[half : 2 * half]
        send_o[...] = value[:half]


def join(upper, mine, other, whole):
    half = mine.shape[0]

    @pl.when(upper == 0)
    def _():
        whole[:half] = mine[...]
        whole[half:] = other[...]

    @pl.when(upper == 1)
    def _():
        whole[:half] = other[...]
        whole[half:] = mine[...]


def layer_shapes(heads_local, ff_local):
    return ((D, 3 * heads_local * HD), (heads_local * HD, D), (D, ff_local), (ff_local, D))


def tile_places(shapes):
    places = []
    for which, (row_total, col_total) in enumerate(shapes):
        for i in range(row_total // BS):
            for k in range(col_total // BS):
                places.append((which, i, k))
    return places


def first_places(heads, ff_local):
    q_cols = 3 * heads * HD // BS
    rows, blocks = [], []
    for which, i, k in tile_places(layer_shapes(heads, ff_local)):
        used = which in (0, 2)
        rows.append(i if used else 0)
        blocks.append(k if which == 0 else q_cols + k if which == 2 else q_cols + ff_local // BS)
    return np.array(rows, np.int32), np.array(blocks, np.int32)


def first_kernel(owner, ints, row_of, block_of, tiles, embed, vec, natural_o, low_o, normed_o, keep_o, send_o, rows, acc, held, sem):
    copy = pltpu.make_async_copy(tiles, held, sem)
    copy.start()
    count = tiles.shape[0]
    begin = ints[0] * count

    def find(b, carry):
        slot = owner[b] - begin
        natural_o[jnp.where((slot >= 0) & (slot < count), slot, count)] = b
        return carry

    lax.fori_loop(0, owner.shape[0], find, 0, unroll=8)
    normed, _ = stats_of(embed[...])
    low = (normed * vec[0:1] + vec[1:2]).astype(bf16)
    normed_o[...] = low
    for i in range(D // BS):
        rows[i] = low[:, i * BS : (i + 1) * BS]
    acc[...] = jnp.zeros_like(acc)
    copy.wait()
    for s in range(count):
        low_o[s] = held[s].astype(bf16)
    products = [dot(rows[row_of[natural_o[s]]], low_o[s]) for s in range(count)]
    for s in range(count):
        acc[block_of[natural_o[s]]] += products[s]
    half = keep_o.shape[0]
    for upper, first, second in ((0, keep_o, send_o), (1, send_o, keep_o)):

        @pl.when((ints[0] & 1) == upper)
        def _():
            first[...] = acc[:half]
            second[...] = acc[half : 2 * half]


def first_tables(owner, ints, tiles, embedding, vectors, heads, ff_local):
    vocab = embedding.shape[0]
    row_of, block_of = first_places(heads, ff_local)
    blocks = int(block_of.max())
    o = jax.ShapeDtypeStruct
    return pl.pallas_call(
        first_kernel,
        in_specs=[SMEM] * 4 + [ANY] + [VMEM] * 2,
        out_specs=[SMEM] + [VMEM] * 4,
        out_shape=[
            o((tiles.shape[0] + 1,), jnp.int32),
            o(tiles.shape, bf16),
            o((vocab, D), bf16),
            o(((blocks + 1) // 2, vocab, BS), f32),
            o(((blocks + 1) // 2, vocab, BS), f32),
        ],
        scratch_shapes=[
            pltpu.VMEM((D // BS, vocab, BS), bf16),
            pltpu.VMEM((blocks + 1, vocab, BS), f32),
            pltpu.VMEM(tiles.shape, f32),
            pltpu.SemaphoreType.DMA,
        ],
        name="first_tables",
        **params(4, 56),
    )(owner, ints, jnp.asarray(row_of), jnp.asarray(block_of), tiles, embedding, vectors)


def second_places(heads, ff_local):
    pairs, across = heads // 2, D // BS
    lefts, blocks = [], []
    for which, i, k in tile_places(layer_shapes(heads, ff_local)):
        lefts.append(i if which == 1 else pairs + i if which == 3 else 0)
        blocks.append(
            i * across + k if which == 1 else (pairs * across + k if which == 3 else pairs * across + across)
        )
    return np.array(lefts, np.int32), np.array(blocks, np.int32)


def segments_of(heads, dp_count):
    return heads // 2 * (D // BS) * HB // dp_count, 32 * (D // BS) // dp_count


def second_kernel(
    heads, dp_count, natural, ints, left_of, block_of, mine, other, bias, low,
    proj_o, upper_o, act_o, values_o, keep_o, send_o, total, lefts, acc,
):
    vocab = proj_o.shape[0]
    me = ints[0]
    count = low.shape[0]
    pairs = heads // 2
    q_cols = 3 * heads * HD // BS
    f_rows = upper_o.shape[1] // BS
    across = D // BS
    join(me & 1, mine, other, total)
    for j in range(q_cols):
        proj_o[:, j * BS : (j + 1) * BS] = total[j]
    upper = jnp.concatenate([total[q_cols + j] for j in range(f_rows)], axis=1)
    upper = upper + bias[...]
    upper_o[...] = upper
    act = 0.5 * upper * (1.0 + jnp.tanh(GELU_A * (upper + GELU_B * (upper * upper * upper))))
    act = act.astype(bf16).astype(f32)
    act_o[...] = act.astype(bf16)
    values = proj_o[:, 2 * heads * HD :]
    shape = (heads * vocab, heads * HD)
    values = jnp.concatenate([values] * heads, axis=0)
    values = jnp.where(sublanes(shape) // vocab == lanes(shape) // HD, values, 0.0)
    values_o[...] = values.astype(bf16)
    for i in range(pairs):
        lefts[i] = values[i * HB : (i + 1) * HB, i * BS : (i + 1) * BS].astype(bf16)
    for i in range(f_rows):
        lefts[pairs + i] = padded(act[:, i * BS : (i + 1) * BS]).astype(bf16)
    acc[...] = jnp.zeros_like(acc)
    products = [dot(lefts[left_of[natural[s]]], low[s]) for s in range(count)]
    for s in range(count):
        rows = pl.ds(pl.multiple_of(block_of[natural[s]] * HB, HB), HB)
        acc[rows] += products[s]
    rows_v, rows_f = segments_of(heads, dp_count)
    base = pairs * across * HB
    for odd, first, second in ((0, keep_o, send_o), (1, send_o, keep_o)):

        @pl.when((me & 1) == odd)
        def _():
            for e in range(dp_count):
                out = second if e & 1 else first
                start = pl.multiple_of(((me ^ e) >> 1) * (rows_v + rows_f), 8)
                out[pl.ds(start, rows_v)] = acc[e * rows_v : (e + 1) * rows_v]
                k, inside = e * rows_f // vocab, e * rows_f % vocab
                at = base + k * HB + inside
                out[pl.ds(pl.multiple_of(start + rows_v, 8), rows_f)] = acc[at : at + rows_f]


def second_tables(natural, ints, mine, other, fc_bias, low, vocab, heads, dp_count):
    ff_local = fc_bias.shape[1]
    left_of, block_of = second_places(heads, ff_local)
    o = jax.ShapeDtypeStruct
    return pl.pallas_call(
        functools.partial(second_kernel, heads, dp_count),
        in_specs=[SMEM] * 4 + [VMEM] * 4,
        out_specs=[VMEM] * 6,
        out_shape=[
            o((vocab, 3 * heads * HD), f32),
            o((vocab, ff_local), f32),
            o((vocab, ff_local), bf16),
            o((heads * vocab, heads * HD), bf16),
            o((dp_count // 2 * sum(segments_of(heads, dp_count)), BS), f32),
            o((dp_count // 2 * sum(segments_of(heads, dp_count)), BS), f32),
        ],
        scratch_shapes=[
            pltpu.VMEM((2 * mine.shape[0],) + mine.shape[1:], f32),
            pltpu.VMEM((heads // 2 + ff_local // BS, HB, BS), bf16),
            pltpu.VMEM(((int(block_of.max()) + 1) * HB, BS), f32),
        ],
        name="second_tables",
        **params(4),
    )(natural, ints, jnp.asarray(left_of), jnp.asarray(block_of), mine, other, fc_bias, low)


def pack_kernel(rows_v, *refs):
    *parts, out = refs
    at = 0
    for part in parts:
        out[at : at + rows_v] = part[:rows_v].astype(bf16)
        at += rows_v
    down = tree_sum([part[rows_v:] for part in parts])
    for piece in split3(down):
        out[at : at + down.shape[0]] = piece
        at += down.shape[0]


def pack_segments(heads, dp_count, parts):
    rows_v, rows_f = segments_of(heads, dp_count)
    return pl.pallas_call(
        functools.partial(pack_kernel, rows_v),
        in_specs=[VMEM] * len(parts),
        out_specs=VMEM,
        out_shape=jax.ShapeDtypeStruct((len(parts) * rows_v + 3 * rows_f, BS), bf16),
        name="pack_segments",
        **params(1),
    )(*parts)


def rotary_tables(seq_len):
    half = ROT // 2
    frequency = np.float32(10000.0) ** (
        np.float32(-2.0) * np.arange(half, dtype=np.float32) / np.float32(ROT)
    )
    angles = np.arange(seq_len, dtype=np.float32)[:, None] * frequency[None, :].astype(np.float32)
    cosine = np.cos(angles.astype(np.float64)).astype(np.float32)
    sine = np.sin(angles.astype(np.float64)).astype(np.float32)
    wide_cos = np.ones((seq_len, WIDE), np.float32)
    wide_sin = np.zeros((seq_len, WIDE), np.float32)
    wide_cos[:, :half], wide_cos[:, half:ROT] = cosine, cosine
    wide_sin[:, :half], wide_sin[:, half:ROT] = sine, sine
    return wide_cos, wide_sin, np.ascontiguousarray(cosine.T), np.ascontiguousarray(sine.T)


def turned(x):
    half = ROT // 2
    lane = lanes(x.shape)
    return jnp.where(
        lane < half,
        -pltpu.roll(x, WIDE - half, 1),
        jnp.where(lane < ROT, pltpu.roll(x, half, 1), 0.0),
    )


def head_lanes(table, index):
    begin = index // 2 * WIDE
    chunk = table[:, begin : begin + WIDE]
    if index % 2:
        chunk = pltpu.roll(chunk, HD, 1)
    return jnp.where(lanes(chunk.shape) < HD, chunk, 0.0)


def stack_parts(table):
    high, middle, rest = split3(table)
    return jnp.concatenate([high, middle, rest, jnp.zeros_like(high)], axis=0)


def attention_kernel(
    heads, pair, length, token_col, proj, cosine, sine, before, query_o, key_o, weight_o, low_o, hot, key_hot, queries, wide
):
    seq = token_col.shape[0]
    vocab = proj.shape[0]
    lane = lanes((seq, WIDE))
    hot[...] = jnp.where(lane % vocab == token_col[...], 1.0, 0.0).astype(bf16)
    for n in range(2):
        first = (2 * pair + n) * vocab
        key_hot[n] = jnp.where(lane == token_col[...] + first, 1.0, 0.0).astype(bf16)
    one = lanes((vocab, WIDE)) == HD
    ones = (lanes((vocab, WIDE)) > HD) & (lanes((vocab, WIDE)) < HD + 4)
    for which in range(2):
        for n in range(2):
            own = head_lanes(proj, which * heads + 2 * pair + n)
            other = turned(own)
            if which == 0:
                own = jnp.where(one, 1.0, own * 0.125)
                other = other * 0.125
            else:
                own = jnp.where(one | ones, 1.0, own)
            begin = (which * 2 + n) * 2 * WIDE
            wide[:, begin : begin + WIDE] = stack_parts(own)
            wide[:, begin + WIDE : begin + 2 * WIDE] = stack_parts(other)
    for i in range(seq // ROWS):
        span = slice(i * ROWS, (i + 1) * ROWS)
        part = hot[span]
        position = i * ROWS + sublanes((ROWS, WIDE))
        bias = jnp.where(position < length[0], 0.0, MASKED)
        cos, sin = cosine[span], sine[span]
        key_cos = jnp.where(lanes((ROWS, WIDE)) == HD, bias, cos)
        for h in range(2):
            both = dot(part, wide[:, h * 2 * WIDE : (h + 1) * 2 * WIDE])
            queries[h, span] = (both[:, :WIDE] * cos + both[:, WIDE:] * sin).astype(bf16)
            k = 2 + h
            both = dot(part, wide[:, k * 2 * WIDE : (k + 1) * 2 * WIDE])
            key_o[h, span] = (both[:, :WIDE] * key_cos + both[:, WIDE:] * sin).astype(bf16)
    allowed = lanes((ROWS, ROWS)) <= sublanes((ROWS, ROWS))
    small = lanes((ROWS, WIDE))
    halves = []
    for i in range(seq // ROWS):
        span = slice(i * ROWS, (i + 1) * ROWS)
        past = i * ROWS
        weights = before[span] if pair else jnp.zeros((ROWS, WIDE), f32)
        query = [queries[h, span] for h in range(2)]
        near = [dot(query[h], key_o[h, span], NT) for h in range(2)]
        if past:
            far = [dot(query[h], key_o[h, :past], NT) for h in range(2)]
        near = [jnp.where(allowed, x, MASKED) for x in near]
        top = [jnp.max(x, axis=-1, keepdims=True) for x in near]
        if past:
            top = [jnp.maximum(m, jnp.max(x, axis=-1, keepdims=True)) for m, x in zip(top, far)]
            far = [jnp.exp(x - m) for m, x in zip(top, far)]
        near = [jnp.exp(x - m) for m, x in zip(top, near)]
        total = [jnp.sum(x, axis=-1, keepdims=True) for x in near]
        if past:
            total = [a + jnp.sum(x, axis=-1, keepdims=True) for a, x in zip(total, far)]
        share = [1.0 / a for a in total]
        near = [(x * a).astype(bf16) for x, a in zip(near, share)]
        if past:
            far = [(x * a).astype(bf16) for x, a in zip(far, share)]
        for h in range(2):
            weights = weights + dot(near[h], key_hot[h, span])
            if past:
                weights = weights + dot(far[h], key_hot[h, :past])
        for h in range(2):
            minus = -(top[h] + jnp.log(total[h]))
            high = minus.astype(bf16).astype(f32)
            middle = (minus - high).astype(bf16).astype(f32)
            rest = minus - high - middle
            value = jnp.where(small == HD + 3, rest, query[h].astype(f32))
            value = jnp.where(small == HD + 2, middle, value)
            query_o[h, span] = jnp.where(small == HD + 1, high, value).astype(bf16)
        weight_o[span] = weights
        own = weights if pair % 2 == 0 else pltpu.roll(weights, HD, 1)
        own = jnp.where(small < HD, own, 0.0)
        if i < seq // ROWS // 2:
            halves.append(own)
        else:
            k = i - seq // ROWS // 2
            low_o[k * ROWS : (k + 1) * ROWS] = (halves[k] + pltpu.roll(own, HD, 1)).astype(bf16)


def attention(pair, length, token_col, proj, cosine, sine, before, heads):
    seq = token_col.shape[0]
    vocab = proj.shape[0]
    o = jax.ShapeDtypeStruct
    return pl.pallas_call(
        functools.partial(attention_kernel, heads, pair),
        in_specs=[SMEM] + [VMEM] * 5,
        out_specs=[VMEM] * 4,
        out_shape=[
            o((2, seq, WIDE), bf16),
            o((2, seq, WIDE), bf16),
            o((seq, WIDE), f32),
            o((seq // 2, WIDE), bf16),
        ],
        scratch_shapes=[
            pltpu.VMEM((seq, WIDE), bf16),
            pltpu.VMEM((2, seq, WIDE), bf16),
            pltpu.VMEM((2, seq, WIDE), bf16),
            pltpu.VMEM((WIDE, 8 * WIDE), bf16),
        ],
        name="attention",
        **params(6),
    )(length, token_col, proj, cosine, sine, before)


def attention_back_kernel(
    heads,
    pair,
    token_col,
    token_row,
    query,
    key,
    weight,
    weight_grad,
    cosine,
    sine,
    cosine_t,
    sine_t,
    table_o,
    hot,
    mixed,
    query_grad,
    key_grad,
):
    seq = token_col.shape[0]
    vocab = table_o.shape[0]
    half = ROT // 2
    lane = lanes((seq, WIDE))
    hot[...] = jnp.where(
        (lane == token_col[...]) | (lane == token_col[...] + vocab) | ((lane >= HD) & (lane < HD + 3)),
        1.0,
        0.0,
    ).astype(bf16)
    grads = weight_grad[...]
    if heads * vocab < WIDE:
        grads = jnp.concatenate([grads, jnp.zeros((seq, WIDE - heads * vocab), f32)], axis=1)
    both = weight[...] * grads
    for n, h in enumerate((2 * pair, 2 * pair + 1)):
        inside = (lane >= h * vocab) & (lane < (h + 1) * vocab)
        minus = -jnp.sum(jnp.where(inside, both, 0.0), axis=-1, keepdims=True)
        own = grads if h == 0 else pltpu.roll(grads, WIDE - h * vocab, 1)
        own = jnp.where(lane < vocab, own, 0.0)
        high, rest = split2(own)
        m_high = minus.astype(bf16).astype(f32)
        m_middle = (minus - m_high).astype(bf16).astype(f32)
        m_rest = minus - m_high - m_middle
        value = high.astype(f32) + pltpu.roll(rest.astype(f32), vocab, 1)
        value = jnp.where(lane == HD, m_high, value)
        value = jnp.where(lane == HD + 1, m_middle, value)
        value = jnp.where(lane == HD + 2, m_rest, value)
        mixed[n] = value.astype(bf16)
    allowed = lanes((ROWS, ROWS)) <= sublanes((ROWS, ROWS))
    key_grad[...] = jnp.zeros_like(key_grad)
    both = range(2)
    for i in range(seq // ROWS):
        span = slice(i * ROWS, (i + 1) * ROWS)
        past = i * ROWS
        part = [query[n, span] for n in both]
        near = [dot(part[n], key[n, span], NT) for n in both]
        slope = [dot(mixed[n, span], hot[span], NT) for n in both]
        if past:
            far = [dot(part[n], key[n, :past], NT) for n in both]
            far_slope = [dot(mixed[n, span], hot[:past], NT) for n in both]
        near = [jnp.where(allowed, jnp.exp(x), 0.0) for x in near]
        near = [(x * y).astype(bf16) for x, y in zip(near, slope)]
        if past:
            far = [(jnp.exp(x) * y).astype(bf16) for x, y in zip(far, far_slope)]
        grad = [dot(near[n], key[n, span]) for n in both]
        if past:
            grad = [grad[n] + dot(far[n], key[n, :past]) for n in both]
        for n in both:
            key_grad[n, :, span] += dot(part[n], near[n], TN)[:HD]
            if past:
                key_grad[n, :, :past] += dot(part[n], far[n], TN)[:HD]
        for n in both:
            x = grad[n] * 0.125
            query_grad[n, span] = (x * cosine[span] - turned(x) * sine[span]).astype(bf16)
    shape = (vocab, seq)
    token_hot = jnp.where(sublanes(shape) == token_row[...], 1.0, 0.0).astype(bf16)
    small = lanes((vocab, WIDE)) < HD
    cos_t, sin_t = cosine_t[...], sine_t[...]
    one = dot(token_hot, query_grad[0])
    two = pltpu.roll(dot(token_hot, query_grad[1]), HD, 1)
    table_o[:, :WIDE] = jnp.where(small, one, two)
    turned_keys = []
    for n in range(2):
        front, back = key_grad[n, :half], key_grad[n, half:ROT]
        turned_keys += [front * cos_t + back * sin_t, back * cos_t - front * sin_t, key_grad[n, ROT:]]
    keys = jnp.concatenate(turned_keys, axis=0).astype(bf16)
    table_o[:, WIDE:] = dot(token_hot, keys, NT)


def attention_back(
    pair, token_col, token_row, query, key, weight, weight_grad, cosine, sine, cosine_t, sine_t, heads
):
    seq = token_col.shape[0]
    vocab = weight_grad.shape[1] // heads
    full = lambda array: pl.BlockSpec(array.shape, lambda i: (0,) * array.ndim)
    two = full(query)
    return pl.pallas_call(
        functools.partial(attention_back_kernel, heads, pair),
        grid=(1,),
        in_specs=[full(token_col), full(token_row), two, two, full(weight), full(weight_grad)]
        + [full(table) for table in (cosine, sine, cosine_t, sine_t)],
        out_specs=pl.BlockSpec((vocab, 2 * WIDE), lambda i: (0, 0)),
        out_shape=jax.ShapeDtypeStruct((vocab, 2 * WIDE), f32),
        scratch_shapes=[
            pltpu.VMEM((seq, WIDE), bf16),
            pltpu.VMEM((2, seq, WIDE), bf16),
            pltpu.VMEM((2, seq, WIDE), bf16),
            pltpu.VMEM((2, HD, seq), f32),
        ],
        name="attention_back",
        **params(6),
    )(token_col, token_row, query, key, weight, weight_grad, cosine, sine, cosine_t, sine_t)


def loss_kernel(
    parts,
    members,
    heads,
    ints,
    floats,
    token_col,
    target_col,
    token_row,
    embed,
    head,
    vec,
    *refs,
):
    pairs = heads // 2
    weights, refs = refs[: pairs * parts], refs[pairs * parts :]
    pieces, refs = refs[:members], refs[members:]
    keep_o, send_o, grad_o, sums_o, mixing, low_weights, table, down = refs
    step = pl.program_id(0)
    me, length, member = ints[0], ints[1], ints[2]
    vocab = embed.shape[0]
    height = heads * vocab

    @pl.when(step == 0)
    def _():
        rows_v, rows_f = segments_of(heads, members)
        small_v = min(rows_v, HB)
        for r in range(members):
            owner = member ^ r
            piece = pieces[r]
            for place in range(parts):
                for u in range(rows_v // small_v):
                    row = owner * rows_v + u * small_v
                    block, inside = row // HB, row % HB
                    i, k = block // (D // BS), block % (D // BS)
                    at = place * rows_v + u * small_v
                    mixing[
                        me ^ place,
                        pl.ds(pl.multiple_of(i * HB + inside, 32), small_v),
                        pl.ds(pl.multiple_of(k * BS, BS), BS),
                    ] = piece[at : at + small_v]
            at = parts * rows_v
            one, two, three = (
                piece[at + n * rows_f : at + (n + 1) * rows_f].astype(f32) for n in range(3)
            )
            row = owner * rows_f
            down[
                pl.ds(pl.multiple_of(row % vocab, 8), rows_f),
                pl.ds(pl.multiple_of(row // vocab * BS, BS), BS),
            ] = one + (two + three)
        table[...] = stack_parts(embed[...] + (down[...] + vec[2:3]))
        sums_o[...] = jnp.zeros_like(sums_o)

    second = step >= pl.num_programs(0) // 2
    small = lanes((ROWS, WIDE)) < HD

    def weights_of(r):
        value = weights[r][...].astype(f32)
        turned_value = pltpu.roll(value, HD, 1)
        value = jnp.where(second, turned_value, value)
        if pairs == 1:
            return jnp.where(small, value, 0.0)
        other = weights[parts + r][...].astype(f32)
        other = jnp.where(second, other, pltpu.roll(other, HD, 1))
        return jnp.where(small, value, other)

    own = weights_of(0)
    low_weights[me] = own.astype(bf16)[:, :height]
    for r in range(1, parts):
        low_weights[me ^ r] = weights_of(r).astype(bf16)[:, :height]
    token = token_col[...]
    hot = jnp.where(lanes((ROWS, WIDE)) % vocab == token, 1.0, 0.0).astype(bf16)
    x = dot(hot, table[...])
    x = x + dot(
        jnp.concatenate([low_weights[g] for g in range(parts)], axis=1),
        jnp.concatenate([mixing[g] for g in range(parts)], axis=0),
    )
    normed, scale = stats_of(x)
    gain = vec[3:4]
    final = (normed * gain + vec[4:5]).astype(bf16)
    head_low = head[:, :D].astype(bf16)
    square = (vocab, vocab)
    bias_row = jnp.sum(
        jnp.where(lanes(square) == sublanes(square), head[:, D : D + 1], 0.0), axis=0, keepdims=True
    )
    logits = dot(final, head_low, NT) + bias_row
    shifted = logits - jnp.max(logits, axis=-1, keepdims=True)
    log_probs = shifted - jnp.log(jnp.sum(jnp.exp(shifted), axis=-1, keepdims=True))
    target = lanes((ROWS, vocab)) == target_col[...]
    position = step * ROWS + sublanes((ROWS, 1))
    slot_weight = jnp.where(position < length - 1, floats[0], 0.0)
    picked = jnp.sum(jnp.where(target, log_probs, 0.0), axis=-1, keepdims=True)
    loss = -jnp.sum(slot_weight * picked, keepdims=True)
    logit_grad = ((jnp.exp(log_probs) - jnp.where(target, 1.0, 0.0)) * slot_weight).astype(bf16)
    final_grad = dot(logit_grad, head_low)
    grad = norm_back(final_grad, normed, scale, gain)
    high = grad.astype(bf16)
    token_hot = jnp.where(sublanes((vocab, ROWS)) == token_row[...], 1.0, 0.0).astype(bf16)
    both = dot(jnp.concatenate([own.T.astype(bf16), token_hot], axis=0), high)
    sums_o[0:vocab] += both[WIDE:]
    sums_o[vocab : 2 * vocab] += dot(logit_grad, final, TN)
    base = 2 * vocab
    sums_o[base : base + 1] += jnp.sum(final_grad * normed, axis=0, keepdims=True)
    sums_o[base + 1 : base + 2] += jnp.sum(final_grad, axis=0, keepdims=True)
    bias_grad = jnp.sum(logit_grad.astype(f32), axis=0, keepdims=True)
    sums_o[base + 2 : base + 3, :vocab] += bias_grad
    lane = lanes((1, WIDE))
    count = jnp.where((step == 0) & (length >= 2), 1.0, 0.0)
    sums_o[base + 3 : base + 4, :WIDE] += jnp.where(
        lane == 0, loss, jnp.where(lane == 1, count, 0.0)
    )
    sums_o[base + 16 : base + 16 + height] += both[:height]
    grad_o[...] = dot(high, mixing[me], NT)

    @pl.when(step == pl.num_programs(0) - 1)
    def _():
        deal(member & 1, sums_o, keep_o, send_o)


def loss_rows(
    ints,
    floats,
    token_col,
    target_col,
    token_row,
    embedding,
    head,
    vectors,
    weights,
    pieces,
    heads,
):
    seq = token_col.shape[0]
    vocab = embedding.shape[0]
    parts = len(weights) // (heads // 2)
    height = heads * vocab
    blocks = seq // ROWS // 2
    col = pl.BlockSpec((ROWS, 1), lambda i: (i, 0))
    o = jax.ShapeDtypeStruct
    full = lambda array: pl.BlockSpec(array.shape, lambda i: (0,) * array.ndim)
    sums_shape = (2 * vocab + 16 + height, D)
    return pl.pallas_call(
        functools.partial(loss_kernel, parts, len(pieces), heads),
        grid=(seq // ROWS,),
        in_specs=[SMEM, SMEM, col, col, pl.BlockSpec((1, ROWS), lambda i: (0, i))]
        + [full(embedding), full(head), full(vectors)]
        + [pl.BlockSpec((ROWS, WIDE), lambda i: (i % blocks, 0))] * len(weights)
        + [full(pieces[0])] * len(pieces),
        out_specs=[
            pl.BlockSpec((sums_shape[0] // 2, D), lambda i: (0, 0)),
            pl.BlockSpec((sums_shape[0] // 2, D), lambda i: (0, 0)),
            pl.BlockSpec((ROWS, height), lambda i: (i, 0)),
        ],
        out_shape=[o((sums_shape[0] // 2, D), f32)] * 2 + [o((seq, height), f32)],
        scratch_shapes=[
            pltpu.VMEM(sums_shape, f32),
            pltpu.VMEM((parts, height, D), bf16),
            pltpu.VMEM((parts, ROWS, height), bf16),
            pltpu.VMEM((4 * vocab, D), bf16),
            pltpu.VMEM((vocab, D), f32),
        ],
        name="loss_rows",
        **params(12),
    )(
        ints,
        floats,
        token_col,
        target_col,
        token_row,
        embedding,
        head,
        vectors,
        *weights,
        *pieces,
    )


def padded(block):
    lacking = HB - block.shape[0]
    if lacking:
        block = jnp.concatenate([block, jnp.zeros((lacking, block.shape[1]), block.dtype)], axis=0)
    return block


def put_left(ref, index, block):
    ref[index] = jnp.concatenate([padded(block)] * 3, axis=0).astype(bf16)


def put_right(ref, index, block):
    ref[index] = jnp.concatenate(split3(padded(block)), axis=0)


def factors_kernel(
    heads,
    ints,
    owner,
    mine,
    other,
    gathered,
    upper,
    normed,
    act,
    values,
    left_o,
    right_o,
    hidden_o,
    bias_o,
    small_o,
    part_o,
    sums,
    tiles,
    sem,
    *mats,
):
    vocab = normed.shape[0]
    width = upper.shape[1]
    copy = pltpu.make_async_copy(gathered, tiles, sem)
    copy.start()
    join(ints[0] & 1, mine, other, sums)
    small_o[...] = sums[: small_o.shape[0]]
    rows = sums[0:vocab]
    mixed = sums[2 * vocab + 16 :]
    low = normed[...].astype(f32)
    own = act[...].astype(f32)
    val = values[...].astype(f32)
    normed_gram = dot6(low, low, NT)
    square = jnp.sum(dot6(own, own, NT) * dot6(rows, rows, NT), keepdims=True) + jnp.sum(
        dot6(val, val, NT) * dot6(mixed, mixed, NT), keepdims=True
    )
    across = D // BS
    f_rows = width // BS
    pair = 2 * vocab
    for i in range(across):
        put_left(left_o, i, low[:, i * BS : (i + 1) * BS])
    for i in range(f_rows):
        put_left(left_o, across + i, own[:, i * BS : (i + 1) * BS])
    for i in range(heads // 2):
        put_left(
            left_o,
            across + f_rows + i,
            val[i * pair : (i + 1) * pair, i * BS : (i + 1) * BS],
        )
    at = heads * HD // BS
    for i in range(heads // 2):
        for k in range(across):
            put_right(right_o, at, mixed[i * pair : (i + 1) * pair, k * BS : (k + 1) * BS])
            at += 1
    for k in range(across):
        put_right(right_o, at + f_rows + k, rows[:, k * BS : (k + 1) * BS])
    copy.wait()
    for index, (which, i, k) in enumerate(tile_places(layer_shapes(heads, width))):
        mats[which][i * BS : (i + 1) * BS, k * BS : (k + 1) * BS] = tiles[owner[index]]
    mat_q, mat_o, mat_u, mat_f = mats
    part_o[...] = mat_q[:, : 2 * heads * HD]
    act_grad = rows_times_low(rows, mat_f[...], NT)
    u = upper[...]
    tanh = jnp.tanh(GELU_A * (u + GELU_B * (u * u * u)))
    slope = 0.5 * (1.0 + tanh) + 0.5 * u * (1.0 - tanh * tanh) * (
        GELU_A * (1.0 + 3.0 * GELU_B * (u * u))
    )
    upper_grad = act_grad * slope
    bias_grad = jnp.sum(upper_grad, axis=0, keepdims=True)
    bias_o[...] = bias_grad
    value_grad = rows_times_low(mixed, mat_o[...], NT)
    shape = value_grad.shape
    value_grad = jnp.where(sublanes(shape) // vocab == lanes(shape) // HD, value_grad, 0.0)
    value_table = value_grad[:vocab]
    for h in range(1, heads):
        value_table = value_table + value_grad[h * vocab : (h + 1) * vocab]
    hidden_o[0:vocab] = rows_times_low(upper_grad, mat_u[...], NT) + rows_times_low(
        value_table, mat_q[:, 2 * heads * HD :], NT
    )
    square = (
        square
        + jnp.sum(
            normed_gram
            * (dot6(value_table, value_table, NT) + dot6(upper_grad, upper_grad, NT)),
            keepdims=True,
        )
        + jnp.sum(bias_grad * bias_grad, keepdims=True)
    )
    hidden_o[vocab : vocab + 16] = jnp.broadcast_to(square, (16, D))
    for k in range(heads * HD // BS):
        put_right(right_o, k, value_table[:, k * BS : (k + 1) * BS])
    for k in range(f_rows):
        put_right(right_o, at + k, upper_grad[:, k * BS : (k + 1) * BS])


def rest_kernel(pairs, ints, mine, other, hidden, mat_q, normed, right_o, hidden_o, half_o, table):
    vocab = normed.shape[0]
    join(ints[0] & 1, mine, other, table)
    blocks = [table[p * vocab : (p + 1) * vocab, :WIDE] for p in range(pairs)]
    blocks += [table[p * vocab : (p + 1) * vocab, WIDE:] for p in range(pairs)]
    grad = jnp.concatenate(blocks, axis=1)
    for k, block in enumerate(blocks):
        put_right(right_o, k, block)
    low = normed[...].astype(f32)
    square = jnp.sum(dot6(low, low, NT) * dot6(grad, grad, NT), keepdims=True)
    hidden_o[0:vocab] = hidden[0:vocab] + rows_times_low(grad, mat_q[...], NT)
    hidden_o[vocab:] = hidden[vocab:] + square
    size = half_o.shape[0]
    half_o[...] = hidden_o[pl.ds(pl.multiple_of((ints[0] & 1) * size, size), size)]


def factor_places(heads, ff_local):
    q_cols = 3 * heads * HD // BS
    o_rows = heads // 2
    across = D // BS
    f_rows = ff_local // BS
    left, right = [], []
    for which, i, k in tile_places(layer_shapes(heads, ff_local)):
        if which == 0:
            left.append(i)
            right.append(k)
        elif which == 1:
            left.append(across + f_rows + i)
            right.append(q_cols + i * across + k)
        elif which == 2:
            left.append(i)
            right.append(q_cols + o_rows * across + k)
        else:
            left.append(across + i)
            right.append(q_cols + o_rows * across + f_rows + k)
    return np.array(left, np.int32), np.array(right, np.int32)


def factors(ints, owner, mine, other, tiles, upper, normed, act, values, heads):
    vocab = normed.shape[0]
    ff_local = upper.shape[1]
    n_left = D // BS + ff_local // BS + heads // 2
    n_right = heads * HD // BS + heads // 2 * (D // BS) + ff_local // BS + D // BS
    o = jax.ShapeDtypeStruct
    return pl.pallas_call(
        functools.partial(factors_kernel, heads),
        in_specs=[SMEM] * 2 + [VMEM] * 2 + [ANY] + [VMEM] * 4,
        out_specs=[VMEM] * 6,
        out_shape=[
            o((n_left, 3 * HB, BS), bf16),
            o((n_right, 3 * HB, BS), bf16),
            o((vocab + 16, D), f32),
            o((1, ff_local), f32),
            o((2 * vocab + 16, D), f32),
            o((D, 2 * heads * HD), bf16),
        ],
        scratch_shapes=[
            pltpu.VMEM((2 * mine.shape[0], D), f32),
            pltpu.VMEM(tiles.shape, bf16),
            pltpu.SemaphoreType.DMA,
        ]
        + [pltpu.VMEM(shape, bf16) for shape in layer_shapes(heads, ff_local)],
        name="factors",
        **params(7, 24),
    )(ints, owner, mine, other, tiles, upper, normed, act, values)


def factors_rest(ints, mine, other, hidden, mat_q, normed, heads):
    o = jax.ShapeDtypeStruct
    pairs = heads // 2
    return pl.pallas_call(
        functools.partial(rest_kernel, pairs),
        in_specs=[SMEM] + [VMEM] * 5,
        out_specs=[VMEM] * 3,
        out_shape=[
            o((2 * pairs, 3 * HB, BS), bf16),
            o(hidden.shape, f32),
            o((hidden.shape[0] // 2, D), f32),
        ],
        scratch_shapes=[pltpu.VMEM((2 * mine.shape[0], 2 * WIDE), f32)],
        name="factors_rest",
        **params(2),
    )(ints, mine, other, hidden, mat_q, normed)


def small_kernel(parts, corrections, ints, sums, own, *refs):
    mine, others, refs = refs[: parts - 1], refs[parts - 1 : 2 * parts - 2], refs[2 * parts - 2 :]
    bias_grad, refs = refs[0], refs[1:]
    weights, refs = refs[:12], refs[12:]
    outs, scalars, total = refs[:12], refs[12], refs[13]
    vocab = weights[0].shape[0]
    base = 2 * vocab
    size = own.shape[0] // 2
    for place, group in ((ints[0], mine), (1 - ints[0], others)):
        span = pl.ds(pl.multiple_of(place * size, size), size)
        total[span] = tree_sum([own[span]] + [ref[...] for ref in group])
    hidden = total[:vocab]
    square = total[vocab : vocab + 1, 0:1]
    rows = sums[0:vocab]
    normed, scale = stats_of(weights[0][...])
    gain = weights[6][0:1]
    embed_grad = rows + norm_back(hidden, normed, scale, gain)
    vector_grad = jnp.concatenate(
        [
            jnp.sum(hidden * normed, axis=0, keepdims=True),
            jnp.sum(hidden, axis=0, keepdims=True),
            jnp.sum(rows, axis=0, keepdims=True),
            sums[base : base + 1],
            sums[base + 1 : base + 2],
        ],
        axis=0,
    )
    head_grad = sums[vocab : 2 * vocab]
    head_bias = sums[base + 2 : base + 3, :vocab]
    add = lambda value: jnp.sum(value * value, keepdims=True)
    square = square + add(embed_grad) + add(vector_grad) + add(head_grad) + add(head_bias)
    count = sums[base + 3 : base + 4, 1:2]
    loss = sums[base + 3 : base + 4, 0:1] / count
    norm = jnp.sqrt(square) / count
    scale_all = jnp.minimum(1.0, CLIP_NORM / norm) / count
    one, two = corrections[0], corrections[1]

    def update(index, pick, grad):
        weight, first, second = (weights[3 * index + k][pick] for k in range(3))
        grad = grad * scale_all
        first = BETA_ONE * first + (1.0 - BETA_ONE) * grad
        second = BETA_TWO * second + (1.0 - BETA_TWO) * grad * grad
        step = first / one / (jnp.sqrt(second / two) + ADAM_EPS)
        outs[3 * index][pick] = weight - RATE_SMALL * (step + WEIGHT_DECAY * weight)
        outs[3 * index + 1][pick] = first
        outs[3 * index + 2][pick] = second

    everything = slice(None)
    update(0, everything, embed_grad)
    shape = (vocab, vocab)
    head_column = jnp.sum(
        jnp.where(lanes(shape) == sublanes(shape), head_bias, 0.0), axis=1, keepdims=True
    )
    update(1, (everything, slice(0, D)), head_grad)
    update(1, (everything, slice(D, D + 1)), head_column)
    update(2, everything, vector_grad)
    update(3, everything, bias_grad[...])
    lane = lanes((1, WIDE))
    scalars[...] = jnp.where(
        lane == 0, scale_all, jnp.where(lane == 1, loss, jnp.where(lane == 2, norm, 0.0))
    )


def small(corrections, upper, sums, hidden, mine, others, bias_grad, weights):
    o = jax.ShapeDtypeStruct
    return pl.pallas_call(
        functools.partial(small_kernel, 1 + len(mine)),
        in_specs=[SMEM] * 2 + [VMEM] * (2 + 2 * len(mine) + 1 + 12),
        out_specs=[VMEM] * 13,
        out_shape=[o(weight.shape, f32) for weight in weights] + [o((1, WIDE), f32)],
        scratch_shapes=[pltpu.VMEM(hidden.shape, f32)],
        name="small",
        **params(4),
    )(corrections, upper, sums, hidden, *mine, *others, bias_grad, *weights)


QB = 32
UNQ = 12
PER = 6


def take(value, at):
    return jnp.take_along_axis(value, at, axis=1, mode="promise_in_bounds")


def eliminate(packed, count):
    shape = (8, BS)
    lane, sub = lanes(shape), sublanes(shape)
    start = lane // QB * QB
    span = range(count)
    for p in range(QB // 8):
        r0 = 8 * p

        def body(step, carry):
            jj = 2 * step
            j = r0 + jj
            pick, pick_two = start + j, start + (j + 1)
            mark, mark_two = lane == pick, lane == pick_two
            below, below_two = sub > jj, sub > jj + 1
            wide = [jnp.broadcast_to(packed[t, pl.ds(j, 1), :], shape) for t in span]
            next_wide = [jnp.broadcast_to(packed[t, pl.ds(j + 1, 1), :], shape) for t in span]
            kept = [[packed[t, 8 * q : 8 * q + 8, :] for q in range(p, QB // 8)] for t in span]
            pivot = [take(w, pick) for w in wide]
            right = [take(w, pick_two) for w in wide]
            lower = [take(w, pick) for w in next_wide]
            corner = [take(w, pick_two) for w in next_wide]
            ones = [[take(a, pick) for a in group] for group in kept]
            twos = [[take(a, pick_two) for a in group] for group in kept]
            inverse = [1.0 / d for d in pivot]
            ratio = [b * i for b, i in zip(right, inverse)]
            inverse_two = [1.0 / (e - b * r) for e, b, r in zip(corner, lower, ratio)]
            scaled = [jnp.where(mark, 1.0, w) * i for w, i in zip(wide, inverse)]
            scaled_two = [
                jnp.where(mark_two, 1.0, jnp.where(mark, 0.0, w) - b * x) * i
                for w, b, x, i in zip(next_wide, lower, scaled, inverse_two)
            ]
            for t in span:
                for k, q in enumerate(range(p, QB // 8)):
                    a, c, d = kept[t][k], ones[t][k], twos[t][k]
                    d = d - c * ratio[t]
                    first = jnp.where(mark, 0.0, a) - c * scaled[t]
                    if k == 0:
                        first = jnp.where(below, first, a)
                    second = jnp.where(mark_two, 0.0, first) - d * scaled_two[t]
                    if k == 0:
                        second = jnp.where(below_two, second, first)
                    packed[t, 8 * q : 8 * q + 8, :] = second
            return carry

        lax.fori_loop(0, 4, body, 0)


def part_inverse(packed):
    shape = (QB, BS)
    lane, sub = lanes(shape), sublanes(shape)
    part, col = lane // QB, lane % QB
    diagonal = jnp.where(col == sub, packed, 0.0)
    pivot = jnp.ones(shape, f32)
    for k in range(BS // QB):
        own = jnp.sum(jnp.where(part == k, diagonal, 0.0), axis=1, keepdims=True)
        pivot = jnp.where(part == k, own, pivot)
    unit = jnp.where(col < sub, packed, jnp.where(col == sub, 1.0, 0.0))
    return unit * lax.rsqrt(pivot)


def inverse_factors(gram, packed, result, count):
    parts = BS // QB
    unroll = next(k for k in (UNQ, 3, 2, 1) if count % k == 0)
    lane32, sub32 = lanes((QB, BS)), sublanes((QB, BS))
    for b in range(parts):
        begin = b * QB
        below = begin + QB
        rows = slice(begin, below)
        here = lane32 // QB == b

        def pack(i, carry):
            for t in [i * unroll + k for k in range(unroll)]:
                value = jnp.zeros((QB, BS), f32)
                for k in range(parts):
                    block = gram[parts * t + k, rows, :]
                    if k != b:
                        block = pltpu.roll(block, (k * QB + BS - begin) % BS, 1)
                    value = jnp.where(lane32 // QB == k, block, value)
                packed[t] = value
            return carry

        lax.fori_loop(0, count // unroll, pack, 0)
        eliminate(packed, count)

        def spread(i, carry):
            groups = [i * unroll + k for k in range(unroll)]
            inverses = [part_inverse(packed[t]) for t in groups]
            firsts = [
                jnp.concatenate([jnp.where(lane32 // QB == k, x, 0.0) for k in range(parts)], axis=0)
                for x in inverses
            ]
            unit = jnp.where(lane32 - begin == sub32, 1.0, 0.0)
            panels = [
                jnp.concatenate(
                    [jnp.where(here, unit, gram[parts * t + k, rows, :]) for k in range(parts)],
                    axis=0,
                )
                for t in groups
            ]
            news = [dot6(x, y, NN) for x, y in zip(firsts, panels)]
            for t, new in zip(groups, news):
                for k in range(parts):
                    value = new[k * QB : (k + 1) * QB]
                    result[parts * t + k, rows, :] = (
                        jnp.where(lane32 < below, value, 0.0) if below < BS else value
                    )
            if below < BS:
                for t, new in zip(groups, news):
                    mats = [new[k * QB : (k + 1) * QB] for k in range(parts)]
                    changes = [dot6(x, x, TN) for x in mats]
                    shape = (BS - below, BS)
                    mark = lanes(shape) // QB == b
                    for k in range(parts):
                        old = gram[parts * t + k, below:, :]
                        gram[parts * t + k, below:, :] = jnp.where(mark, 0.0, old) - changes[k][below:]
            return carry

        lax.fori_loop(0, count // unroll, spread, 0)


def tile_params(count, per):
    blk = pl.BlockSpec((per, BS, BS), lambda i: (i, 0, 0))
    full = pl.BlockSpec((count, BS, BS), lambda i: (0, 0, 0))
    return blk, full, lambda dt: jax.ShapeDtypeStruct((count, BS, BS), dt)


def gradient_kernel(per, rest, natural, left_at, right_at, lefts, rights, more, L, R, QL, QR, *outs):
    step = pl.program_id(0)
    span = range(per)
    pairs = []
    for s in span:
        tile = natural[step * per + s]
        at = right_at[tile]
        right = jnp.where(
            at < rest, more[jnp.minimum(at, rest - 1)], rights[jnp.maximum(at - rest, 0)]
        )
        pairs.append((lefts[left_at[tile]], right))
    g = [dot(a, b, TN) for a, b in pairs]
    gt = [dot(b, a, TN) for a, b in pairs]
    qt = [QL[s].T for s in span]
    left = [dot3(x, x, NT) for x in g]
    right = [dot3(x, x, NT) for x in gt]
    rot = [dot3(q, x, NN) for q, x in zip(qt, g)]
    mixed_left = [dot3(left[s], QL[s], NN) for s in span]
    mixed_right = [dot3(right[s], QR[s], NN) for s in span]
    rot = [dot3(rot[s], QR[s], NN) for s in span]
    old_left = [dot6(L[s], QL[s], NN) for s in span]
    old_right = [dot6(R[s], QR[s], NN) for s in span]
    for s in span:
        for out, value in zip(
            outs, (left, right, rot, mixed_left, mixed_right, old_left, old_right)
        ):
            out[s] = value[s]


def gradient_products(natural, left_at, right_at, lefts, rights, more, L, R, QL, QR):
    count = QL.shape[0]
    blk, _, o = tile_params(count, PER)
    whole = lambda x: pl.BlockSpec(x.shape, lambda i: (0, 0, 0))
    return pl.pallas_call(
        functools.partial(gradient_kernel, PER, more.shape[0]),
        grid=(count // PER,),
        in_specs=[SMEM] * 3 + [whole(lefts), whole(rights), whole(more)] + [blk] * 4,
        out_specs=[blk] * 7,
        out_shape=[o(f32)] * 7,
        name="gradient_products",
        **params(9),
    )(natural, left_at, right_at, lefts, rights, more, L, R, QL, QR)


def soap_kernel(
    count, per, corrections, scal, GL, GR, GT, BL, BR, AL, AR, W, m, v, L, R, QL, QR,
    W_o, low_o, m_o, v_o, L_o, R_o, QL_o, QR_o, ML_s, MR_s, work, inv_s, packed,
):
    step = pl.program_id(0)
    scale = scal[0:1, 0:1]
    c1, c2 = corrections[0], corrections[1]
    span = range(per)
    share = (1 - BETA_TWO) * (scale * scale)
    xs = []
    for s in span:
        rot = GT[s] * scale
        mn = BETA_ONE * m[s] + (1 - BETA_ONE) * rot
        vn = BETA_TWO * v[s] + (1 - BETA_TWO) * rot * rot
        m_o[s] = mn
        v_o[s] = vn
        xs.append((mn / c1) / (jnp.sqrt(vn / c2) + ADAM_EPS))
    ML = [BETA_TWO * AL[s] + share * BL[s] for s in span]
    MR = [BETA_TWO * AR[s] + share * BR[s] for s in span]
    back = [dot3(QL[s], xs[s], NN) for s in span]
    ML = [x * lax.rsqrt(jnp.sum(x * x, keepdims=True)) for x in ML]
    MR = [x * lax.rsqrt(jnp.sum(x * x, keepdims=True)) for x in MR]
    back = [dot3(back[s], QR[s], NT) for s in span]
    gram_left = [dot6(x, x, TN) for x in ML]
    gram_right = [dot6(x, x, TN) for x in MR]
    for s in span:
        L_o[s] = BETA_TWO * L[s] + share * GL[s]
        R_o[s] = BETA_TWO * R[s] + share * GR[s]
        w = W[s]
        wn = w - RATE_TILES * (back[s] + WEIGHT_DECAY * w)
        W_o[s] = wn
        low_o[s] = wn.astype(bf16)
        t = step * per + s
        ML_s[t] = ML[s]
        MR_s[t] = MR[s]
        work[2 * t] = gram_left[s]
        work[2 * t + 1] = gram_right[s]

    @pl.when(step == pl.num_programs(0) - 1)
    def _():
        inverse_factors(work, packed, inv_s, count // 2)
        unroll = next(k for k in (8, 6, 3, 1) if count % k == 0)

        def last(i, carry):
            ts = [i * unroll + k for k in range(unroll)]
            ol = [dot3(ML_s[t], inv_s[2 * t], NT) for t in ts]
            orr = [dot3(MR_s[t], inv_s[2 * t + 1], NT) for t in ts]
            for t, a, b in zip(ts, ol, orr):
                QL_o[t] = a
                QR_o[t] = b
            return carry

        lax.fori_loop(0, count // unroll, last, 0)


def soap(corrections, scal, products, W, m, v, L, R, QL, QR):
    count = W.shape[0]
    blk, full, o = tile_params(count, PER)
    return pl.pallas_call(
        functools.partial(soap_kernel, count, PER),
        grid=(count // PER,),
        in_specs=[SMEM, pl.BlockSpec((1, WIDE), lambda i: (0, 0))] + [blk] * 14,
        out_specs=[blk] * 6 + [full] * 2,
        out_shape=[o(f32), o(bf16), o(f32), o(f32), o(f32), o(f32), o(f32), o(f32)],
        scratch_shapes=[pltpu.VMEM((count, BS, BS), f32)] * 2
        + [pltpu.VMEM((2 * count, BS, BS), f32)] * 2
        + [pltpu.VMEM((count // 2, QB, BS), f32)],
        name="soap_tiles",
        **params(40, 36),
    )(corrections, scal, *products, W, m, v, L, R, QL, QR)


def local(
    tokens,
    lengths,
    tile_owner,
    step_count,
    weight_tiles,
    tiles_first,
    tiles_second,
    stats_left,
    stats_right,
    basis_left,
    basis_right,
    embedding,
    embedding_first,
    embedding_second,
    head_table,
    head_first,
    head_second,
    vectors,
    vectors_first,
    vectors_second,
    fc_bias,
    fc_bias_first,
    fc_bias_second,
):
    seq = tokens.shape[1]
    mp_count = lax.axis_size("mp")
    dp_count = lax.axis_size("dp")
    dp_index = lax.axis_index("dp")
    mp_index = lax.axis_index("mp")
    upper_pair = dp_index & 1
    heads = H // mp_count
    ff_local = fc_bias.shape[1]
    count = weight_tiles.shape[0]
    vocab = embedding.shape[0]
    own_index = dp_index[None]

    natural, low_tiles, normed, keep, send = first_tables(
        tile_owner, own_index, weight_tiles, embedding, vectors, heads, ff_local
    )
    token_col = tokens.reshape(seq, 1)
    target_col = jnp.roll(tokens, -1, axis=1).reshape(seq, 1)
    keep = keep + swap_with(send, "dp", 1)
    mine = direct(keep)
    low_tiles, mine = lax.optimization_barrier((low_tiles, mine))
    gathered = lax.all_gather(low_tiles, "dp", axis=0, tiled=True)
    proj, upper, act, values, keep, send = second_tables(
        natural, own_index, mine, swap_with(mine, "dp", 1), fc_bias, low_tiles, vocab, heads, dp_count
    )
    cosine, sine, cosine_t, sine_t = rotary_tables(seq)
    segment = sum(segments_of(heads, dp_count))
    places = range(1, dp_count // 2)
    received = [swap_with(send, "dp", 1)]
    queries, keys = [], []
    weight = jnp.zeros((8, WIDE), f32)
    for pair in range(heads // 2):
        query, key, weight, weight_low = attention(
            pair, lengths, token_col, proj, cosine, sine, weight, heads
        )
        queries.append(query)
        keys.append(key)
        if pair == 0:
            received, weight, weight_low = lax.optimization_barrier((received, weight, weight_low))
            keep = keep + received[0]
            received = [
                swap_with(keep[q * segment : (q + 1) * segment], "dp", 2 * q) for q in places
            ]
            keep, weight = lax.optimization_barrier((keep, weight))
            weights = gather_xor(weight_low, "mp")
    if heads > 2:
        more = gather_xor(weight_low, "mp")
        received, weights, more[0] = lax.optimization_barrier((received, weights, more[0]))
    mine = tree_sum([keep[:segment]] + list(received))
    packed = pack_segments(heads, dp_count, gather_xor(mine, "mp"))
    even = [packed] + [swap_with(packed, "dp", 2 * q) for q in places]
    if heads > 2:
        weights = weights + more
    odd = [swap_with(piece, "dp", 1) for piece in even]
    pieces = [piece for two in zip(even, odd) for piece in two]
    length = lengths[0]
    inverse_length = 1.0 / jnp.maximum(length - 1, 1).astype(f32)
    keep, send, weight_grad = loss_rows(
        jnp.stack([mp_index, length, dp_index]),
        inverse_length[None],
        token_col,
        target_col,
        tokens,
        embedding,
        head_table.T,
        vectors,
        weights,
        pieces,
        heads,
    )
    keep = keep + swap_with(send, "dp", 1)
    tables_back = []
    for pair in range(heads // 2):
        if pair == 1:
            weight_grad, keep = lax.optimization_barrier((weight_grad, keep))
        tables_back.append(
            attention_back(
                pair,
                token_col,
                tokens,
                queries[pair],
                keys[pair],
                weight,
                weight_grad,
                cosine,
                sine,
                cosine_t,
                sine_t,
                heads,
            )
        )
    mine = butterfly(keep)
    table = jnp.concatenate(tables_back, axis=0)
    half = table.shape[0] // 2
    first, second = table[:half], table[half:]
    is_upper = upper_pair == 1
    table = jnp.where(is_upper, second, first) + swap_with(
        jnp.where(is_upper, first, second), "dp", 1
    )
    table = direct(table)
    left, right, hidden, bias_grad, sums, mat_part = factors(
        own_index, tile_owner, mine, swap_with(mine, "dp", 1), gathered, upper, normed, act, values, heads
    )
    more, hidden, hidden_half = factors_rest(
        own_index, table, swap_with(table, "dp", 1), hidden, mat_part, normed, heads
    )
    hidden_parts = gather_halves(hidden_half)
    left_at, right_at = (jnp.asarray(places) for places in factor_places(heads, ff_local))
    gradients = gradient_products(
        natural, left_at, right_at, left, right, more, stats_left, stats_right, basis_left, basis_right
    )
    hidden_parts, gradients = lax.optimization_barrier((hidden_parts, gradients))
    hidden_others = swap_pair(hidden_parts)
    corrections = 1.0 - jnp.power(
        jnp.array([BETA_ONE, BETA_TWO], f32), step_count.astype(f32)
    )
    small_weights = (
        embedding,
        embedding_first,
        embedding_second,
        head_table.T,
        head_first.T,
        head_second.T,
        vectors,
        vectors_first,
        vectors_second,
        fc_bias,
        fc_bias_first,
        fc_bias_second,
    )
    *small_out, scalars = small(
        corrections,
        upper_pair[None],
        sums,
        hidden,
        hidden_parts,
        hidden_others,
        bias_grad,
        small_weights,
    )
    small_out[3:6] = [value.T for value in small_out[3:6]]
    results = soap(
        corrections,
        scalars,
        gradients,
        weight_tiles,
        tiles_first,
        tiles_second,
        stats_left,
        stats_right,
        basis_left,
        basis_right,
    )
    return (scalars[0, 1], scalars[0, 2], *results, *small_out)


def solution(mesh):
    tiled = P("dp", None, "mp")
    split = P(None, "mp")
    in_specs = (P("dp", None), P("dp"), P(), P(), *[tiled] * 7, *[P()] * 9, *[split] * 3)
    out_specs = (P(), P(), *[tiled] * 8, *[P()] * 9, *[split] * 3)
    return jax.shard_map(local, mesh=mesh, in_specs=in_specs, out_specs=out_specs, check_vma=False)
```

```python
import functools
import math

import jax
import jax.numpy as jnp
import numpy as np
from jax import lax
from jax.experimental import pallas as pl
from jax.experimental.pallas import tpu as pltpu
from jax.sharding import PartitionSpec as P

D = 1024
H = 16
HD = 64
ROT = 32
BS = 128
HB = 64
ROWS = 256
WIDE = 128
MEGA = 1024 * 1024

NORM_EPS = 1e-05
CLIP_NORM = 0.02
RATE_TILES = 0.02
RATE_SMALL = 0.2
BETA_ONE = 0.9
BETA_TWO = 0.95
ADAM_EPS = 1e-08
WEIGHT_DECAY = 0.01
MASKED = -1e30
GELU_A = math.sqrt(2.0 / math.pi)
GELU_B = 0.044715

NN = (((1,), (0,)), ((), ()))
NT = (((1,), (1,)), ((), ()))
TN = (((0,), (0,)), ((), ()))
f32 = jnp.float32
bf16 = jnp.bfloat16
SMEM = pl.BlockSpec(memory_space=pltpu.SMEM)
VMEM = pl.BlockSpec(memory_space=pltpu.VMEM)
ANY = pl.BlockSpec(memory_space=pl.ANY)


def dot(a, b, dims=NN):
    return lax.dot_general(a, b, dims, preferred_element_type=f32)


def split2(a):
    high = a.astype(bf16)
    return high, (a - high.astype(f32)).astype(bf16)


def split3(a):
    high = a.astype(bf16)
    rest = a - high.astype(f32)
    middle = rest.astype(bf16)
    return high, middle, (rest - middle.astype(f32)).astype(bf16)


def dot3(a, b, dims):
    (axis_a,), (axis_b,) = dims[0]
    ah, al = split2(a)
    bh, bl = split2(b)
    return dot(
        jnp.concatenate([ah, ah, al], axis=axis_a),
        jnp.concatenate([bh, bl, bh], axis=axis_b),
        dims,
    )


def dot6(a, b, dims):
    (axis_a,), (axis_b,) = dims[0]
    ah, am, al = split3(a)
    bh, bm, bl = split3(b)
    return dot(
        jnp.concatenate([ah, ah, am, am, ah, al], axis=axis_a),
        jnp.concatenate([bh, bm, bh, bm, bl, bh], axis=axis_b),
        dims,
    )


def rows_times_low(a, low, dims):
    count = a.shape[0]
    parts = dot(jnp.concatenate(split3(a), axis=0), low, dims)
    return parts[:count] + (parts[count : 2 * count] + parts[2 * count :])


def lanes(shape):
    return lax.broadcasted_iota(jnp.int32, shape, len(shape) - 1)


def sublanes(shape):
    return lax.broadcasted_iota(jnp.int32, shape, len(shape) - 2)


def stats_of(values):
    centred = values - jnp.mean(values, axis=-1, keepdims=True)
    spread = jnp.mean(centred * centred, axis=-1, keepdims=True)
    scale = lax.rsqrt(spread + NORM_EPS)
    return centred * scale, scale


def norm_back(grad, normed, scale, gain):
    inner = grad * gain
    mean_one = jnp.mean(inner, axis=-1, keepdims=True)
    mean_two = jnp.mean(inner * normed, axis=-1, keepdims=True)
    return scale * (inner - mean_one - normed * mean_two)


def params(microseconds, megabytes=20):
    return dict(
        compiler_params=pltpu.CompilerParams(vmem_limit_bytes=megabytes * MEGA),
        cost_estimate=pl.CostEstimate(
            flops=int(microseconds * 1.1e9), bytes_accessed=int(microseconds * 1e6), transcendentals=0
        ),
    )


def swap_with(value, axis, mask):
    count = lax.axis_size(axis)
    return lax.ppermute(value, axis, [(i, i ^ mask) for i in range(count)])


def tree_sum(parts):
    while len(parts) > 1:
        parts = [parts[i] + parts[i + 1] for i in range(0, len(parts), 2)]
    return parts[0]


def gather_xor(value, axis):
    return [value] + [swap_with(value, axis, r) for r in range(1, lax.axis_size(axis))]


def gather_halves(mine):
    return [swap_with(mine, "mp", r) for r in range(1, lax.axis_size("mp"))]


def swap_pair(parts):
    return [swap_with(part, "dp", 1) for part in parts]


def butterfly(kept):
    bits = [1 << k for k in range(1, lax.axis_size("dp").bit_length() - 1)]
    half = (kept.shape[0] // 2 + 7) // 8 * 8
    pieces = [kept[:half], kept[half:]]
    for k in range(len(bits)):
        received = [
            swap_with(piece, "dp", order[k])
            for piece, order in zip(pieces, (bits, bits[1:] + bits[:1]))
        ]
        pieces = [piece + other for piece, other in zip(pieces, received)]
    return jnp.concatenate(pieces, axis=0)


def direct(kept):
    return tree_sum([kept] + [swap_with(kept, "dp", r) for r in range(2, lax.axis_size("dp"), 2)])


def deal(upper, value, keep_o, send_o):
    half = keep_o.shape[0]

    @pl.when(upper == 0)
    def _():
        keep_o[...] = value[:half]
        send_o[...] = value[half : 2 * half]

    @pl.when(upper == 1)
    def _():
        keep_o[...] = value[half : 2 * half]
        send_o[...] = value[:half]


def join(upper, mine, other, whole):
    half = mine.shape[0]

    @pl.when(upper == 0)
    def _():
        whole[:half] = mine[...]
        whole[half:] = other[...]

    @pl.when(upper == 1)
    def _():
        whole[:half] = other[...]
        whole[half:] = mine[...]


def layer_shapes(heads_local, ff_local):
    return ((D, 3 * heads_local * HD), (heads_local * HD, D), (D, ff_local), (ff_local, D))


def tile_places(shapes):
    places = []
    for which, (row_total, col_total) in enumerate(shapes):
        for i in range(row_total // BS):
            for k in range(col_total // BS):
                places.append((which, i, k))
    return places


def first_places(heads, ff_local):
    q_cols = 3 * heads * HD // BS
    rows, blocks = [], []
    for which, i, k in tile_places(layer_shapes(heads, ff_local)):
        used = which in (0, 2)
        rows.append(i if used else 0)
        blocks.append(k if which == 0 else q_cols + k if which == 2 else q_cols + ff_local // BS)
    return np.array(rows, np.int32), np.array(blocks, np.int32)


def first_kernel(owner, ints, row_of, block_of, tiles, embed, vec, natural_o, low_o, normed_o, keep_o, send_o, rows, acc, held, sem):
    copy = pltpu.make_async_copy(tiles, held, sem)
    copy.start()
    count = tiles.shape[0]
    begin = ints[0] * count

    def find(b, carry):
        slot = owner[b] - begin
        natural_o[jnp.where((slot >= 0) & (slot < count), slot, count)] = b
        return carry

    lax.fori_loop(0, owner.shape[0], find, 0, unroll=8)
    normed, _ = stats_of(embed[...])
    low = (normed * vec[0:1] + vec[1:2]).astype(bf16)
    normed_o[...] = low
    for i in range(D // BS):
        rows[i] = low[:, i * BS : (i + 1) * BS]
    acc[...] = jnp.zeros_like(acc)
    copy.wait()
    for s in range(count):
        low_o[s] = held[s].astype(bf16)
    products = [dot(rows[row_of[natural_o[s]]], low_o[s]) for s in range(count)]
    for s in range(count):
        acc[block_of[natural_o[s]]] += products[s]
    half = keep_o.shape[0]
    for upper, first, second in ((0, keep_o, send_o), (1, send_o, keep_o)):

        @pl.when((ints[0] & 1) == upper)
        def _():
            first[...] = acc[:half]
            second[...] = acc[half : 2 * half]


def first_tables(owner, ints, tiles, embedding, vectors, heads, ff_local):
    vocab = embedding.shape[0]
    row_of, block_of = first_places(heads, ff_local)
    blocks = int(block_of.max())
    o = jax.ShapeDtypeStruct
    return pl.pallas_call(
        first_kernel,
        in_specs=[SMEM] * 4 + [ANY] + [VMEM] * 2,
        out_specs=[SMEM] + [VMEM] * 4,
        out_shape=[
            o((tiles.shape[0] + 1,), jnp.int32),
            o(tiles.shape, bf16),
            o((vocab, D), bf16),
            o(((blocks + 1) // 2, vocab, BS), f32),
            o(((blocks + 1) // 2, vocab, BS), f32),
        ],
        scratch_shapes=[
            pltpu.VMEM((D // BS, vocab, BS), bf16),
            pltpu.VMEM((blocks + 1, vocab, BS), f32),
            pltpu.VMEM(tiles.shape, f32),
            pltpu.SemaphoreType.DMA,
        ],
        name="first_tables",
        **params(4, 56),
    )(owner, ints, jnp.asarray(row_of), jnp.asarray(block_of), tiles, embedding, vectors)


def second_places(heads, ff_local):
    pairs, across = heads // 2, D // BS
    lefts, blocks = [], []
    for which, i, k in tile_places(layer_shapes(heads, ff_local)):
        lefts.append(i if which == 1 else pairs + i if which == 3 else 0)
        blocks.append(
            i * across + k if which == 1 else (pairs * across + k if which == 3 else pairs * across + across)
        )
    return np.array(lefts, np.int32), np.array(blocks, np.int32)


def segments_of(heads, dp_count):
    return heads // 2 * (D // BS) * HB // dp_count, 32 * (D // BS) // dp_count


def second_kernel(
    heads, dp_count, natural, ints, left_of, block_of, mine, other, bias, low,
    proj_o, upper_o, act_o, values_o, keep_o, send_o, total, lefts, acc,
):
    vocab = proj_o.shape[0]
    me = ints[0]
    count = low.shape[0]
    pairs = heads // 2
    q_cols = 3 * heads * HD // BS
    f_rows = upper_o.shape[1] // BS
    across = D // BS
    join(me & 1, mine, other, total)
    for j in range(q_cols):
        proj_o[:, j * BS : (j + 1) * BS] = total[j]
    upper = jnp.concatenate([total[q_cols + j] for j in range(f_rows)], axis=1)
    upper = upper + bias[...]
    upper_o[...] = upper
    act = 0.5 * upper * (1.0 + jnp.tanh(GELU_A * (upper + GELU_B * (upper * upper * upper))))
    act = act.astype(bf16).astype(f32)
    act_o[...] = act.astype(bf16)
    values = proj_o[:, 2 * heads * HD :]
    shape = (heads * vocab, heads * HD)
    values = jnp.concatenate([values] * heads, axis=0)
    values = jnp.where(sublanes(shape) // vocab == lanes(shape) // HD, values, 0.0)
    values_o[...] = values.astype(bf16)
    for i in range(pairs):
        lefts[i] = values[i * HB : (i + 1) * HB, i * BS : (i + 1) * BS].astype(bf16)
    for i in range(f_rows):
        lefts[pairs + i] = padded(act[:, i * BS : (i + 1) * BS]).astype(bf16)
    acc[...] = jnp.zeros_like(acc)
    products = [dot(lefts[left_of[natural[s]]], low[s]) for s in range(count)]
    for s in range(count):
        rows = pl.ds(pl.multiple_of(block_of[natural[s]] * HB, HB), HB)
        acc[rows] += products[s]
    rows_v, rows_f = segments_of(heads, dp_count)
    base = pairs * across * HB
    for odd, first, second in ((0, keep_o, send_o), (1, send_o, keep_o)):

        @pl.when((me & 1) == odd)
        def _():
            for e in range(dp_count):
                out = second if e & 1 else first
                start = pl.multiple_of(((me ^ e) >> 1) * (rows_v + rows_f), 8)
                out[pl.ds(start, rows_v)] = acc[e * rows_v : (e + 1) * rows_v]
                k, inside = e * rows_f // vocab, e * rows_f % vocab
                at = base + k * HB + inside
                out[pl.ds(pl.multiple_of(start + rows_v, 8), rows_f)] = acc[at : at + rows_f]


def second_tables(natural, ints, mine, other, fc_bias, low, vocab, heads, dp_count):
    ff_local = fc_bias.shape[1]
    left_of, block_of = second_places(heads, ff_local)
    o = jax.ShapeDtypeStruct
    return pl.pallas_call(
        functools.partial(second_kernel, heads, dp_count),
        in_specs=[SMEM] * 4 + [VMEM] * 4,
        out_specs=[VMEM] * 6,
        out_shape=[
            o((vocab, 3 * heads * HD), f32),
            o((vocab, ff_local), f32),
            o((vocab, ff_local), bf16),
            o((heads * vocab, heads * HD), bf16),
            o((dp_count // 2 * sum(segments_of(heads, dp_count)), BS), f32),
            o((dp_count // 2 * sum(segments_of(heads, dp_count)), BS), f32),
        ],
        scratch_shapes=[
            pltpu.VMEM((2 * mine.shape[0],) + mine.shape[1:], f32),
            pltpu.VMEM((heads // 2 + ff_local // BS, HB, BS), bf16),
            pltpu.VMEM(((int(block_of.max()) + 1) * HB, BS), f32),
        ],
        name="second_tables",
        **params(4),
    )(natural, ints, jnp.asarray(left_of), jnp.asarray(block_of), mine, other, fc_bias, low)


def pack_kernel(rows_v, *refs):
    *parts, out = refs
    at = 0
    for part in parts:
        out[at : at + rows_v] = part[:rows_v].astype(bf16)
        at += rows_v
    down = tree_sum([part[rows_v:] for part in parts])
    for piece in split3(down):
        out[at : at + down.shape[0]] = piece
        at += down.shape[0]


def pack_segments(heads, dp_count, parts):
    rows_v, rows_f = segments_of(heads, dp_count)
    return pl.pallas_call(
        functools.partial(pack_kernel, rows_v),
        in_specs=[VMEM] * len(parts),
        out_specs=VMEM,
        out_shape=jax.ShapeDtypeStruct((len(parts) * rows_v + 3 * rows_f, BS), bf16),
        name="pack_segments",
        **params(1),
    )(*parts)


def rotary_tables(seq_len):
    half = ROT // 2
    frequency = np.float32(10000.0) ** (
        np.float32(-2.0) * np.arange(half, dtype=np.float32) / np.float32(ROT)
    )
    angles = np.arange(seq_len, dtype=np.float32)[:, None] * frequency[None, :].astype(np.float32)
    cosine = np.cos(angles.astype(np.float64)).astype(np.float32)
    sine = np.sin(angles.astype(np.float64)).astype(np.float32)
    wide_cos = np.ones((seq_len, WIDE), np.float32)
    wide_sin = np.zeros((seq_len, WIDE), np.float32)
    wide_cos[:, :half], wide_cos[:, half:ROT] = cosine, cosine
    wide_sin[:, :half], wide_sin[:, half:ROT] = sine, sine
    return wide_cos, wide_sin, np.ascontiguousarray(cosine.T), np.ascontiguousarray(sine.T)


def turned(x):
    half = ROT // 2
    lane = lanes(x.shape)
    return jnp.where(
        lane < half,
        -pltpu.roll(x, WIDE - half, 1),
        jnp.where(lane < ROT, pltpu.roll(x, half, 1), 0.0),
    )


def head_lanes(table, index):
    begin = index // 2 * WIDE
    chunk = table[:, begin : begin + WIDE]
    if index % 2:
        chunk = pltpu.roll(chunk, HD, 1)
    return jnp.where(lanes(chunk.shape) < HD, chunk, 0.0)


def stack_parts(table):
    high, middle, rest = split3(table)
    return jnp.concatenate([high, middle, rest, jnp.zeros_like(high)], axis=0)


def attention_kernel(
    heads, pair, length, token_col, proj, cosine, sine, before, query_o, key_o, weight_o, low_o, hot, key_hot, queries, wide
):
    seq = token_col.shape[0]
    vocab = proj.shape[0]
    lane = lanes((seq, WIDE))
    hot[...] = jnp.where(lane % vocab == token_col[...], 1.0, 0.0).astype(bf16)
    for n in range(2):
        first = (2 * pair + n) * vocab
        key_hot[n] = jnp.where(lane == token_col[...] + first, 1.0, 0.0).astype(bf16)
    one = lanes((vocab, WIDE)) == HD
    ones = (lanes((vocab, WIDE)) > HD) & (lanes((vocab, WIDE)) < HD + 4)
    for which in range(2):
        for n in range(2):
            own = head_lanes(proj, which * heads + 2 * pair + n)
            other = turned(own)
            if which == 0:
                own = jnp.where(one, 1.0, own * 0.125)
                other = other * 0.125
            else:
                own = jnp.where(one | ones, 1.0, own)
            begin = (which * 2 + n) * 2 * WIDE
            wide[:, begin : begin + WIDE] = stack_parts(own)
            wide[:, begin + WIDE : begin + 2 * WIDE] = stack_parts(other)
    for i in range(seq // ROWS):
        span = slice(i * ROWS, (i + 1) * ROWS)
        part = hot[span]
        position = i * ROWS + sublanes((ROWS, WIDE))
        bias = jnp.where(position < length[0], 0.0, MASKED)
        cos, sin = cosine[span], sine[span]
        key_cos = jnp.where(lanes((ROWS, WIDE)) == HD, bias, cos)
        for h in range(2):
            both = dot(part, wide[:, h * 2 * WIDE : (h + 1) * 2 * WIDE])
            queries[h, span] = (both[:, :WIDE] * cos + both[:, WIDE:] * sin).astype(bf16)
            k = 2 + h
            both = dot(part, wide[:, k * 2 * WIDE : (k + 1) * 2 * WIDE])
            key_o[h, span] = (both[:, :WIDE] * key_cos + both[:, WIDE:] * sin).astype(bf16)
    allowed = lanes((ROWS, ROWS)) <= sublanes((ROWS, ROWS))
    small = lanes((ROWS, WIDE))
    halves = []
    for i in range(seq // ROWS):
        span = slice(i * ROWS, (i + 1) * ROWS)
        past = i * ROWS
        weights = before[span] if pair else jnp.zeros((ROWS, WIDE), f32)
        query = [queries[h, span] for h in range(2)]
        near = [dot(query[h], key_o[h, span], NT) for h in range(2)]
        if past:
            far = [dot(query[h], key_o[h, :past], NT) for h in range(2)]
        near = [jnp.where(allowed, x, MASKED) for x in near]
        top = [jnp.max(x, axis=-1, keepdims=True) for x in near]
        if past:
            top = [jnp.maximum(m, jnp.max(x, axis=-1, keepdims=True)) for m, x in zip(top, far)]
            far = [jnp.exp(x - m) for m, x in zip(top, far)]
        near = [jnp.exp(x - m) for m, x in zip(top, near)]
        total = [jnp.sum(x, axis=-1, keepdims=True) for x in near]
        if past:
            total = [a + jnp.sum(x, axis=-1, keepdims=True) for a, x in zip(total, far)]
        share = [1.0 / a for a in total]
        near = [(x * a).astype(bf16) for x, a in zip(near, share)]
        if past:
            far = [(x * a).astype(bf16) for x, a in zip(far, share)]
        for h in range(2):
            weights = weights + dot(near[h], key_hot[h, span])
            if past:
                weights = weights + dot(far[h], key_hot[h, :past])
        for h in range(2):
            minus = -(top[h] + jnp.log(total[h]))
            high = minus.astype(bf16).astype(f32)
            middle = (minus - high).astype(bf16).astype(f32)
            rest = minus - high - middle
            value = jnp.where(small == HD + 3, rest, query[h].astype(f32))
            value = jnp.where(small == HD + 2, middle, value)
            query_o[h, span] = jnp.where(small == HD + 1, high, value).astype(bf16)
        weight_o[span] = weights
        own = weights if pair % 2 == 0 else pltpu.roll(weights, HD, 1)
        own = jnp.where(small < HD, own, 0.0)
        if i < seq // ROWS // 2:
            halves.append(own)
        else:
            k = i - seq // ROWS // 2
            low_o[k * ROWS : (k + 1) * ROWS] = (halves[k] + pltpu.roll(own, HD, 1)).astype(bf16)


def attention(pair, length, token_col, proj, cosine, sine, before, heads):
    seq = token_col.shape[0]
    vocab = proj.shape[0]
    o = jax.ShapeDtypeStruct
    return pl.pallas_call(
        functools.partial(attention_kernel, heads, pair),
        in_specs=[SMEM] + [VMEM] * 5,
        out_specs=[VMEM] * 4,
        out_shape=[
            o((2, seq, WIDE), bf16),
            o((2, seq, WIDE), bf16),
            o((seq, WIDE), f32),
            o((seq // 2, WIDE), bf16),
        ],
        scratch_shapes=[
            pltpu.VMEM((seq, WIDE), bf16),
            pltpu.VMEM((2, seq, WIDE), bf16),
            pltpu.VMEM((2, seq, WIDE), bf16),
            pltpu.VMEM((WIDE, 8 * WIDE), bf16),
        ],
        name="attention",
        **params(6),
    )(length, token_col, proj, cosine, sine, before)


def attention_back_kernel(
    heads,
    pair,
    token_col,
    token_row,
    query,
    key,
    weight,
    weight_grad,
    cosine,
    sine,
    cosine_t,
    sine_t,
    table_o,
    hot,
    mixed,
    query_grad,
    key_grad,
):
    seq = token_col.shape[0]
    vocab = table_o.shape[0]
    half = ROT // 2
    lane = lanes((seq, WIDE))
    hot[...] = jnp.where(
        (lane == token_col[...]) | (lane == token_col[...] + vocab) | ((lane >= HD) & (lane < HD + 3)),
        1.0,
        0.0,
    ).astype(bf16)
    grads = weight_grad[...]
    if heads * vocab < WIDE:
        grads = jnp.concatenate([grads, jnp.zeros((seq, WIDE - heads * vocab), f32)], axis=1)
    both = weight[...] * grads
    for n, h in enumerate((2 * pair, 2 * pair + 1)):
        inside = (lane >= h * vocab) & (lane < (h + 1) * vocab)
        minus = -jnp.sum(jnp.where(inside, both, 0.0), axis=-1, keepdims=True)
        own = grads if h == 0 else pltpu.roll(grads, WIDE - h * vocab, 1)
        own = jnp.where(lane < vocab, own, 0.0)
        high, rest = split2(own)
        m_high = minus.astype(bf16).astype(f32)
        m_middle = (minus - m_high).astype(bf16).astype(f32)
        m_rest = minus - m_high - m_middle
        value = high.astype(f32) + pltpu.roll(rest.astype(f32), vocab, 1)
        value = jnp.where(lane == HD, m_high, value)
        value = jnp.where(lane == HD + 1, m_middle, value)
        value = jnp.where(lane == HD + 2, m_rest, value)
        mixed[n] = value.astype(bf16)
    allowed = lanes((ROWS, ROWS)) <= sublanes((ROWS, ROWS))
    key_grad[...] = jnp.zeros_like(key_grad)
    both = range(2)
    for i in range(seq // ROWS):
        span = slice(i * ROWS, (i + 1) * ROWS)
        past = i * ROWS
        part = [query[n, span] for n in both]
        near = [dot(part[n], key[n, span], NT) for n in both]
        slope = [dot(mixed[n, span], hot[span], NT) for n in both]
        if past:
            far = [dot(part[n], key[n, :past], NT) for n in both]
            far_slope = [dot(mixed[n, span], hot[:past], NT) for n in both]
        near = [jnp.where(allowed, jnp.exp(x), 0.0) for x in near]
        near = [(x * y).astype(bf16) for x, y in zip(near, slope)]
        if past:
            far = [(jnp.exp(x) * y).astype(bf16) for x, y in zip(far, far_slope)]
        grad = [dot(near[n], key[n, span]) for n in both]
        if past:
            grad = [grad[n] + dot(far[n], key[n, :past]) for n in both]
        for n in both:
            key_grad[n, :, span] += dot(part[n], near[n], TN)[:HD]
            if past:
                key_grad[n, :, :past] += dot(part[n], far[n], TN)[:HD]
        for n in both:
            x = grad[n] * 0.125
            query_grad[n, span] = (x * cosine[span] - turned(x) * sine[span]).astype(bf16)
    shape = (vocab, seq)
    token_hot = jnp.where(sublanes(shape) == token_row[...], 1.0, 0.0).astype(bf16)
    small = lanes((vocab, WIDE)) < HD
    cos_t, sin_t = cosine_t[...], sine_t[...]
    one = dot(token_hot, query_grad[0])
    two = pltpu.roll(dot(token_hot, query_grad[1]), HD, 1)
    table_o[:, :WIDE] = jnp.where(small, one, two)
    turned_keys = []
    for n in range(2):
        front, back = key_grad[n, :half], key_grad[n, half:ROT]
        turned_keys += [front * cos_t + back * sin_t, back * cos_t - front * sin_t, key_grad[n, ROT:]]
    keys = jnp.concatenate(turned_keys, axis=0).astype(bf16)
    table_o[:, WIDE:] = dot(token_hot, keys, NT)


def attention_back(
    pair, token_col, token_row, query, key, weight, weight_grad, cosine, sine, cosine_t, sine_t, heads
):
    seq = token_col.shape[0]
    vocab = weight_grad.shape[1] // heads
    full = lambda array: pl.BlockSpec(array.shape, lambda i: (0,) * array.ndim)
    two = full(query)
    return pl.pallas_call(
        functools.partial(attention_back_kernel, heads, pair),
        grid=(1,),
        in_specs=[full(token_col), full(token_row), two, two, full(weight), full(weight_grad)]
        + [full(table) for table in (cosine, sine, cosine_t, sine_t)],
        out_specs=pl.BlockSpec((vocab, 2 * WIDE), lambda i: (0, 0)),
        out_shape=jax.ShapeDtypeStruct((vocab, 2 * WIDE), f32),
        scratch_shapes=[
            pltpu.VMEM((seq, WIDE), bf16),
            pltpu.VMEM((2, seq, WIDE), bf16),
            pltpu.VMEM((2, seq, WIDE), bf16),
            pltpu.VMEM((2, HD, seq), f32),
        ],
        name="attention_back",
        **params(6),
    )(token_col, token_row, query, key, weight, weight_grad, cosine, sine, cosine_t, sine_t)


def loss_kernel(
    parts,
    members,
    heads,
    ints,
    floats,
    token_col,
    target_col,
    token_row,
    embed,
    head,
    vec,
    *refs,
):
    pairs = heads // 2
    weights, refs = refs[: pairs * parts], refs[pairs * parts :]
    pieces, refs = refs[:members], refs[members:]
    keep_o, send_o, grad_o, sums_o, mixing, low_weights, table, down = refs
    step = pl.program_id(0)
    me, length, member = ints[0], ints[1], ints[2]
    vocab = embed.shape[0]
    height = heads * vocab

    @pl.when(step == 0)
    def _():
        rows_v, rows_f = segments_of(heads, members)
        small_v = min(rows_v, HB)
        for r in range(members):
            owner = member ^ r
            piece = pieces[r]
            for place in range(parts):
                for u in range(rows_v // small_v):
                    row = owner * rows_v + u * small_v
                    block, inside = row // HB, row % HB
                    i, k = block // (D // BS), block % (D // BS)
                    at = place * rows_v + u * small_v
                    mixing[
                        me ^ place,
                        pl.ds(pl.multiple_of(i * HB + inside, 32), small_v),
                        pl.ds(pl.multiple_of(k * BS, BS), BS),
                    ] = piece[at : at + small_v]
            at = parts * rows_v
            one, two, three = (
                piece[at + n * rows_f : at + (n + 1) * rows_f].astype(f32) for n in range(3)
            )
            row = owner * rows_f
            down[
                pl.ds(pl.multiple_of(row % vocab, 8), rows_f),
                pl.ds(pl.multiple_of(row // vocab * BS, BS), BS),
            ] = one + (two + three)
        table[...] = stack_parts(embed[...] + (down[...] + vec[2:3]))
        sums_o[...] = jnp.zeros_like(sums_o)

    second = step >= pl.num_programs(0) // 2
    small = lanes((ROWS, WIDE)) < HD

    def weights_of(r):
        value = weights[r][...].astype(f32)
        turned_value = pltpu.roll(value, HD, 1)
        value = jnp.where(second, turned_value, value)
        if pairs == 1:
            return jnp.where(small, value, 0.0)
        other = weights[parts + r][...].astype(f32)
        other = jnp.where(second, other, pltpu.roll(other, HD, 1))
        return jnp.where(small, value, other)

    own = weights_of(0)
    low_weights[me] = own.astype(bf16)[:, :height]
    for r in range(1, parts):
        low_weights[me ^ r] = weights_of(r).astype(bf16)[:, :height]
    token = token_col[...]
    hot = jnp.where(lanes((ROWS, WIDE)) % vocab == token, 1.0, 0.0).astype(bf16)
    x = dot(hot, table[...])
    x = x + dot(
        jnp.concatenate([low_weights[g] for g in range(parts)], axis=1),
        jnp.concatenate([mixing[g] for g in range(parts)], axis=0),
    )
    normed, scale = stats_of(x)
    gain = vec[3:4]
    final = (normed * gain + vec[4:5]).astype(bf16)
    head_low = head[:, :D].astype(bf16)
    square = (vocab, vocab)
    bias_row = jnp.sum(
        jnp.where(lanes(square) == sublanes(square), head[:, D : D + 1], 0.0), axis=0, keepdims=True
    )
    logits = dot(final, head_low, NT) + bias_row
    shifted = logits - jnp.max(logits, axis=-1, keepdims=True)
    log_probs = shifted - jnp.log(jnp.sum(jnp.exp(shifted), axis=-1, keepdims=True))
    target = lanes((ROWS, vocab)) == target_col[...]
    position = step * ROWS + sublanes((ROWS, 1))
    slot_weight = jnp.where(position < length - 1, floats[0], 0.0)
    picked = jnp.sum(jnp.where(target, log_probs, 0.0), axis=-1, keepdims=True)
    loss = -jnp.sum(slot_weight * picked, keepdims=True)
    logit_grad = ((jnp.exp(log_probs) - jnp.where(target, 1.0, 0.0)) * slot_weight).astype(bf16)
    final_grad = dot(logit_grad, head_low)
    grad = norm_back(final_grad, normed, scale, gain)
    high = grad.astype(bf16)
    token_hot = jnp.where(sublanes((vocab, ROWS)) == token_row[...], 1.0, 0.0).astype(bf16)
    both = dot(jnp.concatenate([own.T.astype(bf16), token_hot], axis=0), high)
    sums_o[0:vocab] += both[WIDE:]
    sums_o[vocab : 2 * vocab] += dot(logit_grad, final, TN)
    base = 2 * vocab
    sums_o[base : base + 1] += jnp.sum(final_grad * normed, axis=0, keepdims=True)
    sums_o[base + 1 : base + 2] += jnp.sum(final_grad, axis=0, keepdims=True)
    bias_grad = jnp.sum(logit_grad.astype(f32), axis=0, keepdims=True)
    sums_o[base + 2 : base + 3, :vocab] += bias_grad
    lane = lanes((1, WIDE))
    count = jnp.where((step == 0) & (length >= 2), 1.0, 0.0)
    sums_o[base + 3 : base + 4, :WIDE] += jnp.where(
        lane == 0, loss, jnp.where(lane == 1, count, 0.0)
    )
    sums_o[base + 16 : base + 16 + height] += both[:height]
    grad_o[...] = dot(high, mixing[me], NT)

    @pl.when(step == pl.num_programs(0) - 1)
    def _():
        deal(member & 1, sums_o, keep_o, send_o)


def loss_rows(
    ints,
    floats,
    token_col,
    target_col,
    token_row,
    embedding,
    head,
    vectors,
    weights,
    pieces,
    heads,
):
    seq = token_col.shape[0]
    vocab = embedding.shape[0]
    parts = len(weights) // (heads // 2)
    height = heads * vocab
    blocks = seq // ROWS // 2
    col = pl.BlockSpec((ROWS, 1), lambda i: (i, 0))
    o = jax.ShapeDtypeStruct
    full = lambda array: pl.BlockSpec(array.shape, lambda i: (0,) * array.ndim)
    sums_shape = (2 * vocab + 16 + height, D)
    return pl.pallas_call(
        functools.partial(loss_kernel, parts, len(pieces), heads),
        grid=(seq // ROWS,),
        in_specs=[SMEM, SMEM, col, col, pl.BlockSpec((1, ROWS), lambda i: (0, i))]
        + [full(embedding), full(head), full(vectors)]
        + [pl.BlockSpec((ROWS, WIDE), lambda i: (i % blocks, 0))] * len(weights)
        + [full(pieces[0])] * len(pieces),
        out_specs=[
            pl.BlockSpec((sums_shape[0] // 2, D), lambda i: (0, 0)),
            pl.BlockSpec((sums_shape[0] // 2, D), lambda i: (0, 0)),
            pl.BlockSpec((ROWS, height), lambda i: (i, 0)),
        ],
        out_shape=[o((sums_shape[0] // 2, D), f32)] * 2 + [o((seq, height), f32)],
        scratch_shapes=[
            pltpu.VMEM(sums_shape, f32),
            pltpu.VMEM((parts, height, D), bf16),
            pltpu.VMEM((parts, ROWS, height), bf16),
            pltpu.VMEM((4 * vocab, D), bf16),
            pltpu.VMEM((vocab, D), f32),
        ],
        name="loss_rows",
        **params(12),
    )(
        ints,
        floats,
        token_col,
        target_col,
        token_row,
        embedding,
        head,
        vectors,
        *weights,
        *pieces,
    )


def padded(block):
    lacking = HB - block.shape[0]
    if lacking:
        block = jnp.concatenate([block, jnp.zeros((lacking, block.shape[1]), block.dtype)], axis=0)
    return block


def put_left(ref, index, block):
    ref[index] = jnp.concatenate([padded(block)] * 3, axis=0).astype(bf16)


def put_right(ref, index, block):
    ref[index] = jnp.concatenate(split3(padded(block)), axis=0)


def factors_kernel(
    heads,
    ints,
    owner,
    mine,
    other,
    gathered,
    upper,
    normed,
    act,
    values,
    left_o,
    right_o,
    hidden_o,
    bias_o,
    small_o,
    part_o,
    sums,
    tiles,
    sem,
    *mats,
):
    vocab = normed.shape[0]
    width = upper.shape[1]
    copy = pltpu.make_async_copy(gathered, tiles, sem)
    copy.start()
    join(ints[0] & 1, mine, other, sums)
    small_o[...] = sums[: small_o.shape[0]]
    rows = sums[0:vocab]
    mixed = sums[2 * vocab + 16 :]
    low = normed[...].astype(f32)
    own = act[...].astype(f32)
    val = values[...].astype(f32)
    normed_gram = dot6(low, low, NT)
    square = jnp.sum(dot6(own, own, NT) * dot6(rows, rows, NT), keepdims=True) + jnp.sum(
        dot6(val, val, NT) * dot6(mixed, mixed, NT), keepdims=True
    )
    across = D // BS
    f_rows = width // BS
    pair = 2 * vocab
    for i in range(across):
        put_left(left_o, i, low[:, i * BS : (i + 1) * BS])
    for i in range(f_rows):
        put_left(left_o, across + i, own[:, i * BS : (i + 1) * BS])
    for i in range(heads // 2):
        put_left(
            left_o,
            across + f_rows + i,
            val[i * pair : (i + 1) * pair, i * BS : (i + 1) * BS],
        )
    at = heads * HD // BS
    for i in range(heads // 2):
        for k in range(across):
            put_right(right_o, at, mixed[i * pair : (i + 1) * pair, k * BS : (k + 1) * BS])
            at += 1
    for k in range(across):
        put_right(right_o, at + f_rows + k, rows[:, k * BS : (k + 1) * BS])
    copy.wait()
    for index, (which, i, k) in enumerate(tile_places(layer_shapes(heads, width))):
        mats[which][i * BS : (i + 1) * BS, k * BS : (k + 1) * BS] = tiles[owner[index]]
    mat_q, mat_o, mat_u, mat_f = mats
    part_o[...] = mat_q[:, : 2 * heads * HD]
    act_grad = rows_times_low(rows, mat_f[...], NT)
    u = upper[...]
    tanh = jnp.tanh(GELU_A * (u + GELU_B * (u * u * u)))
    slope = 0.5 * (1.0 + tanh) + 0.5 * u * (1.0 - tanh * tanh) * (
        GELU_A * (1.0 + 3.0 * GELU_B * (u * u))
    )
    upper_grad = act_grad * slope
    bias_grad = jnp.sum(upper_grad, axis=0, keepdims=True)
    bias_o[...] = bias_grad
    value_grad = rows_times_low(mixed, mat_o[...], NT)
    shape = value_grad.shape
    value_grad = jnp.where(sublanes(shape) // vocab == lanes(shape) // HD, value_grad, 0.0)
    value_table = value_grad[:vocab]
    for h in range(1, heads):
        value_table = value_table + value_grad[h * vocab : (h + 1) * vocab]
    hidden_o[0:vocab] = rows_times_low(upper_grad, mat_u[...], NT) + rows_times_low(
        value_table, mat_q[:, 2 * heads * HD :], NT
    )
    square = (
        square
        + jnp.sum(
            normed_gram
            * (dot6(value_table, value_table, NT) + dot6(upper_grad, upper_grad, NT)),
            keepdims=True,
        )
        + jnp.sum(bias_grad * bias_grad, keepdims=True)
    )
    hidden_o[vocab : vocab + 16] = jnp.broadcast_to(square, (16, D))
    for k in range(heads * HD // BS):
        put_right(right_o, k, value_table[:, k * BS : (k + 1) * BS])
    for k in range(f_rows):
        put_right(right_o, at + k, upper_grad[:, k * BS : (k + 1) * BS])


def rest_kernel(pairs, ints, mine, other, hidden, mat_q, normed, right_o, hidden_o, half_o, table):
    vocab = normed.shape[0]
    join(ints[0] & 1, mine, other, table)
    blocks = [table[p * vocab : (p + 1) * vocab, :WIDE] for p in range(pairs)]
    blocks += [table[p * vocab : (p + 1) * vocab, WIDE:] for p in range(pairs)]
    grad = jnp.concatenate(blocks, axis=1)
    for k, block in enumerate(blocks):
        put_right(right_o, k, block)
    low = normed[...].astype(f32)
    square = jnp.sum(dot6(low, low, NT) * dot6(grad, grad, NT), keepdims=True)
    hidden_o[0:vocab] = hidden[0:vocab] + rows_times_low(grad, mat_q[...], NT)
    hidden_o[vocab:] = hidden[vocab:] + square
    size = half_o.shape[0]
    half_o[...] = hidden_o[pl.ds(pl.multiple_of((ints[0] & 1) * size, size), size)]


def factor_places(heads, ff_local):
    q_cols = 3 * heads * HD // BS
    o_rows = heads // 2
    across = D // BS
    f_rows = ff_local // BS
    left, right = [], []
    for which, i, k in tile_places(layer_shapes(heads, ff_local)):
        if which == 0:
            left.append(i)
            right.append(k)
        elif which == 1:
            left.append(across + f_rows + i)
            right.append(q_cols + i * across + k)
        elif which == 2:
            left.append(i)
            right.append(q_cols + o_rows * across + k)
        else:
            left.append(across + i)
            right.append(q_cols + o_rows * across + f_rows + k)
    return np.array(left, np.int32), np.array(right, np.int32)


def factors(ints, owner, mine, other, tiles, upper, normed, act, values, heads):
    vocab = normed.shape[0]
    ff_local = upper.shape[1]
    n_left = D // BS + ff_local // BS + heads // 2
    n_right = heads * HD // BS + heads // 2 * (D // BS) + ff_local // BS + D // BS
    o = jax.ShapeDtypeStruct
    return pl.pallas_call(
        functools.partial(factors_kernel, heads),
        in_specs=[SMEM] * 2 + [VMEM] * 2 + [ANY] + [VMEM] * 4,
        out_specs=[VMEM] * 6,
        out_shape=[
            o((n_left, 3 * HB, BS), bf16),
            o((n_right, 3 * HB, BS), bf16),
            o((vocab + 16, D), f32),
            o((1, ff_local), f32),
            o((2 * vocab + 16, D), f32),
            o((D, 2 * heads * HD), bf16),
        ],
        scratch_shapes=[
            pltpu.VMEM((2 * mine.shape[0], D), f32),
            pltpu.VMEM(tiles.shape, bf16),
            pltpu.SemaphoreType.DMA,
        ]
        + [pltpu.VMEM(shape, bf16) for shape in layer_shapes(heads, ff_local)],
        name="factors",
        **params(7, 24),
    )(ints, owner, mine, other, tiles, upper, normed, act, values)


def factors_rest(ints, mine, other, hidden, mat_q, normed, heads):
    o = jax.ShapeDtypeStruct
    pairs = heads // 2
    return pl.pallas_call(
        functools.partial(rest_kernel, pairs),
        in_specs=[SMEM] + [VMEM] * 5,
        out_specs=[VMEM] * 3,
        out_shape=[
            o((2 * pairs, 3 * HB, BS), bf16),
            o(hidden.shape, f32),
            o((hidden.shape[0] // 2, D), f32),
        ],
        scratch_shapes=[pltpu.VMEM((2 * mine.shape[0], 2 * WIDE), f32)],
        name="factors_rest",
        **params(2),
    )(ints, mine, other, hidden, mat_q, normed)


def small_kernel(parts, corrections, ints, sums, own, *refs):
    mine, others, refs = refs[: parts - 1], refs[parts - 1 : 2 * parts - 2], refs[2 * parts - 2 :]
    bias_grad, refs = refs[0], refs[1:]
    weights, refs = refs[:12], refs[12:]
    outs, scalars, total = refs[:12], refs[12], refs[13]
    vocab = weights[0].shape[0]
    base = 2 * vocab
    size = own.shape[0] // 2
    for place, group in ((ints[0], mine), (1 - ints[0], others)):
        span = pl.ds(pl.multiple_of(place * size, size), size)
        total[span] = tree_sum([own[span]] + [ref[...] for ref in group])
    hidden = total[:vocab]
    square = total[vocab : vocab + 1, 0:1]
    rows = sums[0:vocab]
    normed, scale = stats_of(weights[0][...])
    gain = weights[6][0:1]
    embed_grad = rows + norm_back(hidden, normed, scale, gain)
    vector_grad = jnp.concatenate(
        [
            jnp.sum(hidden * normed, axis=0, keepdims=True),
            jnp.sum(hidden, axis=0, keepdims=True),
            jnp.sum(rows, axis=0, keepdims=True),
            sums[base : base + 1],
            sums[base + 1 : base + 2],
        ],
        axis=0,
    )
    head_grad = sums[vocab : 2 * vocab]
    head_bias = sums[base + 2 : base + 3, :vocab]
    add = lambda value: jnp.sum(value * value, keepdims=True)
    square = square + add(embed_grad) + add(vector_grad) + add(head_grad) + add(head_bias)
    count = sums[base + 3 : base + 4, 1:2]
    loss = sums[base + 3 : base + 4, 0:1] / count
    norm = jnp.sqrt(square) / count
    scale_all = jnp.minimum(1.0, CLIP_NORM / norm) / count
    one, two = corrections[0], corrections[1]

    def update(index, pick, grad):
        weight, first, second = (weights[3 * index + k][pick] for k in range(3))
        grad = grad * scale_all
        first = BETA_ONE * first + (1.0 - BETA_ONE) * grad
        second = BETA_TWO * second + (1.0 - BETA_TWO) * grad * grad
        step = first / one / (jnp.sqrt(second / two) + ADAM_EPS)
        outs[3 * index][pick] = weight - RATE_SMALL * (step + WEIGHT_DECAY * weight)
        outs[3 * index + 1][pick] = first
        outs[3 * index + 2][pick] = second

    everything = slice(None)
    update(0, everything, embed_grad)
    shape = (vocab, vocab)
    head_column = jnp.sum(
        jnp.where(lanes(shape) == sublanes(shape), head_bias, 0.0), axis=1, keepdims=True
    )
    update(1, (everything, slice(0, D)), head_grad)
    update(1, (everything, slice(D, D + 1)), head_column)
    update(2, everything, vector_grad)
    update(3, everything, bias_grad[...])
    lane = lanes((1, WIDE))
    scalars[...] = jnp.where(
        lane == 0, scale_all, jnp.where(lane == 1, loss, jnp.where(lane == 2, norm, 0.0))
    )


def small(corrections, upper, sums, hidden, mine, others, bias_grad, weights):
    o = jax.ShapeDtypeStruct
    return pl.pallas_call(
        functools.partial(small_kernel, 1 + len(mine)),
        in_specs=[SMEM] * 2 + [VMEM] * (2 + 2 * len(mine) + 1 + 12),
        out_specs=[VMEM] * 13,
        out_shape=[o(weight.shape, f32) for weight in weights] + [o((1, WIDE), f32)],
        scratch_shapes=[pltpu.VMEM(hidden.shape, f32)],
        name="small",
        **params(4),
    )(corrections, upper, sums, hidden, *mine, *others, bias_grad, *weights)


QB = 32
UNQ = 12
PER = 6


def take(value, at):
    return jnp.take_along_axis(value, at, axis=1, mode="promise_in_bounds")


def eliminate(packed, count):
    shape = (8, BS)
    lane, sub = lanes(shape), sublanes(shape)
    start = lane // QB * QB
    span = range(count)
    for p in range(QB // 8):
        r0 = 8 * p

        def body(step, carry):
            jj = 2 * step
            j = r0 + jj
            pick, pick_two = start + j, start + (j + 1)
            mark, mark_two = lane == pick, lane == pick_two
            below, below_two = sub > jj, sub > jj + 1
            wide = [jnp.broadcast_to(packed[t, pl.ds(j, 1), :], shape) for t in span]
            next_wide = [jnp.broadcast_to(packed[t, pl.ds(j + 1, 1), :], shape) for t in span]
            kept = [[packed[t, 8 * q : 8 * q + 8, :] for q in range(p, QB // 8)] for t in span]
            pivot = [take(w, pick) for w in wide]
            right = [take(w, pick_two) for w in wide]
            lower = [take(w, pick) for w in next_wide]
            corner = [take(w, pick_two) for w in next_wide]
            ones = [[take(a, pick) for a in group] for group in kept]
            twos = [[take(a, pick_two) for a in group] for group in kept]
            inverse = [1.0 / d for d in pivot]
            ratio = [b * i for b, i in zip(right, inverse)]
            inverse_two = [1.0 / (e - b * r) for e, b, r in zip(corner, lower, ratio)]
            scaled = [jnp.where(mark, 1.0, w) * i for w, i in zip(wide, inverse)]
            scaled_two = [
                jnp.where(mark_two, 1.0, jnp.where(mark, 0.0, w) - b * x) * i
                for w, b, x, i in zip(next_wide, lower, scaled, inverse_two)
            ]
            for t in span:
                for k, q in enumerate(range(p, QB // 8)):
                    a, c, d = kept[t][k], ones[t][k], twos[t][k]
                    d = d - c * ratio[t]
                    first = jnp.where(mark, 0.0, a) - c * scaled[t]
                    if k == 0:
                        first = jnp.where(below, first, a)
                    second = jnp.where(mark_two, 0.0, first) - d * scaled_two[t]
                    if k == 0:
                        second = jnp.where(below_two, second, first)
                    packed[t, 8 * q : 8 * q + 8, :] = second
            return carry

        lax.fori_loop(0, 4, body, 0)


def part_inverse(packed):
    shape = (QB, BS)
    lane, sub = lanes(shape), sublanes(shape)
    part, col = lane // QB, lane % QB
    diagonal = jnp.where(col == sub, packed, 0.0)
    pivot = jnp.ones(shape, f32)
    for k in range(BS // QB):
        own = jnp.sum(jnp.where(part == k, diagonal, 0.0), axis=1, keepdims=True)
        pivot = jnp.where(part == k, own, pivot)
    unit = jnp.where(col < sub, packed, jnp.where(col == sub, 1.0, 0.0))
    return unit * lax.rsqrt(pivot)


def inverse_factors(gram, packed, result, count):
    parts = BS // QB
    unroll = next(k for k in (UNQ, 3, 2, 1) if count % k == 0)
    lane32, sub32 = lanes((QB, BS)), sublanes((QB, BS))
    for b in range(parts):
        begin = b * QB
        below = begin + QB
        rows = slice(begin, below)
        here = lane32 // QB == b

        def pack(i, carry):
            for t in [i * unroll + k for k in range(unroll)]:
                value = jnp.zeros((QB, BS), f32)
                for k in range(parts):
                    block = gram[parts * t + k, rows, :]
                    if k != b:
                        block = pltpu.roll(block, (k * QB + BS - begin) % BS, 1)
                    value = jnp.where(lane32 // QB == k, block, value)
                packed[t] = value
            return carry

        lax.fori_loop(0, count // unroll, pack, 0)
        eliminate(packed, count)

        def spread(i, carry):
            groups = [i * unroll + k for k in range(unroll)]
            inverses = [part_inverse(packed[t]) for t in groups]
            firsts = [
                jnp.concatenate([jnp.where(lane32 // QB == k, x, 0.0) for k in range(parts)], axis=0)
                for x in inverses
            ]
            unit = jnp.where(lane32 - begin == sub32, 1.0, 0.0)
            panels = [
                jnp.concatenate(
                    [jnp.where(here, unit, gram[parts * t + k, rows, :]) for k in range(parts)],
                    axis=0,
                )
                for t in groups
            ]
            news = [dot6(x, y, NN) for x, y in zip(firsts, panels)]
            for t, new in zip(groups, news):
                for k in range(parts):
                    value = new[k * QB : (k + 1) * QB]
                    result[parts * t + k, rows, :] = (
                        jnp.where(lane32 < below, value, 0.0) if below < BS else value
                    )
            if below < BS:
                for t, new in zip(groups, news):
                    mats = [new[k * QB : (k + 1) * QB] for k in range(parts)]
                    changes = [dot6(x, x, TN) for x in mats]
                    shape = (BS - below, BS)
                    mark = lanes(shape) // QB == b
                    for k in range(parts):
                        old = gram[parts * t + k, below:, :]
                        gram[parts * t + k, below:, :] = jnp.where(mark, 0.0, old) - changes[k][below:]
            return carry

        lax.fori_loop(0, count // unroll, spread, 0)


def tile_params(count, per):
    blk = pl.BlockSpec((per, BS, BS), lambda i: (i, 0, 0))
    full = pl.BlockSpec((count, BS, BS), lambda i: (0, 0, 0))
    return blk, full, lambda dt: jax.ShapeDtypeStruct((count, BS, BS), dt)


def gradient_kernel(per, rest, natural, left_at, right_at, lefts, rights, more, L, R, QL, QR, *outs):
    step = pl.program_id(0)
    span = range(per)
    pairs = []
    for s in span:
        tile = natural[step * per + s]
        at = right_at[tile]
        right = jnp.where(
            at < rest, more[jnp.minimum(at, rest - 1)], rights[jnp.maximum(at - rest, 0)]
        )
        pairs.append((lefts[left_at[tile]], right))
    g = [dot(a, b, TN) for a, b in pairs]
    gt = [dot(b, a, TN) for a, b in pairs]
    qt = [QL[s].T for s in span]
    left = [dot3(x, x, NT) for x in g]
    right = [dot3(x, x, NT) for x in gt]
    rot = [dot3(q, x, NN) for q, x in zip(qt, g)]
    mixed_left = [dot3(left[s], QL[s], NN) for s in span]
    mixed_right = [dot3(right[s], QR[s], NN) for s in span]
    rot = [dot3(rot[s], QR[s], NN) for s in span]
    old_left = [dot6(L[s], QL[s], NN) for s in span]
    old_right = [dot6(R[s], QR[s], NN) for s in span]
    for s in span:
        for out, value in zip(
            outs, (left, right, rot, mixed_left, mixed_right, old_left, old_right)
        ):
            out[s] = value[s]


def gradient_products(natural, left_at, right_at, lefts, rights, more, L, R, QL, QR):
    count = QL.shape[0]
    blk, _, o = tile_params(count, PER)
    whole = lambda x: pl.BlockSpec(x.shape, lambda i: (0, 0, 0))
    return pl.pallas_call(
        functools.partial(gradient_kernel, PER, more.shape[0]),
        grid=(count // PER,),
        in_specs=[SMEM] * 3 + [whole(lefts), whole(rights), whole(more)] + [blk] * 4,
        out_specs=[blk] * 7,
        out_shape=[o(f32)] * 7,
        name="gradient_products",
        **params(9),
    )(natural, left_at, right_at, lefts, rights, more, L, R, QL, QR)


def soap_kernel(
    count, per, corrections, scal, GL, GR, GT, BL, BR, AL, AR, W, m, v, L, R, QL, QR,
    W_o, low_o, m_o, v_o, L_o, R_o, QL_o, QR_o, ML_s, MR_s, work, inv_s, packed,
):
    step = pl.program_id(0)
    scale = scal[0:1, 0:1]
    c1, c2 = corrections[0], corrections[1]
    span = range(per)
    share = (1 - BETA_TWO) * (scale * scale)
    xs = []
    for s in span:
        rot = GT[s] * scale
        mn = BETA_ONE * m[s] + (1 - BETA_ONE) * rot
        vn = BETA_TWO * v[s] + (1 - BETA_TWO) * rot * rot
        m_o[s] = mn
        v_o[s] = vn
        xs.append((mn / c1) / (jnp.sqrt(vn / c2) + ADAM_EPS))
    ML = [BETA_TWO * AL[s] + share * BL[s] for s in span]
    MR = [BETA_TWO * AR[s] + share * BR[s] for s in span]
    back = [dot3(QL[s], xs[s], NN) for s in span]
    ML = [x * lax.rsqrt(jnp.sum(x * x, keepdims=True)) for x in ML]
    MR = [x * lax.rsqrt(jnp.sum(x * x, keepdims=True)) for x in MR]
    back = [dot3(back[s], QR[s], NT) for s in span]
    gram_left = [dot6(x, x, TN) for x in ML]
    gram_right = [dot6(x, x, TN) for x in MR]
    for s in span:
        L_o[s] = BETA_TWO * L[s] + share * GL[s]
        R_o[s] = BETA_TWO * R[s] + share * GR[s]
        w = W[s]
        wn = w - RATE_TILES * (back[s] + WEIGHT_DECAY * w)
        W_o[s] = wn
        low_o[s] = wn.astype(bf16)
        t = step * per + s
        ML_s[t] = ML[s]
        MR_s[t] = MR[s]
        work[2 * t] = gram_left[s]
        work[2 * t + 1] = gram_right[s]

    @pl.when(step == pl.num_programs(0) - 1)
    def _():
        inverse_factors(work, packed, inv_s, count // 2)
        unroll = next(k for k in (12, 6, 3, 1) if count % k == 0)

        def last(i, carry):
            ts = [i * unroll + k for k in range(unroll)]
            ol = [dot3(ML_s[t], inv_s[2 * t], NT) for t in ts]
            orr = [dot3(MR_s[t], inv_s[2 * t + 1], NT) for t in ts]
            for t, a, b in zip(ts, ol, orr):
                QL_o[t] = a
                QR_o[t] = b
            return carry

        lax.fori_loop(0, count // unroll, last, 0)


def soap(corrections, scal, products, W, m, v, L, R, QL, QR):
    count = W.shape[0]
    blk, full, o = tile_params(count, PER)
    return pl.pallas_call(
        functools.partial(soap_kernel, count, PER),
        grid=(count // PER,),
        in_specs=[SMEM, pl.BlockSpec((1, WIDE), lambda i: (0, 0))] + [blk] * 14,
        out_specs=[blk] * 6 + [full] * 2,
        out_shape=[o(f32), o(bf16), o(f32), o(f32), o(f32), o(f32), o(f32), o(f32)],
        scratch_shapes=[pltpu.VMEM((count, BS, BS), f32)] * 2
        + [pltpu.VMEM((2 * count, BS, BS), f32)] * 2
        + [pltpu.VMEM((count // 2, QB, BS), f32)],
        name="soap_tiles",
        **params(40, 36),
    )(corrections, scal, *products, W, m, v, L, R, QL, QR)


def local(
    tokens,
    lengths,
    tile_owner,
    step_count,
    weight_tiles,
    tiles_first,
    tiles_second,
    stats_left,
    stats_right,
    basis_left,
    basis_right,
    embedding,
    embedding_first,
    embedding_second,
    head_table,
    head_first,
    head_second,
    vectors,
    vectors_first,
    vectors_second,
    fc_bias,
    fc_bias_first,
    fc_bias_second,
):
    seq = tokens.shape[1]
    mp_count = lax.axis_size("mp")
    dp_count = lax.axis_size("dp")
    dp_index = lax.axis_index("dp")
    mp_index = lax.axis_index("mp")
    upper_pair = dp_index & 1
    heads = H // mp_count
    ff_local = fc_bias.shape[1]
    count = weight_tiles.shape[0]
    vocab = embedding.shape[0]
    own_index = dp_index[None]

    natural, low_tiles, normed, keep, send = first_tables(
        tile_owner, own_index, weight_tiles, embedding, vectors, heads, ff_local
    )
    token_col = tokens.reshape(seq, 1)
    target_col = jnp.roll(tokens, -1, axis=1).reshape(seq, 1)
    keep = keep + swap_with(send, "dp", 1)
    mine = direct(keep)
    low_tiles, mine = lax.optimization_barrier((low_tiles, mine))
    gathered = lax.all_gather(low_tiles, "dp", axis=0, tiled=True)
    proj, upper, act, values, keep, send = second_tables(
        natural, own_index, mine, swap_with(mine, "dp", 1), fc_bias, low_tiles, vocab, heads, dp_count
    )
    cosine, sine, cosine_t, sine_t = rotary_tables(seq)
    segment = sum(segments_of(heads, dp_count))
    places = range(1, dp_count // 2)
    received = [swap_with(send, "dp", 1)]
    queries, keys = [], []
    weight = jnp.zeros((8, WIDE), f32)
    for pair in range(heads // 2):
        query, key, weight, weight_low = attention(
            pair, lengths, token_col, proj, cosine, sine, weight, heads
        )
        queries.append(query)
        keys.append(key)
        if pair == 0:
            received, weight, weight_low = lax.optimization_barrier((received, weight, weight_low))
            keep = keep + received[0]
            received = [
                swap_with(keep[q * segment : (q + 1) * segment], "dp", 2 * q) for q in places
            ]
            keep, weight = lax.optimization_barrier((keep, weight))
            weights = gather_xor(weight_low, "mp")
    if heads > 2:
        more = gather_xor(weight_low, "mp")
        received, weights, more[0] = lax.optimization_barrier((received, weights, more[0]))
    mine = tree_sum([keep[:segment]] + list(received))
    packed = pack_segments(heads, dp_count, gather_xor(mine, "mp"))
    even = [packed] + [swap_with(packed, "dp", 2 * q) for q in places]
    if heads > 2:
        weights = weights + more
    odd = [swap_with(piece, "dp", 1) for piece in even]
    pieces = [piece for two in zip(even, odd) for piece in two]
    length = lengths[0]
    inverse_length = 1.0 / jnp.maximum(length - 1, 1).astype(f32)
    keep, send, weight_grad = loss_rows(
        jnp.stack([mp_index, length, dp_index]),
        inverse_length[None],
        token_col,
        target_col,
        tokens,
        embedding,
        head_table.T,
        vectors,
        weights,
        pieces,
        heads,
    )
    keep = keep + swap_with(send, "dp", 1)
    tables_back = []
    for pair in range(heads // 2):
        if pair == 1:
            weight_grad, keep = lax.optimization_barrier((weight_grad, keep))
        tables_back.append(
            attention_back(
                pair,
                token_col,
                tokens,
                queries[pair],
                keys[pair],
                weight,
                weight_grad,
                cosine,
                sine,
                cosine_t,
                sine_t,
                heads,
            )
        )
    mine = butterfly(keep)
    table = jnp.concatenate(tables_back, axis=0)
    half = table.shape[0] // 2
    first, second = table[:half], table[half:]
    is_upper = upper_pair == 1
    table = jnp.where(is_upper, second, first) + swap_with(
        jnp.where(is_upper, first, second), "dp", 1
    )
    table = direct(table)
    left, right, hidden, bias_grad, sums, mat_part = factors(
        own_index, tile_owner, mine, swap_with(mine, "dp", 1), gathered, upper, normed, act, values, heads
    )
    more, hidden, hidden_half = factors_rest(
        own_index, table, swap_with(table, "dp", 1), hidden, mat_part, normed, heads
    )
    hidden_parts = gather_halves(hidden_half)
    left_at, right_at = (jnp.asarray(places) for places in factor_places(heads, ff_local))
    gradients = gradient_products(
        natural, left_at, right_at, left, right, more, stats_left, stats_right, basis_left, basis_right
    )
    hidden_parts, gradients = lax.optimization_barrier((hidden_parts, gradients))
    hidden_others = swap_pair(hidden_parts)
    corrections = 1.0 - jnp.power(
        jnp.array([BETA_ONE, BETA_TWO], f32), step_count.astype(f32)
    )
    small_weights = (
        embedding,
        embedding_first,
        embedding_second,
        head_table.T,
        head_first.T,
        head_second.T,
        vectors,
        vectors_first,
        vectors_second,
        fc_bias,
        fc_bias_first,
        fc_bias_second,
    )
    *small_out, scalars = small(
        corrections,
        upper_pair[None],
        sums,
        hidden,
        hidden_parts,
        hidden_others,
        bias_grad,
        small_weights,
    )
    small_out[3:6] = [value.T for value in small_out[3:6]]
    results = soap(
        corrections,
        scalars,
        gradients,
        weight_tiles,
        tiles_first,
        tiles_second,
        stats_left,
        stats_right,
        basis_left,
        basis_right,
    )
    return (scalars[0, 1], scalars[0, 2], *results, *small_out)


def solution(mesh):
    tiled = P("dp", None, "mp")
    split = P(None, "mp")
    in_specs = (P("dp", None), P("dp"), P(), P(), *[tiled] * 7, *[P()] * 9, *[split] * 3)
    out_specs = (P(), P(), *[tiled] * 8, *[P()] * 9, *[split] * 3)
    return jax.shard_map(local, mesh=mesh, in_specs=in_specs, out_specs=out_specs, check_vma=False)
```
